128 devices in a mesh: dp: 16 (over z_lo, y, core), expert: 8 (over x, z_hi).
Axes of the slice: x: 4, y: 4, z: 4 (z_hi: 2, z_lo: 2; z = z_hi * 2 + z_lo), core: 2. Of those that a mesh axis runs over, the one named last changes fastest.
Arguments:
- tokens: bfloat16 [2, 8, 1280, 1536], P(None, 'expert', 'dp'), may hold values from -6 to 6
- lengths: int32 [2, 8, 3], P(None, 'expert'), may hold values from 1 to 1200, as said below
- routes: int32 [2, 8, 1280, 6], P(None, 'expert', 'dp'), may hold values from 0 to 15, all different within a row; in each aligned block of 80 rows (0 to 79, 80 to 159, ..., all dimensions but the last counted through in order) at most 45 rows name the same one
- cotangent: bfloat16 [2, 8, 1280, 1536], P(None, 'expert', 'dp'), may hold values from -6 to 6
- input_weight: bfloat16 [1536, 6448], P('dp'), may hold values from -0.15625 to 0.15625
- filter_weight: float32 [4, 3328], replicated, may hold values from -3 to 3
- filter_bias: float32 [3328], replicated, may hold values from -3 to 3
- step_bias: float32 [48], replicated, may hold values from -6.9 to -2.25
- decay_log: float32 [48], replicated, may hold values from 0 to 3
- skip_gain: float32 [48], replicated, may hold values from 0.5 to 1.5
- norm_gain: float32 [1536], replicated, may hold values from 0.5 to 1.5
- gated_gain: float32 [3072], replicated, may hold values from 0.5 to 1.5
- output_weight: bfloat16 [3072, 1536], P('dp'), may hold values from -0.109375 to 0.109375
- moe_gain: float32 [1536], replicated, may hold values from 0.5 to 1.5
- router_weight: bfloat16 [1536, 16], P('dp'), may hold values from -0.078125 to 0.078125
- shared_gate_up: bfloat16 [1536, 2048], P('dp'), may hold values from -0.15625 to 0.15625
- shared_down: bfloat16 [1024, 1536], P('dp'), may hold values from -0.375 to 0.375
- expert_gate_up: bfloat16 [16, 1536, 1024], P('expert'), may hold values from -0.15625 to 0.15625
- expert_down: bfloat16 [16, 512, 1536], P('expert'), may hold values from -1 to 1
Outputs:
- block_output: bfloat16 [2, 8, 1280, 1536], P(None, 'expert', 'dp')
- tokens_grad: float32 [2, 8, 1280, 1536], P(None, 'expert', 'dp')
- input_weight_grad: float32 [1536, 6448], P('dp')
- filter_weight_grad: float32 [4, 3328], replicated
- filter_bias_grad: float32 [3328], replicated
- step_bias_grad: float32 [48], replicated
- decay_log_grad: float32 [48], replicated
- skip_gain_grad: float32 [48], replicated
- norm_gain_grad: float32 [1536], replicated
- gated_gain_grad: float32 [3072], replicated
- output_weight_grad: float32 [3072, 1536], P('dp')
- moe_gain_grad: float32 [1536], replicated
- router_weight_grad: float32 [1536, 16], P('dp')
- shared_gate_up_grad: float32 [1536, 2048], P('dp')
- shared_down_grad: float32 [1024, 1536], P('dp')
- expert_gate_up_grad: float32 [16, 1536, 1024], P('expert', 'dp')
- expert_down_grad: float32 [16, 512, 1536], P('expert', 'dp')
The draws below stay inside these ranges and needn't reach their ends.
Inputs may be any that keep to these rules, and one draw needn't show every extreme that they name: Each row gives the lengths of the three documents packed in order into one group's 1280 positions; the first and the last have 80 tokens together, each at least 1, so the middle one has 1200. `routes`: each row names 6 different experts. Within the rows of one device (aligned blocks of 80 rows) no expert is named by more than 45 rows, and in some blocks one expert is named by exactly 45.
All inputs are finite; a program needn't handle non-finite values.
Results may differ from the reference program's by a relative error of at most 0.024.
Values may be sent and summed in bfloat16 or wider, within the bound.
A program may use at most 384 MiB of HBM per device.

```python
import math
import jax
import jax.numpy as jnp
import numpy as np
from jax import lax

D = 1536
H = 48
P_SIZE = 64
S = 128
K = 4
FE = 512
FS = 1024
TOP = 6
MB = 2
DI = 3072
CONV = 3328
IN_W = 6448
EXPERTS = 16
GROUPS = 8
GROUP_TOK = 1280
LOCAL = 80
CAP = 45


def draw_lengths(key, part):
    key = jax.random.fold_in(key, 11)
    first = jax.random.randint(key, (MB, GROUPS, 1), 1, LOCAL)
    middle = jnp.zeros_like(first) + (GROUP_TOK - LOCAL)
    return jnp.concatenate([first, middle, LOCAL - first], axis=2).astype(jnp.int32)


def block_levels(key, shape, cuts, least, high):
    def one(dim, blocks):
        heights = jax.random.uniform(jax.random.fold_in(jax.random.fold_in(key, 6), dim), (blocks,), jnp.float32, least / len(cuts), high / len(cuts))
        return jnp.repeat(jnp.exp(heights), shape[dim] // blocks).reshape((-1,) + (1,) * (len(shape) - dim - 1))

    level = one(*cuts[0])
    for cut in cuts[1:]:
        level = level * one(*cut)
    return level


def assign_block(own_key, own, number, rows, number_of, top, limit, lean):
    sequence = jax.random.permutation(own_key, number_of)
    packed, ordinary = load_shares(number_of, rows * top, limit, lean, True), load_shares(number_of, rows * top, limit, lean, False)
    places = jnp.arange(number_of)

    def named(sizes, turn):
        used = int((sizes > 0).sum())
        fixed = max(1, used // 4)
        shifted = fixed + (places - fixed + turn * (used - fixed)) % max(1, number_of - fixed)
        return jnp.zeros((number_of,), jnp.int32).at[sequence[jnp.where(places < fixed, places, shifted)]].set(jnp.asarray(sizes, jnp.int32))

    sizes = jnp.where(number % 4 == 0, named(packed, number // 4), named(ordinary, number - number // 4 - 1))
    mixed = jax.random.permutation(jax.random.fold_in(own, 3), number_of)
    donor, sink = mixed[0:number_of // 2 * 2:2], mixed[1:number_of // 2 * 2:2]
    room = jnp.minimum(sizes[donor] - 1, limit - sizes[sink]) // 2
    room = jnp.where((donor == sequence[0]) | (sink == sequence[0]) | (sizes[sink] == 0), 0, jnp.maximum(room, 0))
    shifted = jax.random.randint(jax.random.fold_in(own, 4), (number_of // 2,), 0, 1 << 20) % (room + 1)
    sizes = sizes.at[donor].add(-shifted).at[sink].add(shifted)
    items = jnp.searchsorted(jnp.cumsum(sizes), jnp.arange(rows * top), side="right").astype(jnp.int32)
    grid = items.reshape(top, rows).T
    grid = grid[jax.random.permutation(jax.random.fold_in(own, 1), rows)]
    turn = jax.random.randint(jax.random.fold_in(own, 2), (rows, 1), 0, top)
    return jnp.take_along_axis(grid, (jnp.arange(top)[None, :] + turn) % top, axis=1)


def load_shares(count, total, reach, skew, full):
    loads = [(1 << 20) // math.isqrt(rank ** skew) + 1 for rank in range(1, count + 1)]
    largest = reach if full else min(reach, max(-(-total // count), total * loads[0] // sum(loads)))
    least = 1 if total - largest >= count - 1 else 0
    given, surplus = [largest] + [least] * (count - 1), total - largest - least * (count - 1)
    while surplus > 0:
        free = [i for i in range(1, count) if given[i] < largest] or [i for i in range(1, count) if given[i] < reach]
        pool, remaining = sum([loads[i] for i in free]), surplus
        for i in free:
            more = min(reach - given[i], max(1, remaining * loads[i] // pool), surplus)
            given[i] = given[i] + more
            surplus = surplus - more
    return np.array(given)


def noise(key, dims, deviation, most, shards=(), kind=jnp.bfloat16):
    level = block_levels(key, dims, shards, -0.22, 0.18) if shards else 1.0
    drawn = jax.random.normal(key, dims, jnp.float32) * deviation * level
    return jnp.minimum(jnp.maximum(drawn, -most), most).astype(kind)


def setup_inputs(seed: int = 0) -> dict:
    arg_keys = jax.random.split(jax.random.key(seed), 20)
    tokens = noise(arg_keys[0], (MB, GROUPS, GROUP_TOK, D), 1.0, 6.0, ((1, 8), (2, 16)))
    lengths = draw_lengths(jax.random.fold_in(arg_keys[19], 71), 0)
    routes_keys = jax.random.split(jax.random.fold_in(arg_keys[2], 1), MB * GROUPS * GROUP_TOK // LOCAL)
    routes_turns = jax.random.permutation(jax.random.fold_in(arg_keys[2], 3), MB * GROUPS * GROUP_TOK // LOCAL)
    routes = jax.vmap(lambda own, number: assign_block(jax.random.fold_in(arg_keys[2], 2), own, number, LOCAL, EXPERTS, TOP, CAP, 1))(routes_keys, routes_turns).reshape((MB, GROUPS, GROUP_TOK, TOP))
    cotangent = noise(arg_keys[3], (MB, GROUPS, GROUP_TOK, D), 1.0, 6.0, ((1, 8), (2, 16)))
    input_weight = noise(arg_keys[4], (D, IN_W), D ** -0.5, 0.15625, ((0, 16),))
    filter_weight = noise(arg_keys[5], (K, CONV), K ** -0.5, 3.0, (), jnp.float32)
    filter_bias = noise(arg_keys[6], (CONV,), 0.5, 3.0, (), jnp.float32)
    step_bias = jnp.clip(jax.random.uniform(arg_keys[7], (H,), jnp.float32, -6.9, -2.25), -6.9, -2.25)
    decay_log = jnp.clip(jax.random.uniform(arg_keys[8], (H,), jnp.float32, 0.0, 3.0), 0.0, 3.0)
    skip_gain = jnp.clip(jax.random.uniform(arg_keys[9], (H,), jnp.float32, 0.5, 1.5), 0.5, 1.5)
    norm_gain = jnp.clip(1.0 + 0.1 * jax.random.normal(arg_keys[10], (D,), jnp.float32), 0.5, 1.5)
    gated_gain = jnp.clip(1.0 + 0.1 * jax.random.normal(arg_keys[11], (DI,), jnp.float32), 0.5, 1.5)
    output_weight = noise(arg_keys[12], (DI, D), DI ** -0.5, 0.109375, ((0, 16),))
    moe_gain = jnp.clip(1.0 + 0.1 * jax.random.normal(arg_keys[13], (D,), jnp.float32), 0.5, 1.5)
    router_weight = noise(arg_keys[14], (D, EXPERTS), (4 * D) ** -0.5, 0.078125, ((0, 16),))
    shared_gate_up = noise(arg_keys[15], (D, 2 * FS), D ** -0.5, 0.15625, ((0, 16),))
    shared_down = noise(arg_keys[16], (FS, D), (FS // 4) ** -0.5, 0.375, ((0, 16),))
    expert_gate_up = noise(arg_keys[17], (EXPERTS, D, 2 * FE), D ** -0.5, 0.15625, ((0, 8),))
    expert_down = noise(arg_keys[18], (EXPERTS, FE, D), (FE // 16) ** -0.5, 1.0, ((0, 8),))
    return {"tokens": tokens, "lengths": lengths, "routes": routes, "cotangent": cotangent, "input_weight": input_weight, "filter_weight": filter_weight, "filter_bias": filter_bias, "step_bias": step_bias, "decay_log": decay_log, "skip_gain": skip_gain, "norm_gain": norm_gain, "gated_gain": gated_gain, "output_weight": output_weight, "moe_gain": moe_gain, "router_weight": router_weight, "shared_gate_up": shared_gate_up, "shared_down": shared_down, "expert_gate_up": expert_gate_up, "expert_down": expert_down}


HIGHEST = lax.Precision.HIGHEST
EPSILON = 1e-05

@jax.custom_vjp
def low(v):
    return lax.optimization_barrier(v.astype(jnp.bfloat16)).astype(jnp.float32)

@jax.custom_vjp
def low_back(v):
    return v

def low_keep(v):
    return (low(v), None)

def low_pass(kept, grad):
    return (grad,)

def back_keep(v):
    return (v, None)

def back_low(kept, grad):
    return (low(grad),)
low.defvjp(low_keep, low_pass)
low_back.defvjp(back_keep, back_low)

def rms_scale(values, gain):
    return values * lax.rsqrt(lax.optimization_barrier(jnp.mean(values * values, axis=-1, keepdims=True)) + EPSILON) * gain

def doc_number(positions, lengths_row):
    first = (positions >= lengths_row[0]).astype(jnp.int32)
    return first + (positions >= lengths_row[0] + lengths_row[1]).astype(jnp.int32)

def filter_apply(extended, filter_weight, filter_bias, docs_ext, docs):
    count = docs.shape[0]
    total = jnp.zeros((count, CONV), jnp.float32) + filter_bias[None, :]
    for offset in range(K):
        same_doc = (docs_ext[offset:offset + count] == docs).astype(jnp.float32)
        total = total + same_doc[:, None] * filter_weight[offset][None, :] * extended[offset:offset + count]
    return jax.nn.silu(total)

def prepare(filtered, step_raw, step_bias):
    count = filtered.shape[0]
    head_inputs = filtered[:, :DI].reshape(count, H, P_SIZE)
    write_proj = filtered[:, DI:DI + S]
    read_proj = filtered[:, DI + S:]
    step_size = jax.nn.softplus(step_raw + step_bias[None, :])
    return (head_inputs, write_proj, read_proj, step_size)

def block_cumulative(step_size, decay_log):
    return jnp.cumsum(step_size * (-jnp.exp(decay_log))[None, :], axis=0)

def carry_terms(head_inputs, write_proj, step_size, cumulative, docs, keep_last):
    last = cumulative[-1]
    same_last = (docs == docs[-1]).astype(jnp.float32)
    weight = jnp.exp(last[None, :] - cumulative) * same_last[:, None] * step_size
    scaled = head_inputs * weight[:, :, None]
    state = jnp.einsum('shp,sn->hpn', scaled, write_proj, precision=HIGHEST)
    return (jnp.exp(last) * keep_last, state)

def scan_readout(head_inputs, write_proj, read_proj, step_size, cumulative, docs, keep, state_in, skip_gain):
    count = docs.shape[0]
    scores = jnp.dot(read_proj, write_proj.T, precision=HIGHEST)
    rows = lax.broadcasted_iota(jnp.int32, (count, count), 0)
    cols = lax.broadcasted_iota(jnp.int32, (count, count), 1)
    allowed = (cols <= rows) & (docs[:, None] == docs[None, :])
    spans = cumulative.T[:, :, None] - cumulative.T[:, None, :]
    weights = jnp.exp(jnp.where(allowed[None], spans, -1e+30)) * scores[None]
    scaled = head_inputs * step_size[:, :, None]
    inner = jnp.einsum('hts,shp->thp', weights, scaled, precision=HIGHEST)
    carry_gate = jnp.exp(cumulative) * keep[:, None]
    carried = jnp.einsum('tn,hpn->thp', read_proj, state_in, precision=HIGHEST) * carry_gate[:, :, None]
    return inner + carried + skip_gain[None, :, None] * head_inputs

def block_group(stream, lengths_row, route_rows, weights):
    input_weight, filter_weight, filter_bias, step_bias, decay_log, skip_gain, norm_gain, gated_gain, output_weight, moe_gain, router_weight, shared_gate_up, shared_down, expert_gate_up, expert_down = weights
    positions = jnp.arange(GROUP_TOK, dtype=jnp.int32)
    docs = doc_number(positions, lengths_row)
    docs_ext = doc_number(jnp.arange(GROUP_TOK + K - 1, dtype=jnp.int32) - (K - 1), lengths_row)
    normed = low(rms_scale(stream, norm_gain))
    projected = low_back(jnp.dot(normed, input_weight, precision=HIGHEST))
    gate_part = projected[:, :DI]
    filter_in = low(projected[:, DI:DI + CONV])
    step_raw = projected[:, DI + CONV:]
    extended = jnp.concatenate([jnp.zeros((K - 1, CONV), jnp.float32), filter_in], axis=0)
    filtered = filter_apply(extended, filter_weight, filter_bias, docs_ext, docs)
    head_inputs, write_proj, read_proj, step_size = prepare(filtered, step_raw, step_bias)
    blocks = GROUP_TOK // LOCAL

    def block_step(state, pieces):
        block_inputs, block_write, block_read, block_steps, block_docs, start = pieces
        cumulative = block_cumulative(block_steps, decay_log)
        keep = (block_docs == doc_number(start - 1, lengths_row)).astype(jnp.float32)
        decay, local_state = carry_terms(block_inputs, block_write, block_steps, cumulative, block_docs, keep[-1])
        result = scan_readout(block_inputs, block_write, block_read, block_steps, cumulative, block_docs, keep, state, skip_gain)
        return (decay[:, None, None] * state + local_state, result)
    starts = jnp.arange(blocks, dtype=jnp.int32) * LOCAL
    pieces = (head_inputs.reshape(blocks, LOCAL, H, P_SIZE), write_proj.reshape(blocks, LOCAL, S), read_proj.reshape(blocks, LOCAL, S), step_size.reshape(blocks, LOCAL, H), docs.reshape(blocks, LOCAL), starts)
    _, results = lax.scan(jax.checkpoint(block_step), jnp.zeros((H, P_SIZE, S), jnp.float32), pieces)
    scan_out = results.reshape(GROUP_TOK, DI)
    gated = low(rms_scale(scan_out * jax.nn.silu(gate_part), gated_gain))
    mixer = low_back(jnp.dot(gated, output_weight, precision=HIGHEST))
    after_mixer = stream + mixer
    moe_in = low(rms_scale(after_mixer, moe_gain))
    logits = jnp.dot(moe_in, router_weight, precision=HIGHEST)
    gates = jax.nn.softmax(jnp.take_along_axis(logits, route_rows, axis=1), axis=1)
    chosen = (route_rows[:, :, None] == jnp.arange(EXPERTS, dtype=jnp.int32)[None, None, :]).astype(jnp.float32)
    table = lax.optimization_barrier(jnp.sum(chosen * gates[:, :, None], axis=1))
    shared_pre = low_back(jnp.dot(moe_in, shared_gate_up, precision=HIGHEST))
    shared_hidden = low(jax.nn.silu(shared_pre[:, :FS]) * shared_pre[:, FS:])
    shared_out = low_back(jnp.dot(shared_hidden, shared_down, precision=HIGHEST))

    def expert_step(total, pieces):
        gate_up, down_matrix, column = pieces
        expert_pre = low_back(jnp.dot(moe_in, gate_up, precision=HIGHEST))
        expert_hidden = low(jax.nn.silu(expert_pre[:, :FE]) * expert_pre[:, FE:])
        expert_out = low_back(low(jnp.dot(expert_hidden, down_matrix, precision=HIGHEST)))
        return (total + column[:, None] * expert_out, None)
    moe_sum, _ = lax.scan(jax.checkpoint(expert_step), jnp.zeros((GROUP_TOK, D), jnp.float32), (expert_gate_up, expert_down, table.T))
    return after_mixer + moe_sum + shared_out

def reference(tokens, lengths, routes, cotangent, input_weight, filter_weight, filter_bias, step_bias, decay_log, skip_gain, norm_gain, gated_gain, output_weight, moe_gain, router_weight, shared_gate_up, shared_down, expert_gate_up, expert_down):
    weights = (input_weight.astype(jnp.float32), filter_weight.astype(jnp.float32), filter_bias.astype(jnp.float32), step_bias.astype(jnp.float32), decay_log.astype(jnp.float32), skip_gain.astype(jnp.float32), norm_gain.astype(jnp.float32), gated_gain.astype(jnp.float32), output_weight.astype(jnp.float32), moe_gain.astype(jnp.float32), router_weight.astype(jnp.float32), shared_gate_up.astype(jnp.float32), shared_down.astype(jnp.float32), expert_gate_up.astype(jnp.float32), expert_down.astype(jnp.float32))
    stream = tokens.astype(jnp.float32).reshape(MB * GROUPS, GROUP_TOK, D)
    lengths_flat = lengths.reshape(MB * GROUPS, 3)
    routes_flat = routes.reshape(MB * GROUPS, GROUP_TOK, TOP)

    def forward(stream_all, *weight_list):

        def one_group(pieces):
            return block_group(pieces[0], pieces[1], pieces[2], weight_list)
        return lax.map(jax.checkpoint(one_group), (stream_all, lengths_flat, routes_flat))
    result, pull = jax.vjp(forward, stream, *weights)
    grads = pull(cotangent.astype(jnp.float32).reshape(MB * GROUPS, GROUP_TOK, D))
    shape = (MB, GROUPS, GROUP_TOK, D)
    return (result.reshape(shape).astype(jnp.bfloat16), grads[0].reshape(shape), grads[1], grads[2], grads[3], grads[4], grads[5], grads[6], grads[7], grads[8], grads[9], grads[10], grads[11], grads[12], grads[13], grads[14], grads[15])
```

```python
import jax
import jax.numpy as jnp
from jax import lax
from jax.sharding import PartitionSpec as P

D = 1536
H = 48
PS = 64
S = 128
K = 4
FE = 512
FS = 1024
TOP = 6
MB = 2
DI = 3072
CONV = 3328
IN_W = 6448
EPSILON = 1e-05
BF = jnp.bfloat16
F32 = jnp.float32


def mm(a, b):
    return jnp.dot(a, b, preferred_element_type=F32)


def mm_nt(a, b):
    return lax.dot_general(a, b, (((1,), (1,)), ((), ())), preferred_element_type=F32)


def mm_tn(a, b):
    return lax.dot_general(a, b, (((0,), (0,)), ((), ())), preferred_element_type=F32)


def rms_scale(values, gain):
    return values * lax.rsqrt(jnp.mean(values * values, axis=-1, keepdims=True) + EPSILON) * gain


def doc_number(positions, lengths_rows):
    first = (positions >= lengths_rows[:, :1]).astype(jnp.int32)
    return first + (positions >= lengths_rows[:, :1] + lengths_rows[:, 1:2]).astype(jnp.int32)


def hi_lo(v):
    hi = v.astype(BF)
    return hi, (v - hi.astype(F32)).astype(BF)


def mixer_local(proj, taps, tap_bias, bias_steps, decay_log, skip, docs, docs_ext, heads):
    nb, mb, loc, _ = proj.shape
    di = heads * PS
    width = di + 2 * S
    gate = proj[..., :di]
    seq = jnp.moveaxis(proj[..., di : di + width], 0, 1).reshape(mb, nb * loc, width)
    seq = seq.astype(BF).astype(F32)
    raw = proj[..., di + width : di + width + heads]
    ext = jnp.pad(seq, ((0, 0), (K - 1, 0), (0, 0)))
    count = nb * loc
    total = jnp.zeros((mb, count, width), F32) + tap_bias
    for k in range(K):
        same = (docs_ext[:, k : k + count] == docs).astype(F32)
        total = total + same[:, :, None] * taps[k] * ext[:, k : k + count]
    filtered = jnp.moveaxis(jax.nn.silu(total).reshape(mb, nb, loc, width), 1, 0)
    x = filtered[..., :di].reshape(nb, mb, loc, heads, PS)
    write = filtered[..., di : di + S]
    read = filtered[..., di + S :]
    steps = jax.nn.softplus(raw + bias_steps)
    cum = jnp.cumsum(steps * (-jnp.exp(decay_log)), axis=2)
    bdocs = jnp.moveaxis(docs.reshape(mb, nb, loc), 1, 0)
    last_doc = bdocs[:, :, -1]
    prev_doc = jnp.concatenate([jnp.zeros_like(last_doc[:1]), last_doc[:-1]], axis=0)
    keep = (bdocs == prev_doc[:, :, None]).astype(F32)
    last = cum[:, :, -1]
    same_last = (bdocs == last_doc[:, :, None]).astype(F32)
    weight = jnp.exp(last[:, :, None] - cum) * same_last[..., None] * steps
    scaled = x * weight[..., None]
    states = jnp.einsum("bmshp,bmsn->mhbpn", scaled, write)
    running = jnp.cumsum(last, axis=0)
    before = running - last
    spans = before[:, None] - running[None]
    rows = lax.broadcasted_iota(jnp.int32, (nb, nb), 0)
    cols = lax.broadcasted_iota(jnp.int32, (nb, nb), 1)
    passes = (cols < rows)[:, :, None] & (prev_doc[:, None] == last_doc[None])
    chain = jnp.exp(jnp.where(passes[..., None], spans, -1e30))
    state_in = jnp.einsum("bcmh,mhcpn->mhbpn", chain, states)
    scores = jnp.einsum("bmtn,bmsn->bmts", read, write)
    r2 = lax.broadcasted_iota(jnp.int32, (loc, loc), 0)
    c2 = lax.broadcasted_iota(jnp.int32, (loc, loc), 1)
    allowed = (c2 <= r2) & (bdocs[:, :, :, None] == bdocs[:, :, None, :])
    cum_t = jnp.moveaxis(cum, 3, 2)
    inner_spans = cum_t[..., :, None] - cum_t[..., None, :]
    weights = jnp.exp(jnp.where(allowed[:, :, None], inner_spans, -1e30)) * scores[:, :, None]
    inner = jnp.einsum("bmhts,bmshp->bmthp", weights, x * steps[..., None])
    carried = jnp.einsum("bmtn,mhbpn->bmthp", read, state_in)
    carried = carried * (jnp.exp(cum) * keep[..., None])[..., None]
    out = inner + carried + skip[:, None] * x
    return out.reshape(nb, mb, loc, di) * jax.nn.silu(gate)


def body(
    tokens,
    lengths,
    routes,
    cotangent,
    input_weight,
    filter_weight,
    filter_bias,
    step_bias,
    decay_log,
    skip_gain,
    norm_gain,
    gated_gain,
    output_weight,
    moe_gain,
    router_weight,
    shared_gate_up,
    shared_down,
    expert_gate_up,
    expert_down,
):
    nd, ne = lax.axis_size("dp"), lax.axis_size("expert")
    me_d, me_e = lax.axis_index("dp"), lax.axis_index("expert")
    loc = tokens.shape[2]
    heads = H // nd
    di = heads * PS
    rows_t = MB * loc
    experts = expert_gate_up.shape[0] * ne
    el = expert_gate_up.shape[0]
    dr = D // nd
    fs = FS // ne
    fsr = FS // nd
    fsl = fsr // ne

    pad = 128 - heads
    blocks = jnp.concatenate(
        [
            jnp.moveaxis(input_weight[:, :DI].reshape(dr, nd, di), 1, 0),
            jnp.moveaxis(input_weight[:, DI : 2 * DI].reshape(dr, nd, di), 1, 0),
            jnp.broadcast_to(input_weight[None, :, 2 * DI : 2 * DI + 2 * S], (nd, dr, 2 * S)),
            jnp.moveaxis(input_weight[:, DI + CONV :].reshape(dr, nd, heads), 1, 0),
            jnp.zeros((nd, dr, pad), BF),
        ],
        axis=2,
    )
    w_in = lax.all_to_all(blocks, "dp", 0, 0, tiled=True).reshape(D, -1)
    wcols = w_in.shape[1]

    sg = shared_gate_up.reshape(dr, 2, nd, ne, fsl)
    sg = lax.dynamic_index_in_dim(sg, me_e, 3, False).reshape(dr, 2 * fs)
    sd = lax.dynamic_slice_in_dim(shared_down, me_e * fsl, fsl, 0)
    sg_full = lax.all_gather(sg, "dp", axis=0, tiled=True)
    sd_full = lax.all_gather(sd, "dp", axis=0, tiled=True)
    router_full = lax.all_gather(router_weight, "dp", axis=0, tiled=True)

    stream = tokens.reshape(rows_t, D).astype(F32)
    incoming = cotangent.reshape(rows_t, D)
    route_rows = routes.reshape(rows_t, TOP)
    inc_all = lax.all_gather(incoming, "expert", axis=0, tiled=True)

    normed_wide, norm_pull = jax.vjp(rms_scale, stream, norm_gain)
    normed = normed_wide.astype(BF)
    normed_all = lax.all_gather(normed, "dp", axis=0, tiled=True)
    proj = mm(normed_all, w_in).reshape(nd, MB, loc, wcols)

    count = nd * loc
    docs = doc_number(jnp.arange(count, dtype=jnp.int32)[None], lengths[:, 0])
    docs_ext = doc_number(jnp.arange(count + K - 1, dtype=jnp.int32)[None] - (K - 1), lengths[:, 0])
    taps = jnp.concatenate(
        [lax.dynamic_slice_in_dim(filter_weight, me_d * di, di, 1), filter_weight[:, DI:]], axis=1
    )
    tap_bias = jnp.concatenate(
        [lax.dynamic_slice_in_dim(filter_bias, me_d * di, di, 0), filter_bias[DI:]], axis=0
    )
    my_heads = lambda v: lax.dynamic_slice_in_dim(v, me_d * heads, heads, 0)
    my_gain = lax.dynamic_slice_in_dim(gated_gain, me_d * di, di, 0)

    def mixer(p, a, b, c, d, e):
        return mixer_local(p, a, b, c, d, e, docs, docs_ext, heads)

    y, mixer_pull = jax.vjp(
        mixer, proj, taps, tap_bias, my_heads(step_bias), my_heads(decay_log), my_heads(skip_gain)
    )
    y = y.reshape(nd * rows_t, di)
    square = jnp.sum(y * y, axis=1, keepdims=True)
    partial = mm((y * my_gain).astype(BF), output_weight)
    sq_hi, sq_lo = hi_lo(square)
    payload = jnp.concatenate(
        [partial.astype(BF), sq_hi, sq_lo, jnp.zeros((nd * rows_t, 126), BF)], axis=1
    )
    summed = lax.psum_scatter(payload, "dp", scatter_dimension=0, tiled=True).astype(F32)
    r = lax.rsqrt((summed[:, D : D + 1] + summed[:, D + 1 : D + 2]) / DI + EPSILON)
    mixed = summed[:, :D] * r
    after_mixer = stream + mixed
    moe_wide, moe_pull = jax.vjp(rms_scale, after_mixer, moe_gain)
    moe_in = moe_wide.astype(BF)
    logits = mm(moe_in, router_full)
    chosen = (route_rows[:, :, None] == jnp.arange(experts, dtype=jnp.int32)).astype(F32)
    picked = jnp.sum(chosen * logits[:, None, :], axis=2)
    gates = jax.nn.softmax(picked, axis=1)
    table = jnp.sum(chosen * gates[:, :, None], axis=1)
    t_hi, t_lo = hi_lo(table)
    moe_payload = jnp.concatenate(
        [moe_in, t_hi, t_lo, jnp.zeros((rows_t, 128 - 2 * experts), BF)], axis=1
    )
    moe_all = lax.all_gather(moe_payload, "expert", axis=0, tiled=True)
    x_all = moe_all[:, :D]
    table_all = moe_all[:, D : D + experts].astype(F32) + moe_all[
        :, D + experts : D + 2 * experts
    ].astype(F32)
    my_gates = lax.dynamic_slice_in_dim(table_all, me_e * el, el, 1)
    n_tok = x_all.shape[0]

    w_up = jnp.concatenate(
        [expert_gate_up[i][:, :FE] for i in range(el)]
        + [sg_full[:, :fs]]
        + [expert_gate_up[i][:, FE:] for i in range(el)]
        + [sg_full[:, fs:]],
        axis=1,
    )
    w_down = jnp.concatenate([expert_down[i] for i in range(el)] + [sd_full], axis=0)
    width = w_down.shape[0]
    scale = jnp.concatenate(
        [jnp.broadcast_to(my_gates[:, i : i + 1], (n_tok, FE)) for i in range(el)]
        + [jnp.ones((n_tok, fs), F32)],
        axis=1,
    )
    pre = mm(x_all, w_up)
    a, b = pre[:, :width], pre[:, width:]
    sig = jax.nn.sigmoid(a)
    act = a * sig
    hidden = act * b
    u = mm_nt(inc_all, w_down)
    prod = u * hidden
    gate_grad = jnp.concatenate(
        [jnp.sum(prod[:, i * FE : (i + 1) * FE], axis=1, keepdims=True) for i in range(el)], axis=1
    )
    gh = (scale * hidden).astype(BF)
    gu = scale * u
    pre_grad = jnp.concatenate(
        [gu * b * (sig + act * (1.0 - sig)), gu * act], axis=1
    ).astype(BF)
    out_part = mm(gh, w_down)
    dx_part = mm_nt(pre_grad, w_up)
    d_up = mm_tn(x_all, pre_grad)
    d_down = mm_tn(gh, inc_all)
    spread = lax.dynamic_update_slice(
        jnp.zeros((n_tok, experts), F32), gate_grad, (0, me_e * el)
    )
    s_hi, s_lo = hi_lo(spread)
    back = jnp.concatenate(
        [
            out_part.astype(BF),
            dx_part.astype(BF),
            s_hi,
            s_lo,
            jnp.zeros((n_tok, 128 - 2 * experts), BF),
        ],
        axis=1,
    )
    back_sum = lax.psum_scatter(back, "expert", scatter_dimension=0, tiled=True).astype(F32)
    block_output = (after_mixer + back_sum[:, :D]).astype(BF)
    inc = incoming.astype(F32)
    spread_sum = (
        back_sum[:, 2 * D : 2 * D + experts] + back_sum[:, 2 * D + experts : 2 * D + 2 * experts]
    )
    logit_grad = table * (spread_sum - jnp.sum(table * spread_sum, axis=1, keepdims=True))
    logit_low = logit_grad.astype(BF)
    router_part = mm_tn(moe_in, logit_low)
    moe_in_grad = back_sum[:, D : 2 * D] + mm_nt(logit_low, router_full)
    after_from_norm, moe_gain_grad = moe_pull(moe_in_grad)
    after_grad = inc + after_from_norm
    after_low = after_grad.astype(BF)
    s = jnp.sum(after_low.astype(F32) * mixed, axis=1, keepdims=True)
    r_hi, r_lo = hi_lo(r)
    d_hi, d_lo = hi_lo(s)
    grad_payload = jnp.concatenate(
        [after_low, r_hi, r_lo, d_hi, d_lo, jnp.zeros((rows_t, 124), BF)], axis=1
    )
    grad_all = lax.all_gather(grad_payload, "dp", axis=0, tiled=True)
    after_all = grad_all[:, :D]
    extra = grad_all[:, D : D + 4].astype(F32)
    r_all = extra[:, 0:1] + extra[:, 1:2]
    s_all = extra[:, 2:3] + extra[:, 3:4]
    gated_grad = mm_nt(after_all, output_weight)
    yr = y * r_all
    output_part = mm_tn((yr * my_gain).astype(BF), after_all)
    gated_gain_part = jnp.sum(gated_grad * yr, axis=0)
    dy = r_all * (gated_grad * my_gain) - yr * (r_all * s_all / DI)
    pulls = mixer_pull(dy.reshape(nd, MB, loc, di))
    d_proj = pulls[0].astype(BF).reshape(nd * rows_t, wcols)
    normed_part = mm_nt(d_proj, w_in)
    normed_grad = lax.psum_scatter(
        normed_part.astype(BF), "dp", scatter_dimension=0, tiled=True
    ).astype(F32)
    d_win = mm_tn(normed_all, d_proj).astype(BF)
    stream_from_norm, norm_gain_grad = norm_pull(normed_grad)
    tokens_grad = after_grad + stream_from_norm

    back_in = lax.all_to_all(d_win.reshape(nd, dr, wcols), "dp", 0, 0, tiled=True)
    in_rows = jnp.concatenate(
        [
            jnp.moveaxis(back_in[:, :, :di], 0, 1).reshape(dr, DI),
            jnp.moveaxis(back_in[:, :, di : 2 * di], 0, 1).reshape(dr, DI),
            jnp.sum(back_in[:, :, 2 * di : 2 * di + 2 * S].astype(F32), axis=0).astype(BF),
            jnp.moveaxis(back_in[:, :, 2 * di + 2 * S : 2 * di + 2 * S + heads], 0, 1).reshape(
                dr, H
            ),
        ],
        axis=1,
    )
    input_grad, output_grad = lax.psum((in_rows, output_part.astype(BF)), "expert")
    d_up = d_up.astype(BF)
    d_down = d_down.astype(BF)
    up_blocks = d_up.reshape(nd, dr, 2 * width)
    down_blocks = jnp.stack(
        [d_down[i * FE : (i + 1) * FE].reshape(nd, FE // nd, D) for i in range(el)], axis=1
    ).reshape(nd, el * FE // nd, D)
    down_blocks = jnp.concatenate([down_blocks, d_down[el * FE :].reshape(nd, fsl, D)], axis=1)
    up_sum = lax.psum_scatter(up_blocks, "dp", scatter_dimension=0, tiled=True)[0]
    down_sum = lax.psum_scatter(down_blocks, "dp", scatter_dimension=0, tiled=True)[0]
    expert_up_grad = jnp.stack(
        [
            jnp.concatenate(
                [
                    up_sum[:, i * FE : (i + 1) * FE],
                    up_sum[:, width + i * FE : width + (i + 1) * FE],
                ],
                axis=1,
            )
            for i in range(el)
        ],
        axis=0,
    ).astype(F32)
    expert_down_grad = down_sum[: el * FE // nd].reshape(el, FE // nd, D).astype(F32)
    sg_part = jnp.concatenate([up_sum[:, el * FE : width], up_sum[:, width + el * FE :]], axis=1)
    sg_all = lax.all_gather(sg_part, "expert")
    sd_all = lax.all_gather(down_sum[el * FE // nd :], "expert")
    shared_up_grad = (
        jnp.moveaxis(sg_all.reshape(ne, dr, 2, nd, fsl), 0, 3).reshape(dr, 2 * FS).astype(F32)
    )
    shared_down_grad = sd_all.reshape(fsr, D).astype(F32)

    def spread_heads(v, size, chunk):
        return lax.dynamic_update_slice(
            jnp.zeros(v.shape[:-1] + (size,), F32), v, (0,) * (v.ndim - 1) + (me_d * chunk,)
        )

    fw = jnp.concatenate([spread_heads(pulls[1][:, :di], DI, di), pulls[1][:, di:]], axis=1)
    fb = jnp.concatenate([spread_heads(pulls[2][:di], DI, di), pulls[2][di:]], axis=0)
    small = lax.psum(
        (
            fw,
            fb,
            spread_heads(pulls[3], H, heads),
            spread_heads(pulls[4], H, heads),
            spread_heads(pulls[5], H, heads),
            norm_gain_grad,
            spread_heads(gated_gain_part, DI, di),
            moe_gain_grad,
            router_part,
        ),
        ("dp", "expert"),
    )
    router_grad = lax.dynamic_slice_in_dim(small[8], me_d * dr, dr, 0)
    shape = (MB, 1, loc, D)
    return (
        block_output.reshape(shape),
        tokens_grad.reshape(shape),
        input_grad.astype(F32),
        small[0],
        small[1],
        small[2],
        small[3],
        small[4],
        small[5],
        small[6],
        output_grad.astype(F32),
        small[7],
        router_grad,
        shared_up_grad,
        shared_down_grad,
        expert_up_grad,
        expert_down_grad,
    )


def solution(mesh):
    in_specs = (
        P(None, "expert", "dp", None),
        P(None, "expert", None),
        P(None, "expert", "dp", None),
        P(None, "expert", "dp", None),
        P("dp", None),
        P(),
        P(),
        P(),
        P(),
        P(),
        P(),
        P(),
        P("dp", None),
        P(),
        P("dp", None),
        P("dp", None),
        P("dp", None),
        P("expert", None, None),
        P("expert", None, None),
    )
    out_specs = (
        P(None, "expert", "dp", None),
        P(None, "expert", "dp", None),
        P("dp", None),
        P(),
        P(),
        P(),
        P(),
        P(),
        P(),
        P(),
        P("dp", None),
        P(),
        P("dp", None),
        P("dp", None),
        P("dp", None),
        P("expert", "dp", None),
        P("expert", "dp", None),
    )
    return jax.shard_map(body, mesh=mesh, in_specs=in_specs, out_specs=out_specs, check_vma=False)
```

```python
import functools

import jax
import jax.numpy as jnp
from jax import lax
from jax.experimental import pallas as pl
from jax.experimental.pallas import tpu as pltpu
from jax.sharding import PartitionSpec as P

D = 1536
H = 48
PS = 64
S = 128
K = 4
FE = 512
FS = 1024
TOP = 6
MB = 2
DI = 3072
CONV = 3328
IN_W = 6448
EPSILON = 1e-05
BF = jnp.bfloat16
F32 = jnp.float32
MESH = pl.DeviceIdType.MESH
VMEM_LIMIT = 60 * 1024 * 1024


def mm(a, b):
    return jnp.dot(a, b, preferred_element_type=F32)


def mm_nt(a, b):
    return lax.dot_general(a, b, (((1,), (1,)), ((), ())), preferred_element_type=F32)


def mm_tn(a, b):
    return lax.dot_general(a, b, (((0,), (0,)), ((), ())), preferred_element_type=F32)


def rms_scale(values, gain):
    return values * lax.rsqrt(jnp.mean(values * values, axis=-1, keepdims=True) + EPSILON) * gain


def doc_number(positions, lengths_rows):
    first = (positions >= lengths_rows[:, :1]).astype(jnp.int32)
    return first + (positions >= lengths_rows[:, :1] + lengths_rows[:, 1:2]).astype(jnp.int32)


def hi_lo(v):
    hi = v.astype(BF)
    return hi, (v - hi.astype(F32)).astype(BF)


def mixer_local(proj, taps, tap_bias, bias_steps, decay_log, skip, docs, docs_ext, heads):
    nb, mb, loc, _ = proj.shape
    di = heads * PS
    width = di + 2 * S
    gate = proj[..., :di]
    seq = jnp.moveaxis(proj[..., di : di + width], 0, 1).reshape(mb, nb * loc, width)
    seq = seq.astype(BF).astype(F32)
    raw = proj[..., di + width : di + width + heads]
    ext = jnp.pad(seq, ((0, 0), (K - 1, 0), (0, 0)))
    count = nb * loc
    total = jnp.zeros((mb, count, width), F32) + tap_bias
    for k in range(K):
        same = (docs_ext[:, k : k + count] == docs).astype(F32)
        total = total + same[:, :, None] * taps[k] * ext[:, k : k + count]
    filtered = jnp.moveaxis(jax.nn.silu(total).reshape(mb, nb, loc, width), 1, 0)
    x = filtered[..., :di].reshape(nb, mb, loc, heads, PS)
    write = filtered[..., di : di + S]
    read = filtered[..., di + S :]
    steps = jax.nn.softplus(raw + bias_steps)
    cum = jnp.cumsum(steps * (-jnp.exp(decay_log)), axis=2)
    bdocs = jnp.moveaxis(docs.reshape(mb, nb, loc), 1, 0)
    last_doc = bdocs[:, :, -1]
    prev_doc = jnp.concatenate([jnp.zeros_like(last_doc[:1]), last_doc[:-1]], axis=0)
    keep = (bdocs == prev_doc[:, :, None]).astype(F32)
    last = cum[:, :, -1]
    same_last = (bdocs == last_doc[:, :, None]).astype(F32)
    weight = jnp.exp(last[:, :, None] - cum) * same_last[..., None] * steps
    scaled = x * weight[..., None]
    states = jnp.einsum("bmshp,bmsn->mhbpn", scaled, write)
    running = jnp.cumsum(last, axis=0)
    before = running - last
    spans = before[:, None] - running[None]
    rows = lax.broadcasted_iota(jnp.int32, (nb, nb), 0)
    cols = lax.broadcasted_iota(jnp.int32, (nb, nb), 1)
    passes = (cols < rows)[:, :, None] & (prev_doc[:, None] == last_doc[None])
    chain = jnp.exp(jnp.where(passes[..., None], spans, -1e30))
    state_in = jnp.einsum("bcmh,mhcpn->mhbpn", chain, states)
    scores = jnp.einsum("bmtn,bmsn->bmts", read, write)
    r2 = lax.broadcasted_iota(jnp.int32, (loc, loc), 0)
    c2 = lax.broadcasted_iota(jnp.int32, (loc, loc), 1)
    allowed = (c2 <= r2) & (bdocs[:, :, :, None] == bdocs[:, :, None, :])
    cum_t = jnp.moveaxis(cum, 3, 2)
    inner_spans = cum_t[..., :, None] - cum_t[..., None, :]
    weights = jnp.exp(jnp.where(allowed[:, :, None], inner_spans, -1e30)) * scores[:, :, None]
    inner = jnp.einsum("bmhts,bmshp->bmthp", weights, x * steps[..., None])
    carried = jnp.einsum("bmtn,mhbpn->bmthp", read, state_in)
    carried = carried * (jnp.exp(cum) * keep[..., None])[..., None]
    out = inner + carried + skip[:, None] * x
    return out.reshape(nb, mb, loc, di) * jax.nn.silu(gate)


def places(axis):
    me = lax.axis_index(axis)
    if axis == "dp":
        core, ring, pair = lax.rem(me, 2), lax.rem(me // 2, 4), me // 8

        def at(hop, other, sibling=0):
            z = lax.rem(pair + other, 2)
            return (z * 4 + lax.rem(ring + hop + 4, 4)) * 2 + lax.rem(core + sibling, 2)
    else:
        pair, ring = lax.rem(me, 2), me // 2

        def at(hop, other, sibling=0):
            return lax.rem(ring + hop + 4, 4) * 2 + lax.rem(pair + other, 2)

    return me, at


def greet(axis, peers):
    barrier = pltpu.get_barrier_semaphore()
    for peer in peers:
        pl.semaphore_signal(barrier, inc=1, device_id={axis: peer}, device_id_type=MESH)
    pl.semaphore_wait(barrier, len(peers))


def gather_kernel(axis, x, out, send, recv, own_sem):
    me, at = places(axis)
    cores = axis == "dp"
    half = x.shape[0] // 2
    up, down, pair, sib = at(1, 0), at(-1, 0), at(0, 1), at(0, 0, 1)
    greet(axis, [up, down, pair] + ([sib] if cores else []))
    whole = pl.ds(0, 2 * half)
    first, second = pl.ds(0, half), pl.ds(half, half)
    started = []

    def push(number, slot, rows, peer, src=None):
        copy = pltpu.make_async_remote_copy(
            src_ref=(out.at[slot] if src is None else src).at[rows],
            dst_ref=out.at[slot].at[rows],
            send_sem=send.at[number],
            recv_sem=recv.at[number],
            device_id={axis: peer},
            device_id_type=MESH,
        )
        copy.start()
        started.append(copy)

    def arrived(number, slot, rows):
        pltpu.make_async_copy(out.at[slot].at[rows], out.at[slot].at[rows], recv.at[number]).wait()

    push(0, me, whole, up, x)
    push(1, me, whole, down, x)
    push(2, me, whole, pair, x)
    if cores:
        push(3, me, whole, sib, x)
    own = pltpu.make_async_copy(x, out.at[me], own_sem)
    own.start()
    arrived(2, pair, whole)
    push(4, pair, whole, up)
    push(5, pair, whole, down)
    if cores:
        push(6, pair, whole, sib)
    arrived(0, down, whole)
    push(7, down, first, up)
    arrived(1, up, whole)
    push(8, up, second, down)
    if cores:
        push(9, down, whole, sib)
        push(10, up, whole, sib)
    arrived(4, at(-1, 1), whole)
    push(11, at(-1, 1), first, up)
    arrived(5, at(1, 1), whole)
    push(12, at(1, 1), second, down)
    if cores:
        push(13, at(-1, 1), whole, sib)
        push(14, at(1, 1), whole, sib)
    arrived(7, at(2, 0), first)
    arrived(8, at(2, 0), second)
    if cores:
        push(15, at(2, 0), whole, sib)
    arrived(11, at(2, 1), first)
    arrived(12, at(2, 1), second)
    if cores:
        push(16, at(2, 1), whole, sib)
        for number, hop, other in (
            (3, 0, 0),
            (6, 0, 1),
            (9, -1, 0),
            (10, 1, 0),
            (13, -1, 1),
            (14, 1, 1),
            (15, 2, 0),
            (16, 2, 1),
        ):
            arrived(number, at(hop, other, 1), whole)
    own.wait()
    for copy in started:
        copy.wait_send()


def gather(x, axis, number):
    n = lax.axis_size(axis)
    return pl.pallas_call(
        functools.partial(gather_kernel, axis),
        out_shape=jax.ShapeDtypeStruct((n,) + x.shape, x.dtype),
        in_specs=[pl.BlockSpec(memory_space=pl.ANY)],
        out_specs=pl.BlockSpec(memory_space=pl.ANY),
        scratch_shapes=[
            pltpu.SemaphoreType.DMA((17,)),
            pltpu.SemaphoreType.DMA((17,)),
            pltpu.SemaphoreType.DMA,
        ],
        compiler_params=pltpu.CompilerParams(
            collective_id=number, has_side_effects=True, vmem_limit_bytes=VMEM_LIMIT
        ),
        name="gather_" + axis,
    )(x)


ORDER = ((2, 1), (2, 0), (1, 1), (-1, 1), (1, 0), (-1, 0), (0, 1), (0, 0))


def reduce_kernel(axis, x, out, acc, sib_buf, a_buf, b_buf, c_buf, d_buf, e_buf, send, recv, load):
    me, at = places(axis)
    cores = axis == "dp"
    rows = x.shape[1]
    half = rows // 2
    step = 32 if half % 32 == 0 else 16
    up, down, pair, sib = at(1, 0), at(-1, 0), at(0, 1), at(0, 0, 1)
    greet(axis, [up, down, pair] + ([sib] if cores else []))
    whole, first, second = pl.ds(0, rows), pl.ds(0, half), pl.ds(half, half)
    started = []

    def push(number, src, dst, peer):
        copy = pltpu.make_async_remote_copy(
            src_ref=src,
            dst_ref=dst,
            send_sem=send.at[number],
            recv_sem=recv.at[number],
            device_id={axis: peer},
            device_id_type=MESH,
        )
        copy.start()
        started.append(copy)

    def arrived(number, dst):
        pltpu.make_async_copy(dst, dst, recv.at[number]).wait()

    def add(dst, offset, count, *srcs):
        @pl.loop(0, count // step)
        def _(i):
            at_rows = pl.ds(pl.multiple_of(offset + i * step, step), step)
            total = dst[at_rows, :].astype(F32)
            for src, src_offset in srcs:
                total += src[pl.ds(pl.multiple_of(src_offset + i * step, step), step), :].astype(F32)
            dst[at_rows, :] = total.astype(dst.dtype)

    loads = []
    for k, (hop, other) in enumerate(ORDER):
        if cores:
            push(k, x.at[at(hop, other, 1)], sib_buf.at[k], sib)
        copy = pltpu.make_async_copy(x.at[at(hop, other)], acc.at[k], load.at[k])
        copy.start()
        loads.append(copy)

    def ready(k):
        loads[k].wait()
        if cores:
            arrived(k, sib_buf.at[k])
            add(acc.at[k], 0, rows, (sib_buf.at[k], 0))

    ready(0)
    push(8, acc.at[0].at[first], a_buf.at[0], up)
    push(9, acc.at[0].at[second], b_buf.at[0], down)
    ready(1)
    push(10, acc.at[1].at[first], a_buf.at[1], up)
    push(11, acc.at[1].at[second], b_buf.at[1], down)
    ready(2)
    ready(3)
    arrived(8, a_buf.at[0])
    add(acc.at[2], 0, half, (a_buf.at[0], 0))
    push(12, acc.at[2], c_buf.at[0], up)
    arrived(9, b_buf.at[0])
    add(acc.at[3], half, half, (b_buf.at[0], 0))
    push(13, acc.at[3], d_buf.at[0], down)
    ready(4)
    ready(5)
    arrived(10, a_buf.at[1])
    add(acc.at[4], 0, half, (a_buf.at[1], 0))
    push(14, acc.at[4], c_buf.at[1], up)
    arrived(11, b_buf.at[1])
    add(acc.at[5], half, half, (b_buf.at[1], 0))
    push(15, acc.at[5], d_buf.at[1], down)
    ready(6)
    ready(7)
    arrived(12, c_buf.at[0])
    arrived(13, d_buf.at[0])
    add(acc.at[6], 0, rows, (c_buf.at[0], 0), (d_buf.at[0], 0))
    push(16, acc.at[6], e_buf, pair)
    arrived(14, c_buf.at[1])
    arrived(15, d_buf.at[1])
    arrived(16, e_buf)

    @pl.loop(0, rows // step)
    def _(i):
        at_rows = pl.ds(pl.multiple_of(i * step, step), step)
        out[at_rows, :] = (
            acc[7, at_rows, :].astype(F32)
            + c_buf[1, at_rows, :].astype(F32)
            + d_buf[1, at_rows, :].astype(F32)
            + e_buf[at_rows, :].astype(F32)
        )

    for copy in started:
        copy.wait_send()


def reduce_scatter(x, axis, number):
    n, rows, columns = x.shape
    half = rows // 2
    buf = lambda *shape: pltpu.VMEM(shape + (columns,), BF)
    return pl.pallas_call(
        functools.partial(reduce_kernel, axis),
        out_shape=jax.ShapeDtypeStruct((rows, columns), F32),
        in_specs=[pl.BlockSpec(memory_space=pl.ANY)],
        out_specs=pl.BlockSpec(memory_space=pltpu.VMEM),
        scratch_shapes=[
            buf(8, rows),
            buf(8 if axis == "dp" else 1, rows if axis == "dp" else 16),
            buf(2, half),
            buf(2, half),
            buf(2, rows),
            buf(2, rows),
            buf(rows),
            pltpu.SemaphoreType.DMA((17,)),
            pltpu.SemaphoreType.DMA((17,)),
            pltpu.SemaphoreType.DMA((8,)),
        ],
        compiler_params=pltpu.CompilerParams(
            collective_id=number, has_side_effects=True, vmem_limit_bytes=VMEM_LIMIT
        ),
        name="reduce_" + axis,
    )(x)


def exchange_kernel(plan, *refs):
    count = len(plan)
    ins, outs = refs[:count], refs[count : 2 * count]
    send, recv, own_sem = refs[2 * count :]
    axes = sorted({axis for _, axis in plan})
    barrier = pltpu.get_barrier_semaphore()
    total = 0
    for axis in axes:
        n, me = lax.axis_size(axis), lax.axis_index(axis)
        for k in range(1, n):
            pl.semaphore_signal(
                barrier, inc=1, device_id={axis: lax.rem(me + k, n)}, device_id_type=MESH
            )
        total += n - 1
    pl.semaphore_wait(barrier, total)
    copies = []
    number = 0
    for index, (kind, axis) in enumerate(plan):
        n, me = lax.axis_size(axis), lax.axis_index(axis)
        x, out = ins[index], outs[index]
        for k in range(1, n):
            peer = lax.rem(me + k, n)
            copy = pltpu.make_async_remote_copy(
                src_ref=x if kind == "gather" else x.at[peer],
                dst_ref=out.at[me],
                send_sem=send.at[number],
                recv_sem=recv.at[number],
                device_id={axis: peer},
                device_id_type=MESH,
            )
            copy.start()
            copies.append(copy)
            number += 1
        own = pltpu.make_async_copy(
            x if kind == "gather" else x.at[me], out.at[me], own_sem.at[index]
        )
        own.start()
        copies.append(own)
    for copy in copies:
        copy.wait()


def exchange(plan, arrays, number):
    shapes, transfers = [], 0
    for (kind, axis), x in zip(plan, arrays):
        n = lax.axis_size(axis)
        transfers += n - 1
        shapes.append(
            jax.ShapeDtypeStruct((n,) + x.shape if kind == "gather" else x.shape, x.dtype)
        )
    return pl.pallas_call(
        functools.partial(exchange_kernel, plan),
        out_shape=shapes,
        in_specs=[pl.BlockSpec(memory_space=pl.ANY)] * len(arrays),
        out_specs=[pl.BlockSpec(memory_space=pl.ANY)] * len(arrays),
        scratch_shapes=[
            pltpu.SemaphoreType.DMA((transfers,)),
            pltpu.SemaphoreType.DMA((transfers,)),
            pltpu.SemaphoreType.DMA((len(arrays),)),
        ],
        compiler_params=pltpu.CompilerParams(
            collective_id=number, has_side_effects=True, vmem_limit_bytes=VMEM_LIMIT
        ),
        name="exchange",
    )(*arrays)


def body(
    tokens,
    lengths,
    routes,
    cotangent,
    input_weight,
    filter_weight,
    filter_bias,
    step_bias,
    decay_log,
    skip_gain,
    norm_gain,
    gated_gain,
    output_weight,
    moe_gain,
    router_weight,
    shared_gate_up,
    shared_down,
    expert_gate_up,
    expert_down,
):
    nd, ne = lax.axis_size("dp"), lax.axis_size("expert")
    me_d, me_e = lax.axis_index("dp"), lax.axis_index("expert")
    loc = tokens.shape[2]
    heads = H // nd
    di = heads * PS
    rows_t = MB * loc
    experts = expert_gate_up.shape[0] * ne
    el = expert_gate_up.shape[0]
    dr = D // nd
    fs = FS // ne
    fsr = FS // nd
    fsl = fsr // ne

    pad = 128 - heads
    blocks = jnp.concatenate(
        [
            jnp.moveaxis(input_weight[:, :DI].reshape(dr, nd, di), 1, 0),
            jnp.moveaxis(input_weight[:, DI : 2 * DI].reshape(dr, nd, di), 1, 0),
            jnp.broadcast_to(input_weight[None, :, 2 * DI : 2 * DI + 2 * S], (nd, dr, 2 * S)),
            jnp.moveaxis(input_weight[:, DI + CONV :].reshape(dr, nd, heads), 1, 0),
            jnp.zeros((nd, dr, pad), BF),
        ],
        axis=2,
    )
    w_in = lax.all_to_all(blocks, "dp", 0, 0, tiled=True).reshape(D, -1)
    wcols = w_in.shape[1]

    sg = shared_gate_up.reshape(dr, 2, nd, ne, fsl)
    sg = lax.dynamic_index_in_dim(sg, me_e, 3, False).reshape(dr, 2 * fs)
    sd = lax.dynamic_slice_in_dim(shared_down, me_e * fsl, fsl, 0)
    packed = jnp.concatenate([sg.reshape(-1), sd.reshape(-1), router_weight.reshape(-1)])
    packed_cols = packed.size // rows_t
    packed = jnp.pad(packed.reshape(rows_t, -1), ((0, 0), (0, 256 - packed_cols)))

    stream = tokens.reshape(rows_t, D).astype(F32)
    incoming = cotangent.reshape(rows_t, D)
    route_rows = routes.reshape(rows_t, TOP)
    inc_all = lax.all_gather(incoming, "expert", axis=0, tiled=True)

    normed_wide, norm_pull = jax.vjp(rms_scale, stream, norm_gain)
    normed = normed_wide.astype(BF)
    normed_all = gather(jnp.concatenate([normed, packed], axis=1), "dp", 1)
    packed_all = normed_all[:, :, D:].reshape(nd, rows_t, 256)[:, :, : packed_cols]
    packed_all = packed_all.reshape(nd, -1)
    sg_full = packed_all[:, : sg.size].reshape(D, 2 * fs)
    sd_full = packed_all[:, sg.size : sg.size + sd.size].reshape(fs, D)
    router_full = packed_all[:, sg.size + sd.size :].reshape(D, experts)
    normed_all = normed_all.reshape(nd * rows_t, D + 256)
    w_wide = jnp.pad(w_in, ((0, 256), (0, 0)))
    proj = mm(normed_all, w_wide).reshape(nd, MB, loc, wcols)

    count = nd * loc
    docs = doc_number(jnp.arange(count, dtype=jnp.int32)[None], lengths[:, 0])
    docs_ext = doc_number(jnp.arange(count + K - 1, dtype=jnp.int32)[None] - (K - 1), lengths[:, 0])
    taps = jnp.concatenate(
        [lax.dynamic_slice_in_dim(filter_weight, me_d * di, di, 1), filter_weight[:, DI:]], axis=1
    )
    tap_bias = jnp.concatenate(
        [lax.dynamic_slice_in_dim(filter_bias, me_d * di, di, 0), filter_bias[DI:]], axis=0
    )
    my_heads = lambda v: lax.dynamic_slice_in_dim(v, me_d * heads, heads, 0)
    my_gain = lax.dynamic_slice_in_dim(gated_gain, me_d * di, di, 0)

    def mixer(p, a, b, c, d, e):
        return mixer_local(p, a, b, c, d, e, docs, docs_ext, heads)

    y, mixer_pull = jax.vjp(
        mixer, proj, taps, tap_bias, my_heads(step_bias), my_heads(decay_log), my_heads(skip_gain)
    )
    y = y.reshape(nd * rows_t, di)
    square = jnp.sum(y * y, axis=1, keepdims=True)
    out_wide = jnp.pad(output_weight, ((0, 0), (0, 128)))
    column = lax.broadcasted_iota(jnp.int32, (1, D + 128), 1)
    partial = mm((y * my_gain).astype(BF), out_wide)
    sq_hi, sq_lo = hi_lo(square)
    payload = jnp.where(column == D, sq_hi.astype(F32), partial)
    payload = jnp.where(column == D + 1, sq_lo.astype(F32), payload).astype(BF)
    summed = reduce_scatter(payload.reshape(nd, rows_t, D + 128), "dp", 2)
    r = lax.rsqrt((summed[:, D : D + 1] + summed[:, D + 1 : D + 2]) / DI + EPSILON)
    mixed = summed[:, :D] * r
    after_mixer = stream + mixed
    moe_wide, moe_pull = jax.vjp(rms_scale, after_mixer, moe_gain)
    moe_in = moe_wide.astype(BF)
    logits = mm(moe_in, router_full)
    chosen = (route_rows[:, :, None] == jnp.arange(experts, dtype=jnp.int32)).astype(F32)
    picked = jnp.sum(chosen * logits[:, None, :], axis=2)
    gates = jax.nn.softmax(picked, axis=1)
    table = jnp.sum(chosen * gates[:, :, None], axis=1)
    t_hi, t_lo = hi_lo(table)
    moe_payload = jnp.concatenate(
        [moe_in, t_hi, t_lo, jnp.zeros((rows_t, 128 - 2 * experts), BF)], axis=1
    )
    moe_all = gather(moe_payload, "expert", 3).reshape(ne * rows_t, D + 128)
    table_all = moe_all[:, D : D + experts].astype(F32) + moe_all[
        :, D + experts : D + 2 * experts
    ].astype(F32)
    my_gates = lax.dynamic_slice_in_dim(table_all, me_e * el, el, 1)
    n_tok = ne * rows_t

    w_up = jnp.concatenate(
        [expert_gate_up[i][:, :FE] for i in range(el)]
        + [sg_full[:, :fs]]
        + [expert_gate_up[i][:, FE:] for i in range(el)]
        + [sg_full[:, fs:]],
        axis=1,
    )
    w_up = jnp.pad(w_up, ((0, 128), (0, 0)))
    w_down = jnp.concatenate([expert_down[i] for i in range(el)] + [sd_full], axis=0)
    width = w_down.shape[0]
    scale = jnp.concatenate(
        [jnp.broadcast_to(my_gates[:, i : i + 1], (n_tok, FE)) for i in range(el)]
        + [jnp.ones((n_tok, fs), F32)],
        axis=1,
    )
    pre = mm(moe_all, w_up)
    a, b = pre[:, :width], pre[:, width:]
    sig = jax.nn.sigmoid(a)
    act = a * sig
    hidden = act * b
    u = mm_nt(inc_all, w_down)
    prod = u * hidden
    gate_grad = jnp.concatenate(
        [jnp.sum(prod[:, i * FE : (i + 1) * FE], axis=1, keepdims=True) for i in range(el)], axis=1
    )
    gh = (scale * hidden).astype(BF)
    gu = scale * u
    pre_grad = jnp.concatenate(
        [gu * b * (sig + act * (1.0 - sig)), gu * act], axis=1
    ).astype(BF)
    out_part = mm(gh, w_down)
    dx_part = mm_nt(pre_grad, w_up)
    d_up = mm_tn(moe_all, pre_grad)[:D]
    d_down = mm_tn(gh, inc_all)
    for i in range(el):
        g_hi, g_lo = hi_lo(gate_grad[:, i : i + 1])
        place = D + me_e * el + i
        dx_part = jnp.where(column == place, g_hi.astype(F32), dx_part)
        dx_part = jnp.where(column == place + experts, g_lo.astype(F32), dx_part)
    out_sum = lax.psum_scatter(out_part.astype(BF), "expert", scatter_dimension=0, tiled=True)
    back_sum = reduce_scatter(dx_part.astype(BF).reshape(ne, rows_t, D + 128), "expert", 4)
    inc = incoming.astype(F32)
    spread_sum = back_sum[:, D : D + experts] + back_sum[:, D + experts : D + 2 * experts]
    logit_grad = table * (spread_sum - jnp.sum(table * spread_sum, axis=1, keepdims=True))
    logit_low = logit_grad.astype(BF)
    router_part = mm_tn(moe_in, logit_low)
    moe_in_grad = back_sum[:, :D] + mm_nt(logit_low, router_full)
    after_from_norm, moe_gain_grad = moe_pull(moe_in_grad)
    after_grad = inc + after_from_norm
    after_low = after_grad.astype(BF)
    s = jnp.sum(after_low.astype(F32) * mixed, axis=1, keepdims=True)
    r_hi, r_lo = hi_lo(r)
    d_hi, d_lo = hi_lo(s)
    grad_payload = jnp.concatenate(
        [after_low, r_hi, r_lo, d_hi, d_lo, jnp.zeros((rows_t, 124), BF)], axis=1
    )
    grad_all = gather(grad_payload, "dp", 5).reshape(nd * rows_t, D + 128)
    extra = grad_all[:, D : D + 4].astype(F32)
    r_all = extra[:, 0:1] + extra[:, 1:2]
    s_all = extra[:, 2:3] + extra[:, 3:4]
    gated_grad = mm_nt(grad_all, out_wide)
    yr = y * r_all
    output_part = mm_tn((yr * my_gain).astype(BF), grad_all)[:, :D]
    gated_gain_part = jnp.sum(gated_grad * yr, axis=0)
    dy = r_all * (gated_grad * my_gain) - yr * (r_all * s_all / DI)
    pulls = mixer_pull(dy.reshape(nd, MB, loc, di))
    d_proj = pulls[0].astype(BF).reshape(nd * rows_t, wcols)
    normed_part = mm_nt(d_proj, w_in)
    normed_grad = reduce_scatter(normed_part.astype(BF).reshape(nd, rows_t, D), "dp", 6)
    d_win = mm_tn(normed_all, d_proj)[:D].astype(BF)
    stream_from_norm, norm_gain_grad = norm_pull(normed_grad)
    tokens_grad = after_grad + stream_from_norm

    d_up = d_up.astype(BF)
    d_down = d_down.astype(BF)
    up_blocks = d_up.reshape(nd, dr, 2 * width)
    down_blocks = jnp.stack(
        [d_down[i * FE : (i + 1) * FE].reshape(nd, FE // nd, D) for i in range(el)], axis=1
    ).reshape(nd, el * FE // nd, D)
    down_blocks = jnp.concatenate([down_blocks, d_down[el * FE :].reshape(nd, fsl, D)], axis=1)
    up_sum = lax.psum_scatter(up_blocks, "dp", scatter_dimension=0, tiled=True)[0]
    down_sum = lax.psum_scatter(down_blocks, "dp", scatter_dimension=0, tiled=True)[0]
    expert_up_grad = jnp.stack(
        [
            jnp.concatenate(
                [
                    up_sum[:, i * FE : (i + 1) * FE],
                    up_sum[:, width + i * FE : width + (i + 1) * FE],
                ],
                axis=1,
            )
            for i in range(el)
        ],
        axis=0,
    ).astype(F32)
    expert_down_grad = down_sum[: el * FE // nd].reshape(el, FE // nd, D).astype(F32)
    shared_part = jnp.concatenate(
        [
            up_sum[:, el * FE : width],
            up_sum[:, width + el * FE :],
            down_sum[el * FE // nd :].reshape(dr, -1),
        ],
        axis=1,
    )

    def spread_heads(v, size, chunk):
        return lax.dynamic_update_slice(
            jnp.zeros(v.shape[:-1] + (size,), F32), v, (0,) * (v.ndim - 1) + (me_d * chunk,)
        )

    small_parts = (
        jnp.concatenate([spread_heads(pulls[1][:, :di], DI, di), pulls[1][:, di:]], axis=1),
        jnp.concatenate([spread_heads(pulls[2][:di], DI, di), pulls[2][di:]], axis=0),
        spread_heads(pulls[3], H, heads),
        spread_heads(pulls[4], H, heads),
        spread_heads(pulls[5], H, heads),
        norm_gain_grad,
        spread_heads(gated_gain_part, DI, di),
        moe_gain_grad,
        router_part,
    )
    sizes = [part.size for part in small_parts]
    lanes = -(-sum(sizes) // (nd * 1024)) * 8
    small_flat = jnp.concatenate([part.reshape(-1) for part in small_parts])
    small_flat = jnp.pad(small_flat, (0, nd * lanes * 128 - sum(sizes))).reshape(nd, lanes, 128)

    main = 2 * di
    back_in, small_in = exchange(
        (("all", "dp"), ("all", "dp")), (d_win.reshape(nd, dr, wcols), small_flat), 7
    )
    misc = jnp.concatenate(
        [
            jnp.sum(back_in[:, :, main : main + 2 * S].astype(F32), axis=0),
            jnp.moveaxis(back_in[:, :, main + 2 * S : main + 2 * S + heads], 0, 1)
            .reshape(dr, H)
            .astype(F32),
        ],
        axis=1,
    )
    misc_size = misc.size
    misc_rows = -(-misc_size // (ne * 1024)) * 8
    misc = jnp.pad(misc.reshape(-1), (0, ne * misc_rows * 128 - misc_size))
    got = exchange(
        (("all", "expert"), ("all", "expert"), ("all", "expert"), ("gather", "expert")),
        (
            back_in[:, :, :main].reshape(ne, nd // ne * dr, main),
            misc.reshape(ne, misc_rows, 128),
            output_part.astype(BF).reshape(ne, 48, -1),
            jnp.sum(small_in, axis=0),
        ),
        8,
    )
    main_sum, misc_sum, out_grad_sum, small_sum = [jnp.sum(v.astype(F32), axis=0) for v in got]
    main_all, misc_all, out_grad_all, shared_all, small_all = exchange(
        (
            ("gather", "expert"),
            ("gather", "expert"),
            ("gather", "expert"),
            ("gather", "expert"),
            ("gather", "dp"),
        ),
        (main_sum.astype(BF), misc_sum, out_grad_sum.astype(BF), shared_part, small_sum),
        9,
    )
    main_all = main_all.reshape(nd, dr, main).astype(F32)
    misc_all = misc_all.reshape(-1)[:misc_size].reshape(dr, 2 * S + H)
    input_grad = jnp.concatenate(
        [
            jnp.moveaxis(main_all[:, :, :di], 0, 1).reshape(dr, DI),
            jnp.moveaxis(main_all[:, :, di:], 0, 1).reshape(dr, DI),
            misc_all,
        ],
        axis=1,
    )
    output_grad = out_grad_all.reshape(output_weight.shape)
    shared_up_grad = (
        jnp.moveaxis(shared_all[:, :, : 2 * fs].reshape(ne, dr, 2, nd, fsl), 0, 3)
        .reshape(dr, 2 * FS)
        .astype(F32)
    )
    shared_down_grad = shared_all[:, :, 2 * fs :].reshape(fsr, D).astype(F32)
    small_all = small_all.reshape(-1)
    small, start = [], 0
    for part, size in zip(small_parts, sizes):
        small.append(small_all[start : start + size].reshape(part.shape))
        start += size
    router_grad = lax.dynamic_slice_in_dim(small[8], me_d * dr, dr, 0)
    block_output = (after_mixer + out_sum.astype(F32)).astype(BF)
    shape = (MB, 1, loc, D)
    return (
        block_output.reshape(shape),
        tokens_grad.reshape(shape),
        input_grad,
        small[0],
        small[1],
        small[2],
        small[3],
        small[4],
        small[5],
        small[6],
        output_grad.astype(F32),
        small[7],
        router_grad,
        shared_up_grad,
        shared_down_grad,
        expert_up_grad,
        expert_down_grad,
    )


def solution(mesh):
    in_specs = (
        P(None, "expert", "dp", None),
        P(None, "expert", None),
        P(None, "expert", "dp", None),
        P(None, "expert", "dp", None),
        P("dp", None),
        P(),
        P(),
        P(),
        P(),
        P(),
        P(),
        P(),
        P("dp", None),
        P(),
        P("dp", None),
        P("dp", None),
        P("dp", None),
        P("expert", None, None),
        P("expert", None, None),
    )
    out_specs = (
        P(None, "expert", "dp", None),
        P(None, "expert", "dp", None),
        P("dp", None),
        P(),
        P(),
        P(),
        P(),
        P(),
        P(),
        P(),
        P("dp", None),
        P(),
        P("dp", None),
        P("dp", None),
        P("dp", None),
        P("expert", "dp", None),
        P("expert", "dp", None),
    )
    return jax.shard_map(body, mesh=mesh, in_specs=in_specs, out_specs=out_specs, check_vma=False)
```

```python
import functools

import jax
import jax.numpy as jnp
from jax import lax
from jax.experimental import pallas as pl
from jax.experimental.pallas import tpu as pltpu
from jax.sharding import PartitionSpec as P

D = 1536
H = 48
PS = 64
S = 128
K = 4
FE = 512
FS = 1024
TOP = 6
MB = 2
DI = 3072
CONV = 3328
IN_W = 6448
EPSILON = 1e-05
BF = jnp.bfloat16
F32 = jnp.float32
MESH = pl.DeviceIdType.MESH
VMEM_LIMIT = 60 * 1024 * 1024


def mm(a, b):
    return jnp.dot(a, b, preferred_element_type=F32)


def mm_nt(a, b):
    return lax.dot_general(a, b, (((1,), (1,)), ((), ())), preferred_element_type=F32)


def mm_tn(a, b):
    return lax.dot_general(a, b, (((0,), (0,)), ((), ())), preferred_element_type=F32)


def rms_scale(values, gain):
    return values * lax.rsqrt(jnp.mean(values * values, axis=-1, keepdims=True) + EPSILON) * gain


def hi_lo(v):
    hi = v.astype(BF)
    return hi, (v - hi.astype(F32)).astype(BF)


def places(axis):
    me = lax.axis_index(axis)
    if axis == "dp":
        core, ring, pair = lax.rem(me, 2), lax.rem(me // 2, 4), me // 8

        def at(hop, other, sibling=0):
            z = lax.rem(pair + other, 2)
            return (z * 4 + lax.rem(ring + hop + 4, 4)) * 2 + lax.rem(core + sibling, 2)
    else:
        pair, ring = lax.rem(me, 2), me // 2

        def at(hop, other, sibling=0):
            return lax.rem(ring + hop + 4, 4) * 2 + lax.rem(pair + other, 2)

    return me, at


def greet(axis, peers):
    barrier = pltpu.get_barrier_semaphore()
    for peer in peers:
        pl.semaphore_signal(barrier, inc=1, device_id={axis: peer}, device_id_type=MESH)
    pl.semaphore_wait(barrier, len(peers))


def gather_kernel(axis, x, out, send, recv, own_sem):
    me, at = places(axis)
    cores = axis == "dp"
    half = x.shape[0] // 2
    up, down, pair, sib = at(1, 0), at(-1, 0), at(0, 1), at(0, 0, 1)
    greet(axis, [up, down, pair] + ([sib] if cores else []))
    whole = pl.ds(0, 2 * half)
    first, second = pl.ds(0, half), pl.ds(half, half)
    started = []

    def push(number, slot, rows, peer, src=None):
        copy = pltpu.make_async_remote_copy(
            src_ref=(out.at[slot] if src is None else src).at[rows],
            dst_ref=out.at[slot].at[rows],
            send_sem=send.at[number],
            recv_sem=recv.at[number],
            device_id={axis: peer},
            device_id_type=MESH,
        )
        copy.start()
        started.append(copy)

    def arrived(number, slot, rows):
        pltpu.make_async_copy(out.at[slot].at[rows], out.at[slot].at[rows], recv.at[number]).wait()

    push(0, me, whole, up, x)
    push(1, me, whole, down, x)
    push(2, me, whole, pair, x)
    if cores:
        push(3, me, whole, sib, x)
    own = pltpu.make_async_copy(x, out.at[me], own_sem)
    own.start()
    arrived(2, pair, whole)
    push(4, pair, whole, up)
    push(5, pair, whole, down)
    if cores:
        push(6, pair, whole, sib)
    arrived(0, down, whole)
    push(7, down, first, up)
    arrived(1, up, whole)
    push(8, up, second, down)
    if cores:
        push(9, down, whole, sib)
        push(10, up, whole, sib)
    arrived(4, at(-1, 1), whole)
    push(11, at(-1, 1), first, up)
    arrived(5, at(1, 1), whole)
    push(12, at(1, 1), second, down)
    if cores:
        push(13, at(-1, 1), whole, sib)
        push(14, at(1, 1), whole, sib)
    arrived(7, at(2, 0), first)
    arrived(8, at(2, 0), second)
    if cores:
        push(15, at(2, 0), whole, sib)
    arrived(11, at(2, 1), first)
    arrived(12, at(2, 1), second)
    if cores:
        push(16, at(2, 1), whole, sib)
        for number, hop, other in (
            (3, 0, 0),
            (6, 0, 1),
            (9, -1, 0),
            (10, 1, 0),
            (13, -1, 1),
            (14, 1, 1),
            (15, 2, 0),
            (16, 2, 1),
        ):
            arrived(number, at(hop, other, 1), whole)
    own.wait()
    for copy in started:
        copy.wait_send()


def gather(x, axis, number):
    n = lax.axis_size(axis)
    return pl.pallas_call(
        functools.partial(gather_kernel, axis),
        out_shape=jax.ShapeDtypeStruct((n,) + x.shape, x.dtype),
        in_specs=[pl.BlockSpec(memory_space=pl.ANY)],
        out_specs=pl.BlockSpec(memory_space=pl.ANY),
        scratch_shapes=[
            pltpu.SemaphoreType.DMA((17,)),
            pltpu.SemaphoreType.DMA((17,)),
            pltpu.SemaphoreType.DMA,
        ],
        compiler_params=pltpu.CompilerParams(
            collective_id=number, has_side_effects=True, vmem_limit_bytes=VMEM_LIMIT
        ),
        name="gather_" + axis,
    )(x)


ORDER = ((2, 1), (2, 0), (1, 1), (-1, 1), (1, 0), (-1, 0), (0, 1), (0, 0))


def reduce_kernel(axis, x, out, acc, sib_buf, a_buf, b_buf, c_buf, d_buf, e_buf, send, recv, load):
    me, at = places(axis)
    cores = axis == "dp"
    rows = x.shape[1]
    half = rows // 2
    step = 32 if half % 32 == 0 else 16
    up, down, pair, sib = at(1, 0), at(-1, 0), at(0, 1), at(0, 0, 1)
    greet(axis, [up, down, pair] + ([sib] if cores else []))
    whole, first, second = pl.ds(0, rows), pl.ds(0, half), pl.ds(half, half)
    started = []

    def push(number, src, dst, peer):
        copy = pltpu.make_async_remote_copy(
            src_ref=src,
            dst_ref=dst,
            send_sem=send.at[number],
            recv_sem=recv.at[number],
            device_id={axis: peer},
            device_id_type=MESH,
        )
        copy.start()
        started.append(copy)

    def arrived(number, dst):
        pltpu.make_async_copy(dst, dst, recv.at[number]).wait()

    def add(dst, offset, count, *srcs):
        @pl.loop(0, count // step)
        def _(i):
            at_rows = pl.ds(pl.multiple_of(offset + i * step, step), step)
            total = dst[at_rows, :].astype(F32)
            for src, src_offset in srcs:
                total += src[pl.ds(pl.multiple_of(src_offset + i * step, step), step), :].astype(F32)
            dst[at_rows, :] = total.astype(dst.dtype)

    loads = []
    for k, (hop, other) in enumerate(ORDER):
        if cores:
            push(k, x.at[at(hop, other, 1)], sib_buf.at[k], sib)
        copy = pltpu.make_async_copy(x.at[at(hop, other)], acc.at[k], load.at[k])
        copy.start()
        loads.append(copy)

    def ready(k):
        loads[k].wait()
        if cores:
            arrived(k, sib_buf.at[k])
            add(acc.at[k], 0, rows, (sib_buf.at[k], 0))

    ready(0)
    push(8, acc.at[0].at[first], a_buf.at[0], up)
    push(9, acc.at[0].at[second], b_buf.at[0], down)
    ready(1)
    push(10, acc.at[1].at[first], a_buf.at[1], up)
    push(11, acc.at[1].at[second], b_buf.at[1], down)
    ready(2)
    ready(3)
    arrived(8, a_buf.at[0])
    add(acc.at[2], 0, half, (a_buf.at[0], 0))
    push(12, acc.at[2], c_buf.at[0], up)
    arrived(9, b_buf.at[0])
    add(acc.at[3], half, half, (b_buf.at[0], 0))
    push(13, acc.at[3], d_buf.at[0], down)
    ready(4)
    ready(5)
    arrived(10, a_buf.at[1])
    add(acc.at[4], 0, half, (a_buf.at[1], 0))
    push(14, acc.at[4], c_buf.at[1], up)
    arrived(11, b_buf.at[1])
    add(acc.at[5], half, half, (b_buf.at[1], 0))
    push(15, acc.at[5], d_buf.at[1], down)
    ready(6)
    ready(7)
    arrived(12, c_buf.at[0])
    arrived(13, d_buf.at[0])
    add(acc.at[6], 0, rows, (c_buf.at[0], 0), (d_buf.at[0], 0))
    push(16, acc.at[6], e_buf, pair)
    arrived(14, c_buf.at[1])
    arrived(15, d_buf.at[1])
    arrived(16, e_buf)

    @pl.loop(0, rows // step)
    def _(i):
        at_rows = pl.ds(pl.multiple_of(i * step, step), step)
        out[at_rows, :] = (
            acc[7, at_rows, :].astype(F32)
            + c_buf[1, at_rows, :].astype(F32)
            + d_buf[1, at_rows, :].astype(F32)
            + e_buf[at_rows, :].astype(F32)
        )

    for copy in started:
        copy.wait_send()


def reduce_scatter(x, axis, number):
    n, rows, columns = x.shape
    half = rows // 2
    buf = lambda *shape: pltpu.VMEM(shape + (columns,), BF)
    return pl.pallas_call(
        functools.partial(reduce_kernel, axis),
        out_shape=jax.ShapeDtypeStruct((rows, columns), F32),
        in_specs=[pl.BlockSpec(memory_space=pl.ANY)],
        out_specs=pl.BlockSpec(memory_space=pltpu.VMEM),
        scratch_shapes=[
            buf(8, rows),
            buf(8 if axis == "dp" else 1, rows if axis == "dp" else 16),
            buf(2, half),
            buf(2, half),
            buf(2, rows),
            buf(2, rows),
            buf(rows),
            pltpu.SemaphoreType.DMA((17,)),
            pltpu.SemaphoreType.DMA((17,)),
            pltpu.SemaphoreType.DMA((8,)),
        ],
        compiler_params=pltpu.CompilerParams(
            collective_id=number, has_side_effects=True, vmem_limit_bytes=VMEM_LIMIT
        ),
        name="reduce_" + axis,
    )(x)


def exchange_kernel(plan, *refs):
    count = len(plan)
    ins, outs = refs[:count], refs[count : 2 * count]
    send, recv, own_sem = refs[2 * count :]
    axes = sorted({axis for _, axis in plan})
    barrier = pltpu.get_barrier_semaphore()
    total = 0
    for axis in axes:
        n, me = lax.axis_size(axis), lax.axis_index(axis)
        for k in range(1, n):
            pl.semaphore_signal(
                barrier, inc=1, device_id={axis: lax.rem(me + k, n)}, device_id_type=MESH
            )
        total += n - 1
    pl.semaphore_wait(barrier, total)
    copies = []
    number = 0
    for index, (kind, axis) in enumerate(plan):
        n, me = lax.axis_size(axis), lax.axis_index(axis)
        x, out = ins[index], outs[index]
        for k in range(1, n):
            peer = lax.rem(me + k, n)
            copy = pltpu.make_async_remote_copy(
                src_ref=x if kind == "gather" else x.at[peer],
                dst_ref=out.at[me],
                send_sem=send.at[number],
                recv_sem=recv.at[number],
                device_id={axis: peer},
                device_id_type=MESH,
            )
            copy.start()
            copies.append(copy)
            number += 1
        own = pltpu.make_async_copy(
            x if kind == "gather" else x.at[me], out.at[me], own_sem.at[index]
        )
        own.start()
        copies.append(own)
    for copy in copies:
        copy.wait()


def exchange(plan, arrays, number):
    shapes, transfers = [], 0
    for (kind, axis), x in zip(plan, arrays):
        n = lax.axis_size(axis)
        transfers += n - 1
        shapes.append(
            jax.ShapeDtypeStruct((n,) + x.shape if kind == "gather" else x.shape, x.dtype)
        )
    return pl.pallas_call(
        functools.partial(exchange_kernel, plan),
        out_shape=shapes,
        in_specs=[pl.BlockSpec(memory_space=pl.ANY)] * len(arrays),
        out_specs=[pl.BlockSpec(memory_space=pl.ANY)] * len(arrays),
        scratch_shapes=[
            pltpu.SemaphoreType.DMA((transfers,)),
            pltpu.SemaphoreType.DMA((transfers,)),
            pltpu.SemaphoreType.DMA((len(arrays),)),
        ],
        compiler_params=pltpu.CompilerParams(
            collective_id=number, has_side_effects=True, vmem_limit_bytes=VMEM_LIMIT
        ),
        name="exchange",
    )(*arrays)


EDGE = 8
HIGHEST = lax.Precision.HIGHEST


def exact(a, b, dims):
    return lax.dot_general(a, b, (dims, ((), ())), precision=HIGHEST, preferred_element_type=F32)


def iota(shape, axis):
    return lax.broadcasted_iota(jnp.int32, shape, axis)


class Block:
    def __init__(self, m, start, proj, ext, lengths, taps, heads_vec, heads):
        loc = proj.shape[0]
        di = heads * PS
        width = di + 2 * S
        self.heads, self.di = heads, di
        first = lengths[m, 0]
        second = first + lengths[m, 1]

        def doc(p):
            return (p >= first).astype(jnp.int32) + (p >= second).astype(jnp.int32)

        self.doc = doc
        self.at = start + iota((loc, 1), 0)
        docs = doc(self.at)
        docs_row = doc(start + iota((1, loc), 1))
        last_doc, before_doc = doc(start + loc - 1), doc(start - 1)
        self.keep = (docs == before_doc).astype(F32)
        self.keep_last = (last_doc == before_doc).astype(F32)
        self.same_last = (docs == last_doc).astype(F32)
        self.gate = proj[:, :di]
        ext[m, EDGE : EDGE + loc, :] = proj[:, di : di + width].astype(BF).astype(F32)
        total = jnp.broadcast_to(taps[K : K + 1, :], (loc, width))
        self.shifted = []
        for k in range(K):
            back = K - 1 - k
            value = ext[m, EDGE - back : EDGE - back + loc, :]
            if back:
                value = value * (docs == doc(self.at - back)).astype(F32)
            self.shifted.append(value)
            total = total + taps[k : k + 1, :] * value
        self.sig = jax.nn.sigmoid(total)
        self.total = total
        filtered = total * self.sig
        self.x = filtered[:, :di]
        self.write = filtered[:, di : di + S].astype(BF)
        self.read = filtered[:, di + S :].astype(BF)
        self.raw = proj[:, di + width :] + heads_vec[0:1, :]
        self.steps = jnp.maximum(self.raw, 0.0) + jnp.log1p(jnp.exp(-jnp.abs(self.raw)))
        self.rate = heads_vec[1:2, :]
        rise = self.steps * self.rate
        rows, cols = iota((loc, loc), 0), iota((loc, loc), 1)
        self.lower = (cols <= rows).astype(F32)
        self.cum = exact(self.lower, rise, ((1,), (0,)))
        cum_rows = exact(rise, (rows <= cols).astype(F32), ((0,), (0,)))
        self.last = self.cum[loc - 1 : loc, :]
        self.grow = jnp.exp(self.cum) * self.keep
        self.fall = jnp.exp(self.last - self.cum) * self.same_last
        self.decay = jnp.exp(self.last) * self.keep_last
        allowed = (cols <= rows) & (docs == docs_row)
        scores = mm_nt(self.read, self.write)
        self.spread, self.mixing = [], []
        for h in range(heads):
            span = self.cum[:, h : h + 1] - cum_rows[h : h + 1, :]
            shape = jnp.exp(jnp.where(allowed, span, -1e30))
            self.spread.append(shape)
            self.mixing.append(shape * scores)
        self.lane = iota((1, di), 1)
        self.steps_wide = self.widen(self.steps)
        self.grow_wide = self.widen(self.grow)
        self.weight_wide = self.widen(self.fall * self.steps)
        self.scaled = self.x * self.steps_wide
        self.pushed = self.x * self.weight_wide

    def widen(self, v):
        out = jnp.broadcast_to(v[:, 0:1], (v.shape[0], self.di))
        for h in range(1, self.heads):
            out = jnp.where(self.lane >= h * PS, v[:, h : h + 1], out)
        return out

    def per_head(self, parts):
        out = parts[0]
        for h in range(1, self.heads):
            out = jnp.where(self.lane >= h * PS, parts[h], out)
        return out

    def decay_rows(self):
        rows = iota((self.di, 1), 0)
        out = jnp.broadcast_to(self.decay[:, 0:1], (self.di, 1))
        for h in range(1, self.heads):
            out = jnp.where(rows >= h * PS, self.decay[:, h : h + 1], out)
        return out


def forward_kernel(
    heads, lengths, g, w, w_out, taps, heads_vec, lanes_vec, payload, proj, scan, states, ext, state
):
    b = pl.program_id(0)
    loc = g.shape[1] // MB
    di = heads * PS

    @pl.when(b == 0)
    def _():
        ext[...] = jnp.zeros_like(ext)
        state[...] = jnp.zeros_like(state)

    proj[0] = mm(g[0], w[...])
    column = iota((1, payload.shape[2]), 1)
    for m in range(MB):
        rows = slice(m * loc, (m + 1) * loc)
        ext[m, 0:EDGE, :] = ext[m, loc : loc + EDGE, :]
        part = Block(m, b * loc, proj[0, rows, :], ext, lengths, taps, heads_vec, heads)
        before = state[m]
        states[0, m] = before
        scaled = part.scaled.astype(BF)
        inner = part.per_head([mm(part.mixing[h].astype(BF), scaled) for h in range(heads)])
        carried = mm_nt(part.read, before.astype(BF)) * part.grow_wide
        out = inner + carried + lanes_vec[1:2, :] * part.x
        scan[0, rows, :] = out
        state[m] = part.decay_rows() * before + mm_tn(part.pushed.astype(BF), part.write)
        y = out * (part.gate * jax.nn.sigmoid(part.gate))
        square = jnp.sum(y * y, axis=1, keepdims=True)
        high = square.astype(BF).astype(F32)
        sent = mm((y * lanes_vec[0:1, :]).astype(BF), w_out[...])
        sent = jnp.where(column == D, high, jnp.where(column == D + 1, square - high, sent))
        payload[0, rows, :] = sent.astype(BF)


def backward_kernel(
    heads,
    lengths,
    grad,
    w,
    w_out,
    taps,
    heads_vec,
    lanes_vec,
    proj,
    proj_before,
    scan,
    states,
    d_proj,
    normed_part,
    d_out,
    d_taps,
    d_heads,
    d_lanes,
    ext,
    d_ext,
    d_state,
):
    step = pl.program_id(0)
    b = pl.num_programs(0) - 1 - step
    loc = grad.shape[1] // MB
    di = heads * PS
    width = di + 2 * S

    @pl.when(step == 0)
    def _():
        for ref in (d_ext, d_state, d_out, d_taps, d_heads, d_lanes):
            ref[...] = jnp.zeros_like(ref)

    gated_grad = mm_nt(grad[0], w_out[...])
    extra = grad[0, :, D:].astype(F32)
    has_before = (b > 0).astype(F32)
    pick = (iota((di, S), 0) // PS == iota((di, S), 1)).astype(F32)
    for m in range(MB):
        rows = slice(m * loc, (m + 1) * loc)
        edge = proj_before[0, (m + 1) * loc - EDGE : (m + 1) * loc, di : di + width]
        ext[m, 0:EDGE, :] = edge.astype(BF).astype(F32) * has_before
        part = Block(m, b * loc, proj[0, rows, :], ext, lengths, taps, heads_vec, heads)
        gain, skip = lanes_vec[0:1, :], lanes_vec[1:2, :]
        r = extra[rows, 0:1] + extra[rows, 1:2]
        s = extra[rows, 2:3] + extra[rows, 3:4]
        out = scan[0, rows, :]
        sig = jax.nn.sigmoid(part.gate)
        act = part.gate * sig
        yr = out * act * r
        gg = gated_grad[rows]
        d_lanes[0:1, :] += jnp.sum(gg * yr, axis=0, keepdims=True)
        d_out[...] += mm_tn((yr * gain).astype(BF), grad[0, rows, :])
        dy = r * (gg * gain) - yr * (r * s / DI)
        d_gate = dy * out * (sig + act * (1.0 - sig))
        do = dy * act
        do_low = do.astype(BF)
        x = part.x
        d_lanes[1:2, :] += jnp.sum(do * x, axis=0, keepdims=True)
        dx = skip * do
        before = states[0, m]
        before_low = before.astype(BF)
        ds = d_state[m]
        ds_low = ds.astype(BF)

        d_scores = jnp.zeros((loc, loc), F32)
        d_scaled, d_cum = [], jnp.zeros((loc, S), F32)
        head_lane = iota((loc, S), 1)
        for h in range(heads):
            inside = (part.lane >= h * PS) & (part.lane < (h + 1) * PS)
            own = jnp.where(inside, part.scaled, 0.0).astype(BF)
            d_mix = mm_nt(do_low, own)
            d_scaled.append(mm_tn(part.mixing[h].astype(BF), do_low))
            d_scores = d_scores + d_mix * part.spread[h]
            d_span = d_mix * part.mixing[h]
            ones = (head_lane == h).astype(F32)
            d_cum = d_cum + exact(d_span, ones, ((1,), (0,))) - exact(d_span, ones, ((0,), (0,)))
        d_scaled = part.per_head(d_scaled)
        dx = dx + d_scaled * part.steps_wide
        d_scores_low = d_scores.astype(BF)
        d_read = mm(d_scores_low, part.write)
        d_write = mm_tn(d_scores_low, part.read)

        d_carry = do * part.grow_wide
        d_carry_low = d_carry.astype(BF)
        carried = mm_nt(part.read, before_low)
        d_read = d_read + mm(d_carry_low, before_low)

        d_pushed = mm_nt(part.write, ds_low)
        d_write = d_write + mm(part.pushed.astype(BF), ds_low)
        dx = dx + d_pushed * part.weight_wide
        sums = exact(
            jnp.concatenate([d_carry * carried, d_pushed * x, d_scaled * x], axis=0),
            pick,
            ((1,), (0,)),
        )
        d_weight = sums[loc : 2 * loc]
        d_fall = d_weight * part.fall * part.steps
        d_cum = d_cum + sums[:loc] - d_fall
        d_steps = sums[2 * loc :] + d_weight * part.fall
        state_dot = jnp.sum(ds * before, axis=1, keepdims=True)
        d_decay = exact(jnp.broadcast_to(state_dot, (di, S)), pick, ((0,), (0,)))[0:1, :]
        d_last = jnp.sum(d_fall, axis=0, keepdims=True) + d_decay * part.decay
        d_cum = d_cum + jnp.where(iota((loc, 1), 0) == loc - 1, d_last, 0.0)
        d_state[m] = part.decay_rows() * ds + mm_tn(d_carry_low, part.read)

        d_rise = exact(part.lower, d_cum, ((0,), (0,)))
        d_steps = d_steps + d_rise * part.rate
        d_raw = d_steps * jax.nn.sigmoid(part.raw)
        d_heads[0:1, :] += jnp.sum(d_raw, axis=0, keepdims=True)
        d_heads[1:2, :] += jnp.sum(d_rise * part.steps * part.rate, axis=0, keepdims=True)

        d_total = jnp.concatenate([dx, d_write, d_read], axis=1)
        d_total = d_total * (part.sig + part.total * part.sig * (1.0 - part.sig))
        for k in range(K):
            d_taps[k : k + 1, :] += jnp.sum(d_total * part.shifted[k], axis=0, keepdims=True)
        d_taps[K : K + 1, :] += jnp.sum(d_total, axis=0, keepdims=True)
        d_ext[m, loc : loc + EDGE, :] = d_ext[m, 0:EDGE, :]
        d_ext[m, 0:loc, :] = d_total
        d_seq = taps[K - 1 : K, :] * d_total
        docs = part.doc(part.at)
        for ahead in range(1, K):
            same = (docs == part.doc(part.at + ahead)).astype(F32)
            d_seq = d_seq + taps[K - 1 - ahead : K - ahead, :] * (
                same * d_ext[m, ahead : ahead + loc, :]
            )
        d_proj[0, rows, :di] = d_gate.astype(BF)
        d_proj[0, rows, di : di + width] = d_seq.astype(BF)
        d_proj[0, rows, di + width :] = jnp.where(head_lane < heads, d_raw, 0.0).astype(BF)
    normed_part[0] = mm_nt(d_proj[0], w[0:D, :]).astype(BF)


def block_spec(shape, index):
    return pl.BlockSpec((1,) + shape[1:], lambda i: (index(i),) + (0,) * (len(shape) - 1))


def whole_spec(shape):
    return pl.BlockSpec(shape, lambda i: (0,) * len(shape))


def mixer_forward(lengths, g, w, w_out, taps, heads_vec, lanes_vec, heads):
    nb, rows, _ = g.shape
    di = heads * PS
    width = di + 2 * S
    shapes = [
        jax.ShapeDtypeStruct((nb, rows, w_out.shape[1]), BF),
        jax.ShapeDtypeStruct((nb, rows, w.shape[1]), F32),
        jax.ShapeDtypeStruct((nb, rows, di), F32),
        jax.ShapeDtypeStruct((nb, MB, di, S), F32),
    ]
    same = lambda i: i
    return pl.pallas_call(
        functools.partial(forward_kernel, heads),
        grid=(nb,),
        out_shape=shapes,
        in_specs=[pl.BlockSpec(memory_space=pltpu.SMEM), block_spec(g.shape, same)]
        + [whole_spec(v.shape) for v in (w, w_out, taps, heads_vec, lanes_vec)],
        out_specs=[block_spec(v.shape, same) for v in shapes],
        scratch_shapes=[
            pltpu.VMEM((MB, rows // MB + EDGE, width), F32),
            pltpu.VMEM((MB, di, S), F32),
        ],
        compiler_params=pltpu.CompilerParams(vmem_limit_bytes=VMEM_LIMIT),
        name="mixer_forward",
    )(lengths, g, w, w_out, taps, heads_vec, lanes_vec)


def mixer_backward(lengths, grad, w, w_out, taps, heads_vec, lanes_vec, proj, scan, states, heads):
    nb, rows, _ = grad.shape
    di = heads * PS
    width = di + 2 * S
    back = lambda i: nb - 1 - i
    before = lambda i: jnp.maximum(nb - 2 - i, 0)
    per_block = [
        jax.ShapeDtypeStruct((nb, rows, w.shape[1]), BF),
        jax.ShapeDtypeStruct((nb, rows, D), BF),
    ]
    sums = [
        jax.ShapeDtypeStruct((di, w_out.shape[1]), F32),
        jax.ShapeDtypeStruct((8, width), F32),
        jax.ShapeDtypeStruct((8, S), F32),
        jax.ShapeDtypeStruct((8, di), F32),
    ]
    return pl.pallas_call(
        functools.partial(backward_kernel, heads),
        grid=(nb,),
        out_shape=per_block + sums,
        in_specs=[pl.BlockSpec(memory_space=pltpu.SMEM), block_spec(grad.shape, back)]
        + [whole_spec(v.shape) for v in (w, w_out, taps, heads_vec, lanes_vec)]
        + [block_spec(proj.shape, back), block_spec(proj.shape, before)]
        + [block_spec(scan.shape, back), block_spec(states.shape, back)],
        out_specs=[block_spec(v.shape, back) for v in per_block]
        + [whole_spec(v.shape) for v in sums],
        scratch_shapes=[
            pltpu.VMEM((MB, rows // MB + EDGE, width), F32),
            pltpu.VMEM((MB, rows // MB + EDGE, width), F32),
            pltpu.VMEM((MB, di, S), F32),
        ],
        compiler_params=pltpu.CompilerParams(vmem_limit_bytes=VMEM_LIMIT),
        name="mixer_backward",
    )(lengths, grad, w, w_out, taps, heads_vec, lanes_vec, proj, proj, scan, states)


def body(
    tokens,
    lengths,
    routes,
    cotangent,
    input_weight,
    filter_weight,
    filter_bias,
    step_bias,
    decay_log,
    skip_gain,
    norm_gain,
    gated_gain,
    output_weight,
    moe_gain,
    router_weight,
    shared_gate_up,
    shared_down,
    expert_gate_up,
    expert_down,
):
    nd, ne = lax.axis_size("dp"), lax.axis_size("expert")
    me_d, me_e = lax.axis_index("dp"), lax.axis_index("expert")
    loc = tokens.shape[2]
    heads = H // nd
    di = heads * PS
    rows_t = MB * loc
    experts = expert_gate_up.shape[0] * ne
    el = expert_gate_up.shape[0]
    dr = D // nd
    fs = FS // ne
    fsr = FS // nd
    fsl = fsr // ne

    pad = 128 - heads
    blocks = jnp.concatenate(
        [
            jnp.moveaxis(input_weight[:, :DI].reshape(dr, nd, di), 1, 0),
            jnp.moveaxis(input_weight[:, DI : 2 * DI].reshape(dr, nd, di), 1, 0),
            jnp.broadcast_to(input_weight[None, :, 2 * DI : 2 * DI + 2 * S], (nd, dr, 2 * S)),
            jnp.moveaxis(input_weight[:, DI + CONV :].reshape(dr, nd, heads), 1, 0),
            jnp.zeros((nd, dr, pad), BF),
        ],
        axis=2,
    )
    w_in = lax.all_to_all(blocks, "dp", 0, 0, tiled=True).reshape(D, -1)
    wcols = w_in.shape[1]

    sg = shared_gate_up.reshape(dr, 2, nd, ne, fsl)
    sg = lax.dynamic_index_in_dim(sg, me_e, 3, False).reshape(dr, 2 * fs)
    sd = lax.dynamic_slice_in_dim(shared_down, me_e * fsl, fsl, 0)
    packed = jnp.concatenate([sg.reshape(-1), sd.reshape(-1), router_weight.reshape(-1)])
    packed_cols = packed.size // rows_t
    packed = jnp.pad(packed.reshape(rows_t, -1), ((0, 0), (0, 256 - packed_cols)))

    stream = tokens.reshape(rows_t, D).astype(F32)
    incoming = cotangent.reshape(rows_t, D)
    route_rows = routes.reshape(rows_t, TOP)
    normed_wide, norm_pull = jax.vjp(rms_scale, stream, norm_gain)
    normed = normed_wide.astype(BF)
    normed_all = gather(jnp.concatenate([normed, packed], axis=1), "dp", 1)
    early, _ = lax.optimization_barrier((incoming, normed_all))
    inc_all = lax.all_gather(early, "expert", axis=0, tiled=True)
    packed_all = normed_all[:, :, D:].reshape(nd, rows_t, 256)[:, :, : packed_cols]
    packed_all = packed_all.reshape(nd, -1)
    sg_full = packed_all[:, : sg.size].reshape(D, 2 * fs)
    sd_full = packed_all[:, sg.size : sg.size + sd.size].reshape(fs, D)
    router_full = packed_all[:, sg.size + sd.size :].reshape(D, experts)
    w_wide = jnp.pad(w_in, ((0, 256), (0, 0)))
    taps = jnp.concatenate(
        [lax.dynamic_slice_in_dim(filter_weight, me_d * di, di, 1), filter_weight[:, DI:]], axis=1
    )
    tap_bias = jnp.concatenate(
        [lax.dynamic_slice_in_dim(filter_bias, me_d * di, di, 0), filter_bias[DI:]], axis=0
    )
    my_heads = lambda v: lax.dynamic_slice_in_dim(v, me_d * heads, heads, 0)
    my_gain = lax.dynamic_slice_in_dim(gated_gain, me_d * di, di, 0)

    taps_vec = jnp.concatenate([taps, tap_bias[None], jnp.zeros((3, di + 2 * S), F32)], axis=0)
    heads_vec = jnp.stack([my_heads(step_bias), -jnp.exp(my_heads(decay_log))])
    heads_vec = jnp.pad(heads_vec, ((0, 6), (0, S - heads)))
    lanes_vec = jnp.pad(
        jnp.stack([my_gain, jnp.repeat(my_heads(skip_gain), PS)]), ((0, 6), (0, 0))
    )
    out_wide = jnp.pad(output_weight, ((0, 0), (0, 128)))
    vectors = (taps_vec, heads_vec, lanes_vec)
    payload, proj, scan, states = mixer_forward(
        lengths[:, 0], normed_all, w_wide, out_wide, *vectors, heads
    )
    column = lax.broadcasted_iota(jnp.int32, (1, D + 128), 1)
    summed = reduce_scatter(payload, "dp", 2)
    r = lax.rsqrt((summed[:, D : D + 1] + summed[:, D + 1 : D + 2]) / DI + EPSILON)
    mixed = summed[:, :D] * r
    after_mixer = stream + mixed
    moe_wide, moe_pull = jax.vjp(rms_scale, after_mixer, moe_gain)
    moe_in = moe_wide.astype(BF)
    logits = mm(moe_in, router_full)
    chosen = (route_rows[:, :, None] == jnp.arange(experts, dtype=jnp.int32)).astype(F32)
    picked = jnp.sum(chosen * logits[:, None, :], axis=2)
    gates = jax.nn.softmax(picked, axis=1)
    table = jnp.sum(chosen * gates[:, :, None], axis=1)
    t_hi, t_lo = hi_lo(table)
    moe_payload = jnp.concatenate(
        [moe_in, t_hi, t_lo, jnp.zeros((rows_t, 128 - 2 * experts), BF)], axis=1
    )
    moe_all = gather(moe_payload, "expert", 3).reshape(ne * rows_t, D + 128)
    table_all = moe_all[:, D : D + experts].astype(F32) + moe_all[
        :, D + experts : D + 2 * experts
    ].astype(F32)
    my_gates = lax.dynamic_slice_in_dim(table_all, me_e * el, el, 1)
    n_tok = ne * rows_t

    w_up = jnp.concatenate(
        [expert_gate_up[i][:, :FE] for i in range(el)]
        + [sg_full[:, :fs]]
        + [expert_gate_up[i][:, FE:] for i in range(el)]
        + [sg_full[:, fs:]],
        axis=1,
    )
    w_up = jnp.pad(w_up, ((0, 128), (0, 0)))
    w_down = jnp.concatenate([expert_down[i] for i in range(el)] + [sd_full], axis=0)
    width = w_down.shape[0]
    scale = jnp.concatenate(
        [jnp.broadcast_to(my_gates[:, i : i + 1], (n_tok, FE)) for i in range(el)]
        + [jnp.ones((n_tok, fs), F32)],
        axis=1,
    )
    pre = mm(moe_all, w_up)
    a, b = pre[:, :width], pre[:, width:]
    sig = jax.nn.sigmoid(a)
    act = a * sig
    hidden = act * b
    u = mm_nt(inc_all, w_down)
    prod = u * hidden
    gate_grad = jnp.concatenate(
        [jnp.sum(prod[:, i * FE : (i + 1) * FE], axis=1, keepdims=True) for i in range(el)], axis=1
    )
    gh = (scale * hidden).astype(BF)
    gu = scale * u
    pre_grad = jnp.concatenate(
        [gu * b * (sig + act * (1.0 - sig)), gu * act], axis=1
    ).astype(BF)
    out_part = mm(gh, w_down)
    dx_part = mm_nt(pre_grad, w_up)
    d_up = mm_tn(moe_all, pre_grad)[:D]
    d_down = mm_tn(gh, inc_all)
    for i in range(el):
        g_hi, g_lo = hi_lo(gate_grad[:, i : i + 1])
        place = D + me_e * el + i
        dx_part = jnp.where(column == place, g_hi.astype(F32), dx_part)
        dx_part = jnp.where(column == place + experts, g_lo.astype(F32), dx_part)
    back_sum = reduce_scatter(dx_part.astype(BF).reshape(ne, rows_t, D + 128), "expert", 4)
    inc = incoming.astype(F32)
    spread_sum = back_sum[:, D : D + experts] + back_sum[:, D + experts : D + 2 * experts]
    logit_grad = table * (spread_sum - jnp.sum(table * spread_sum, axis=1, keepdims=True))
    logit_low = logit_grad.astype(BF)
    router_part = mm_tn(moe_in, logit_low)
    moe_in_grad = back_sum[:, :D] + mm_nt(logit_low, router_full)
    after_from_norm, moe_gain_grad = moe_pull(moe_in_grad)
    after_grad = inc + after_from_norm
    after_low = after_grad.astype(BF)
    s = jnp.sum(after_low.astype(F32) * mixed, axis=1, keepdims=True)
    r_hi, r_lo = hi_lo(r)
    d_hi, d_lo = hi_lo(s)
    grad_payload = jnp.concatenate(
        [after_low, r_hi, r_lo, d_hi, d_lo, jnp.zeros((rows_t, 124), BF)], axis=1
    )
    grad_all = gather(grad_payload, "dp", 5)
    d_proj, normed_part, output_part, d_taps, d_heads, d_lanes = mixer_backward(
        lengths[:, 0], grad_all, w_wide, out_wide, *vectors, proj, scan, states, heads
    )
    output_part = output_part[:, :D]
    out_part, _ = lax.optimization_barrier((out_part.astype(BF), d_proj))
    out_sum = lax.psum_scatter(out_part, "expert", scatter_dimension=0, tiled=True)
    normed_grad = reduce_scatter(normed_part, "dp", 6)
    d_win = mm_tn(normed_all.reshape(nd * rows_t, -1), d_proj.reshape(nd * rows_t, wcols))
    d_win = d_win[:D].astype(BF)
    stream_from_norm, norm_gain_grad = norm_pull(normed_grad)
    tokens_grad = after_grad + stream_from_norm

    d_up = d_up.astype(BF)
    d_down = d_down.astype(BF)
    up_blocks = d_up.reshape(nd, dr, 2 * width)
    down_blocks = jnp.stack(
        [d_down[i * FE : (i + 1) * FE].reshape(nd, FE // nd, D) for i in range(el)], axis=1
    ).reshape(nd, el * FE // nd, D)
    down_blocks = jnp.concatenate([down_blocks, d_down[el * FE :].reshape(nd, fsl, D)], axis=1)
    down_blocks = down_blocks.reshape(nd, -1, 2 * width)
    all_blocks = jnp.concatenate([up_blocks, down_blocks], axis=1)
    all_sum = lax.psum_scatter(all_blocks, "dp", scatter_dimension=0, tiled=True)[0]
    up_sum, down_sum = all_sum[:dr], all_sum[dr:].reshape(-1, D)
    expert_up_grad = jnp.stack(
        [
            jnp.concatenate(
                [
                    up_sum[:, i * FE : (i + 1) * FE],
                    up_sum[:, width + i * FE : width + (i + 1) * FE],
                ],
                axis=1,
            )
            for i in range(el)
        ],
        axis=0,
    ).astype(F32)
    expert_down_grad = down_sum[: el * FE // nd].reshape(el, FE // nd, D).astype(F32)
    shared_part = jnp.concatenate(
        [
            up_sum[:, el * FE : width],
            up_sum[:, width + el * FE :],
            down_sum[el * FE // nd :].reshape(dr, -1),
        ],
        axis=1,
    )

    def spread_heads(v, size, chunk):
        return lax.dynamic_update_slice(
            jnp.zeros(v.shape[:-1] + (size,), F32), v, (0,) * (v.ndim - 1) + (me_d * chunk,)
        )

    small_parts = (
        jnp.concatenate([spread_heads(d_taps[:K, :di], DI, di), d_taps[:K, di:]], axis=1),
        jnp.concatenate([spread_heads(d_taps[K, :di], DI, di), d_taps[K, di:]], axis=0),
        spread_heads(d_heads[0, :heads], H, heads),
        spread_heads(d_heads[1, :heads], H, heads),
        spread_heads(jnp.sum(d_lanes[1].reshape(heads, PS), axis=1), H, heads),
        norm_gain_grad,
        spread_heads(d_lanes[0], DI, di),
        moe_gain_grad,
        router_part,
    )
    sizes = [part.size for part in small_parts]
    lanes = -(-sum(sizes) // (nd * 1024)) * 8
    small_flat = jnp.concatenate([part.reshape(-1) for part in small_parts])
    small_flat = jnp.pad(small_flat, (0, nd * lanes * 128 - sum(sizes))).reshape(nd, lanes, 128)

    main = 2 * di
    back_in, small_in = exchange(
        (("all", "dp"), ("all", "dp")), (d_win.reshape(nd, dr, wcols), small_flat), 7
    )
    misc = jnp.concatenate(
        [
            jnp.sum(back_in[:, :, main : main + 2 * S].astype(F32), axis=0),
            jnp.moveaxis(back_in[:, :, main + 2 * S : main + 2 * S + heads], 0, 1)
            .reshape(dr, H)
            .astype(F32),
        ],
        axis=1,
    )
    misc_size = misc.size
    misc_rows = -(-misc_size // (ne * 1024)) * 8
    misc = jnp.pad(misc.reshape(-1), (0, ne * misc_rows * 128 - misc_size))
    got = exchange(
        (("all", "expert"), ("all", "expert"), ("all", "expert"), ("gather", "expert")),
        (
            back_in[:, :, :main].reshape(ne, nd // ne * dr, main),
            misc.reshape(ne, misc_rows, 128),
            output_part.astype(BF).reshape(ne, 48, -1),
            jnp.sum(small_in, axis=0),
        ),
        8,
    )
    main_sum, misc_sum, out_grad_sum, small_sum = [jnp.sum(v.astype(F32), axis=0) for v in got]
    main_all, misc_all, out_grad_all, shared_all, small_all = exchange(
        (
            ("gather", "expert"),
            ("gather", "expert"),
            ("gather", "expert"),
            ("gather", "expert"),
            ("gather", "dp"),
        ),
        (main_sum.astype(BF), misc_sum, out_grad_sum.astype(BF), shared_part, small_sum),
        9,
    )
    main_all = main_all.reshape(nd, dr, main).astype(F32)
    misc_all = misc_all.reshape(-1)[:misc_size].reshape(dr, 2 * S + H)
    input_grad = jnp.concatenate(
        [
            jnp.moveaxis(main_all[:, :, :di], 0, 1).reshape(dr, DI),
            jnp.moveaxis(main_all[:, :, di:], 0, 1).reshape(dr, DI),
            misc_all,
        ],
        axis=1,
    )
    output_grad = out_grad_all.reshape(output_weight.shape)
    shared_up_grad = (
        jnp.moveaxis(shared_all[:, :, : 2 * fs].reshape(ne, dr, 2, nd, fsl), 0, 3)
        .reshape(dr, 2 * FS)
        .astype(F32)
    )
    shared_down_grad = shared_all[:, :, 2 * fs :].reshape(fsr, D).astype(F32)
    small_all = small_all.reshape(-1)
    small, start = [], 0
    for part, size in zip(small_parts, sizes):
        small.append(small_all[start : start + size].reshape(part.shape))
        start += size
    router_grad = lax.dynamic_slice_in_dim(small[8], me_d * dr, dr, 0)
    block_output = (after_mixer + out_sum.astype(F32)).astype(BF)
    shape = (MB, 1, loc, D)
    return (
        block_output.reshape(shape),
        tokens_grad.reshape(shape),
        input_grad,
        small[0],
        small[1],
        small[2],
        small[3],
        small[4],
        small[5],
        small[6],
        output_grad.astype(F32),
        small[7],
        router_grad,
        shared_up_grad,
        shared_down_grad,
        expert_up_grad,
        expert_down_grad,
    )


def solution(mesh):
    in_specs = (
        P(None, "expert", "dp", None),
        P(None, "expert", None),
        P(None, "expert", "dp", None),
        P(None, "expert", "dp", None),
        P("dp", None),
        P(),
        P(),
        P(),
        P(),
        P(),
        P(),
        P(),
        P("dp", None),
        P(),
        P("dp", None),
        P("dp", None),
        P("dp", None),
        P("expert", None, None),
        P("expert", None, None),
    )
    out_specs = (
        P(None, "expert", "dp", None),
        P(None, "expert", "dp", None),
        P("dp", None),
        P(),
        P(),
        P(),
        P(),
        P(),
        P(),
        P(),
        P("dp", None),
        P(),
        P("dp", None),
        P("dp", None),
        P("dp", None),
        P("expert", "dp", None),
        P("expert", "dp", None),
    )
    return jax.shard_map(body, mesh=mesh, in_specs=in_specs, out_specs=out_specs, check_vma=False)
```

```python
import functools

import jax
import jax.numpy as jnp
from jax import lax
from jax.experimental import pallas as pl
from jax.experimental.pallas import tpu as pltpu
from jax.sharding import PartitionSpec as P

D = 1536
H = 48
PS = 64
S = 128
K = 4
FE = 512
FS = 1024
TOP = 6
MB = 2
DI = 3072
CONV = 3328
IN_W = 6448
EPSILON = 1e-05
BF = jnp.bfloat16
F32 = jnp.float32
MESH = pl.DeviceIdType.MESH
VMEM_LIMIT = 60 * 1024 * 1024


def mm(a, b):
    return jnp.dot(a, b, preferred_element_type=F32)


def mm_nt(a, b):
    return lax.dot_general(a, b, (((1,), (1,)), ((), ())), preferred_element_type=F32)


def mm_tn(a, b):
    return lax.dot_general(a, b, (((0,), (0,)), ((), ())), preferred_element_type=F32)


def rms_scale(values, gain):
    return values * lax.rsqrt(jnp.mean(values * values, axis=-1, keepdims=True) + EPSILON) * gain


def hi_lo(v):
    hi = v.astype(BF)
    return hi, (v - hi.astype(F32)).astype(BF)


ANY = pl.BlockSpec(memory_space=pl.ANY)
IN_VMEM = pl.BlockSpec(memory_space=pltpu.VMEM)


def places(axis):
    me = lax.axis_index(axis)
    if axis == "dp":
        core, ring, pair = lax.rem(me, 2), lax.rem(me // 2, 4), me // 8

        def at(hop, other, sibling=0):
            z = lax.rem(pair + other, 2)
            return (z * 4 + lax.rem(ring + hop + 4, 4)) * 2 + lax.rem(core + sibling, 2)
    else:
        pair, ring = lax.rem(me, 2), me // 2

        def at(hop, other, sibling=0):
            return lax.rem(ring + hop + 4, 4) * 2 + lax.rem(pair + other, 2)

    return me, at


class Task:
    ins, outs, scratch, reaches = (), (), (), ()


def peers_of(axis, everyone):
    me, at = places(axis)
    if everyone:
        n = lax.axis_size(axis)
        return [lax.rem(me + k, n) for k in range(1, n)]
    near = [at(1, 0), at(-1, 0), at(0, 1)]
    return near + [at(0, 0, 1)] if axis == "dp" else near


class Links:
    def __init__(self, axis, send, recv):
        self.axis, self.send, self.recv, self.started = axis, send, recv, []

    def push(self, number, src, dst, peer):
        copy = pltpu.make_async_remote_copy(
            src_ref=src,
            dst_ref=dst,
            send_sem=self.send.at[number],
            recv_sem=self.recv.at[number],
            device_id={self.axis: peer},
            device_id_type=MESH,
        )
        copy.start()
        self.started.append(copy)

    def arrived(self, number, dst):
        pltpu.make_async_copy(dst, dst, self.recv.at[number]).wait()

    def finish(self):
        for copy in self.started:
            copy.wait_send()


def halves(rows):
    cut = rows // 32 * 16
    return pl.ds(0, rows), pl.ds(0, cut), pl.ds(cut, rows - cut), cut


class Gather(Task):
    def __init__(self, axis, x):
        self.axis, self.reaches = axis, ((axis, False),)
        self.ins = ((x, ANY),)
        n = lax.axis_size(axis)
        self.outs = ((jax.ShapeDtypeStruct((n,) + x.shape, x.dtype), ANY),)
        dma = pltpu.SemaphoreType.DMA
        self.scratch = (dma((17,)), dma((17,)), dma)

    def steps(self, ins, outs, scratch):
        return gather_steps(self.axis, ins[0], outs[0], *scratch)


def gather_steps(axis, x, out, send, recv, own_sem):
    me, at = places(axis)
    cores = axis == "dp"
    up, down, pair, sib = at(1, 0), at(-1, 0), at(0, 1), at(0, 0, 1)
    whole, first, second, _ = halves(x.shape[0])
    links = Links(axis, send, recv)

    def push(number, slot, rows, peer, src=None):
        src = out.at[slot] if src is None else src
        links.push(number, src.at[rows], out.at[slot].at[rows], peer)

    def arrived(number, slot, rows):
        links.arrived(number, out.at[slot].at[rows])

    push(0, me, whole, up, x)
    push(1, me, whole, down, x)
    push(2, me, whole, pair, x)
    if cores:
        push(3, me, whole, sib, x)
    own = pltpu.make_async_copy(x, out.at[me], own_sem)
    own.start()
    yield
    arrived(2, pair, whole)
    push(4, pair, whole, up)
    push(5, pair, whole, down)
    if cores:
        push(6, pair, whole, sib)
    yield
    arrived(0, down, whole)
    push(7, down, first, up)
    arrived(1, up, whole)
    push(8, up, second, down)
    if cores:
        push(9, down, whole, sib)
        push(10, up, whole, sib)
    yield
    arrived(4, at(-1, 1), whole)
    push(11, at(-1, 1), first, up)
    arrived(5, at(1, 1), whole)
    push(12, at(1, 1), second, down)
    if cores:
        push(13, at(-1, 1), whole, sib)
        push(14, at(1, 1), whole, sib)
    yield
    arrived(7, at(2, 0), first)
    arrived(8, at(2, 0), second)
    if cores:
        push(15, at(2, 0), whole, sib)
    yield
    arrived(11, at(2, 1), first)
    arrived(12, at(2, 1), second)
    if cores:
        push(16, at(2, 1), whole, sib)
        yield
        for number, hop, other in (
            (3, 0, 0),
            (6, 0, 1),
            (9, -1, 0),
            (10, 1, 0),
            (13, -1, 1),
            (14, 1, 1),
            (15, 2, 0),
            (16, 2, 1),
        ):
            arrived(number, at(hop, other, 1), whole)
    own.wait()
    links.finish()


ORDER = ((2, 1), (2, 0), (1, 1), (-1, 1), (1, 0), (-1, 0), (0, 1), (0, 0))


class Reduce(Task):
    def __init__(self, axis, x, dtype=F32):
        self.axis, self.reaches = axis, ((axis, False),)
        n, rows, columns = x.shape
        self.ins = ((x, ANY),)
        self.outs = ((jax.ShapeDtypeStruct((rows, columns), dtype), IN_VMEM),)
        _, _, _, cut = halves(rows)
        buf = lambda *dims: pltpu.VMEM(dims + (columns,), BF)
        dma = pltpu.SemaphoreType.DMA
        dp = axis == "dp"
        self.scratch = (
            buf(8, rows),
            buf(8 if dp else 1, rows if dp else 16),
            buf(2, cut),
            buf(2, rows - cut),
            buf(2, rows),
            buf(2, rows),
            buf(rows),
            dma((17,)),
            dma((17,)),
            dma((8,)),
        )

    def steps(self, ins, outs, scratch):
        return reduce_steps(self.axis, ins[0], outs[0], *scratch)


def reduce_steps(axis, x, out, acc, sib_buf, a_buf, b_buf, c_buf, d_buf, e_buf, send, recv, load):
    me, at = places(axis)
    cores = axis == "dp"
    rows = acc.shape[1]
    step = 16
    block = lambda k: x.at[k] if len(x.shape) == 3 else x.at[pl.ds(pl.multiple_of(k * rows, 16), rows)]
    up, down, pair, sib = at(1, 0), at(-1, 0), at(0, 1), at(0, 0, 1)
    whole, first, second, cut = halves(rows)
    links = Links(axis, send, recv)
    push, arrived = links.push, links.arrived

    def add(dst, offset, count, *srcs):
        @pl.loop(0, count // step)
        def _(i):
            at_rows = pl.ds(pl.multiple_of(offset + i * step, step), step)
            total = dst[at_rows, :].astype(F32)
            for src in srcs:
                total += src[pl.ds(pl.multiple_of(i * step, step), step), :].astype(F32)
            dst[at_rows, :] = total.astype(dst.dtype)

    loads = []
    for k, (hop, other) in enumerate(ORDER):
        if cores:
            push(k, block(at(hop, other, 1)), sib_buf.at[k], sib)
        copy = pltpu.make_async_copy(block(at(hop, other)), acc.at[k], load.at[k])
        copy.start()
        loads.append(copy)

    def ready(k):
        loads[k].wait()
        if cores:
            arrived(k, sib_buf.at[k])
            add(acc.at[k], 0, rows, sib_buf.at[k])

    yield
    for k in range(2):
        ready(k)
        push(8 + 2 * k, acc.at[k].at[first], a_buf.at[k], up)
        push(9 + 2 * k, acc.at[k].at[second], b_buf.at[k], down)
    for k in range(2):
        above, below = 2 + 2 * k, 3 + 2 * k
        ready(above)
        ready(below)
        if k:
            yield
        arrived(8 + 2 * k, a_buf.at[k])
        add(acc.at[above], 0, cut, a_buf.at[k])
        push(12 + 2 * k, acc.at[above], c_buf.at[k], up)
        arrived(9 + 2 * k, b_buf.at[k])
        add(acc.at[below], cut, rows - cut, b_buf.at[k])
        push(13 + 2 * k, acc.at[below], d_buf.at[k], down)
    ready(6)
    ready(7)
    yield
    arrived(12, c_buf.at[0])
    arrived(13, d_buf.at[0])
    add(acc.at[6], 0, rows, c_buf.at[0], d_buf.at[0])
    push(16, acc.at[6], e_buf, pair)
    yield
    arrived(14, c_buf.at[1])
    arrived(15, d_buf.at[1])
    yield
    arrived(16, e_buf)

    @pl.loop(0, rows // step)
    def _(i):
        at_rows = pl.ds(pl.multiple_of(i * step, step), step)
        total = acc[7, at_rows, :].astype(F32) + c_buf[1, at_rows, :].astype(F32)
        total += d_buf[1, at_rows, :].astype(F32) + e_buf[at_rows, :].astype(F32)
        out[at_rows, :] = total.astype(out.dtype)

    links.finish()


class Direct(Task):
    def __init__(self, kind, axis, x):
        self.kind, self.axis, self.reaches = kind, axis, ((axis, True),)
        n = lax.axis_size(axis)
        shape = (n,) + x.shape if kind == "gather" else x.shape
        self.ins = ((x, ANY),)
        self.outs = ((jax.ShapeDtypeStruct(shape, x.dtype), ANY),)
        dma = pltpu.SemaphoreType.DMA
        self.scratch = (dma((n,)), dma((n,)), dma)

    def steps(self, ins, outs, scratch):
        return direct_steps(self.kind, self.axis, ins[0], outs[0], *scratch)


def direct_steps(kind, axis, x, out, send, recv, own_sem):
    n, me = lax.axis_size(axis), lax.axis_index(axis)
    links = Links(axis, send, recv)
    piece = lambda k: x if kind == "gather" else x.at[k]
    for k in range(1, n):
        peer = lax.rem(me + k, n)
        links.push(k, piece(peer), out.at[me], peer)
    own = pltpu.make_async_copy(piece(me), out.at[me], own_sem)
    own.start()
    yield
    for k in range(1, n):
        links.arrived(k, out.at[lax.rem(me - k + n, n)])
    own.wait()
    links.finish()


class Swap(Task):
    reaches = (("dp", True),)

    def __init__(self, x):
        self.ins = ((x, ANY),)
        relay = jax.ShapeDtypeStruct((2,) + x.shape[1:], x.dtype)
        self.outs = ((jax.ShapeDtypeStruct(x.shape, x.dtype), ANY), (relay, ANY))
        dma = pltpu.SemaphoreType.DMA
        self.scratch = (dma((18,)), dma((18,)), dma)

    def steps(self, ins, outs, scratch):
        return swap_steps(ins[0], *outs, *scratch)


def swap_steps(x, out, relay, send, recv, own_sem):
    me, at = places("dp")
    links = Links("dp", send, recv)
    number = 2
    plain = []
    for sibling in range(2):
        links.push(sibling, x.at[at(2, 1, sibling)], relay.at[sibling], at(-1, 0))
    for hop in (1, -1, 2, 0):
        for other in range(2):
            for sibling in range(2):
                if (hop, other) == (2, 1) or (hop, other, sibling) == (0, 0, 0):
                    continue
                peer = at(hop, other, sibling)
                links.push(number, x.at[peer], out.at[me], peer)
                plain.append((number, at(-hop, other, sibling)))
                number += 1
    own = pltpu.make_async_copy(x.at[me], out.at[me], own_sem)
    own.start()
    yield
    for sibling in range(2):
        links.arrived(sibling, relay.at[sibling])
        links.push(number + sibling, relay.at[sibling], out.at[at(1, 0)], at(-1, 1, sibling))
    yield
    for k, source in plain:
        links.arrived(k, out.at[source])
    for sibling in range(2):
        links.arrived(number + sibling, out.at[at(2, 1, sibling)])
    own.wait()
    links.finish()


def run_tasks(tasks, number, name):
    operands, in_specs, out_shapes, out_specs, scratch, spans = [], [], [], [], [], []
    for task in tasks:
        spans.append((len(operands), len(out_shapes), len(scratch)))
        operands += [x for x, _ in task.ins]
        in_specs += [spec for _, spec in task.ins]
        out_shapes += [shape for shape, _ in task.outs]
        out_specs += [spec for _, spec in task.outs]
        scratch += list(task.scratch)

    def kernel(*refs):
        ins = refs[: len(operands)]
        outs = refs[len(operands) : len(operands) + len(out_shapes)]
        temps = refs[len(operands) + len(out_shapes) :]
        barrier = pltpu.get_barrier_semaphore()
        count = 0
        for axis in ("dp", "expert"):
            here = [everyone for task in tasks for name, everyone in task.reaches if name == axis]
            if here:
                peers = peers_of(axis, any(here))
                for peer in peers:
                    pl.semaphore_signal(
                        barrier, inc=1, device_id={axis: peer}, device_id_type=MESH
                    )
                count += len(peers)
        pl.semaphore_wait(barrier, count)
        running = []
        for task, (i, o, s) in zip(tasks, spans):
            running.append(
                task.steps(
                    ins[i : i + len(task.ins)],
                    outs[o : o + len(task.outs)],
                    temps[s : s + len(task.scratch)],
                )
            )
        while running:
            running = [steps for steps in running if next(steps, "end") != "end"]

    results = pl.pallas_call(
        kernel,
        out_shape=out_shapes,
        in_specs=in_specs,
        out_specs=out_specs,
        scratch_shapes=scratch,
        compiler_params=pltpu.CompilerParams(
            collective_id=number, has_side_effects=True, vmem_limit_bytes=VMEM_LIMIT
        ),
        name=name,
    )(*operands)
    return [results[o : o + len(task.outs)] for task, (_, o, _) in zip(tasks, spans)]


class Weights(Task):
    def __init__(self, x):
        self.reaches = (("dp", True), ("expert", False))
        self.swap, self.spread = Direct("all", "dp", x), Gather("expert", x)
        n = lax.axis_size("expert")
        full = jax.ShapeDtypeStruct((n,) + x.shape, x.dtype)
        self.ins = ((x, ANY),)
        self.outs = self.swap.outs + ((full, ANY),)
        self.scratch = self.swap.scratch + self.spread.scratch

    def steps(self, ins, outs, scratch):
        yield from direct_steps("all", "dp", ins[0], outs[0], *scratch[:3])
        yield
        yield from gather_steps("expert", outs[0], outs[1], *scratch[3:])


class ExpertTail(Task):
    def __init__(self, x, pre_grad, gh, inc, w_down, experts, blocks):
        self.reaches = (("expert", False),)
        self.experts = experts
        tokens, width = gh.shape
        depth = inc.shape[1]
        n = lax.axis_size("expert")
        part = jax.ShapeDtypeStruct((n, tokens // n, depth), BF)
        self.reduce = Reduce("expert", part)
        rows = depth // blocks + 2 * (FE // blocks)
        grads = jax.ShapeDtypeStruct((blocks, rows, 2 * width), BF)
        self.ins = tuple((v, ANY) for v in (x, pre_grad, gh, inc, w_down))
        self.outs = self.reduce.outs + ((grads, ANY),)
        dma = pltpu.SemaphoreType.DMA
        vmem = lambda v: pltpu.VMEM(v.shape, BF)
        self.scratch = (
            tuple(vmem(v) for v in (x, pre_grad, gh, inc, w_down))
            + (dma((6,)), vmem(part), pltpu.VMEM((depth, tokens), BF))
            + (pltpu.VMEM((width, tokens), BF), vmem(grads))
            + self.reduce.scratch
        )

    def steps(self, ins, outs, scratch):
        x, pre_grad, gh, inc, w_down, sems, part, x_t, gh_t, grads = scratch[:10]
        loads = []
        for k, (src, dst) in enumerate(zip(ins, scratch[:5])):
            copy = pltpu.make_async_copy(src, dst, sems.at[k])
            copy.start()
            loads.append(copy)
        tokens, width = gh.shape
        depth = inc.shape[1]
        tile = 256
        loads[2].wait()
        loads[4].wait()
        n, rows = part.shape[0], part.shape[1]
        col = lambda i: pl.ds(pl.multiple_of(i * tile, tile), tile)
        for half in range(2):

            @pl.loop(half * depth // tile // 2, (half + 1) * depth // tile // 2)
            def _(i):
                part[:, :, col(i)] = mm(gh[...], w_down[:, col(i)]).astype(BF).reshape(
                    n, rows, tile
                )

            yield
        summing = reduce_steps("expert", part, outs[0], *scratch[10:])
        next(summing)
        yield
        for load in (loads[0], loads[1], loads[3]):
            load.wait()

        @pl.loop(0, depth // tile)
        def _(i):
            x_t[col(i), :] = x[:, col(i)].T

        @pl.loop(0, width // 128)
        def _(i):
            at_cols = pl.ds(pl.multiple_of(i * 128, 128), 128)
            gh_t[at_cols, :] = gh[:, at_cols].T

        next(summing)
        yield
        blocks = grads.shape[0]
        up_rows = depth // blocks
        for third in range(3):
            steps = 2 * width // tile // 3

            @pl.loop(third * steps, (third + 1) * steps)
            def _(i):
                value = mm(x_t[...], pre_grad[:, col(i)]).astype(BF)
                grads[:, :up_rows, col(i)] = value.reshape(blocks, up_rows, tile)

            next(summing, None)
            yield
        each = FE // blocks
        shared = width - self.experts * FE
        own = shared // blocks
        span = depth // 2
        spots = (((0, 0), (0, 2)), ((0, 1), (each, 0)))
        for half in range(2):

            @pl.loop(0, span // tile)
            def _(i):
                value = mm(gh_t[...], inc[:, col(half * span // tile + i)])
                for e in range(self.experts):
                    row, place = spots[half][e]
                    piece = value[e * FE : (e + 1) * FE].astype(BF)
                    grads[
                        :, up_rows + row : up_rows + row + each, col(place * span // tile + i)
                    ] = piece.reshape(blocks, each, tile)
                piece = value[self.experts * FE :].reshape(blocks, own, tile)
                empty = jnp.zeros((blocks, each - own, tile), F32)
                piece = jnp.concatenate([piece, empty], axis=1).astype(BF)
                grads[:, up_rows + each :, col((1 + half) * span // tile + i)] = piece

            next(summing, None)
            yield
        store = pltpu.make_async_copy(grads, outs[1], sems.at[5])
        store.start()
        for _ in summing:
            yield
        store.wait()


class InputGrad(Task):
    def __init__(self, g, d_proj, out_grad):
        self.reaches = (("expert", False),)
        rows, wide = D + out_grad.shape[0], d_proj.shape[1]
        n = lax.axis_size("expert")
        self.reduce = Reduce("expert", jax.ShapeDtypeStruct((n, rows // n, wide), BF), BF)
        self.ins = tuple((v, ANY) for v in (g, d_proj, out_grad))
        self.outs = self.reduce.outs
        dma = pltpu.SemaphoreType.DMA
        self.scratch = (
            pltpu.VMEM(g.shape[:2] + (D,), BF),
            pltpu.VMEM(d_proj.shape, BF),
            pltpu.VMEM((rows, wide), BF),
            dma((3,)),
        ) + self.reduce.scratch

    def steps(self, ins, outs, scratch):
        g, d_proj, total, sems = scratch[:4]
        loads = (
            pltpu.make_async_copy(ins[0].at[:, :, pl.ds(0, D)], g, sems.at[0]),
            pltpu.make_async_copy(ins[1], d_proj, sems.at[1]),
            pltpu.make_async_copy(ins[2], total.at[pl.ds(D, ins[2].shape[0])], sems.at[2]),
        )
        for load in loads:
            load.start()
        yield
        for load in loads:
            load.wait()
        tile = 256
        flat = g.shape[0] * g.shape[1]
        for part in range(3):

            @pl.loop(part * D // tile // 3, (part + 1) * D // tile // 3)
            def _(i):
                at_rows = pl.ds(pl.multiple_of(i * tile, tile), tile)
                total[at_rows, :] = mm_tn(g[:, :, at_rows].reshape(flat, tile), d_proj[...]).astype(BF)

            yield
        yield from reduce_steps("expert", total, outs[0], *scratch[4:])


EDGE = 8
HIGHEST = lax.Precision.HIGHEST


def exact(a, b, dims):
    return lax.dot_general(a, b, (dims, ((), ())), precision=HIGHEST, preferred_element_type=F32)


def iota(shape, axis):
    return lax.broadcasted_iota(jnp.int32, shape, axis)


class Block:
    def __init__(self, m, start, proj, ext, lengths, taps, heads_vec, heads):
        loc = proj.shape[0]
        di = heads * PS
        width = di + 2 * S
        self.heads, self.di = heads, di
        first = lengths[m, 0]
        second = first + lengths[m, 1]

        def doc(p):
            return (p >= first).astype(jnp.int32) + (p >= second).astype(jnp.int32)

        self.doc = doc
        self.at = start + iota((loc, 1), 0)
        docs = doc(self.at)
        docs_row = doc(start + iota((1, loc), 1))
        last_doc, before_doc = doc(start + loc - 1), doc(start - 1)
        self.keep = (docs == before_doc).astype(F32)
        self.keep_last = (last_doc == before_doc).astype(F32)
        self.same_last = (docs == last_doc).astype(F32)
        self.gate = proj[:, :di]
        ext[m, EDGE : EDGE + loc, :] = proj[:, di : di + width].astype(BF).astype(F32)
        total = jnp.broadcast_to(taps[K : K + 1, :], (loc, width))
        self.shifted = []
        for k in range(K):
            back = K - 1 - k
            value = ext[m, EDGE - back : EDGE - back + loc, :]
            if back:
                value = value * (docs == doc(self.at - back)).astype(F32)
            self.shifted.append(value)
            total = total + taps[k : k + 1, :] * value
        self.sig = jax.nn.sigmoid(total)
        self.total = total
        filtered = total * self.sig
        self.x = filtered[:, :di]
        self.write = filtered[:, di : di + S].astype(BF)
        self.read = filtered[:, di + S :].astype(BF)
        self.raw = proj[:, di + width :] + heads_vec[0:1, :]
        self.steps = jnp.maximum(self.raw, 0.0) + jnp.log1p(jnp.exp(-jnp.abs(self.raw)))
        self.rate = heads_vec[1:2, :]
        rise = self.steps * self.rate
        rows, cols = iota((loc, loc), 0), iota((loc, loc), 1)
        self.lower = (cols <= rows).astype(F32)
        self.cum = exact(self.lower, rise, ((1,), (0,)))
        cum_rows = exact(rise, (rows <= cols).astype(F32), ((0,), (0,)))
        self.last = self.cum[loc - 1 : loc, :]
        self.grow = jnp.exp(self.cum) * self.keep
        self.fall = jnp.exp(self.last - self.cum) * self.same_last
        self.decay = jnp.exp(self.last) * self.keep_last
        allowed = (cols <= rows) & (docs == docs_row)
        scores = mm_nt(self.read, self.write)
        self.spread, self.mixing = [], []
        for h in range(heads):
            span = self.cum[:, h : h + 1] - cum_rows[h : h + 1, :]
            shape = jnp.exp(jnp.where(allowed, span, -1e30))
            self.spread.append(shape)
            self.mixing.append(shape * scores)
        self.lane = iota((1, di), 1)
        self.steps_wide = self.widen(self.steps)
        self.grow_wide = self.widen(self.grow)
        self.weight_wide = self.widen(self.fall * self.steps)
        self.scaled = self.x * self.steps_wide
        self.pushed = self.x * self.weight_wide

    def widen(self, v):
        out = jnp.broadcast_to(v[:, 0:1], (v.shape[0], self.di))
        for h in range(1, self.heads):
            out = jnp.where(self.lane >= h * PS, v[:, h : h + 1], out)
        return out

    def per_head(self, parts):
        out = parts[0]
        for h in range(1, self.heads):
            out = jnp.where(self.lane >= h * PS, parts[h], out)
        return out

    def decay_rows(self):
        rows = iota((self.di, 1), 0)
        out = jnp.broadcast_to(self.decay[:, 0:1], (self.di, 1))
        for h in range(1, self.heads):
            out = jnp.where(rows >= h * PS, self.decay[:, h : h + 1], out)
        return out


def forward_kernel(
    heads, lengths, g, w, w_out, taps, heads_vec, lanes_vec, payload, proj, scan, states, ext, state
):
    b = pl.program_id(0)
    loc = g.shape[1] // MB
    di = heads * PS

    @pl.when(b == 0)
    def _():
        ext[...] = jnp.zeros_like(ext)
        state[...] = jnp.zeros_like(state)

    proj[0] = mm(g[0, :, :D], w[...])
    column = iota((loc, payload.shape[2] - D), 1)
    for m in range(MB):
        rows = slice(m * loc, (m + 1) * loc)
        ext[m, 0:EDGE, :] = ext[m, loc : loc + EDGE, :]
        part = Block(m, b * loc, proj[0, rows, :], ext, lengths, taps, heads_vec, heads)
        before = state[m]
        states[0, m] = before
        scaled = part.scaled.astype(BF)
        inner = part.per_head([mm(part.mixing[h].astype(BF), scaled) for h in range(heads)])
        carried = mm_nt(part.read, before.astype(BF)) * part.grow_wide
        out = inner + carried + lanes_vec[1:2, :] * part.x
        scan[0, rows, :] = out
        state[m] = part.decay_rows() * before + mm_tn(part.pushed.astype(BF), part.write)
        y = out * (part.gate * jax.nn.sigmoid(part.gate))
        square = jnp.sum(y * y, axis=1, keepdims=True)
        high = square.astype(BF).astype(F32)
        payload[0, rows, :D] = mm((y * lanes_vec[0:1, :]).astype(BF), w_out[...]).astype(BF)
        sums = jnp.where(column == 0, high, jnp.where(column == 1, square - high, 0.0))
        payload[0, rows, D:] = sums.astype(BF)


def backward_kernel(
    heads,
    lengths,
    grad,
    w,
    w_out,
    taps,
    heads_vec,
    lanes_vec,
    proj,
    proj_before,
    scan,
    states,
    d_proj,
    normed_part,
    d_out,
    d_taps,
    d_heads,
    d_lanes,
    ext,
    d_ext,
    d_state,
):
    step = pl.program_id(0)
    b = pl.num_programs(0) - 1 - step
    loc = grad.shape[1] // MB
    di = heads * PS
    width = di + 2 * S

    @pl.when(step == 0)
    def _():
        for ref in (d_ext, d_state, d_out, d_taps, d_heads, d_lanes):
            ref[...] = jnp.zeros_like(ref)

    gated_grad = mm_nt(grad[0, :, :D], w_out[...])
    extra = grad[0, :, D:].astype(F32)
    has_before = (b > 0).astype(F32)
    pick = (iota((di, S), 0) // PS == iota((di, S), 1)).astype(F32)
    for m in range(MB):
        rows = slice(m * loc, (m + 1) * loc)
        edge = proj_before[0, (m + 1) * loc - EDGE : (m + 1) * loc, di : di + width]
        ext[m, 0:EDGE, :] = edge.astype(BF).astype(F32) * has_before
        part = Block(m, b * loc, proj[0, rows, :], ext, lengths, taps, heads_vec, heads)
        gain, skip = lanes_vec[0:1, :], lanes_vec[1:2, :]
        r = extra[rows, 0:1] + extra[rows, 1:2]
        s = extra[rows, 2:3] + extra[rows, 3:4]
        out = scan[0, rows, :]
        sig = jax.nn.sigmoid(part.gate)
        act = part.gate * sig
        yr = out * act * r
        gg = gated_grad[rows]
        d_lanes[0:1, :] += jnp.sum(gg * yr, axis=0, keepdims=True)
        d_out[...] += mm_tn((yr * gain).astype(BF), grad[0, rows, :D])
        dy = r * (gg * gain) - yr * (r * s / DI)
        d_gate = dy * out * (sig + act * (1.0 - sig))
        do = dy * act
        do_low = do.astype(BF)
        x = part.x
        d_lanes[1:2, :] += jnp.sum(do * x, axis=0, keepdims=True)
        dx = skip * do
        before = states[0, m]
        before_low = before.astype(BF)
        ds = d_state[m]
        ds_low = ds.astype(BF)

        d_scores = jnp.zeros((loc, loc), F32)
        d_scaled, d_cum = [], jnp.zeros((loc, S), F32)
        head_lane = iota((loc, S), 1)
        for h in range(heads):
            inside = (part.lane >= h * PS) & (part.lane < (h + 1) * PS)
            own = jnp.where(inside, part.scaled, 0.0).astype(BF)
            d_mix = mm_nt(do_low, own)
            d_scaled.append(mm_tn(part.mixing[h].astype(BF), do_low))
            d_scores = d_scores + d_mix * part.spread[h]
            d_span = d_mix * part.mixing[h]
            ones = (head_lane == h).astype(F32)
            d_cum = d_cum + exact(d_span, ones, ((1,), (0,))) - exact(d_span, ones, ((0,), (0,)))
        d_scaled = part.per_head(d_scaled)
        dx = dx + d_scaled * part.steps_wide
        d_scores_low = d_scores.astype(BF)
        d_read = mm(d_scores_low, part.write)
        d_write = mm_tn(d_scores_low, part.read)

        d_carry = do * part.grow_wide
        d_carry_low = d_carry.astype(BF)
        carried = mm_nt(part.read, before_low)
        d_read = d_read + mm(d_carry_low, before_low)

        d_pushed = mm_nt(part.write, ds_low)
        d_write = d_write + mm(part.pushed.astype(BF), ds_low)
        dx = dx + d_pushed * part.weight_wide
        sums = exact(
            jnp.concatenate([d_carry * carried, d_pushed * x, d_scaled * x], axis=0),
            pick,
            ((1,), (0,)),
        )
        d_weight = sums[loc : 2 * loc]
        d_fall = d_weight * part.fall * part.steps
        d_cum = d_cum + sums[:loc] - d_fall
        d_steps = sums[2 * loc :] + d_weight * part.fall
        state_dot = jnp.sum(ds * before, axis=1, keepdims=True)
        d_decay = exact(jnp.broadcast_to(state_dot, (di, S)), pick, ((0,), (0,)))[0:1, :]
        d_last = jnp.sum(d_fall, axis=0, keepdims=True) + d_decay * part.decay
        d_cum = d_cum + jnp.where(iota((loc, 1), 0) == loc - 1, d_last, 0.0)
        d_state[m] = part.decay_rows() * ds + mm_tn(d_carry_low, part.read)

        d_rise = exact(part.lower, d_cum, ((0,), (0,)))
        d_steps = d_steps + d_rise * part.rate
        d_raw = d_steps * jax.nn.sigmoid(part.raw)
        d_heads[0:1, :] += jnp.sum(d_raw, axis=0, keepdims=True)
        d_heads[1:2, :] += jnp.sum(d_rise * part.steps * part.rate, axis=0, keepdims=True)

        d_total = jnp.concatenate([dx, d_write, d_read], axis=1)
        d_total = d_total * (part.sig + part.total * part.sig * (1.0 - part.sig))
        for k in range(K):
            d_taps[k : k + 1, :] += jnp.sum(d_total * part.shifted[k], axis=0, keepdims=True)
        d_taps[K : K + 1, :] += jnp.sum(d_total, axis=0, keepdims=True)
        d_ext[m, loc : loc + EDGE, :] = d_ext[m, 0:EDGE, :]
        d_ext[m, 0:loc, :] = d_total
        d_seq = taps[K - 1 : K, :] * d_total
        docs = part.doc(part.at)
        for ahead in range(1, K):
            same = (docs == part.doc(part.at + ahead)).astype(F32)
            d_seq = d_seq + taps[K - 1 - ahead : K - ahead, :] * (
                same * d_ext[m, ahead : ahead + loc, :]
            )
        d_proj[0, rows, :di] = d_gate.astype(BF)
        d_proj[0, rows, di : di + width] = d_seq.astype(BF)
        d_proj[0, rows, di + width :] = jnp.where(head_lane < heads, d_raw, 0.0).astype(BF)
    normed_part[0] = mm_nt(d_proj[0], w[...]).astype(BF)


def block_spec(shape, index):
    return pl.BlockSpec((1,) + shape[1:], lambda i: (index(i),) + (0,) * (len(shape) - 1))


def whole_spec(shape):
    return pl.BlockSpec(shape, lambda i: (0,) * len(shape))


def mixer_forward(lengths, g, w, w_out, taps, heads_vec, lanes_vec, heads):
    nb, rows, _ = g.shape
    di = heads * PS
    width = di + 2 * S
    shapes = [
        jax.ShapeDtypeStruct((nb, rows, D + 128), BF),
        jax.ShapeDtypeStruct((nb, rows, w.shape[1]), F32),
        jax.ShapeDtypeStruct((nb, rows, di), F32),
        jax.ShapeDtypeStruct((nb, MB, di, S), F32),
    ]
    same = lambda i: i
    return pl.pallas_call(
        functools.partial(forward_kernel, heads),
        grid=(nb,),
        out_shape=shapes,
        in_specs=[pl.BlockSpec(memory_space=pltpu.SMEM), block_spec(g.shape, same)]
        + [whole_spec(v.shape) for v in (w, w_out, taps, heads_vec, lanes_vec)],
        out_specs=[block_spec(v.shape, same) for v in shapes],
        scratch_shapes=[
            pltpu.VMEM((MB, rows // MB + EDGE, width), F32),
            pltpu.VMEM((MB, di, S), F32),
        ],
        compiler_params=pltpu.CompilerParams(vmem_limit_bytes=VMEM_LIMIT),
        name="mixer_forward",
    )(lengths, g, w, w_out, taps, heads_vec, lanes_vec)


def mixer_backward(lengths, grad, w, w_out, taps, heads_vec, lanes_vec, proj, scan, states, heads):
    nb, rows, _ = grad.shape
    di = heads * PS
    width = di + 2 * S
    back = lambda i: nb - 1 - i
    before = lambda i: jnp.maximum(nb - 2 - i, 0)
    per_block = [
        jax.ShapeDtypeStruct((nb, rows, w.shape[1]), BF),
        jax.ShapeDtypeStruct((nb, rows, D), BF),
    ]
    sums = [
        jax.ShapeDtypeStruct((di, w_out.shape[1]), F32),
        jax.ShapeDtypeStruct((8, width), F32),
        jax.ShapeDtypeStruct((8, S), F32),
        jax.ShapeDtypeStruct((8, di), F32),
    ]
    return pl.pallas_call(
        functools.partial(backward_kernel, heads),
        grid=(nb,),
        out_shape=per_block + sums,
        in_specs=[pl.BlockSpec(memory_space=pltpu.SMEM), block_spec(grad.shape, back)]
        + [whole_spec(v.shape) for v in (w, w_out, taps, heads_vec, lanes_vec)]
        + [block_spec(proj.shape, back), block_spec(proj.shape, before)]
        + [block_spec(scan.shape, back), block_spec(states.shape, back)],
        out_specs=[block_spec(v.shape, back) for v in per_block]
        + [whole_spec(v.shape) for v in sums],
        scratch_shapes=[
            pltpu.VMEM((MB, rows // MB + EDGE, width), F32),
            pltpu.VMEM((MB, rows // MB + EDGE, width), F32),
            pltpu.VMEM((MB, di, S), F32),
        ],
        compiler_params=pltpu.CompilerParams(vmem_limit_bytes=VMEM_LIMIT),
        name="mixer_backward",
    )(lengths, grad, w, w_out, taps, heads_vec, lanes_vec, proj, proj, scan, states)


def assemble_kernel(heads, got, out):
    n, rows, _ = got.shape
    di = heads * PS
    piece = lambda j, start, size: got[j, :, start : start + size].astype(F32)
    for j in range(0, n, 2):
        for half in range(2):
            pair = [piece(j + k, half * di, di) for k in range(2)]
            start = half * n * di + j * di
            out[:, start : start + 2 * di] = jnp.concatenate(pair, axis=1)
    total = piece(0, 2 * di, 2 * S)
    for j in range(1, n):
        total = total + piece(j, 2 * di, 2 * S)
    start = 2 * n * di
    out[:, start : start + 2 * S] = total
    steps = [piece(j, 2 * di + 2 * S, 128)[:, :heads] for j in range(n)]
    out[:, start + 2 * S :] = jnp.concatenate(steps, axis=1)


def assemble(got, heads):
    n, rows, _ = got.shape
    return pl.pallas_call(
        functools.partial(assemble_kernel, heads),
        out_shape=jax.ShapeDtypeStruct((rows, IN_W), F32),
        in_specs=[IN_VMEM],
        out_specs=IN_VMEM,
        compiler_params=pltpu.CompilerParams(vmem_limit_bytes=VMEM_LIMIT),
        name="assemble",
    )(got)


def body(
    tokens,
    lengths,
    routes,
    cotangent,
    input_weight,
    filter_weight,
    filter_bias,
    step_bias,
    decay_log,
    skip_gain,
    norm_gain,
    gated_gain,
    output_weight,
    moe_gain,
    router_weight,
    shared_gate_up,
    shared_down,
    expert_gate_up,
    expert_down,
):
    nd, ne = lax.axis_size("dp"), lax.axis_size("expert")
    me_d, me_e = lax.axis_index("dp"), lax.axis_index("expert")
    loc = tokens.shape[2]
    heads = H // nd
    di = heads * PS
    rows_t = MB * loc
    experts = expert_gate_up.shape[0] * ne
    el = expert_gate_up.shape[0]
    dr = D // nd
    fs = FS // ne
    fsr = FS // nd
    fsl = fsr // ne

    pad = 128 - heads
    piece = dr // ne
    mine = lax.dynamic_slice_in_dim(input_weight, me_e * piece, piece, 0)
    blocks = jnp.concatenate(
        [
            jnp.moveaxis(mine[:, :DI].reshape(piece, nd, di), 1, 0),
            jnp.moveaxis(mine[:, DI : 2 * DI].reshape(piece, nd, di), 1, 0),
            jnp.broadcast_to(mine[None, :, 2 * DI : 2 * DI + 2 * S], (nd, piece, 2 * S)),
            jnp.moveaxis(mine[:, DI + CONV :].reshape(piece, nd, heads), 1, 0),
            jnp.zeros((nd, piece, pad), BF),
        ],
        axis=2,
    )
    blocks = jnp.pad(blocks, ((0, 0), (0, -piece % 16), (0, 0)))
    wcols = blocks.shape[2]

    sg = shared_gate_up.reshape(dr, 2, nd, ne, fsl)
    sg = lax.dynamic_index_in_dim(sg, me_e, 3, False).reshape(dr, 2 * fs)
    sd = lax.dynamic_slice_in_dim(shared_down, me_e * fsl, fsl, 0)
    packed = jnp.concatenate([sg.reshape(-1), sd.reshape(-1), router_weight.reshape(-1)])
    packed_cols = packed.size // rows_t
    packed = jnp.pad(packed.reshape(rows_t, -1), ((0, 0), (0, 256 - packed_cols)))

    stream = tokens.reshape(rows_t, D).astype(F32)
    incoming = cotangent.reshape(rows_t, D)
    route_rows = routes.reshape(rows_t, TOP)
    normed_wide, norm_pull = jax.vjp(rms_scale, stream, norm_gain)
    normed = normed_wide.astype(BF)
    (_, w_in), (normed_all,) = run_tasks(
        [Weights(blocks), Gather("dp", jnp.concatenate([normed, packed], axis=1))], 1, "begin"
    )
    w_in = jnp.swapaxes(w_in[:, :, :piece], 0, 1).reshape(D, wcols)
    early, _ = lax.optimization_barrier((incoming, normed_all))
    inc_all = lax.all_gather(early, "expert", axis=0, tiled=True)
    packed_all = normed_all[:, :, D:].reshape(nd, rows_t, 256)[:, :, : packed_cols]
    packed_all = packed_all.reshape(nd, -1)
    sg_full = packed_all[:, : sg.size].reshape(D, 2 * fs)
    sd_full = packed_all[:, sg.size : sg.size + sd.size].reshape(fs, D)
    router_full = packed_all[:, sg.size + sd.size :].reshape(D, experts)
    taps = jnp.concatenate(
        [lax.dynamic_slice_in_dim(filter_weight, me_d * di, di, 1), filter_weight[:, DI:]], axis=1
    )
    tap_bias = jnp.concatenate(
        [lax.dynamic_slice_in_dim(filter_bias, me_d * di, di, 0), filter_bias[DI:]], axis=0
    )
    my_heads = lambda v: lax.dynamic_slice_in_dim(v, me_d * heads, heads, 0)
    my_gain = lax.dynamic_slice_in_dim(gated_gain, me_d * di, di, 0)

    taps_vec = jnp.concatenate([taps, tap_bias[None], jnp.zeros((3, di + 2 * S), F32)], axis=0)
    heads_vec = jnp.stack([my_heads(step_bias), -jnp.exp(my_heads(decay_log))])
    heads_vec = jnp.pad(heads_vec, ((0, 6), (0, S - heads)))
    lanes_vec = jnp.pad(
        jnp.stack([my_gain, jnp.repeat(my_heads(skip_gain), PS)]), ((0, 6), (0, 0))
    )
    vectors = (taps_vec, heads_vec, lanes_vec)
    payload, proj, scan, states = mixer_forward(
        lengths[:, 0], normed_all, w_in, output_weight, *vectors, heads
    )
    column = lax.broadcasted_iota(jnp.int32, (1, D + 128), 1)
    summed = run_tasks([Reduce("dp", payload)], 2, "reduce_mixer")[0][0]
    r = lax.rsqrt((summed[:, D : D + 1] + summed[:, D + 1 : D + 2]) / DI + EPSILON)
    mixed = summed[:, :D] * r
    after_mixer = stream + mixed
    moe_wide, moe_pull = jax.vjp(rms_scale, after_mixer, moe_gain)
    moe_in = moe_wide.astype(BF)
    logits = mm(moe_in, router_full)
    chosen = (route_rows[:, :, None] == jnp.arange(experts, dtype=jnp.int32)).astype(F32)
    picked = jnp.sum(chosen * logits[:, None, :], axis=2)
    gates = jax.nn.softmax(picked, axis=1)
    table = jnp.sum(chosen * gates[:, :, None], axis=1)
    t_hi, t_lo = hi_lo(table)
    moe_payload = jnp.concatenate(
        [moe_in, t_hi, t_lo, jnp.zeros((rows_t, 128 - 2 * experts), BF)], axis=1
    )
    moe_all = run_tasks([Gather("expert", moe_payload)], 3, "gather_moe")[0][0]
    moe_all = moe_all.reshape(ne * rows_t, D + 128)
    table_all = moe_all[:, D : D + experts].astype(F32) + moe_all[
        :, D + experts : D + 2 * experts
    ].astype(F32)
    my_gates = lax.dynamic_slice_in_dim(table_all, me_e * el, el, 1)
    n_tok = ne * rows_t

    w_up = jnp.concatenate(
        [expert_gate_up[i][:, :FE] for i in range(el)]
        + [sg_full[:, :fs]]
        + [expert_gate_up[i][:, FE:] for i in range(el)]
        + [sg_full[:, fs:]],
        axis=1,
    )
    w_up = jnp.pad(w_up, ((0, 128), (0, 0)))
    w_down = jnp.concatenate([expert_down[i] for i in range(el)] + [sd_full], axis=0)
    width = w_down.shape[0]
    scale = jnp.concatenate(
        [jnp.broadcast_to(my_gates[:, i : i + 1], (n_tok, FE)) for i in range(el)]
        + [jnp.ones((n_tok, fs), F32)],
        axis=1,
    )
    pre = mm(moe_all, w_up)
    a, b = pre[:, :width], pre[:, width:]
    sig = jax.nn.sigmoid(a)
    act = a * sig
    hidden = act * b
    u = mm_nt(inc_all, w_down)
    prod = u * hidden
    gate_grad = jnp.concatenate(
        [jnp.sum(prod[:, i * FE : (i + 1) * FE], axis=1, keepdims=True) for i in range(el)], axis=1
    )
    gh = (scale * hidden).astype(BF)
    gu = scale * u
    pre_grad = jnp.concatenate(
        [gu * b * (sig + act * (1.0 - sig)), gu * act], axis=1
    ).astype(BF)
    dx_part = mm_nt(pre_grad, w_up)
    for i in range(el):
        g_hi, g_lo = hi_lo(gate_grad[:, i : i + 1])
        place = D + me_e * el + i
        dx_part = jnp.where(column == place, g_hi.astype(F32), dx_part)
        dx_part = jnp.where(column == place + experts, g_lo.astype(F32), dx_part)
    back_sum = run_tasks(
        [Reduce("expert", dx_part.astype(BF).reshape(ne, rows_t, D + 128))], 4, "reduce_moe"
    )[0][0]
    inc = incoming.astype(F32)
    spread_sum = back_sum[:, D : D + experts] + back_sum[:, D + experts : D + 2 * experts]
    logit_grad = table * (spread_sum - jnp.sum(table * spread_sum, axis=1, keepdims=True))
    logit_low = logit_grad.astype(BF)
    router_part = mm_tn(moe_in, logit_low)
    moe_in_grad = back_sum[:, :D] + mm_nt(logit_low, router_full)
    after_from_norm, moe_gain_grad = moe_pull(moe_in_grad)
    after_grad = inc + after_from_norm
    after_low = after_grad.astype(BF)
    s = jnp.sum(after_low.astype(F32) * mixed, axis=1, keepdims=True)
    r_hi, r_lo = hi_lo(r)
    d_hi, d_lo = hi_lo(s)
    grad_payload = jnp.concatenate(
        [after_low, r_hi, r_lo, d_hi, d_lo, jnp.zeros((rows_t, 124), BF)], axis=1
    )
    (grad_all,), (out_sum, grad_blocks) = run_tasks(
        [
            Gather("dp", grad_payload),
            ExpertTail(moe_all[:, :D], pre_grad, gh, inc_all, w_down, el, nd),
        ],
        5,
        "gather_grad",
    )
    all_sum = lax.psum_scatter(grad_blocks, "dp", scatter_dimension=0, tiled=True)[0]
    up_sum = all_sum[:dr]
    each, span = FE // nd, D // 2
    down_sum = all_sum[dr : dr + each]
    last_sum = all_sum[dr + each :]
    d_proj, normed_part, output_part, d_taps, d_heads, d_lanes = mixer_backward(
        lengths[:, 0], grad_all, w_in, output_weight, *vectors, proj, scan, states, heads
    )
    def rows_of(parts, count):
        flat = jnp.concatenate([part.reshape(-1) for part in parts])
        return jnp.pad(flat, (0, count * 128 - flat.size)).reshape(count, 128)

    added = (d_taps[:K, di:], d_taps[K, di:], moe_gain_grad, router_part)
    own = (
        d_taps[:K, :di],
        d_taps[K, :di],
        d_heads[0, :heads],
        d_heads[1, :heads],
        jnp.sum(d_lanes[1].reshape(heads, PS), axis=1),
        d_lanes[0],
    )
    added_size = sum(part.size for part in added)
    added_rows = -(-added_size // (nd * 1024)) * 8
    own_rows = -(-sum(part.size for part in own) // 128)
    norm_rows = D // 128
    (normed_grad,), (d_sum,), (added_in,) = run_tasks(
        [
            Reduce("dp", normed_part),
            InputGrad(
                normed_all,
                d_proj.reshape(nd * rows_t, wcols),
                output_part.astype(BF).reshape(-1, wcols),
            ),
            Direct("all", "dp", rows_of(added, nd * added_rows).reshape(nd, added_rows, 128)),
        ],
        6,
        "reduce_grads",
    )
    stream_from_norm, norm_gain_grad = norm_pull(normed_grad)
    tokens_grad = after_grad + stream_from_norm
    small = jnp.concatenate(
        [jnp.sum(added_in, axis=0), rows_of(own, own_rows), rows_of((norm_gain_grad,), norm_rows)],
        axis=0,
    )
    small = jnp.pad(small, ((0, -small.shape[0] % 8), (0, 0)))
    shared_part = jnp.concatenate(
        [
            up_sum[:, el * FE : width],
            up_sum[:, width + el * FE :],
            last_sum[:fsl, span:].reshape(dr, -1),
        ],
        axis=1,
    ).reshape(-1, wcols)
    (d_full,), (small_in,) = run_tasks(
        [
            Gather("expert", jnp.concatenate([d_sum, shared_part], axis=0)),
            Direct("gather", "expert", small),
        ],
        7,
        "gather_grads",
    )
    shared_all = d_full[:, d_sum.shape[0] :].reshape(ne, dr, -1)
    d_full = d_full[:, : d_sum.shape[0]].reshape(-1, wcols)
    (got, _), (small_all,) = run_tasks(
        [
            Swap(d_full[:D].reshape(nd, dr, wcols)),
            Direct("gather", "dp", jnp.sum(small_in, axis=0)),
        ],
        8,
        "swap_grads",
    )
    input_grad = assemble(got, heads)
    output_grad = d_full[D:].reshape(output_weight.shape)
    added_all = small_all[:, :added_rows].reshape(-1)
    own_all = small_all[:, added_rows : added_rows + own_rows].reshape(nd, -1)
    norm_gain_grad = jnp.sum(
        small_all[:, added_rows + own_rows : added_rows + own_rows + norm_rows], axis=0
    ).reshape(D)

    def split(flat, parts):
        out, start = [], 0
        for part in parts:
            out.append(flat[..., start : start + part.size].reshape(flat.shape[:-1] + part.shape))
            start += part.size
        return out

    added_taps, added_bias, moe_gain_grad, router_all = split(added_all, added)
    own_taps, own_bias, own_steps, own_decay, own_skip, own_gain = split(own_all, own)
    small = (
        jnp.concatenate([jnp.moveaxis(own_taps, 0, 1).reshape(K, DI), added_taps], axis=1),
        jnp.concatenate([own_bias.reshape(-1), added_bias]),
        own_steps.reshape(-1),
        own_decay.reshape(-1),
        own_skip.reshape(-1),
        norm_gain_grad,
        own_gain.reshape(-1),
        moe_gain_grad,
    )
    router_grad = lax.dynamic_slice_in_dim(router_all, me_d * dr, dr, 0)
    expert_up_grad = jnp.stack(
        [
            jnp.concatenate(
                [
                    up_sum[:, i * FE : (i + 1) * FE],
                    up_sum[:, width + i * FE : width + (i + 1) * FE],
                ],
                axis=1,
            )
            for i in range(el)
        ],
        axis=0,
    ).astype(F32)
    expert_down_grad = jnp.stack(
        [
            down_sum[:, : 2 * span],
            jnp.concatenate([down_sum[:, 2 * span :], last_sum[:, :span]], axis=1),
        ],
        axis=0,
    ).astype(F32)
    shared_up_grad = (
        jnp.moveaxis(shared_all[:, :, : 2 * fs].reshape(ne, dr, 2, nd, fsl), 0, 3)
        .reshape(dr, 2 * FS)
        .astype(F32)
    )
    shared_down_grad = shared_all[:, :, 2 * fs :].reshape(fsr, D).astype(F32)
    block_output = (after_mixer + out_sum).astype(BF)
    shape = (MB, 1, loc, D)
    return (
        block_output.reshape(shape),
        tokens_grad.reshape(shape),
        input_grad,
        small[0],
        small[1],
        small[2],
        small[3],
        small[4],
        small[5],
        small[6],
        output_grad.astype(F32),
        small[7],
        router_grad,
        shared_up_grad,
        shared_down_grad,
        expert_up_grad,
        expert_down_grad,
    )


def solution(mesh):
    in_specs = (
        P(None, "expert", "dp", None),
        P(None, "expert", None),
        P(None, "expert", "dp", None),
        P(None, "expert", "dp", None),
        P("dp", None),
        P(),
        P(),
        P(),
        P(),
        P(),
        P(),
        P(),
        P("dp", None),
        P(),
        P("dp", None),
        P("dp", None),
        P("dp", None),
        P("expert", None, None),
        P("expert", None, None),
    )
    out_specs = (
        P(None, "expert", "dp", None),
        P(None, "expert", "dp", None),
        P("dp", None),
        P(),
        P(),
        P(),
        P(),
        P(),
        P(),
        P(),
        P("dp", None),
        P(),
        P("dp", None),
        P("dp", None),
        P("dp", None),
        P("expert", "dp", None),
        P("expert", "dp", None),
    )
    return jax.shard_map(body, mesh=mesh, in_specs=in_specs, out_specs=out_specs, check_vma=False)
```

```python
import functools

import jax
import jax.numpy as jnp
from jax import lax
from jax.experimental import pallas as pl
from jax.experimental.pallas import tpu as pltpu
from jax.sharding import PartitionSpec as P

D = 1536
H = 48
PS = 64
S = 128
K = 4
FE = 512
FS = 1024
TOP = 6
MB = 2
DI = 3072
CONV = 3328
IN_W = 6448
EPSILON = 1e-05
BF = jnp.bfloat16
F32 = jnp.float32
MESH = pl.DeviceIdType.MESH
VMEM_LIMIT = 60 * 1024 * 1024


def mm(a, b):
    return jnp.dot(a, b, preferred_element_type=F32)


def mm_nt(a, b):
    return lax.dot_general(a, b, (((1,), (1,)), ((), ())), preferred_element_type=F32)


def mm_tn(a, b):
    return lax.dot_general(a, b, (((0,), (0,)), ((), ())), preferred_element_type=F32)


def rms_scale(values, gain):
    return values * lax.rsqrt(jnp.mean(values * values, axis=-1, keepdims=True) + EPSILON) * gain


def hi_lo(v):
    hi = v.astype(BF)
    return hi, (v - hi.astype(F32)).astype(BF)


ANY = pl.BlockSpec(memory_space=pl.ANY)
IN_VMEM = pl.BlockSpec(memory_space=pltpu.VMEM)


def places(axis):
    me = lax.axis_index(axis)
    if axis == "dp":
        core, ring, pair = lax.rem(me, 2), lax.rem(me // 2, 4), me // 8

        def at(hop, other, sibling=0):
            z = lax.rem(pair + other, 2)
            return (z * 4 + lax.rem(ring + hop + 4, 4)) * 2 + lax.rem(core + sibling, 2)
    else:
        pair, ring = lax.rem(me, 2), me // 2

        def at(hop, other, sibling=0):
            return lax.rem(ring + hop + 4, 4) * 2 + lax.rem(pair + other, 2)

    return me, at


class Task:
    ins, outs, scratch, reaches = (), (), (), ()


def peers_of(axis, everyone):
    me, at = places(axis)
    if everyone:
        n = lax.axis_size(axis)
        return [lax.rem(me + k, n) for k in range(1, n)]
    near = [at(1, 0), at(-1, 0), at(0, 1)]
    return near + [at(0, 0, 1)] if axis == "dp" else near


class Links:
    def __init__(self, axis, send, recv):
        self.axis, self.send, self.recv, self.started = axis, send, recv, []

    def push(self, number, src, dst, peer):
        copy = pltpu.make_async_remote_copy(
            src_ref=src,
            dst_ref=dst,
            send_sem=self.send.at[number],
            recv_sem=self.recv.at[number],
            device_id={self.axis: peer},
            device_id_type=MESH,
        )
        copy.start()
        self.started.append(copy)

    def arrived(self, number, dst):
        pltpu.make_async_copy(dst, dst, self.recv.at[number]).wait()

    def finish(self):
        for copy in self.started:
            copy.wait_send()


def halves(rows):
    cut = rows // 32 * 16
    return pl.ds(0, rows), pl.ds(0, cut), pl.ds(cut, rows - cut), cut


class Gather(Task):
    def __init__(self, axis, x):
        self.axis, self.reaches = axis, ((axis, False),)
        self.ins = ((x, ANY),)
        n = lax.axis_size(axis)
        self.outs = ((jax.ShapeDtypeStruct((n,) + x.shape, x.dtype), ANY),)
        dma = pltpu.SemaphoreType.DMA
        self.scratch = (dma((17,)), dma((17,)), dma)

    def steps(self, ins, outs, scratch):
        return gather_steps(self.axis, ins[0], outs[0], *scratch)


def gather_steps(axis, x, out, send, recv, own_sem):
    me, at = places(axis)
    cores = axis == "dp"
    up, down, pair, sib = at(1, 0), at(-1, 0), at(0, 1), at(0, 0, 1)
    whole, first, second, _ = halves(x.shape[0])
    links = Links(axis, send, recv)

    def push(number, slot, rows, peer, src=None):
        src = out.at[slot] if src is None else src
        links.push(number, src.at[rows], out.at[slot].at[rows], peer)

    def arrived(number, slot, rows):
        links.arrived(number, out.at[slot].at[rows])

    push(0, me, whole, up, x)
    push(1, me, whole, down, x)
    push(2, me, whole, pair, x)
    if cores:
        push(3, me, whole, sib, x)
    own = pltpu.make_async_copy(x, out.at[me], own_sem)
    own.start()
    yield
    own.wait()
    arrived(2, pair, whole)
    push(4, pair, whole, up)
    push(5, pair, whole, down)
    if cores:
        push(6, pair, whole, sib)
    yield
    arrived(0, down, whole)
    push(7, down, first, up)
    arrived(1, up, whole)
    push(8, up, second, down)
    if cores:
        push(9, down, whole, sib)
        push(10, up, whole, sib)
    yield
    arrived(4, at(-1, 1), whole)
    push(11, at(-1, 1), first, up)
    arrived(5, at(1, 1), whole)
    push(12, at(1, 1), second, down)
    if cores:
        push(13, at(-1, 1), whole, sib)
        push(14, at(1, 1), whole, sib)
    yield
    arrived(7, at(2, 0), first)
    arrived(8, at(2, 0), second)
    if cores:
        push(15, at(2, 0), whole, sib)
    yield
    arrived(11, at(2, 1), first)
    arrived(12, at(2, 1), second)
    if cores:
        push(16, at(2, 1), whole, sib)
        yield
        for number, hop, other in (
            (3, 0, 0),
            (6, 0, 1),
            (9, -1, 0),
            (10, 1, 0),
            (13, -1, 1),
            (14, 1, 1),
            (15, 2, 0),
            (16, 2, 1),
        ):
            arrived(number, at(hop, other, 1), whole)
    links.finish()


ORDER = ((2, 1), (2, 0), (1, 1), (-1, 1), (1, 0), (-1, 0), (0, 1), (0, 0))


class Reduce(Task):
    def __init__(self, axis, x, dtype=F32):
        self.axis, self.reaches = axis, ((axis, False),)
        n, rows, columns = x.shape
        self.ins = ((x, ANY),)
        self.outs = ((jax.ShapeDtypeStruct((rows, columns), dtype), IN_VMEM),)
        _, _, _, cut = halves(rows)
        buf = lambda *dims: pltpu.VMEM(dims + (columns,), BF)
        dma = pltpu.SemaphoreType.DMA
        dp = axis == "dp"
        self.scratch = (
            buf(8, rows),
            buf(8 if dp else 1, rows if dp else 16),
            buf(2, cut),
            buf(2, rows - cut),
            buf(2, rows),
            buf(2, rows),
            buf(rows),
            dma((17,)),
            dma((17,)),
            dma((8,)),
        )

    def steps(self, ins, outs, scratch):
        return reduce_steps(self.axis, ins[0], outs[0], *scratch)


def reduce_steps(axis, x, out, acc, sib_buf, a_buf, b_buf, c_buf, d_buf, e_buf, send, recv, load):
    me, at = places(axis)
    cores = axis == "dp"
    rows = acc.shape[1]
    step = 16
    block = lambda k: x.at[k] if len(x.shape) == 3 else x.at[pl.ds(pl.multiple_of(k * rows, 16), rows)]
    up, down, pair, sib = at(1, 0), at(-1, 0), at(0, 1), at(0, 0, 1)
    whole, first, second, cut = halves(rows)
    links = Links(axis, send, recv)
    push, arrived = links.push, links.arrived

    def add(dst, offset, count, *srcs):
        @pl.loop(0, count // step)
        def _(i):
            at_rows = pl.ds(pl.multiple_of(offset + i * step, step), step)
            total = dst[at_rows, :].astype(F32)
            for src in srcs:
                total += src[pl.ds(pl.multiple_of(i * step, step), step), :].astype(F32)
            dst[at_rows, :] = total.astype(dst.dtype)

    loads = []
    for k, (hop, other) in enumerate(ORDER if x is not None else ()):
        if cores:
            push(k, block(at(hop, other, 1)), sib_buf.at[k], sib)
        copy = pltpu.make_async_copy(block(at(hop, other)), acc.at[k], load.at[k])
        copy.start()
        loads.append(copy)

    def ready(k):
        if loads:
            loads[k].wait()
        if cores:
            arrived(k, sib_buf.at[k])
            add(acc.at[k], 0, rows, sib_buf.at[k])

    yield
    for k in range(2):
        ready(k)
        push(8 + 2 * k, acc.at[k].at[first], a_buf.at[k], up)
        push(9 + 2 * k, acc.at[k].at[second], b_buf.at[k], down)
    for k in range(2):
        above, below = 2 + 2 * k, 3 + 2 * k
        ready(above)
        ready(below)
        if k:
            yield
        arrived(8 + 2 * k, a_buf.at[k])
        add(acc.at[above], 0, cut, a_buf.at[k])
        push(12 + 2 * k, acc.at[above], c_buf.at[k], up)
        arrived(9 + 2 * k, b_buf.at[k])
        add(acc.at[below], cut, rows - cut, b_buf.at[k])
        push(13 + 2 * k, acc.at[below], d_buf.at[k], down)
    ready(6)
    ready(7)
    yield
    arrived(12, c_buf.at[0])
    arrived(13, d_buf.at[0])
    add(acc.at[6], 0, rows, c_buf.at[0], d_buf.at[0])
    push(16, acc.at[6], e_buf, pair)
    yield
    arrived(14, c_buf.at[1])
    arrived(15, d_buf.at[1])
    yield
    arrived(16, e_buf)

    @pl.loop(0, rows // step)
    def _(i):
        at_rows = pl.ds(pl.multiple_of(i * step, step), step)
        total = acc[7, at_rows, :].astype(F32) + c_buf[1, at_rows, :].astype(F32)
        total += d_buf[1, at_rows, :].astype(F32) + e_buf[at_rows, :].astype(F32)
        out[at_rows, :] = total.astype(out.dtype)

    links.finish()


class Direct(Task):
    def __init__(self, kind, axis, x):
        self.kind, self.axis, self.reaches = kind, axis, ((axis, True),)
        n = lax.axis_size(axis)
        shape = (n,) + x.shape if kind == "gather" else x.shape
        self.ins = ((x, ANY),)
        self.outs = ((jax.ShapeDtypeStruct(shape, x.dtype), ANY),)
        dma = pltpu.SemaphoreType.DMA
        self.scratch = (dma((n,)), dma((n,)), dma)

    def steps(self, ins, outs, scratch):
        return direct_steps(self.kind, self.axis, ins[0], outs[0], *scratch)


def direct_steps(kind, axis, x, out, send, recv, own_sem):
    n, me = lax.axis_size(axis), lax.axis_index(axis)
    links = Links(axis, send, recv)
    piece = lambda k: x if kind == "gather" else x.at[k]
    for k in range(1, n):
        peer = lax.rem(me + k, n)
        links.push(k, piece(peer), out.at[me], peer)
    own = pltpu.make_async_copy(piece(me), out.at[me], own_sem)
    own.start()
    yield
    for k in range(1, n):
        links.arrived(k, out.at[lax.rem(me - k + n, n)])
    own.wait()
    links.finish()


class Swap(Task):
    reaches = (("dp", True),)

    def __init__(self, x):
        self.ins = ((x, ANY),)
        relay = jax.ShapeDtypeStruct((2,) + x.shape[1:], x.dtype)
        self.outs = ((jax.ShapeDtypeStruct(x.shape, x.dtype), ANY), (relay, ANY))
        dma = pltpu.SemaphoreType.DMA
        self.scratch = (dma((18,)), dma((18,)), dma)

    def steps(self, ins, outs, scratch):
        return swap_steps(ins[0], *outs, *scratch)


def swap_steps(x, out, relay, send, recv, own_sem):
    me, at = places("dp")
    links = Links("dp", send, recv)
    number = 2
    plain = []
    for sibling in range(2):
        links.push(sibling, x.at[at(2, 1, sibling)], relay.at[sibling], at(-1, 0))
    for hop in (1, -1, 2, 0):
        for other in range(2):
            for sibling in range(2):
                if (hop, other) == (2, 1) or (hop, other, sibling) == (0, 0, 0):
                    continue
                peer = at(hop, other, sibling)
                links.push(number, x.at[peer], out.at[me], peer)
                plain.append((number, at(-hop, other, sibling)))
                number += 1
    own = pltpu.make_async_copy(x.at[me], out.at[me], own_sem)
    own.start()
    yield
    for sibling in range(2):
        links.arrived(sibling, relay.at[sibling])
        links.push(number + sibling, relay.at[sibling], out.at[at(1, 0)], at(-1, 1, sibling))
    for _ in range(6):
        yield
    for k, source in plain:
        links.arrived(k, out.at[source])
    for sibling in range(2):
        links.arrived(number + sibling, out.at[at(2, 1, sibling)])
    own.wait()
    links.finish()


def run_tasks(tasks, number, name):
    operands, in_specs, out_shapes, out_specs, scratch, spans = [], [], [], [], [], []
    for task in tasks:
        spans.append((len(operands), len(out_shapes), len(scratch)))
        operands += [x for x, _ in task.ins]
        in_specs += [spec for _, spec in task.ins]
        out_shapes += [shape for shape, _ in task.outs]
        out_specs += [spec for _, spec in task.outs]
        scratch += list(task.scratch)

    def kernel(*refs):
        ins = refs[: len(operands)]
        outs = refs[len(operands) : len(operands) + len(out_shapes)]
        temps = refs[len(operands) + len(out_shapes) :]
        barrier = pltpu.get_barrier_semaphore()
        count = 0
        for axis in ("dp", "expert"):
            here = [everyone for task in tasks for name, everyone in task.reaches if name == axis]
            if here:
                peers = peers_of(axis, any(here))
                for peer in peers:
                    pl.semaphore_signal(
                        barrier, inc=1, device_id={axis: peer}, device_id_type=MESH
                    )
                count += len(peers)
        pl.semaphore_wait(barrier, count)
        running = []
        for task, (i, o, s) in zip(tasks, spans):
            running.append(
                task.steps(
                    ins[i : i + len(task.ins)],
                    outs[o : o + len(task.outs)],
                    temps[s : s + len(task.scratch)],
                )
            )
        while running:
            running = [steps for steps in running if next(steps, "end") != "end"]

    results = pl.pallas_call(
        kernel,
        out_shape=out_shapes,
        in_specs=in_specs,
        out_specs=out_specs,
        scratch_shapes=scratch,
        compiler_params=pltpu.CompilerParams(
            collective_id=number, has_side_effects=True, vmem_limit_bytes=VMEM_LIMIT
        ),
        name=name,
    )(*operands)
    return [results[o : o + len(task.outs)] for task, (_, o, _) in zip(tasks, spans)]


class Weights(Task):
    def __init__(self, x):
        self.reaches = (("dp", True), ("expert", False))
        self.swap, self.spread = Direct("all", "dp", x), Gather("expert", x)
        n = lax.axis_size("expert")
        full = jax.ShapeDtypeStruct((n,) + x.shape, x.dtype)
        self.ins = ((x, ANY),)
        self.outs = self.swap.outs + ((full, ANY),)
        self.scratch = self.swap.scratch + self.spread.scratch

    def steps(self, ins, outs, scratch):
        yield from direct_steps("all", "dp", ins[0], outs[0], *scratch[:3])
        yield
        yield from gather_steps("expert", outs[0], outs[1], *scratch[3:])


class ExpertGrads(Task):
    def __init__(self, x, pre_grad, gh, inc, w_down, s_down, blocks):
        n, rows, _ = x.shape
        width, depth = gh.shape[2], inc.shape[1]
        experts, each, _ = w_down.shape
        part = jax.ShapeDtypeStruct((n, rows, depth), BF)
        grads = jax.ShapeDtypeStruct(
            (blocks, depth // blocks + 2 * (each // blocks), 2 * width), BF
        )
        self.ins = tuple((v, ANY) for v in (x, pre_grad, gh, inc, w_down, s_down))
        self.outs = ((part, ANY), (grads, ANY))
        dma = pltpu.SemaphoreType.DMA
        vmem = lambda *dims: pltpu.VMEM(dims, BF)
        self.scratch = (
            vmem(n, rows, depth),
            vmem(*pre_grad.shape),
            vmem(*gh.shape),
            vmem(*inc.shape),
            vmem(width, depth),
            dma((8 + experts,)),
            vmem(*part.shape),
            vmem(depth, n * rows),
            vmem(width, n * rows),
            vmem(*grads.shape),
        )

    def steps(self, ins, outs, scratch):
        x, pre_grad, gh, inc, w_down, sems, part, x_t, gh_t, grads = scratch
        n, rows, depth = x.shape
        width = gh.shape[2]
        experts, each, _ = ins[4].shape
        copy = lambda src, dst, k: pltpu.make_async_copy(src, dst, sems.at[k])
        load_x = copy(ins[0].at[:, :, pl.ds(0, depth)], x, 0)
        load_pre = copy(ins[1], pre_grad, 1)
        load_inc = copy(ins[3], inc, 3)
        load_first = [copy(ins[2], gh, 2)]
        for e in range(experts):
            load_first.append(copy(ins[4].at[e], w_down.at[pl.ds(e * each, each)], 8 + e))
        rest = pl.ds(experts * each, width - experts * each)
        load_first.append(copy(ins[5], w_down.at[rest], 4))
        for load in load_first + [load_x, load_pre, load_inc]:
            load.start()
        yield
        tile = 256
        col = lambda i: pl.ds(pl.multiple_of(i * tile, tile), tile)
        for load in load_first:
            load.wait()

        @pl.loop(0, width // 128)
        def _(i):
            at_cols = pl.ds(pl.multiple_of(i * 128, 128), 128)
            gh_t[at_cols, :] = gh[:, :, at_cols].reshape(n * rows, 128).T

        for half in range(2):

            @pl.loop(half * depth // tile // 2, (half + 1) * depth // tile // 2)
            def _(i):
                value = mm(gh[...].reshape(n * rows, width), w_down[:, col(i)])
                part[:, :, col(i)] = value.astype(BF).reshape(n, rows, tile)

            yield
        store_part = copy(part, outs[0], 5)
        store_part.start()
        load_x.wait()
        load_pre.wait()

        @pl.loop(0, depth // tile)
        def _(i):
            x_t[col(i), :] = x[:, :, col(i)].reshape(n * rows, tile).T

        yield
        blocks = grads.shape[0]
        up_rows = depth // blocks
        for third in range(3):
            steps = 2 * width // tile // 3

            @pl.loop(third * steps, (third + 1) * steps)
            def _(i):
                value = mm(x_t[...], pre_grad[:, :, col(i)].reshape(n * rows, tile)).astype(BF)
                grads[:, :up_rows, col(i)] = value.reshape(blocks, up_rows, tile)

            yield
        load_inc.wait()
        piece_rows = each // blocks
        own = (width - experts * each) // blocks
        span = depth // 2
        spots = (((0, 0), (0, 2)), ((0, 1), (piece_rows, 0)))
        for half in range(2):

            @pl.loop(0, span // tile)
            def _(i):
                value = mm(gh_t[...], inc[:, col(half * span // tile + i)])
                for e in range(experts):
                    row, place = spots[half][e]
                    piece = value[e * each : (e + 1) * each].astype(BF)
                    grads[
                        :,
                        up_rows + row : up_rows + row + piece_rows,
                        col(place * span // tile + i),
                    ] = piece.reshape(blocks, piece_rows, tile)
                piece = value[experts * each :].reshape(blocks, own, tile)
                empty = jnp.zeros((blocks, piece_rows - own, tile), F32)
                piece = jnp.concatenate([piece, empty], axis=1).astype(BF)
                grads[:, up_rows + piece_rows :, col((1 + half) * span // tile + i)] = piece

            yield
        store = copy(grads, outs[1], 6)
        store.start()
        store_part.wait()
        store.wait()


class InputGrad(Task):
    def __init__(self, g, d_proj, out_grad):
        self.reaches = (("expert", False),)
        rows, wide = D + out_grad.shape[0], d_proj.shape[1]
        n = lax.axis_size("expert")
        self.reduce = Reduce("expert", jax.ShapeDtypeStruct((n, rows // n, wide), BF), BF)
        self.ins = tuple((v, ANY) for v in (g, d_proj, out_grad))
        self.outs = self.reduce.outs
        dma = pltpu.SemaphoreType.DMA
        self.scratch = (
            pltpu.VMEM(g.shape[:2] + (D,), BF),
            pltpu.VMEM(d_proj.shape, BF),
            pltpu.VMEM((rows, wide), BF),
            dma((3,)),
        ) + self.reduce.scratch

    def steps(self, ins, outs, scratch):
        g, d_proj, total, sems = scratch[:4]
        loads = (
            pltpu.make_async_copy(ins[0].at[:, :, pl.ds(0, D)], g, sems.at[0]),
            pltpu.make_async_copy(ins[1], d_proj, sems.at[1]),
            pltpu.make_async_copy(ins[2], total.at[pl.ds(D, ins[2].shape[0])], sems.at[2]),
        )
        for load in loads:
            load.start()
        yield
        for load in loads:
            load.wait()
        tile = 256
        flat = g.shape[0] * g.shape[1]

        @pl.loop(0, D // tile)
        def _(i):
            at_rows = pl.ds(pl.multiple_of(i * tile, tile), tile)
            total[at_rows, :] = mm_tn(g[:, :, at_rows].reshape(flat, tile), d_proj[...]).astype(BF)

        yield from reduce_steps("expert", total, outs[0], *scratch[4:])


class Experts(Task):
    def __init__(self, x, inc, w_up, w_down, s_up, s_down):
        self.reaches = (("expert", False),)
        self.gather = Gather("expert", x)
        n = lax.axis_size("expert")
        rows, wide = x.shape
        depth = inc.shape[1]
        experts, _, both = w_up.shape
        self.experts = experts
        all_rows = jax.ShapeDtypeStruct((n, rows, wide), BF)
        self.reduce = Reduce("expert", all_rows)
        hidden = experts * both // 2 + s_down.shape[0]
        pre = jax.ShapeDtypeStruct((n, rows, 2 * hidden), BF)
        gh = jax.ShapeDtypeStruct((n, rows, hidden), BF)
        self.ins = tuple((v, ANY) for v in (x, inc, w_up, w_down, s_up, s_down))
        self.outs = ((all_rows, IN_VMEM),) + self.reduce.outs + ((pre, ANY), (gh, ANY))
        dma = pltpu.SemaphoreType.DMA
        self.scratch = (
            (pltpu.VMEM((n, rows, depth), BF),)
            + tuple(pltpu.VMEM(v.shape, BF) for v in (w_up, w_down, s_up, s_down))
            + (pltpu.VMEM((2 * rows, wide), BF), pltpu.VMEM((2 * rows, depth), BF))
            + (pltpu.VMEM((2 * rows, 2 * hidden), BF), pltpu.VMEM((2 * rows, hidden), BF))
            + (pltpu.VMEM(pre.shape, BF), pltpu.VMEM(gh.shape, BF))
            + (pltpu.VMEM((2 * rows, 128), F32), dma((21,)))
            + self.gather.scratch
            + self.reduce.scratch
        )

    def steps(self, ins, outs, scratch):
        x, inc_in = ins[:2]
        x_all, dx_out, pre_out, gh_out = outs
        inc, w_up, w_down, s_up, s_down, xs, incs, pg, ghs, pre, gh, extra, sems = scratch[:13]
        gather_scratch, reduce_scratch = scratch[13:16], scratch[16:]
        acc = reduce_scratch[0]
        me, at = places("expert")
        n, rows, depth = inc.shape
        experts, _, both = w_up.shape
        each = both // 2
        shared = s_down.shape[0]
        tile = min(256, each)
        loads = [
            pltpu.make_async_copy(src, dst, sems.at[k])
            for k, (src, dst) in enumerate(zip(ins[2:], (w_up, w_down, s_up, s_down)))
        ]
        loads += [
            pltpu.make_async_copy(inc_in.at[pl.ds(k * rows, rows)], inc.at[k], sems.at[13 + k])
            for k in range(n)
        ]
        arriving = gather_steps("expert", x, x_all, *gather_scratch)
        next(arriving)
        for load in loads:
            load.start()
        next(arriving)
        next(arriving)
        for load in loads:
            load.wait()
        lane = lax.broadcasted_iota(jnp.int32, (1, 128), 1)
        stores = []

        def unit(a, b, u, scale):
            sig = jax.nn.sigmoid(a)
            act = a * sig
            hidden = act * b
            gu = u * scale
            da = gu * b * (sig + act * (1.0 - sig))
            return hidden * scale, da, gu * act, u * hidden

        def compute(hop, places_in_acc):
            slots = (at(hop, 0), at(hop, 1))
            for k, slot in enumerate(slots):
                part = pl.ds(k * rows, rows)
                xs[part, :] = x_all[slot]
                incs[part, :] = inc[slot]
            extra[...] = jnp.zeros_like(extra)

            @pl.loop(0, experts * (each // tile))
            def _(i):
                e, f = i // (each // tile), lax.rem(i, each // tile)
                place = me * experts + e
                table = xs[:, depth:].astype(F32)
                chosen = (lane == place) | (lane == place + n * experts)
                scale = jnp.sum(jnp.where(chosen, table, 0.0), axis=1, keepdims=True)
                left = pl.ds(pl.multiple_of(f * tile, tile), tile)
                right = pl.ds(pl.multiple_of(each + f * tile, tile), tile)
                a = mm(xs[:, :depth], w_up[e, :, left])
                b = mm(xs[:, :depth], w_up[e, :, right])
                u = mm_nt(incs[...], w_down[e, left, :])
                h, da, db, dots = unit(a, b, u, scale)
                ghs[:, pl.ds(pl.multiple_of(e * each + f * tile, tile), tile)] = h.astype(BF)
                pg[:, pl.ds(pl.multiple_of(e * both + f * tile, tile), tile)] = da.astype(BF)
                pg[:, pl.ds(pl.multiple_of(e * both + each + f * tile, tile), tile)] = db.astype(BF)
                extra[...] += jnp.where(lane == place, jnp.sum(dots, axis=1, keepdims=True), 0.0)

            a = mm(xs[:, :depth], s_up[:, :shared])
            b = mm(xs[:, :depth], s_up[:, shared:])
            u = mm_nt(incs[...], s_down[...])
            h, da, db, _ = unit(a, b, u, 1.0)
            ghs[:, experts * each :] = h.astype(BF)
            pg[:, experts * both : experts * both + shared] = da.astype(BF)
            pg[:, experts * both + shared :] = db.astype(BF)

            @pl.loop(0, depth // tile)
            def _(i):
                columns = pl.ds(pl.multiple_of(i * tile, tile), tile)
                total = mm_nt(pg[:, experts * both :], s_up[columns, :])
                for e in range(experts):
                    total += mm_nt(pg[:, e * both : (e + 1) * both], w_up[e, columns, :])
                for k, place in enumerate(places_in_acc):
                    acc[place, :, columns] = total[k * rows : (k + 1) * rows].astype(BF)

            grads = extra[...]
            high = grads.astype(BF).astype(F32)
            turn = (
                iota((128, 128), 0) + n * experts == iota((128, 128), 1)
            ).astype(F32)
            rest = exact(grads - high, turn, ((1,), (0,)))
            both_parts = (high + rest).astype(BF)
            for k, (slot, place) in enumerate(zip(slots, places_in_acc)):
                part = pl.ds(k * rows, rows)
                acc[place, :, depth:] = both_parts[k * rows : (k + 1) * rows]
                pre[slot] = pg[part, :]
                gh[slot] = ghs[part, :]
                store = pltpu.make_async_copy(pre.at[slot], pre_out.at[slot], sems.at[4 + len(stores)])
                store.start()
                stores.append(store)

        compute(0, (7, 6))
        next(arriving)
        compute(1, (4, 2))
        compute(-1, (5, 3))
        for _ in arriving:
            pass
        compute(2, (1, 0))
        store = pltpu.make_async_copy(gh, gh_out, sems.at[12])
        store.start()
        stores.append(store)
        yield from reduce_steps("expert", None, dx_out, *reduce_scratch)
        for store in stores:
            store.wait()


EDGE = 8
HIGHEST = lax.Precision.HIGHEST


def exact(a, b, dims):
    return lax.dot_general(a, b, (dims, ((), ())), precision=HIGHEST, preferred_element_type=F32)


def iota(shape, axis):
    return lax.broadcasted_iota(jnp.int32, shape, axis)


class Block:
    def __init__(self, m, start, proj, ext, lengths, taps, heads_vec, heads):
        loc = proj.shape[0]
        di = heads * PS
        width = di + 2 * S
        self.heads, self.di = heads, di
        first = lengths[m, 0]
        second = first + lengths[m, 1]

        def doc(p):
            return (p >= first).astype(jnp.int32) + (p >= second).astype(jnp.int32)

        self.doc = doc
        self.at = start + iota((loc, 1), 0)
        docs = doc(self.at)
        docs_row = doc(start + iota((1, loc), 1))
        last_doc, before_doc = doc(start + loc - 1), doc(start - 1)
        self.keep = (docs == before_doc).astype(F32)
        self.keep_last = (last_doc == before_doc).astype(F32)
        self.same_last = (docs == last_doc).astype(F32)
        self.gate = proj[:, :di]
        ext[m, EDGE : EDGE + loc, :] = proj[:, di : di + width].astype(BF).astype(F32)
        total = jnp.broadcast_to(taps[K : K + 1, :], (loc, width))
        self.shifted = []
        for k in range(K):
            back = K - 1 - k
            value = ext[m, EDGE - back : EDGE - back + loc, :]
            if back:
                value = value * (docs == doc(self.at - back)).astype(F32)
            self.shifted.append(value)
            total = total + taps[k : k + 1, :] * value
        self.sig = jax.nn.sigmoid(total)
        self.total = total
        filtered = total * self.sig
        self.x = filtered[:, :di]
        self.write = filtered[:, di : di + S].astype(BF)
        self.read = filtered[:, di + S :].astype(BF)
        self.raw = proj[:, di + width :] + heads_vec[0:1, :]
        self.steps = jnp.maximum(self.raw, 0.0) + jnp.log1p(jnp.exp(-jnp.abs(self.raw)))
        self.rate = heads_vec[1:2, :]
        rise = self.steps * self.rate
        rows, cols = iota((loc, loc), 0), iota((loc, loc), 1)
        self.lower = (cols <= rows).astype(F32)
        self.cum = exact(self.lower, rise, ((1,), (0,)))
        cum_rows = exact(rise, (rows <= cols).astype(F32), ((0,), (0,)))
        self.last = self.cum[loc - 1 : loc, :]
        self.grow = jnp.exp(self.cum) * self.keep
        self.fall = jnp.exp(self.last - self.cum) * self.same_last
        self.decay = jnp.exp(self.last) * self.keep_last
        allowed = (cols <= rows) & (docs == docs_row)
        scores = mm_nt(self.read, self.write)
        self.spread, self.mixing = [], []
        for h in range(heads):
            span = self.cum[:, h : h + 1] - cum_rows[h : h + 1, :]
            shape = jnp.exp(jnp.where(allowed, span, -1e30))
            self.spread.append(shape)
            self.mixing.append(shape * scores)
        self.lane = iota((1, di), 1)
        self.steps_wide = self.widen(self.steps)
        self.grow_wide = self.widen(self.grow)
        self.weight_wide = self.widen(self.fall * self.steps)
        self.scaled = self.x * self.steps_wide
        self.pushed = self.x * self.weight_wide

    def widen(self, v):
        out = jnp.broadcast_to(v[:, 0:1], (v.shape[0], self.di))
        for h in range(1, self.heads):
            out = jnp.where(self.lane >= h * PS, v[:, h : h + 1], out)
        return out

    def per_head(self, parts):
        out = parts[0]
        for h in range(1, self.heads):
            out = jnp.where(self.lane >= h * PS, parts[h], out)
        return out

    def decay_rows(self):
        rows = iota((self.di, 1), 0)
        out = jnp.broadcast_to(self.decay[:, 0:1], (self.di, 1))
        for h in range(1, self.heads):
            out = jnp.where(rows >= h * PS, self.decay[:, h : h + 1], out)
        return out


def forward_kernel(
    heads, lengths, g, w, w_out, taps, heads_vec, lanes_vec, payload, proj, scan, states, ext, state
):
    b = pl.program_id(0)
    loc = g.shape[1] // MB
    di = heads * PS

    @pl.when(b == 0)
    def _():
        ext[...] = jnp.zeros_like(ext)
        state[...] = jnp.zeros_like(state)

    proj[0] = mm(g[0, :, :D], w[...])
    column = iota((loc, payload.shape[2] - D), 1)
    for m in range(MB):
        rows = slice(m * loc, (m + 1) * loc)
        ext[m, 0:EDGE, :] = ext[m, loc : loc + EDGE, :]
        part = Block(m, b * loc, proj[0, rows, :], ext, lengths, taps, heads_vec, heads)
        before = state[m]
        states[0, m] = before
        scaled = part.scaled.astype(BF)
        inner = part.per_head([mm(part.mixing[h].astype(BF), scaled) for h in range(heads)])
        carried = mm_nt(part.read, before.astype(BF)) * part.grow_wide
        out = inner + carried + lanes_vec[1:2, :] * part.x
        scan[0, rows, :] = out
        state[m] = part.decay_rows() * before + mm_tn(part.pushed.astype(BF), part.write)
        y = out * (part.gate * jax.nn.sigmoid(part.gate))
        square = jnp.sum(y * y, axis=1, keepdims=True)
        high = square.astype(BF).astype(F32)
        payload[0, rows, :D] = mm((y * lanes_vec[0:1, :]).astype(BF), w_out[...]).astype(BF)
        sums = jnp.where(column == 0, high, jnp.where(column == 1, square - high, 0.0))
        payload[0, rows, D:] = sums.astype(BF)


def backward_kernel(
    heads,
    lengths,
    grad,
    w,
    w_out,
    taps,
    heads_vec,
    lanes_vec,
    proj,
    proj_before,
    scan,
    states,
    d_proj,
    normed_part,
    d_out,
    d_taps,
    d_heads,
    d_lanes,
    ext,
    d_ext,
    d_state,
):
    step = pl.program_id(0)
    b = pl.num_programs(0) - 1 - step
    loc = grad.shape[1] // MB
    di = heads * PS
    width = di + 2 * S

    @pl.when(step == 0)
    def _():
        for ref in (d_ext, d_state, d_out, d_taps, d_heads, d_lanes):
            ref[...] = jnp.zeros_like(ref)

    gated_grad = mm_nt(grad[0, :, :D], w_out[...])
    extra = grad[0, :, D:].astype(F32)
    has_before = (b > 0).astype(F32)
    pick = (iota((di, S), 0) // PS == iota((di, S), 1)).astype(F32)
    for m in range(MB):
        rows = slice(m * loc, (m + 1) * loc)
        edge = proj_before[0, (m + 1) * loc - EDGE : (m + 1) * loc, di : di + width]
        ext[m, 0:EDGE, :] = edge.astype(BF).astype(F32) * has_before
        part = Block(m, b * loc, proj[0, rows, :], ext, lengths, taps, heads_vec, heads)
        gain, skip = lanes_vec[0:1, :], lanes_vec[1:2, :]
        r = extra[rows, 0:1] + extra[rows, 1:2]
        s = extra[rows, 2:3] + extra[rows, 3:4]
        out = scan[0, rows, :]
        sig = jax.nn.sigmoid(part.gate)
        act = part.gate * sig
        yr = out * act * r
        gg = gated_grad[rows]
        d_lanes[0:1, :] += jnp.sum(gg * yr, axis=0, keepdims=True)
        d_out[...] += mm_tn((yr * gain).astype(BF), grad[0, rows, :D])
        dy = r * (gg * gain) - yr * (r * s / DI)
        d_gate = dy * out * (sig + act * (1.0 - sig))
        do = dy * act
        do_low = do.astype(BF)
        x = part.x
        d_lanes[1:2, :] += jnp.sum(do * x, axis=0, keepdims=True)
        dx = skip * do
        before = states[0, m]
        before_low = before.astype(BF)
        ds = d_state[m]
        ds_low = ds.astype(BF)

        d_scores = jnp.zeros((loc, loc), F32)
        d_scaled, d_cum = [], jnp.zeros((loc, S), F32)
        head_lane = iota((loc, S), 1)
        for h in range(heads):
            inside = (part.lane >= h * PS) & (part.lane < (h + 1) * PS)
            own = jnp.where(inside, part.scaled, 0.0).astype(BF)
            d_mix = mm_nt(do_low, own)
            d_scaled.append(mm_tn(part.mixing[h].astype(BF), do_low))
            d_scores = d_scores + d_mix * part.spread[h]
            d_span = d_mix * part.mixing[h]
            ones = (head_lane == h).astype(F32)
            d_cum = d_cum + exact(d_span, ones, ((1,), (0,))) - exact(d_span, ones, ((0,), (0,)))
        d_scaled = part.per_head(d_scaled)
        dx = dx + d_scaled * part.steps_wide
        d_scores_low = d_scores.astype(BF)
        d_read = mm(d_scores_low, part.write)
        d_write = mm_tn(d_scores_low, part.read)

        d_carry = do * part.grow_wide
        d_carry_low = d_carry.astype(BF)
        carried = mm_nt(part.read, before_low)
        d_read = d_read + mm(d_carry_low, before_low)

        d_pushed = mm_nt(part.write, ds_low)
        d_write = d_write + mm(part.pushed.astype(BF), ds_low)
        dx = dx + d_pushed * part.weight_wide
        sums = exact(
            jnp.concatenate([d_carry * carried, d_pushed * x, d_scaled * x], axis=0),
            pick,
            ((1,), (0,)),
        )
        d_weight = sums[loc : 2 * loc]
        d_fall = d_weight * part.fall * part.steps
        d_cum = d_cum + sums[:loc] - d_fall
        d_steps = sums[2 * loc :] + d_weight * part.fall
        state_dot = jnp.sum(ds * before, axis=1, keepdims=True)
        d_decay = exact(jnp.broadcast_to(state_dot, (di, S)), pick, ((0,), (0,)))[0:1, :]
        d_last = jnp.sum(d_fall, axis=0, keepdims=True) + d_decay * part.decay
        d_cum = d_cum + jnp.where(iota((loc, 1), 0) == loc - 1, d_last, 0.0)
        d_state[m] = part.decay_rows() * ds + mm_tn(d_carry_low, part.read)

        d_rise = exact(part.lower, d_cum, ((0,), (0,)))
        d_steps = d_steps + d_rise * part.rate
        d_raw = d_steps * jax.nn.sigmoid(part.raw)
        d_heads[0:1, :] += jnp.sum(d_raw, axis=0, keepdims=True)
        d_heads[1:2, :] += jnp.sum(d_rise * part.steps * part.rate, axis=0, keepdims=True)

        d_total = jnp.concatenate([dx, d_write, d_read], axis=1)
        d_total = d_total * (part.sig + part.total * part.sig * (1.0 - part.sig))
        for k in range(K):
            d_taps[k : k + 1, :] += jnp.sum(d_total * part.shifted[k], axis=0, keepdims=True)
        d_taps[K : K + 1, :] += jnp.sum(d_total, axis=0, keepdims=True)
        d_ext[m, loc : loc + EDGE, :] = d_ext[m, 0:EDGE, :]
        d_ext[m, 0:loc, :] = d_total
        d_seq = taps[K - 1 : K, :] * d_total
        docs = part.doc(part.at)
        for ahead in range(1, K):
            same = (docs == part.doc(part.at + ahead)).astype(F32)
            d_seq = d_seq + taps[K - 1 - ahead : K - ahead, :] * (
                same * d_ext[m, ahead : ahead + loc, :]
            )
        d_proj[0, rows, :di] = d_gate.astype(BF)
        d_proj[0, rows, di : di + width] = d_seq.astype(BF)
        d_proj[0, rows, di + width :] = jnp.where(head_lane < heads, d_raw, 0.0).astype(BF)
    normed_part[0] = mm_nt(d_proj[0], w[...]).astype(BF)


def block_spec(shape, index):
    return pl.BlockSpec((1,) + shape[1:], lambda i: (index(i),) + (0,) * (len(shape) - 1))


def whole_spec(shape):
    return pl.BlockSpec(shape, lambda i: (0,) * len(shape))


def mixer_forward(lengths, g, w, w_out, taps, heads_vec, lanes_vec, heads):
    nb, rows, _ = g.shape
    di = heads * PS
    width = di + 2 * S
    shapes = [
        jax.ShapeDtypeStruct((nb, rows, D + 128), BF),
        jax.ShapeDtypeStruct((nb, rows, w.shape[1]), F32),
        jax.ShapeDtypeStruct((nb, rows, di), F32),
        jax.ShapeDtypeStruct((nb, MB, di, S), F32),
    ]
    same = lambda i: i
    return pl.pallas_call(
        functools.partial(forward_kernel, heads),
        grid=(nb,),
        out_shape=shapes,
        in_specs=[pl.BlockSpec(memory_space=pltpu.SMEM), block_spec(g.shape, same)]
        + [whole_spec(v.shape) for v in (w, w_out, taps, heads_vec, lanes_vec)],
        out_specs=[block_spec(v.shape, same) for v in shapes],
        scratch_shapes=[
            pltpu.VMEM((MB, rows // MB + EDGE, width), F32),
            pltpu.VMEM((MB, di, S), F32),
        ],
        compiler_params=pltpu.CompilerParams(vmem_limit_bytes=VMEM_LIMIT),
        name="mixer_forward",
    )(lengths, g, w, w_out, taps, heads_vec, lanes_vec)


def mixer_backward(lengths, grad, w, w_out, taps, heads_vec, lanes_vec, proj, scan, states, heads):
    nb, rows, _ = grad.shape
    di = heads * PS
    width = di + 2 * S
    back = lambda i: nb - 1 - i
    before = lambda i: jnp.maximum(nb - 2 - i, 0)
    per_block = [
        jax.ShapeDtypeStruct((nb, rows, w.shape[1]), BF),
        jax.ShapeDtypeStruct((nb, rows, D), BF),
    ]
    sums = [
        jax.ShapeDtypeStruct((di, w_out.shape[1]), F32),
        jax.ShapeDtypeStruct((8, width), F32),
        jax.ShapeDtypeStruct((8, S), F32),
        jax.ShapeDtypeStruct((8, di), F32),
    ]
    return pl.pallas_call(
        functools.partial(backward_kernel, heads),
        grid=(nb,),
        out_shape=per_block + sums,
        in_specs=[pl.BlockSpec(memory_space=pltpu.SMEM), block_spec(grad.shape, back)]
        + [whole_spec(v.shape) for v in (w, w_out, taps, heads_vec, lanes_vec)]
        + [block_spec(proj.shape, back), block_spec(proj.shape, before)]
        + [block_spec(scan.shape, back), block_spec(states.shape, back)],
        out_specs=[block_spec(v.shape, back) for v in per_block]
        + [whole_spec(v.shape) for v in sums],
        scratch_shapes=[
            pltpu.VMEM((MB, rows // MB + EDGE, width), F32),
            pltpu.VMEM((MB, rows // MB + EDGE, width), F32),
            pltpu.VMEM((MB, di, S), F32),
        ],
        compiler_params=pltpu.CompilerParams(vmem_limit_bytes=VMEM_LIMIT),
        name="mixer_backward",
    )(lengths, grad, w, w_out, taps, heads_vec, lanes_vec, proj, proj, scan, states)


def assemble_kernel(heads, got, out):
    n, rows, _ = got.shape
    di = heads * PS
    piece = lambda j, start, size: got[j, :, start : start + size].astype(F32)
    for j in range(0, n, 2):
        for half in range(2):
            pair = [piece(j + k, half * di, di) for k in range(2)]
            start = half * n * di + j * di
            out[:, start : start + 2 * di] = jnp.concatenate(pair, axis=1)
    total = piece(0, 2 * di, 2 * S)
    for j in range(1, n):
        total = total + piece(j, 2 * di, 2 * S)
    start = 2 * n * di
    out[:, start : start + 2 * S] = total
    steps = [piece(j, 2 * di + 2 * S, 128)[:, :heads] for j in range(n)]
    out[:, start + 2 * S :] = jnp.concatenate(steps, axis=1)


def assemble(got, heads):
    n, rows, _ = got.shape
    return pl.pallas_call(
        functools.partial(assemble_kernel, heads),
        out_shape=jax.ShapeDtypeStruct((rows, IN_W), F32),
        in_specs=[IN_VMEM],
        out_specs=IN_VMEM,
        compiler_params=pltpu.CompilerParams(vmem_limit_bytes=VMEM_LIMIT),
        name="assemble",
    )(got)


def body(
    tokens,
    lengths,
    routes,
    cotangent,
    input_weight,
    filter_weight,
    filter_bias,
    step_bias,
    decay_log,
    skip_gain,
    norm_gain,
    gated_gain,
    output_weight,
    moe_gain,
    router_weight,
    shared_gate_up,
    shared_down,
    expert_gate_up,
    expert_down,
):
    nd, ne = lax.axis_size("dp"), lax.axis_size("expert")
    me_d, me_e = lax.axis_index("dp"), lax.axis_index("expert")
    loc = tokens.shape[2]
    heads = H // nd
    di = heads * PS
    rows_t = MB * loc
    experts = expert_gate_up.shape[0] * ne
    el = expert_gate_up.shape[0]
    dr = D // nd
    fs = FS // ne
    fsr = FS // nd
    fsl = fsr // ne

    pad = 128 - heads
    piece = dr // ne
    mine = lax.dynamic_slice_in_dim(input_weight, me_e * piece, piece, 0)
    blocks = jnp.concatenate(
        [
            jnp.moveaxis(mine[:, :DI].reshape(piece, nd, di), 1, 0),
            jnp.moveaxis(mine[:, DI : 2 * DI].reshape(piece, nd, di), 1, 0),
            jnp.broadcast_to(mine[None, :, 2 * DI : 2 * DI + 2 * S], (nd, piece, 2 * S)),
            jnp.moveaxis(mine[:, DI + CONV :].reshape(piece, nd, heads), 1, 0),
            jnp.zeros((nd, piece, pad), BF),
        ],
        axis=2,
    )
    blocks = jnp.pad(blocks, ((0, 0), (0, -piece % 16), (0, 0)))
    wcols = blocks.shape[2]

    sg = shared_gate_up.reshape(dr, 2, nd, ne, fsl)
    sg = lax.dynamic_index_in_dim(sg, me_e, 3, False).reshape(dr, 2 * fs)
    sd = lax.dynamic_slice_in_dim(shared_down, me_e * fsl, fsl, 0)
    packed = jnp.concatenate([sg.reshape(-1), sd.reshape(-1), router_weight.reshape(-1)])
    packed_cols = packed.size // rows_t
    packed = jnp.pad(packed.reshape(rows_t, -1), ((0, 0), (0, 256 - packed_cols)))

    stream = tokens.reshape(rows_t, D).astype(F32)
    incoming = cotangent.reshape(rows_t, D)
    route_rows = routes.reshape(rows_t, TOP)
    normed_wide, norm_pull = jax.vjp(rms_scale, stream, norm_gain)
    normed = normed_wide.astype(BF)
    (_, w_in), (normed_all,) = run_tasks(
        [Weights(blocks), Gather("dp", jnp.concatenate([normed, packed], axis=1))], 1, "begin"
    )
    w_in = jnp.swapaxes(w_in[:, :, :piece], 0, 1).reshape(D, wcols)
    early, _ = lax.optimization_barrier((incoming, normed_all))
    inc_all = lax.all_gather(early, "expert", axis=0, tiled=True)
    packed_all = normed_all[:, :, D:].reshape(nd, rows_t, 256)[:, :, : packed_cols]
    packed_all = packed_all.reshape(nd, -1)
    sg_full = packed_all[:, : sg.size].reshape(D, 2 * fs)
    sd_full = packed_all[:, sg.size : sg.size + sd.size].reshape(fs, D)
    router_full = packed_all[:, sg.size + sd.size :].reshape(D, experts)
    taps = jnp.concatenate(
        [lax.dynamic_slice_in_dim(filter_weight, me_d * di, di, 1), filter_weight[:, DI:]], axis=1
    )
    tap_bias = jnp.concatenate(
        [lax.dynamic_slice_in_dim(filter_bias, me_d * di, di, 0), filter_bias[DI:]], axis=0
    )
    my_heads = lambda v: lax.dynamic_slice_in_dim(v, me_d * heads, heads, 0)
    my_gain = lax.dynamic_slice_in_dim(gated_gain, me_d * di, di, 0)

    taps_vec = jnp.concatenate([taps, tap_bias[None], jnp.zeros((3, di + 2 * S), F32)], axis=0)
    heads_vec = jnp.stack([my_heads(step_bias), -jnp.exp(my_heads(decay_log))])
    heads_vec = jnp.pad(heads_vec, ((0, 6), (0, S - heads)))
    lanes_vec = jnp.pad(
        jnp.stack([my_gain, jnp.repeat(my_heads(skip_gain), PS)]), ((0, 6), (0, 0))
    )
    vectors = (taps_vec, heads_vec, lanes_vec)
    payload, proj, scan, states = mixer_forward(
        lengths[:, 0], normed_all, w_in, output_weight, *vectors, heads
    )
    column = lax.broadcasted_iota(jnp.int32, (1, D + 128), 1)
    summed = run_tasks([Reduce("dp", payload)], 2, "reduce_mixer")[0][0]
    r = lax.rsqrt((summed[:, D : D + 1] + summed[:, D + 1 : D + 2]) / DI + EPSILON)
    mixed = summed[:, :D] * r
    after_mixer = stream + mixed
    moe_wide, moe_pull = jax.vjp(rms_scale, after_mixer, moe_gain)
    moe_in = moe_wide.astype(BF)
    logits = mm(moe_in, router_full)
    chosen = (route_rows[:, :, None] == jnp.arange(experts, dtype=jnp.int32)).astype(F32)
    picked = jnp.sum(chosen * logits[:, None, :], axis=2)
    gates = jax.nn.softmax(picked, axis=1)
    table = jnp.sum(chosen * gates[:, :, None], axis=1)
    t_hi, t_lo = hi_lo(table)
    moe_payload = jnp.concatenate(
        [moe_in, t_hi, t_lo, jnp.zeros((rows_t, 128 - 2 * experts), BF)], axis=1
    )
    (moe_all, back_sum, pre_grad, gh), = run_tasks(
        [Experts(moe_payload, inc_all, expert_gate_up, expert_down, sg_full, sd_full)], 3, "experts"
    )
    width = gh.shape[2]
    inc = incoming.astype(F32)
    spread_sum = back_sum[:, D : D + experts] + back_sum[:, D + experts : D + 2 * experts]
    logit_grad = table * (spread_sum - jnp.sum(table * spread_sum, axis=1, keepdims=True))
    logit_low = logit_grad.astype(BF)
    router_part = mm_tn(moe_in, logit_low)
    moe_in_grad = back_sum[:, :D] + mm_nt(logit_low, router_full)
    after_from_norm, moe_gain_grad = moe_pull(moe_in_grad)
    after_grad = inc + after_from_norm
    after_low = after_grad.astype(BF)
    s = jnp.sum(after_low.astype(F32) * mixed, axis=1, keepdims=True)
    r_hi, r_lo = hi_lo(r)
    d_hi, d_lo = hi_lo(s)
    grad_payload = jnp.concatenate(
        [after_low, r_hi, r_lo, d_hi, d_lo, jnp.zeros((rows_t, 124), BF)], axis=1
    )
    (grad_all,), (out_part, grad_blocks) = run_tasks(
        [
            Gather("dp", grad_payload),
            ExpertGrads(moe_all, pre_grad, gh, inc_all, expert_down, sd_full, nd),
        ],
        5,
        "gather_grad",
    )
    all_sum = lax.psum_scatter(grad_blocks, "dp", scatter_dimension=0, tiled=True)[0]
    up_sum = all_sum[:dr]
    each, span = FE // nd, D // 2
    down_sum = all_sum[dr : dr + each]
    last_sum = all_sum[dr + each :]
    d_proj, normed_part, output_part, d_taps, d_heads, d_lanes = mixer_backward(
        lengths[:, 0], grad_all, w_in, output_weight, *vectors, proj, scan, states, heads
    )
    def rows_of(parts, count):
        flat = jnp.concatenate([part.reshape(-1) for part in parts])
        return jnp.pad(flat, (0, count * 128 - flat.size)).reshape(count, 128)

    added = (d_taps[:K, di:], d_taps[K, di:], moe_gain_grad, router_part)
    own = (
        d_taps[:K, :di],
        d_taps[K, :di],
        d_heads[0, :heads],
        d_heads[1, :heads],
        jnp.sum(d_lanes[1].reshape(heads, PS), axis=1),
        d_lanes[0],
    )
    added_size = sum(part.size for part in added)
    added_rows = -(-added_size // (nd * 1024)) * 8
    own_rows = -(-sum(part.size for part in own) // 128)
    norm_rows = D // 128
    (normed_grad,), (d_sum,), (added_in,) = run_tasks(
        [
            Reduce("dp", normed_part),
            InputGrad(
                normed_all,
                d_proj.reshape(nd * rows_t, wcols),
                output_part.astype(BF).reshape(-1, wcols),
            ),
            Direct("all", "dp", rows_of(added, nd * added_rows).reshape(nd, added_rows, 128)),
        ],
        6,
        "reduce_grads",
    )
    stream_from_norm, norm_gain_grad = norm_pull(normed_grad)
    tokens_grad = after_grad + stream_from_norm
    small = jnp.concatenate(
        [jnp.sum(added_in, axis=0), rows_of(own, own_rows), rows_of((norm_gain_grad,), norm_rows)],
        axis=0,
    )
    small = jnp.pad(small, ((0, -small.shape[0] % 8), (0, 0)))
    shared_part = jnp.concatenate(
        [
            up_sum[:, 2 * el * FE :],
            last_sum[:fsl, span:].reshape(dr, -1),
        ],
        axis=1,
    ).reshape(-1, wcols)
    (d_full,), (small_in,) = run_tasks(
        [
            Gather("expert", jnp.concatenate([d_sum, shared_part], axis=0)),
            Direct("gather", "expert", small),
        ],
        7,
        "gather_grads",
    )
    shared_all = d_full[:, d_sum.shape[0] :].reshape(ne, dr, -1)
    d_full = d_full[:, : d_sum.shape[0]].reshape(-1, wcols)
    (got, _), (out_sum,), (small_all,) = run_tasks(
        [
            Swap(d_full[:D].reshape(nd, dr, wcols)),
            Reduce("expert", out_part),
            Direct("gather", "dp", jnp.sum(small_in, axis=0)),
        ],
        8,
        "swap_grads",
    )
    input_grad = assemble(got, heads)
    output_grad = d_full[D:].reshape(output_weight.shape)
    added_all = small_all[:, :added_rows].reshape(-1)
    own_all = small_all[:, added_rows : added_rows + own_rows].reshape(nd, -1)
    norm_gain_grad = jnp.sum(
        small_all[:, added_rows + own_rows : added_rows + own_rows + norm_rows], axis=0
    ).reshape(D)

    def split(flat, parts):
        out, start = [], 0
        for part in parts:
            out.append(flat[..., start : start + part.size].reshape(flat.shape[:-1] + part.shape))
            start += part.size
        return out

    added_taps, added_bias, moe_gain_grad, router_all = split(added_all, added)
    own_taps, own_bias, own_steps, own_decay, own_skip, own_gain = split(own_all, own)
    small = (
        jnp.concatenate([jnp.moveaxis(own_taps, 0, 1).reshape(K, DI), added_taps], axis=1),
        jnp.concatenate([own_bias.reshape(-1), added_bias]),
        own_steps.reshape(-1),
        own_decay.reshape(-1),
        own_skip.reshape(-1),
        norm_gain_grad,
        own_gain.reshape(-1),
        moe_gain_grad,
    )
    router_grad = lax.dynamic_slice_in_dim(router_all, me_d * dr, dr, 0)
    expert_up_grad = jnp.moveaxis(up_sum[:, : 2 * el * FE].reshape(dr, el, 2 * FE), 1, 0)
    expert_up_grad = expert_up_grad.astype(F32)
    expert_down_grad = jnp.stack(
        [
            down_sum[:, : 2 * span],
            jnp.concatenate([down_sum[:, 2 * span :], last_sum[:, :span]], axis=1),
        ],
        axis=0,
    ).astype(F32)
    shared_up_grad = (
        jnp.moveaxis(shared_all[:, :, : 2 * fs].reshape(ne, dr, 2, nd, fsl), 0, 3)
        .reshape(dr, 2 * FS)
        .astype(F32)
    )
    shared_down_grad = shared_all[:, :, 2 * fs :].reshape(fsr, D).astype(F32)
    block_output = (after_mixer + out_sum).astype(BF)
    shape = (MB, 1, loc, D)
    return (
        block_output.reshape(shape),
        tokens_grad.reshape(shape),
        input_grad,
        small[0],
        small[1],
        small[2],
        small[3],
        small[4],
        small[5],
        small[6],
        output_grad.astype(F32),
        small[7],
        router_grad,
        shared_up_grad,
        shared_down_grad,
        expert_up_grad,
        expert_down_grad,
    )


def solution(mesh):
    in_specs = (
        P(None, "expert", "dp", None),
        P(None, "expert", None),
        P(None, "expert", "dp", None),
        P(None, "expert", "dp", None),
        P("dp", None),
        P(),
        P(),
        P(),
        P(),
        P(),
        P(),
        P(),
        P("dp", None),
        P(),
        P("dp", None),
        P("dp", None),
        P("dp", None),
        P("expert", None, None),
        P("expert", None, None),
    )
    out_specs = (
        P(None, "expert", "dp", None),
        P(None, "expert", "dp", None),
        P("dp", None),
        P(),
        P(),
        P(),
        P(),
        P(),
        P(),
        P(),
        P("dp", None),
        P(),
        P("dp", None),
        P("dp", None),
        P("dp", None),
        P("expert", "dp", None),
        P("expert", "dp", None),
    )
    return jax.shard_map(body, mesh=mesh, in_specs=in_specs, out_specs=out_specs, check_vma=False)
```

```python
import functools

import jax
import jax.numpy as jnp
from jax import lax
from jax.experimental import pallas as pl
from jax.experimental.pallas import tpu as pltpu
from jax.sharding import PartitionSpec as P

D = 1536
H = 48
PS = 64
S = 128
K = 4
FE = 512
FS = 1024
TOP = 6
MB = 2
DI = 3072
CONV = 3328
IN_W = 6448
EPSILON = 1e-05
BF = jnp.bfloat16
F32 = jnp.float32
MESH = pl.DeviceIdType.MESH
VMEM_LIMIT = 60 * 1024 * 1024


def mm(a, b):
    return jnp.dot(a, b, preferred_element_type=F32)


def mm_nt(a, b):
    return lax.dot_general(a, b, (((1,), (1,)), ((), ())), preferred_element_type=F32)


def mm_tn(a, b):
    return lax.dot_general(a, b, (((0,), (0,)), ((), ())), preferred_element_type=F32)


def rms_scale(values, gain):
    return values * lax.rsqrt(jnp.mean(values * values, axis=-1, keepdims=True) + EPSILON) * gain


def hi_lo(v):
    hi = v.astype(BF)
    return hi, (v - hi.astype(F32)).astype(BF)


ANY = pl.BlockSpec(memory_space=pl.ANY)
IN_VMEM = pl.BlockSpec(memory_space=pltpu.VMEM)


def places(axis):
    me = lax.axis_index(axis)
    if axis == "dp":
        core, ring, pair = lax.rem(me, 2), lax.rem(me // 2, 4), me // 8

        def at(hop, other, sibling=0):
            z = lax.rem(pair + other, 2)
            return (z * 4 + lax.rem(ring + hop + 4, 4)) * 2 + lax.rem(core + sibling, 2)
    else:
        pair, ring = lax.rem(me, 2), me // 2

        def at(hop, other, sibling=0):
            return lax.rem(ring + hop + 4, 4) * 2 + lax.rem(pair + other, 2)

    return me, at


class Task:
    ins, outs, scratch, reaches, turns = (), (), (), (), 1

    def greet(self, barrier):
        return 0


def peers_of(axis, everyone):
    me, at = places(axis)
    if everyone:
        n = lax.axis_size(axis)
        return [lax.rem(me + k, n) for k in range(1, n)]
    near = [at(1, 0), at(-1, 0), at(0, 1)]
    return near + [at(0, 0, 1)] if axis == "dp" else near


class Links:
    def __init__(self, axis, send, recv):
        self.axis, self.send, self.recv, self.started = axis, send, recv, []

    def push(self, number, src, dst, peer):
        copy = pltpu.make_async_remote_copy(
            src_ref=src,
            dst_ref=dst,
            send_sem=self.send.at[number],
            recv_sem=self.recv.at[number],
            device_id={self.axis: peer},
            device_id_type=MESH,
        )
        copy.start()
        self.started.append(copy)

    def arrived(self, number, dst):
        pltpu.make_async_copy(dst, dst, self.recv.at[number]).wait()

    def finish(self):
        for copy in self.started:
            copy.wait_send()


def halves(shape):
    rows = shape[0]
    cut = rows // 2 if len(shape) == 3 else rows // 32 * 16
    return pl.ds(0, rows), pl.ds(0, cut), pl.ds(cut, rows - cut), cut


class Gather(Task):
    def __init__(self, axis, x):
        self.axis, self.reaches = axis, ((axis, False),)
        self.ins = ((x, ANY),)
        n = lax.axis_size(axis)
        self.outs = ((jax.ShapeDtypeStruct((n,) + x.shape, x.dtype), ANY),)
        dma = pltpu.SemaphoreType.DMA
        self.scratch = (dma((17,)), dma((17,)), dma)

    def steps(self, ins, outs, scratch):
        return gather_steps(self.axis, ins[0], outs[0], *scratch)


def gather_steps(axis, x, out, send, recv, own_sem):
    me, at = places(axis)
    cores = axis == "dp"
    up, down, pair, sib = at(1, 0), at(-1, 0), at(0, 1), at(0, 0, 1)
    whole, first, second, _ = halves(x.shape)
    links = Links(axis, send, recv)

    def push(number, slot, rows, peer, src=None):
        src = out.at[slot] if src is None else src
        links.push(number, src.at[rows], out.at[slot].at[rows], peer)

    def arrived(number, slot, rows):
        links.arrived(number, out.at[slot].at[rows])

    push(0, me, whole, up, x)
    push(1, me, whole, down, x)
    push(2, me, whole, pair, x)
    if cores:
        push(3, me, whole, sib, x)
    own = pltpu.make_async_copy(x, out.at[me], own_sem)
    own.start()
    yield
    own.wait()
    arrived(2, pair, whole)
    push(4, pair, whole, up)
    push(5, pair, whole, down)
    if cores:
        push(6, pair, whole, sib)
    yield
    arrived(0, down, whole)
    push(7, down, first, up)
    arrived(1, up, whole)
    push(8, up, second, down)
    if cores:
        push(9, down, whole, sib)
        push(10, up, whole, sib)
    yield
    arrived(4, at(-1, 1), whole)
    push(11, at(-1, 1), first, up)
    arrived(5, at(1, 1), whole)
    push(12, at(1, 1), second, down)
    if cores:
        push(13, at(-1, 1), whole, sib)
        push(14, at(1, 1), whole, sib)
    yield
    arrived(7, at(2, 0), first)
    arrived(8, at(2, 0), second)
    if cores:
        push(15, at(2, 0), whole, sib)
    yield
    arrived(11, at(2, 1), first)
    arrived(12, at(2, 1), second)
    if cores:
        push(16, at(2, 1), whole, sib)
        yield
        for number, hop, other in (
            (3, 0, 0),
            (6, 0, 1),
            (9, -1, 0),
            (10, 1, 0),
            (13, -1, 1),
            (14, 1, 1),
            (15, 2, 0),
            (16, 2, 1),
        ):
            arrived(number, at(hop, other, 1), whole)
    links.finish()


ORDER = ((2, 1), (2, 0), (1, 1), (-1, 1), (1, 0), (-1, 0), (0, 1), (0, 0))


class Reduce(Task):
    def __init__(self, axis, x, dtype=F32):
        self.axis, self.reaches = axis, ((axis, False),)
        n, rows, columns = x.shape
        self.ins = ((x, ANY),)
        self.outs = ((jax.ShapeDtypeStruct((rows, columns), dtype), IN_VMEM),)
        _, _, _, cut = halves((rows, columns))
        buf = lambda *dims: pltpu.VMEM(dims + (columns,), BF)
        dma = pltpu.SemaphoreType.DMA
        dp = axis == "dp"
        self.scratch = (
            buf(8, rows),
            buf(8 if dp else 1, rows if dp else 16),
            buf(2, cut),
            buf(2, rows - cut),
            buf(2, rows),
            buf(2, rows),
            buf(rows),
            dma((17,)),
            dma((17,)),
            dma((8,)),
        )

    def steps(self, ins, outs, scratch):
        return reduce_steps(self.axis, ins[0], outs[0], *scratch)


def reduce_steps(axis, x, out, acc, sib_buf, a_buf, b_buf, c_buf, d_buf, e_buf, send, recv, load):
    me, at = places(axis)
    cores = axis == "dp"
    rows = acc.shape[1]
    step = 16
    block = lambda k: x.at[k] if len(x.shape) == 3 else x.at[pl.ds(pl.multiple_of(k * rows, 16), rows)]
    up, down, pair, sib = at(1, 0), at(-1, 0), at(0, 1), at(0, 0, 1)
    whole, first, second, cut = halves(acc.shape[1:])
    links = Links(axis, send, recv)
    push, arrived = links.push, links.arrived

    def add(dst, offset, count, *srcs):
        @pl.loop(0, count // step)
        def _(i):
            at_rows = pl.ds(pl.multiple_of(offset + i * step, step), step)
            total = dst[at_rows, :].astype(F32)
            for src in srcs:
                total += src[pl.ds(pl.multiple_of(i * step, step), step), :].astype(F32)
            dst[at_rows, :] = total.astype(dst.dtype)

    loads = []
    for k, (hop, other) in enumerate(ORDER if x is not None else ()):
        if cores:
            push(k, block(at(hop, other, 1)), sib_buf.at[k], sib)
        copy = pltpu.make_async_copy(block(at(hop, other)), acc.at[k], load.at[k])
        copy.start()
        loads.append(copy)

    def ready(k):
        if loads:
            loads[k].wait()
        if cores:
            arrived(k, sib_buf.at[k])
            add(acc.at[k], 0, rows, sib_buf.at[k])

    yield
    for k in range(2):
        ready(k)
        push(8 + 2 * k, acc.at[k].at[first], a_buf.at[k], up)
        push(9 + 2 * k, acc.at[k].at[second], b_buf.at[k], down)
    yield
    for k in range(2):
        above, below = 2 + 2 * k, 3 + 2 * k
        ready(above)
        ready(below)
        if k:
            yield
        arrived(8 + 2 * k, a_buf.at[k])
        add(acc.at[above], 0, cut, a_buf.at[k])
        push(12 + 2 * k, acc.at[above], c_buf.at[k], up)
        arrived(9 + 2 * k, b_buf.at[k])
        add(acc.at[below], cut, rows - cut, b_buf.at[k])
        push(13 + 2 * k, acc.at[below], d_buf.at[k], down)
    ready(6)
    ready(7)
    yield
    arrived(12, c_buf.at[0])
    arrived(13, d_buf.at[0])
    add(acc.at[6], 0, rows, c_buf.at[0], d_buf.at[0])
    push(16, acc.at[6], e_buf, pair)
    yield
    arrived(14, c_buf.at[1])
    arrived(15, d_buf.at[1])
    yield
    arrived(16, e_buf)

    @pl.loop(0, rows // step)
    def _(i):
        at_rows = pl.ds(pl.multiple_of(i * step, step), step)
        total = acc[7, at_rows, :].astype(F32) + c_buf[1, at_rows, :].astype(F32)
        total += d_buf[1, at_rows, :].astype(F32) + e_buf[at_rows, :].astype(F32)
        out[at_rows, :] = total.astype(out.dtype)

    links.finish()


class Direct(Task):
    def __init__(self, kind, axis, x):
        self.kind, self.axis, self.reaches = kind, axis, ((axis, True),)
        n = lax.axis_size(axis)
        shape = (n,) + x.shape if kind == "gather" else x.shape
        self.ins = ((x, ANY),)
        self.outs = ((jax.ShapeDtypeStruct(shape, x.dtype), ANY),)
        dma = pltpu.SemaphoreType.DMA
        self.scratch = (dma((n,)), dma((n,)), dma)

    def steps(self, ins, outs, scratch):
        return direct_steps(self.kind, self.axis, ins[0], outs[0], *scratch)


def direct_steps(kind, axis, x, out, send, recv, own_sem):
    n, me = lax.axis_size(axis), lax.axis_index(axis)
    links = Links(axis, send, recv)
    piece = lambda k: x if kind == "gather" else x.at[k]
    for k in range(1, n):
        peer = lax.rem(me + k, n)
        links.push(k, piece(peer), out.at[me], peer)
    own = pltpu.make_async_copy(piece(me), out.at[me], own_sem)
    own.start()
    yield
    for k in range(1, n):
        links.arrived(k, out.at[lax.rem(me - k + n, n)])
    own.wait()
    links.finish()


def run_tasks(tasks, number, name):
    operands, in_specs, out_shapes, out_specs, scratch, spans = [], [], [], [], [], []
    for task in tasks:
        spans.append((len(operands), len(out_shapes), len(scratch)))
        operands += [x for x, _ in task.ins]
        in_specs += [spec for _, spec in task.ins]
        out_shapes += [shape for shape, _ in task.outs]
        out_specs += [spec for _, spec in task.outs]
        scratch += list(task.scratch)

    def kernel(*refs):
        ins = refs[: len(operands)]
        outs = refs[len(operands) : len(operands) + len(out_shapes)]
        temps = refs[len(operands) + len(out_shapes) :]
        barrier = pltpu.get_barrier_semaphore()
        count = 0
        for axis in ("dp", "expert"):
            here = [everyone for task in tasks for name, everyone in task.reaches if name == axis]
            if here:
                peers = peers_of(axis, any(here))
                for peer in peers:
                    pl.semaphore_signal(
                        barrier, inc=1, device_id={axis: peer}, device_id_type=MESH
                    )
                count += len(peers)
        for task in tasks:
            count += task.greet(barrier)
        pl.semaphore_wait(barrier, count)
        running = []
        for task, (i, o, s) in zip(tasks, spans):
            steps = task.steps(
                ins[i : i + len(task.ins)],
                outs[o : o + len(task.outs)],
                temps[s : s + len(task.scratch)],
            )
            running.append((task.turns, steps))
        while running:
            left = []
            for turns, steps in running:
                if all(next(steps, "end") != "end" for _ in range(turns)):
                    left.append((turns, steps))
            running = left

    results = pl.pallas_call(
        kernel,
        out_shape=out_shapes,
        in_specs=in_specs,
        out_specs=out_specs,
        scratch_shapes=scratch,
        compiler_params=pltpu.CompilerParams(
            collective_id=number, has_side_effects=True, vmem_limit_bytes=VMEM_LIMIT
        ),
        name=name,
    )(*operands)
    return [results[o : o + len(task.outs)] for task, (_, o, _) in zip(tasks, spans)]


class Weights(Task):
    def __init__(self, x):
        self.reaches, self.turns = (("dp", True), ("expert", False)), 2
        self.swap, self.spread = Direct("all", "dp", x), Gather("expert", x)
        n = lax.axis_size("expert")
        full = jax.ShapeDtypeStruct((n,) + x.shape, x.dtype)
        self.ins = ((x, ANY),)
        self.outs = self.swap.outs + ((full, ANY),)
        self.scratch = self.swap.scratch + self.spread.scratch

    def steps(self, ins, outs, scratch):
        yield from direct_steps("all", "dp", ins[0], outs[0], *scratch[:3])
        yield
        yield from gather_steps("expert", outs[0], outs[1], *scratch[3:])


class ExpertGrads(Task):
    def __init__(self, x, pre_grad, gh, inc, experts, each, blocks):
        n, rows, _ = x.shape
        width, depth = gh.shape[2], inc.shape[1]
        self.experts, self.each = experts, each
        grads = jax.ShapeDtypeStruct(
            (blocks, depth // blocks + 2 * (each // blocks), 2 * width), BF
        )
        self.ins = tuple((v, ANY) for v in (x, pre_grad, gh, inc))
        self.outs = ((grads, ANY),)
        dma = pltpu.SemaphoreType.DMA
        vmem = lambda *dims: pltpu.VMEM(dims, BF)
        self.scratch = (
            vmem(n, rows, depth),
            vmem(*pre_grad.shape),
            vmem(*gh.shape),
            vmem(*inc.shape),
            dma((5,)),
            vmem(depth, n * rows),
            vmem(width, n * rows),
            vmem(*grads.shape),
        )

    def steps(self, ins, outs, scratch):
        x, pre_grad, gh, inc, sems, x_t, gh_t, grads = scratch
        n, rows, depth = x.shape
        width = gh.shape[2]
        experts, each = self.experts, self.each
        copy = lambda src, dst, k: pltpu.make_async_copy(src, dst, sems.at[k])
        load_x = copy(ins[0].at[:, :, pl.ds(0, depth)], x, 0)
        load_pre = copy(ins[1], pre_grad, 1)
        load_inc = copy(ins[3], inc, 3)
        load_gh = copy(ins[2], gh, 2)
        for load in (load_x, load_pre, load_gh, load_inc):
            load.start()
        yield
        tile = 256
        col = lambda i: pl.ds(pl.multiple_of(i * tile, tile), tile)
        load_x.wait()

        @pl.loop(0, depth // tile)
        def _(i):
            x_t[col(i), :] = x[:, :, col(i)].reshape(n * rows, tile).T

        load_gh.wait()

        @pl.loop(0, width // 128)
        def _(i):
            at_cols = pl.ds(pl.multiple_of(i * 128, 128), 128)
            gh_t[at_cols, :] = gh[:, :, at_cols].reshape(n * rows, 128).T

        load_pre.wait()
        blocks = grads.shape[0]
        up_rows = depth // blocks
        for third in range(3):
            steps = 2 * width // tile // 3

            @pl.loop(third * steps, (third + 1) * steps)
            def _(i):
                value = mm(x_t[...], pre_grad[:, :, col(i)].reshape(n * rows, tile)).astype(BF)
                grads[:, :up_rows, col(i)] = value.reshape(blocks, up_rows, tile)

            yield
        load_inc.wait()
        piece_rows = each // blocks
        own = (width - experts * each) // blocks
        span = depth // 2
        spots = (((0, 0), (0, 2)), ((0, 1), (piece_rows, 0)))
        for half in range(2):

            @pl.loop(0, span // tile)
            def _(i):
                value = mm(gh_t[...], inc[:, col(half * span // tile + i)])
                for e in range(experts):
                    row, place = spots[half][e]
                    piece = value[e * each : (e + 1) * each].astype(BF)
                    grads[
                        :,
                        up_rows + row : up_rows + row + piece_rows,
                        col(place * span // tile + i),
                    ] = piece.reshape(blocks, piece_rows, tile)
                piece = value[experts * each :].reshape(blocks, own, tile)
                empty = jnp.zeros((blocks, piece_rows - own, tile), F32)
                piece = jnp.concatenate([piece, empty], axis=1).astype(BF)
                grads[:, up_rows + piece_rows :, col((1 + half) * span // tile + i)] = piece

            yield
        store = copy(grads, outs[0], 4)
        store.start()
        store.wait()


class InputGrad(Task):
    def __init__(self, g, d_proj, out_grad):
        self.reaches = (("expert", False),)
        n = lax.axis_size("expert")
        wide = d_proj.shape[1]
        rows = (D + out_grad.size // wide) // n
        self.reduce = Reduce("expert", jax.ShapeDtypeStruct((n, rows, wide), BF), BF)
        self.ins = tuple((v, ANY) for v in (g, d_proj, out_grad.reshape(n, -1, wide)))
        self.outs = self.reduce.outs
        dma = pltpu.SemaphoreType.DMA
        self.scratch = (
            pltpu.VMEM(g.shape[:2] + (D,), BF),
            pltpu.VMEM(d_proj.shape, BF),
            pltpu.VMEM((n, rows, wide), BF),
            dma((3,)),
        ) + self.reduce.scratch

    def steps(self, ins, outs, scratch):
        g, d_proj, total, sems = scratch[:4]
        n, _, wide = total.shape
        each = D // n
        below = pl.ds(each, total.shape[1] - each)
        loads = (
            pltpu.make_async_copy(ins[0].at[:, :, pl.ds(0, D)], g, sems.at[0]),
            pltpu.make_async_copy(ins[1], d_proj, sems.at[1]),
            pltpu.make_async_copy(ins[2], total.at[:, below], sems.at[2]),
        )
        for load in loads:
            load.start()
        yield
        for load in loads:
            load.wait()
        flat = g.shape[0] * g.shape[1]

        @pl.loop(0, n // 2)
        def _(i):
            columns = pl.ds(pl.multiple_of(i * 2 * each, 2 * each), 2 * each)
            value = mm_tn(g[:, :, columns].reshape(flat, 2 * each), d_proj[...]).astype(BF)
            total[pl.ds(2 * i, 2), :each, :] = value.reshape(2, each, wide)

        yield from reduce_steps("expert", total, outs[0], *scratch[4:])


class InputRows(Task):
    turns = 2

    def __init__(self, x, heads):
        nd, ne = lax.axis_size("dp"), lax.axis_size("expert")
        self.heads = heads
        self.slices = D // nd // 16
        self.reaches = (("expert", False),)
        wide = 2 * DI + 2 * S + 128
        row = jax.ShapeDtypeStruct((16, wide), BF)
        self.gather = Gather("expert", row)
        self.ins = ((x, ANY),)
        self.outs = ((jax.ShapeDtypeStruct((D // nd, IN_W), F32), IN_VMEM),)
        dma = pltpu.SemaphoreType.DMA
        self.scratch = (
            pltpu.VMEM((nd, 16, x.shape[1]), BF),
            pltpu.VMEM((16, wide), BF),
            pltpu.VMEM((ne, 16, wide), BF),
            dma((2 * ne,)),
            dma((nd,)),
        ) + self.gather.scratch

    def greet(self, barrier):
        nd = lax.axis_size("dp")
        j = lax.axis_index("dp")
        for source in range(nd):
            pl.semaphore_signal(
                barrier, inc=1, device_id={"dp": source, "expert": j // 2}, device_id_type=MESH
            )
        return 2 * lax.axis_size("expert")

    def steps(self, ins, outs, scratch):
        x = ins[0]
        got, row, full, send, recv = scratch[:5]
        nd, ne = lax.axis_size("dp"), lax.axis_size("expert")
        j, e = lax.axis_index("dp"), lax.axis_index("expert")
        heads, di = self.heads, self.heads * PS
        sent = []
        for k in range(2):
            for c in range(ne):
                src = x.at[pl.ds((k * self.slices + min(c, self.slices - 1)) * 16, 16)]
                mine = (j == 2 * e + k) & (e == c)
                away = pltpu.make_async_remote_copy(
                    src_ref=src,
                    dst_ref=got.at[j],
                    send_sem=send.at[k * ne + c],
                    recv_sem=recv.at[j],
                    device_id={"dp": 2 * e + k, "expert": c},
                    device_id_type=MESH,
                )
                here = pltpu.make_async_copy(src, got.at[j], recv.at[j])
                pl.when(mine)(here.start)
                pl.when(jnp.logical_not(mine))(away.start)
                sent.append((mine, away))
        yield
        for source in range(nd):
            pltpu.make_async_copy(got.at[source], got.at[source], recv.at[source]).wait()
        piece = lambda source, start, size: got[source, :, start : start + size].astype(F32)
        for source in range(0, nd, 2):
            for half in range(2):
                pair = [piece(source + k, half * di, di) for k in range(2)]
                start = half * DI + source * di
                row[:, start : start + 2 * di] = jnp.concatenate(pair, axis=1).astype(BF)
        total = piece(0, 2 * di, 2 * S)
        for source in range(1, nd):
            total = total + piece(source, 2 * di, 2 * S)
        row[:, 2 * DI : 2 * DI + 2 * S] = total.astype(BF)
        steps = [piece(source, 2 * di + 2 * S, 128)[:, :heads] for source in range(nd)]
        steps.append(jnp.zeros((16, 128 - nd * heads), F32))
        row[:, 2 * DI + 2 * S :] = jnp.concatenate(steps, axis=1).astype(BF)
        yield from gather_steps("expert", row, full, *scratch[5:])
        for c in range(self.slices):
            outs[0][c * 16 : (c + 1) * 16, :] = full[c, :, :IN_W].astype(F32)
        for mine, away in sent:
            pl.when(jnp.logical_not(mine))(away.wait_send)


class Small(Task):
    def __init__(self, x):
        self.reaches = (("expert", True), ("dp", True))
        nd, ne = lax.axis_size("dp"), lax.axis_size("expert")
        self.ins = ((x, ANY),)
        self.outs = ((jax.ShapeDtypeStruct((nd,) + x.shape, x.dtype), ANY),)
        dma = pltpu.SemaphoreType.DMA
        self.scratch = (
            pltpu.VMEM((ne,) + x.shape, x.dtype),
            pltpu.VMEM(x.shape, x.dtype),
            dma((ne,)),
            dma((ne,)),
            dma,
            dma((nd,)),
            dma((nd,)),
            dma,
        )

    def steps(self, ins, outs, scratch):
        parts, total = scratch[:2]
        yield from direct_steps("gather", "expert", ins[0], parts, *scratch[2:5])
        total[...] = jnp.sum(parts[...], axis=0)
        yield from direct_steps("gather", "dp", total, outs[0], *scratch[5:8])


class Experts(Task):
    def __init__(self, x, inc, w_up, w_down, s_up, s_down):
        self.reaches = (("expert", False),)
        self.gather = Gather("expert", x)
        n = lax.axis_size("expert")
        rows, wide = x.shape
        depth = inc.shape[1]
        experts, _, both = w_up.shape
        self.experts = experts
        all_rows = jax.ShapeDtypeStruct((n, rows, wide), BF)
        self.reduce = Reduce("expert", all_rows)
        hidden = experts * both // 2 + s_down.shape[0]
        pre = jax.ShapeDtypeStruct((n, rows, 2 * hidden), BF)
        gh = jax.ShapeDtypeStruct((n, rows, hidden), BF)
        self.ins = tuple((v, ANY) for v in (x, inc, w_up, w_down, s_up, s_down))
        part = jax.ShapeDtypeStruct((n, rows, depth), BF)
        self.outs = ((all_rows, IN_VMEM),) + self.reduce.outs + tuple(
            (v, ANY) for v in (pre, gh, part)
        )
        dma = pltpu.SemaphoreType.DMA
        self.scratch = (
            (pltpu.VMEM((n, rows, depth), BF),)
            + tuple(pltpu.VMEM(v.shape, BF) for v in (w_up, w_down, s_up, s_down))
            + (pltpu.VMEM((2 * rows, wide), BF), pltpu.VMEM((2 * rows, depth), BF))
            + (pltpu.VMEM((2 * rows, 2 * hidden), BF), pltpu.VMEM((2 * rows, hidden), BF))
            + (pltpu.VMEM(pre.shape, BF), pltpu.VMEM(gh.shape, BF))
            + (pltpu.VMEM((2 * rows, 128), F32), dma((22,)), pltpu.VMEM(part.shape, BF))
            + self.gather.scratch
            + self.reduce.scratch
        )

    def steps(self, ins, outs, scratch):
        x, inc_in = ins[:2]
        x_all, dx_out, pre_out, gh_out, part_out = outs
        inc, w_up, w_down, s_up, s_down, xs, incs, pg, ghs, pre, gh, extra, sems = scratch[:13]
        part, gather_scratch, reduce_scratch = scratch[13], scratch[14:17], scratch[17:]
        acc = reduce_scratch[0]
        me, at = places("expert")
        n, rows, depth = inc.shape
        experts, _, both = w_up.shape
        each = both // 2
        shared = s_down.shape[0]
        tile = min(256, each)
        loads = [
            pltpu.make_async_copy(src, dst, sems.at[k])
            for k, (src, dst) in enumerate(zip(ins[2:], (w_up, w_down, s_up, s_down)))
        ]
        loads += [
            pltpu.make_async_copy(inc_in.at[pl.ds(k * rows, rows)], inc.at[k], sems.at[13 + k])
            for k in range(n)
        ]
        arriving = gather_steps("expert", x, x_all, *gather_scratch)
        next(arriving)
        for load in loads:
            load.start()
        next(arriving)
        next(arriving)
        for load in loads:
            load.wait()
        lane = lax.broadcasted_iota(jnp.int32, (1, 128), 1)
        stores = []

        def unit(a, b, u, scale):
            sig = jax.nn.sigmoid(a)
            act = a * sig
            hidden = act * b
            gu = u * scale
            da = gu * b * (sig + act * (1.0 - sig))
            return hidden * scale, da, gu * act, u * hidden

        def compute(hop, places_in_acc):
            slots = (at(hop, 0), at(hop, 1))
            for k, slot in enumerate(slots):
                part = pl.ds(k * rows, rows)
                xs[part, :] = x_all[slot]
                incs[part, :] = inc[slot]
            extra[...] = jnp.zeros_like(extra)

            @pl.loop(0, experts * (each // tile))
            def _(i):
                e, f = i // (each // tile), lax.rem(i, each // tile)
                place = me * experts + e
                table = xs[:, depth:].astype(F32)
                chosen = (lane == place) | (lane == place + n * experts)
                scale = jnp.sum(jnp.where(chosen, table, 0.0), axis=1, keepdims=True)
                left = pl.ds(pl.multiple_of(f * tile, tile), tile)
                right = pl.ds(pl.multiple_of(each + f * tile, tile), tile)
                a = mm(xs[:, :depth], w_up[e, :, left])
                b = mm(xs[:, :depth], w_up[e, :, right])
                u = mm_nt(incs[...], w_down[e, left, :])
                h, da, db, dots = unit(a, b, u, scale)
                ghs[:, pl.ds(pl.multiple_of(e * each + f * tile, tile), tile)] = h.astype(BF)
                pg[:, pl.ds(pl.multiple_of(e * both + f * tile, tile), tile)] = da.astype(BF)
                pg[:, pl.ds(pl.multiple_of(e * both + each + f * tile, tile), tile)] = db.astype(BF)
                extra[...] += jnp.where(lane == place, jnp.sum(dots, axis=1, keepdims=True), 0.0)

            a = mm(xs[:, :depth], s_up[:, :shared])
            b = mm(xs[:, :depth], s_up[:, shared:])
            u = mm_nt(incs[...], s_down[...])
            h, da, db, _ = unit(a, b, u, 1.0)
            ghs[:, experts * each :] = h.astype(BF)
            pg[:, experts * both : experts * both + shared] = da.astype(BF)
            pg[:, experts * both + shared :] = db.astype(BF)

            @pl.loop(0, depth // tile)
            def _(i):
                columns = pl.ds(pl.multiple_of(i * tile, tile), tile)
                total = mm_nt(pg[:, experts * both :], s_up[columns, :])
                for e in range(experts):
                    total += mm_nt(pg[:, e * both : (e + 1) * both], w_up[e, columns, :])
                for k, place in enumerate(places_in_acc):
                    acc[place, :, columns] = total[k * rows : (k + 1) * rows].astype(BF)

            grads = extra[...]
            high = grads.astype(BF).astype(F32)
            turn = (
                iota((128, 128), 0) + n * experts == iota((128, 128), 1)
            ).astype(F32)
            rest = exact(grads - high, turn, ((1,), (0,)))
            both_parts = (high + rest).astype(BF)
            for k, (slot, place) in enumerate(zip(slots, places_in_acc)):
                part = pl.ds(k * rows, rows)
                acc[place, :, depth:] = both_parts[k * rows : (k + 1) * rows]
                pre[slot] = pg[part, :]
                gh[slot] = ghs[part, :]
                store = pltpu.make_async_copy(pre.at[slot], pre_out.at[slot], sems.at[4 + len(stores)])
                store.start()
                stores.append(store)

        compute(0, (7, 6))
        next(arriving)
        compute(1, (4, 2))
        compute(-1, (5, 3))
        for _ in arriving:
            pass
        compute(2, (1, 0))
        store = pltpu.make_async_copy(gh, gh_out, sems.at[12])
        store.start()
        stores.append(store)
        summing = reduce_steps("expert", None, dx_out, *reduce_scratch)
        next(summing)
        for half in range(2):
            next(summing)

            @pl.loop(half * depth // tile // 2, (half + 1) * depth // tile // 2)
            def _(i):
                columns = pl.ds(pl.multiple_of(i * tile, tile), tile)
                hid = lambda start, size: gh[:, :, start : start + size].reshape(n * rows, size)
                total = mm(hid(experts * each, shared), s_down[:, columns])
                for e in range(experts):
                    total += mm(hid(e * each, each), w_down[e, :, columns])
                part[:, :, columns] = total.astype(BF).reshape(n, rows, tile)

        store = pltpu.make_async_copy(part, part_out, sems.at[21])
        store.start()
        stores.append(store)
        yield from summing
        for store in stores:
            store.wait()


EDGE = 8


def pieces(v, count):
    out = []
    for _ in range(count):
        out.append(v.astype(BF))
        v = v - out[-1].astype(F32)
    return out


def exact(v, ones, dims, count=2):
    ones = ones.astype(BF)
    parts = [
        lax.dot_general(p, ones, (dims, ((), ())), preferred_element_type=F32)
        for p in pieces(v, count)
    ]
    return sum(parts[1:], parts[0])


def exact_right(ones, v, dims, count=2):
    ones = ones.astype(BF)
    parts = [
        lax.dot_general(ones, p, (dims, ((), ())), preferred_element_type=F32)
        for p in pieces(v, count)
    ]
    return sum(parts[1:], parts[0])


def iota(shape, axis):
    return lax.broadcasted_iota(jnp.int32, shape, axis)


class Block:
    def __init__(self, m, start, proj, ext, lengths, taps, heads_vec, heads):
        loc = proj.shape[0]
        di = heads * PS
        width = di + 2 * S
        self.heads, self.di = heads, di
        first = lengths[m, 0]
        second = first + lengths[m, 1]

        def doc(p):
            return (p >= first).astype(jnp.int32) + (p >= second).astype(jnp.int32)

        self.doc = doc
        self.at = start + iota((loc, 1), 0)
        docs = doc(self.at)
        docs_row = doc(start + iota((1, loc), 1))
        last_doc, before_doc = doc(start + loc - 1), doc(start - 1)
        self.keep = (docs == before_doc).astype(F32)
        self.keep_last = (last_doc == before_doc).astype(F32)
        self.same_last = (docs == last_doc).astype(F32)
        self.gate = proj[:, :di]
        ext[m, EDGE : EDGE + loc, :] = proj[:, di : di + width].astype(BF).astype(F32)
        total = jnp.broadcast_to(taps[K : K + 1, :], (loc, width))
        self.shifted = []
        for k in range(K):
            back = K - 1 - k
            value = ext[m, EDGE - back : EDGE - back + loc, :]
            if back:
                value = value * (docs == doc(self.at - back)).astype(F32)
            self.shifted.append(value)
            total = total + taps[k : k + 1, :] * value
        self.sig = jax.nn.sigmoid(total)
        self.total = total
        filtered = total * self.sig
        self.x = filtered[:, :di]
        self.write = filtered[:, di : di + S].astype(BF)
        self.read = filtered[:, di + S :].astype(BF)
        self.raw = proj[:, di + width :] + heads_vec[0:1, :]
        self.steps = jnp.maximum(self.raw, 0.0) + jnp.log1p(jnp.exp(-jnp.abs(self.raw)))
        self.rate = heads_vec[1:2, :]
        rise = self.steps * self.rate
        rows, cols = iota((loc, loc), 0), iota((loc, loc), 1)
        self.lower = (cols <= rows).astype(F32)
        self.cum = exact_right(self.lower, rise, ((1,), (0,)), 3)
        cum_rows = exact(rise, (rows <= cols).astype(F32), ((0,), (0,)), 3)
        self.last = self.cum[loc - 1 : loc, :]
        self.grow = jnp.exp(self.cum) * self.keep
        self.fall = jnp.exp(self.last - self.cum) * self.same_last
        self.decay = jnp.exp(self.last) * self.keep_last
        allowed = (cols <= rows) & (docs == docs_row)
        scores = mm_nt(self.read, self.write)
        self.spread, self.mixing = [], []
        for h in range(heads):
            span = self.cum[:, h : h + 1] - cum_rows[h : h + 1, :]
            shape = jnp.exp(jnp.where(allowed, span, -1e30))
            self.spread.append(shape)
            self.mixing.append(shape * scores)
        self.lane = iota((1, di), 1)
        self.steps_wide = self.widen(self.steps)
        self.grow_wide = self.widen(self.grow)
        self.weight_wide = self.widen(self.fall * self.steps)
        self.scaled = self.x * self.steps_wide
        self.pushed = self.x * self.weight_wide

    def widen(self, v):
        out = jnp.broadcast_to(v[:, 0:1], (v.shape[0], self.di))
        for h in range(1, self.heads):
            out = jnp.where(self.lane >= h * PS, v[:, h : h + 1], out)
        return out

    def per_head(self, parts):
        out = parts[0]
        for h in range(1, self.heads):
            out = jnp.where(self.lane >= h * PS, parts[h], out)
        return out

    def decay_rows(self):
        rows = iota((self.di, 1), 0)
        out = jnp.broadcast_to(self.decay[:, 0:1], (self.di, 1))
        for h in range(1, self.heads):
            out = jnp.where(rows >= h * PS, self.decay[:, h : h + 1], out)
        return out


def load_weights(pieces_ref, w, sem):
    copies = [
        pltpu.make_async_copy(pieces_ref.at[k], w.at[:, k], sem.at[k]) for k in range(w.shape[1])
    ]
    for copy in copies:
        copy.start()
    for copy in copies:
        copy.wait()


def forward_kernel(
    heads,
    lengths,
    g,
    w_pieces,
    w_out,
    taps,
    heads_vec,
    lanes_vec,
    payload,
    proj,
    scan,
    states,
    ext,
    state,
    w,
    w_sem,
):
    b = pl.program_id(0)
    loc = g.shape[1] // MB
    di = heads * PS

    @pl.when(b == 0)
    def _():
        ext[...] = jnp.zeros_like(ext)
        state[...] = jnp.zeros_like(state)
        load_weights(w_pieces, w, w_sem)

    proj[0] = mm(g[0, :, :D], w[...].reshape(D, -1))
    column = iota((loc, payload.shape[2] - D), 1)
    for m in range(MB):
        rows = slice(m * loc, (m + 1) * loc)
        ext[m, 0:EDGE, :] = ext[m, loc : loc + EDGE, :]
        part = Block(m, b * loc, proj[0, rows, :], ext, lengths, taps, heads_vec, heads)
        before = state[m]
        states[0, m] = before
        scaled = part.scaled.astype(BF)
        inner = part.per_head([mm(part.mixing[h].astype(BF), scaled) for h in range(heads)])
        carried = mm_nt(part.read, before.astype(BF)) * part.grow_wide
        out = inner + carried + lanes_vec[1:2, :] * part.x
        scan[0, rows, :] = out
        state[m] = part.decay_rows() * before + mm_tn(part.pushed.astype(BF), part.write)
        y = out * (part.gate * jax.nn.sigmoid(part.gate))
        square = jnp.sum(y * y, axis=1, keepdims=True)
        high = square.astype(BF).astype(F32)
        payload[0, rows, :D] = mm((y * lanes_vec[0:1, :]).astype(BF), w_out[...]).astype(BF)
        sums = jnp.where(column == 0, high, jnp.where(column == 1, square - high, 0.0))
        payload[0, rows, D:] = sums.astype(BF)


def backward_kernel(
    heads,
    lengths,
    grad,
    w_pieces,
    w_out,
    taps,
    heads_vec,
    lanes_vec,
    proj,
    proj_before,
    scan,
    states,
    d_proj,
    normed_part,
    d_out,
    d_taps,
    d_heads,
    d_lanes,
    ext,
    d_ext,
    d_state,
    w,
    w_sem,
):
    step = pl.program_id(0)
    b = pl.num_programs(0) - 1 - step
    loc = grad.shape[1] // MB
    di = heads * PS
    width = di + 2 * S

    @pl.when(step == 0)
    def _():
        for ref in (d_ext, d_state, d_out, d_taps, d_heads, d_lanes):
            ref[...] = jnp.zeros_like(ref)
        load_weights(w_pieces, w, w_sem)

    gated_grad = mm_nt(grad[0, :, :D], w_out[...])
    extra = grad[0, :, D:].astype(F32)
    has_before = (b > 0).astype(F32)
    pick = (iota((di, S), 0) // PS == iota((di, S), 1)).astype(F32)
    for m in range(MB):
        rows = slice(m * loc, (m + 1) * loc)
        edge = proj_before[0, (m + 1) * loc - EDGE : (m + 1) * loc, di : di + width]
        ext[m, 0:EDGE, :] = edge.astype(BF).astype(F32) * has_before
        part = Block(m, b * loc, proj[0, rows, :], ext, lengths, taps, heads_vec, heads)
        gain, skip = lanes_vec[0:1, :], lanes_vec[1:2, :]
        r = extra[rows, 0:1] + extra[rows, 1:2]
        s = extra[rows, 2:3] + extra[rows, 3:4]
        out = scan[0, rows, :]
        sig = jax.nn.sigmoid(part.gate)
        act = part.gate * sig
        yr = out * act * r
        gg = gated_grad[rows]
        d_lanes[0:1, :] += jnp.sum(gg * yr, axis=0, keepdims=True)
        d_out[...] += mm_tn((yr * gain).astype(BF), grad[0, rows, :D])
        dy = r * (gg * gain) - yr * (r * s / DI)
        d_gate = dy * out * (sig + act * (1.0 - sig))
        do = dy * act
        do_low = do.astype(BF)
        x = part.x
        d_lanes[1:2, :] += jnp.sum(do * x, axis=0, keepdims=True)
        dx = skip * do
        before = states[0, m]
        before_low = before.astype(BF)
        ds = d_state[m]
        ds_low = ds.astype(BF)

        d_scores = jnp.zeros((loc, loc), F32)
        d_scaled, d_cum = [], jnp.zeros((loc, S), F32)
        head_lane = iota((loc, S), 1)
        for h in range(heads):
            inside = (part.lane >= h * PS) & (part.lane < (h + 1) * PS)
            own = jnp.where(inside, part.scaled, 0.0).astype(BF)
            d_mix = mm_nt(do_low, own)
            d_scaled.append(mm_tn(part.mixing[h].astype(BF), do_low))
            d_scores = d_scores + d_mix * part.spread[h]
            d_span = d_mix * part.mixing[h]
            ones = (head_lane == h).astype(F32)
            d_cum = d_cum + exact(d_span, ones, ((1,), (0,))) - exact(d_span, ones, ((0,), (0,)))
        d_scaled = part.per_head(d_scaled)
        dx = dx + d_scaled * part.steps_wide
        d_scores_low = d_scores.astype(BF)
        d_read = mm(d_scores_low, part.write)
        d_write = mm_tn(d_scores_low, part.read)

        d_carry = do * part.grow_wide
        d_carry_low = d_carry.astype(BF)
        carried = mm_nt(part.read, before_low)
        d_read = d_read + mm(d_carry_low, before_low)

        d_pushed = mm_nt(part.write, ds_low)
        d_write = d_write + mm(part.pushed.astype(BF), ds_low)
        dx = dx + d_pushed * part.weight_wide
        sums = exact(
            jnp.concatenate([d_carry * carried, d_pushed * x, d_scaled * x], axis=0),
            pick,
            ((1,), (0,)),
        )
        d_weight = sums[loc : 2 * loc]
        d_fall = d_weight * part.fall * part.steps
        d_cum = d_cum + sums[:loc] - d_fall
        d_steps = sums[2 * loc :] + d_weight * part.fall
        state_dot = jnp.sum(ds * before, axis=1, keepdims=True)
        d_decay = exact(jnp.broadcast_to(state_dot, (di, S)), pick, ((0,), (0,)))[0:1, :]
        d_last = jnp.sum(d_fall, axis=0, keepdims=True) + d_decay * part.decay
        d_cum = d_cum + jnp.where(iota((loc, 1), 0) == loc - 1, d_last, 0.0)
        d_state[m] = part.decay_rows() * ds + mm_tn(d_carry_low, part.read)

        d_rise = exact_right(part.lower, d_cum, ((0,), (0,)))
        d_steps = d_steps + d_rise * part.rate
        d_raw = d_steps * jax.nn.sigmoid(part.raw)
        d_heads[0:1, :] += jnp.sum(d_raw, axis=0, keepdims=True)
        d_heads[1:2, :] += jnp.sum(d_rise * part.steps * part.rate, axis=0, keepdims=True)

        d_total = jnp.concatenate([dx, d_write, d_read], axis=1)
        d_total = d_total * (part.sig + part.total * part.sig * (1.0 - part.sig))
        for k in range(K):
            d_taps[k : k + 1, :] += jnp.sum(d_total * part.shifted[k], axis=0, keepdims=True)
        d_taps[K : K + 1, :] += jnp.sum(d_total, axis=0, keepdims=True)
        d_ext[m, loc : loc + EDGE, :] = d_ext[m, 0:EDGE, :]
        d_ext[m, 0:loc, :] = d_total
        d_seq = taps[K - 1 : K, :] * d_total
        docs = part.doc(part.at)
        for ahead in range(1, K):
            same = (docs == part.doc(part.at + ahead)).astype(F32)
            d_seq = d_seq + taps[K - 1 - ahead : K - ahead, :] * (
                same * d_ext[m, ahead : ahead + loc, :]
            )
        d_proj[0, rows, :di] = d_gate.astype(BF)
        d_proj[0, rows, di : di + width] = d_seq.astype(BF)
        d_proj[0, rows, di + width :] = jnp.where(head_lane < heads, d_raw, 0.0).astype(BF)
    normed_part[0] = mm_nt(d_proj[0], w[...].reshape(D, -1)).astype(BF)


def weight_scratch(w):
    slices = D // w.shape[1] // w.shape[2]
    return [
        pltpu.VMEM((w.shape[1], slices) + w.shape[2:], BF),
        pltpu.SemaphoreType.DMA((slices,)),
    ]


def block_spec(shape, index):
    return pl.BlockSpec((1,) + shape[1:], lambda i: (index(i),) + (0,) * (len(shape) - 1))


def whole_spec(shape):
    return pl.BlockSpec(shape, lambda i: (0,) * len(shape))


def mixer_forward(lengths, g, w, w_out, taps, heads_vec, lanes_vec, heads):
    nb, rows, _ = g.shape
    di = heads * PS
    width = di + 2 * S
    shapes = [
        jax.ShapeDtypeStruct((nb, rows, D + 128), BF),
        jax.ShapeDtypeStruct((nb, rows, w.shape[-1]), F32),
        jax.ShapeDtypeStruct((nb, rows, di), F32),
        jax.ShapeDtypeStruct((nb, MB, di, S), F32),
    ]
    same = lambda i: i
    return pl.pallas_call(
        functools.partial(forward_kernel, heads),
        grid=(nb,),
        out_shape=shapes,
        in_specs=[pl.BlockSpec(memory_space=pltpu.SMEM), block_spec(g.shape, same)]
        + [pl.BlockSpec(memory_space=pl.ANY)]
        + [whole_spec(v.shape) for v in (w_out, taps, heads_vec, lanes_vec)],
        out_specs=[block_spec(v.shape, same) for v in shapes],
        scratch_shapes=[
            pltpu.VMEM((MB, rows // MB + EDGE, width), F32),
            pltpu.VMEM((MB, di, S), F32),
        ]
        + weight_scratch(w),
        compiler_params=pltpu.CompilerParams(vmem_limit_bytes=VMEM_LIMIT),
        name="mixer_forward",
    )(lengths, g, w, w_out, taps, heads_vec, lanes_vec)


def mixer_backward(lengths, grad, w, w_out, taps, heads_vec, lanes_vec, proj, scan, states, heads):
    nb, rows, _ = grad.shape
    di = heads * PS
    width = di + 2 * S
    back = lambda i: nb - 1 - i
    before = lambda i: jnp.maximum(nb - 2 - i, 0)
    per_block = [
        jax.ShapeDtypeStruct((nb, rows, w.shape[-1]), BF),
        jax.ShapeDtypeStruct((nb, rows, D), BF),
    ]
    sums = [
        jax.ShapeDtypeStruct((di, w_out.shape[1]), F32),
        jax.ShapeDtypeStruct((8, width), F32),
        jax.ShapeDtypeStruct((8, S), F32),
        jax.ShapeDtypeStruct((8, di), F32),
    ]
    return pl.pallas_call(
        functools.partial(backward_kernel, heads),
        grid=(nb,),
        out_shape=per_block + sums,
        in_specs=[pl.BlockSpec(memory_space=pltpu.SMEM), block_spec(grad.shape, back)]
        + [pl.BlockSpec(memory_space=pl.ANY)]
        + [whole_spec(v.shape) for v in (w_out, taps, heads_vec, lanes_vec)]
        + [block_spec(proj.shape, back), block_spec(proj.shape, before)]
        + [block_spec(scan.shape, back), block_spec(states.shape, back)],
        out_specs=[block_spec(v.shape, back) for v in per_block]
        + [whole_spec(v.shape) for v in sums],
        scratch_shapes=[
            pltpu.VMEM((MB, rows // MB + EDGE, width), F32),
            pltpu.VMEM((MB, rows // MB + EDGE, width), F32),
            pltpu.VMEM((MB, di, S), F32),
        ]
        + weight_scratch(w),
        compiler_params=pltpu.CompilerParams(vmem_limit_bytes=VMEM_LIMIT),
        name="mixer_backward",
    )(lengths, grad, w, w_out, taps, heads_vec, lanes_vec, proj, proj, scan, states)


def body(
    tokens,
    lengths,
    routes,
    cotangent,
    input_weight,
    filter_weight,
    filter_bias,
    step_bias,
    decay_log,
    skip_gain,
    norm_gain,
    gated_gain,
    output_weight,
    moe_gain,
    router_weight,
    shared_gate_up,
    shared_down,
    expert_gate_up,
    expert_down,
):
    nd, ne = lax.axis_size("dp"), lax.axis_size("expert")
    me_d, me_e = lax.axis_index("dp"), lax.axis_index("expert")
    loc = tokens.shape[2]
    heads = H // nd
    di = heads * PS
    rows_t = MB * loc
    experts = expert_gate_up.shape[0] * ne
    el = expert_gate_up.shape[0]
    dr = D // nd
    fs = FS // ne
    fsr = FS // nd
    fsl = fsr // ne

    pad = 128 - heads
    piece = 16
    place = jnp.minimum(me_e, dr // piece - 1) * piece
    mine = lax.dynamic_slice_in_dim(input_weight, place, piece, 0)
    blocks = jnp.concatenate(
        [
            jnp.moveaxis(mine[:, :DI].reshape(piece, nd, di), 1, 0),
            jnp.moveaxis(mine[:, DI : 2 * DI].reshape(piece, nd, di), 1, 0),
            jnp.broadcast_to(mine[None, :, 2 * DI : 2 * DI + 2 * S], (nd, piece, 2 * S)),
            jnp.moveaxis(mine[:, DI + CONV :].reshape(piece, nd, heads), 1, 0),
            jnp.zeros((nd, piece, pad), BF),
        ],
        axis=2,
    )
    wcols = blocks.shape[2]

    sg = shared_gate_up.reshape(dr, 2, nd, ne, fsl)
    sg = lax.dynamic_index_in_dim(sg, me_e, 3, False).reshape(dr, 2 * fs)
    sd = lax.dynamic_slice_in_dim(shared_down, me_e * fsl, fsl, 0)
    packed = jnp.concatenate([sg.reshape(-1), sd.reshape(-1), router_weight.reshape(-1)])
    packed_cols = packed.size // rows_t
    packed = jnp.pad(packed.reshape(rows_t, -1), ((0, 0), (0, 256 - packed_cols)))

    stream = tokens.reshape(rows_t, D).astype(F32)
    incoming = cotangent.reshape(rows_t, D)
    route_rows = routes.reshape(rows_t, TOP)
    normed_wide, norm_pull = jax.vjp(rms_scale, stream, norm_gain)
    normed = normed_wide.astype(BF)
    (_, w_in), (normed_all,) = run_tasks(
        [Weights(blocks), Gather("dp", jnp.concatenate([normed, packed], axis=1))], 1, "begin"
    )
    early, _ = lax.optimization_barrier((incoming, normed_all))
    inc_all = lax.all_gather(early, "expert", axis=0, tiled=True)
    packed_all = normed_all[:, :, D:].reshape(nd, rows_t, 256)[:, :, : packed_cols]
    packed_all = packed_all.reshape(nd, -1)
    sg_full = packed_all[:, : sg.size].reshape(D, 2 * fs)
    sd_full = packed_all[:, sg.size : sg.size + sd.size].reshape(fs, D)
    router_full = packed_all[:, sg.size + sd.size :].reshape(D, experts)
    taps = jnp.concatenate(
        [lax.dynamic_slice_in_dim(filter_weight, me_d * di, di, 1), filter_weight[:, DI:]], axis=1
    )
    tap_bias = jnp.concatenate(
        [lax.dynamic_slice_in_dim(filter_bias, me_d * di, di, 0), filter_bias[DI:]], axis=0
    )
    my_heads = lambda v: lax.dynamic_slice_in_dim(v, me_d * heads, heads, 0)
    my_gain = lax.dynamic_slice_in_dim(gated_gain, me_d * di, di, 0)

    taps_vec = jnp.concatenate([taps, tap_bias[None], jnp.zeros((3, di + 2 * S), F32)], axis=0)
    heads_vec = jnp.stack([my_heads(step_bias), -jnp.exp(my_heads(decay_log))])
    heads_vec = jnp.pad(heads_vec, ((0, 6), (0, S - heads)))
    lanes_vec = jnp.pad(
        jnp.stack([my_gain, jnp.repeat(my_heads(skip_gain), PS)]), ((0, 6), (0, 0))
    )
    vectors = (taps_vec, heads_vec, lanes_vec)
    payload, proj, scan, states = mixer_forward(
        lengths[:, 0], normed_all, w_in, output_weight, *vectors, heads
    )
    column = lax.broadcasted_iota(jnp.int32, (1, D + 128), 1)
    summed = run_tasks([Reduce("dp", payload)], 2, "reduce_mixer")[0][0]
    r = lax.rsqrt((summed[:, D : D + 1] + summed[:, D + 1 : D + 2]) / DI + EPSILON)
    mixed = summed[:, :D] * r
    after_mixer = stream + mixed
    moe_wide, moe_pull = jax.vjp(rms_scale, after_mixer, moe_gain)
    moe_in = moe_wide.astype(BF)
    logits = mm(moe_in, router_full)
    chosen = (route_rows[:, :, None] == jnp.arange(experts, dtype=jnp.int32)).astype(F32)
    picked = jnp.sum(chosen * logits[:, None, :], axis=2)
    gates = jax.nn.softmax(picked, axis=1)
    table = jnp.sum(chosen * gates[:, :, None], axis=1)
    t_hi, t_lo = hi_lo(table)
    moe_payload = jnp.concatenate(
        [moe_in, t_hi, t_lo, jnp.zeros((rows_t, 128 - 2 * experts), BF)], axis=1
    )
    (moe_all, back_sum, pre_grad, gh, out_part), = run_tasks(
        [Experts(moe_payload, inc_all, expert_gate_up, expert_down, sg_full, sd_full)], 3, "experts"
    )
    width = gh.shape[2]
    inc = incoming.astype(F32)
    spread_sum = back_sum[:, D : D + experts] + back_sum[:, D + experts : D + 2 * experts]
    logit_grad = table * (spread_sum - jnp.sum(table * spread_sum, axis=1, keepdims=True))
    logit_low = logit_grad.astype(BF)
    router_part = mm_tn(moe_in, logit_low)
    moe_in_grad = back_sum[:, :D] + mm_nt(logit_low, router_full)
    after_from_norm, moe_gain_grad = moe_pull(moe_in_grad)
    after_grad = inc + after_from_norm
    after_low = after_grad.astype(BF)
    s = jnp.sum(after_low.astype(F32) * mixed, axis=1, keepdims=True)
    r_hi, r_lo = hi_lo(r)
    d_hi, d_lo = hi_lo(s)
    grad_payload = jnp.concatenate(
        [after_low, r_hi, r_lo, d_hi, d_lo, jnp.zeros((rows_t, 124), BF)], axis=1
    )
    (grad_all,), (out_sum,), (grad_blocks,) = run_tasks(
        [
            Gather("dp", grad_payload),
            Reduce("expert", out_part),
            ExpertGrads(moe_all, pre_grad, gh, inc_all, el, FE, nd),
        ],
        5,
        "gather_grad",
    )
    all_sum = lax.psum_scatter(grad_blocks, "dp", scatter_dimension=0, tiled=True)[0]
    up_sum = all_sum[:dr]
    each, span = FE // nd, D // 2
    down_sum = all_sum[dr : dr + each]
    last_sum = all_sum[dr + each :]
    d_proj, normed_part, output_part, d_taps, d_heads, d_lanes = mixer_backward(
        lengths[:, 0], grad_all, w_in, output_weight, *vectors, proj, scan, states, heads
    )
    def rows_of(parts, count):
        flat = jnp.concatenate([part.reshape(-1) for part in parts])
        return jnp.pad(flat, (0, count * 128 - flat.size)).reshape(count, 128)

    added = (d_taps[:K, di:], d_taps[K, di:], moe_gain_grad, router_part)
    own = (
        d_taps[:K, :di],
        d_taps[K, :di],
        d_heads[0, :heads],
        d_heads[1, :heads],
        jnp.sum(d_lanes[1].reshape(heads, PS), axis=1),
        d_lanes[0],
    )
    added_size = sum(part.size for part in added)
    added_rows = -(-added_size // (nd * 1024)) * 8
    own_rows = -(-sum(part.size for part in own) // 128)
    norm_rows = D // 128
    (normed_grad,), (d_sum,), (added_in,) = run_tasks(
        [
            Reduce("dp", normed_part),
            InputGrad(
                normed_all,
                d_proj.reshape(nd * rows_t, wcols),
                output_part.astype(BF),
            ),
            Direct("all", "dp", rows_of(added, nd * added_rows).reshape(nd, added_rows, 128)),
        ],
        6,
        "reduce_grads",
    )
    stream_from_norm, norm_gain_grad = norm_pull(normed_grad)
    tokens_grad = after_grad + stream_from_norm
    small = jnp.concatenate(
        [jnp.sum(added_in, axis=0), rows_of(own, own_rows), rows_of((norm_gain_grad,), norm_rows)],
        axis=0,
    )
    small = jnp.pad(small, ((0, -small.shape[0] % 8), (0, 0)))
    shared_part = jnp.concatenate(
        [up_sum[:, 2 * el * FE :], last_sum[:fsl, span:].reshape(dr, -1)], axis=1
    ).reshape(-1, wcols)
    main_rows = D // ne
    (input_grad,), (rest_all,), (small_all,) = run_tasks(
        [
            InputRows(d_sum[:main_rows], heads),
            Gather("expert", jnp.concatenate([d_sum[main_rows:], shared_part], axis=0)),
            Small(small),
        ],
        7,
        "finish",
    )
    cut_rows = d_sum.shape[0] - main_rows
    output_grad = rest_all[:, :cut_rows].reshape(output_weight.shape)
    shared_all = rest_all[:, cut_rows:].reshape(ne, dr, -1)
    added_all = small_all[:, :added_rows].reshape(-1)
    own_all = small_all[:, added_rows : added_rows + own_rows].reshape(nd, -1)
    norm_gain_grad = jnp.sum(
        small_all[:, added_rows + own_rows : added_rows + own_rows + norm_rows], axis=0
    ).reshape(D)

    def split(flat, parts):
        out, start = [], 0
        for part in parts:
            out.append(flat[..., start : start + part.size].reshape(flat.shape[:-1] + part.shape))
            start += part.size
        return out

    added_taps, added_bias, moe_gain_grad, router_all = split(added_all, added)
    own_taps, own_bias, own_steps, own_decay, own_skip, own_gain = split(own_all, own)
    small = (
        jnp.concatenate([jnp.moveaxis(own_taps, 0, 1).reshape(K, DI), added_taps], axis=1),
        jnp.concatenate([own_bias.reshape(-1), added_bias]),
        own_steps.reshape(-1),
        own_decay.reshape(-1),
        own_skip.reshape(-1),
        norm_gain_grad,
        own_gain.reshape(-1),
        moe_gain_grad,
    )
    router_grad = lax.dynamic_slice_in_dim(router_all, me_d * dr, dr, 0)
    expert_up_grad = jnp.moveaxis(up_sum[:, : 2 * el * FE].reshape(dr, el, 2 * FE), 1, 0)
    expert_up_grad = expert_up_grad.astype(F32)
    expert_down_grad = jnp.stack(
        [
            down_sum[:, : 2 * span],
            jnp.concatenate([down_sum[:, 2 * span :], last_sum[:, :span]], axis=1),
        ],
        axis=0,
    ).astype(F32)
    shared_up_grad = (
        jnp.moveaxis(shared_all[:, :, : 2 * fs].reshape(ne, dr, 2, nd, fsl), 0, 3)
        .reshape(dr, 2 * FS)
        .astype(F32)
    )
    shared_down_grad = shared_all[:, :, 2 * fs :].reshape(fsr, D).astype(F32)
    block_output = (after_mixer + out_sum).astype(BF)
    shape = (MB, 1, loc, D)
    return (
        block_output.reshape(shape),
        tokens_grad.reshape(shape),
        input_grad,
        small[0],
        small[1],
        small[2],
        small[3],
        small[4],
        small[5],
        small[6],
        output_grad.astype(F32),
        small[7],
        router_grad,
        shared_up_grad,
        shared_down_grad,
        expert_up_grad,
        expert_down_grad,
    )


def solution(mesh):
    in_specs = (
        P(None, "expert", "dp", None),
        P(None, "expert", None),
        P(None, "expert", "dp", None),
        P(None, "expert", "dp", None),
        P("dp", None),
        P(),
        P(),
        P(),
        P(),
        P(),
        P(),
        P(),
        P("dp", None),
        P(),
        P("dp", None),
        P("dp", None),
        P("dp", None),
        P("expert", None, None),
        P("expert", None, None),
    )
    out_specs = (
        P(None, "expert", "dp", None),
        P(None, "expert", "dp", None),
        P("dp", None),
        P(),
        P(),
        P(),
        P(),
        P(),
        P(),
        P(),
        P("dp", None),
        P(),
        P("dp", None),
        P("dp", None),
        P("dp", None),
        P("expert", "dp", None),
        P("expert", "dp", None),
    )
    return jax.shard_map(body, mesh=mesh, in_specs=in_specs, out_specs=out_specs, check_vma=False)
```

```python
import functools

import jax
import jax.numpy as jnp
from jax import lax
from jax.experimental import pallas as pl
from jax.experimental.pallas import tpu as pltpu
from jax.sharding import PartitionSpec as P

D = 1536
H = 48
PS = 64
S = 128
K = 4
FE = 512
FS = 1024
TOP = 6
MB = 2
DI = 3072
CONV = 3328
IN_W = 6448
EPSILON = 1e-05
BF = jnp.bfloat16
F32 = jnp.float32
MESH = pl.DeviceIdType.MESH
VMEM_LIMIT = 60 * 1024 * 1024


def mm(a, b):
    return jnp.dot(a, b, preferred_element_type=F32)


def mm_nt(a, b):
    return lax.dot_general(a, b, (((1,), (1,)), ((), ())), preferred_element_type=F32)


def mm_tn(a, b):
    return lax.dot_general(a, b, (((0,), (0,)), ((), ())), preferred_element_type=F32)


def rms_scale(values, gain):
    return values * lax.rsqrt(jnp.mean(values * values, axis=-1, keepdims=True) + EPSILON) * gain


ANY = pl.BlockSpec(memory_space=pl.ANY)
IN_VMEM = pl.BlockSpec(memory_space=pltpu.VMEM)


def places(axis):
    me = lax.axis_index(axis)
    if axis == "dp":
        core, ring, pair = lax.rem(me, 2), lax.rem(me // 2, 4), me // 8

        def at(hop, other, sibling=0):
            z = lax.rem(pair + other, 2)
            return (z * 4 + lax.rem(ring + hop + 4, 4)) * 2 + lax.rem(core + sibling, 2)
    else:
        pair, ring = lax.rem(me, 2), me // 2

        def at(hop, other, sibling=0):
            return lax.rem(ring + hop + 4, 4) * 2 + lax.rem(pair + other, 2)

    return me, at


class Task:
    ins, outs, scratch, reaches, turns = (), (), (), (), 1

    def greet(self, barrier):
        return 0


def peers_of(axis, everyone):
    me, at = places(axis)
    if everyone:
        n = lax.axis_size(axis)
        return [lax.rem(me + k, n) for k in range(1, n)]
    near = [at(1, 0), at(-1, 0), at(0, 1)]
    return near + [at(0, 0, 1)] if axis == "dp" else near


class Links:
    def __init__(self, axis, send, recv):
        self.axis, self.send, self.recv, self.started = axis, send, recv, []

    def push(self, number, src, dst, peer):
        copy = pltpu.make_async_remote_copy(
            src_ref=src,
            dst_ref=dst,
            send_sem=self.send.at[number],
            recv_sem=self.recv.at[number],
            device_id={self.axis: peer},
            device_id_type=MESH,
        )
        copy.start()
        self.started.append(copy)

    def arrived(self, number, dst):
        pltpu.make_async_copy(dst, dst, self.recv.at[number]).wait()

    def finish(self):
        for copy in self.started:
            copy.wait_send()


def halves(shape):
    rows = shape[0]
    cut = rows // 2 if len(shape) == 3 else rows // 32 * 16
    return pl.ds(0, rows), pl.ds(0, cut), pl.ds(cut, rows - cut), cut


class Gather(Task):
    def __init__(self, axis, x):
        self.axis, self.reaches = axis, ((axis, False),)
        self.ins = ((x, ANY),)
        n = lax.axis_size(axis)
        self.outs = ((jax.ShapeDtypeStruct((n,) + x.shape, x.dtype), ANY),)
        dma = pltpu.SemaphoreType.DMA
        self.scratch = (dma((17,)), dma((17,)), dma)

    def steps(self, ins, outs, scratch):
        return gather_steps(self.axis, ins[0], outs[0], *scratch)


def gather_steps(axis, x, out, send, recv, own_sem):
    me, at = places(axis)
    cores = axis == "dp"
    up, down, pair, sib = at(1, 0), at(-1, 0), at(0, 1), at(0, 0, 1)
    whole, first, second, _ = halves(x.shape)
    links = Links(axis, send, recv)

    def push(number, slot, rows, peer, src=None):
        src = out.at[slot] if src is None else src
        links.push(number, src.at[rows], out.at[slot].at[rows], peer)

    def arrived(number, slot, rows):
        links.arrived(number, out.at[slot].at[rows])

    push(0, me, whole, up, x)
    push(1, me, whole, down, x)
    push(2, me, whole, pair, x)
    if cores:
        push(3, me, whole, sib, x)
    own = pltpu.make_async_copy(x, out.at[me], own_sem)
    own.start()
    yield
    own.wait()
    arrived(2, pair, whole)
    push(4, pair, whole, up)
    push(5, pair, whole, down)
    arrived(0, down, whole)
    push(7, down, first, up)
    arrived(1, up, whole)
    push(8, up, second, down)
    if cores:
        push(6, pair, whole, sib)
        push(9, down, whole, sib)
        push(10, up, whole, sib)
    yield
    arrived(4, at(-1, 1), whole)
    push(11, at(-1, 1), first, up)
    arrived(5, at(1, 1), whole)
    push(12, at(1, 1), second, down)
    arrived(7, at(2, 0), first)
    arrived(8, at(2, 0), second)
    if cores:
        push(13, at(-1, 1), whole, sib)
        push(14, at(1, 1), whole, sib)
        push(15, at(2, 0), whole, sib)
    yield
    arrived(11, at(2, 1), first)
    arrived(12, at(2, 1), second)
    if cores:
        push(16, at(2, 1), whole, sib)
        yield
        for number, hop, other in (
            (3, 0, 0),
            (6, 0, 1),
            (9, -1, 0),
            (10, 1, 0),
            (13, -1, 1),
            (14, 1, 1),
            (15, 2, 0),
            (16, 2, 1),
        ):
            arrived(number, at(hop, other, 1), whole)
    links.finish()


ORDER = ((2, 1), (2, 0), (1, 1), (-1, 1), (1, 0), (-1, 0), (0, 1), (0, 0))


class Reduce(Task):
    def __init__(self, axis, x, dtype=F32):
        self.axis, self.reaches = axis, ((axis, False),)
        n, rows, columns = x.shape
        self.ins = ((x, ANY),)
        self.outs = ((jax.ShapeDtypeStruct((rows, columns), dtype), IN_VMEM),)
        _, _, _, cut = halves((rows, columns))
        buf = lambda *dims: pltpu.VMEM(dims + (columns,), BF)
        dma = pltpu.SemaphoreType.DMA
        dp = axis == "dp"
        self.scratch = (
            buf(8, rows),
            buf(8 if dp else 1, rows if dp else 16),
            buf(2, cut),
            buf(2, rows - cut),
            buf(2, rows),
            buf(2, rows),
            buf(rows),
            dma((17,)),
            dma((17,)),
            dma((8,)),
        )

    def steps(self, ins, outs, scratch):
        return reduce_steps(self.axis, ins[0], outs[0], *scratch)


def reduce_steps(axis, x, out, acc, sib_buf, a_buf, b_buf, c_buf, d_buf, e_buf, send, recv, load):
    me, at = places(axis)
    cores = axis == "dp"
    rows = acc.shape[1]
    step = 16
    block = lambda k: x.at[k] if len(x.shape) == 3 else x.at[pl.ds(pl.multiple_of(k * rows, 16), rows)]
    up, down, pair, sib = at(1, 0), at(-1, 0), at(0, 1), at(0, 0, 1)
    whole, first, second, cut = halves(acc.shape[1:])
    links = Links(axis, send, recv)
    push, arrived = links.push, links.arrived

    def add(dst, offset, count, *srcs):
        @pl.loop(0, count // step)
        def _(i):
            at_rows = pl.ds(pl.multiple_of(offset + i * step, step), step)
            total = dst[at_rows, :].astype(F32)
            for src in srcs:
                total += src[pl.ds(pl.multiple_of(i * step, step), step), :].astype(F32)
            dst[at_rows, :] = total.astype(dst.dtype)

    loads = []
    for k, (hop, other) in enumerate(ORDER if x is not None else ()):
        if cores:
            push(k, block(at(hop, other, 1)), sib_buf.at[k], sib)
        copy = pltpu.make_async_copy(block(at(hop, other)), acc.at[k], load.at[k])
        copy.start()
        loads.append(copy)

    def ready(k):
        if loads:
            loads[k].wait()
        if cores:
            arrived(k, sib_buf.at[k])
            add(acc.at[k], 0, rows, sib_buf.at[k])

    yield
    for k in range(2):
        ready(k)
        push(8 + 2 * k, acc.at[k].at[first], a_buf.at[k], up)
        push(9 + 2 * k, acc.at[k].at[second], b_buf.at[k], down)
    yield
    for k in range(2):
        above, below = 2 + 2 * k, 3 + 2 * k
        ready(above)
        ready(below)
        arrived(8 + 2 * k, a_buf.at[k])
        add(acc.at[above], 0, cut, a_buf.at[k])
        push(12 + 2 * k, acc.at[above], c_buf.at[k], up)
        arrived(9 + 2 * k, b_buf.at[k])
        add(acc.at[below], cut, rows - cut, b_buf.at[k])
        push(13 + 2 * k, acc.at[below], d_buf.at[k], down)
    yield
    ready(6)
    ready(7)
    arrived(12, c_buf.at[0])
    arrived(13, d_buf.at[0])
    add(acc.at[6], 0, rows, c_buf.at[0], d_buf.at[0])
    push(16, acc.at[6], e_buf, pair)
    yield
    arrived(14, c_buf.at[1])
    arrived(15, d_buf.at[1])
    yield
    arrived(16, e_buf)

    @pl.loop(0, rows // step)
    def _(i):
        at_rows = pl.ds(pl.multiple_of(i * step, step), step)
        total = acc[7, at_rows, :].astype(F32) + c_buf[1, at_rows, :].astype(F32)
        total += d_buf[1, at_rows, :].astype(F32) + e_buf[at_rows, :].astype(F32)
        out[at_rows, :] = total.astype(out.dtype)

    links.finish()


class Direct(Task):
    def __init__(self, kind, axis, x):
        self.kind, self.axis, self.reaches = kind, axis, ((axis, True),)
        n = lax.axis_size(axis)
        shape = (n,) + x.shape if kind == "gather" else x.shape
        self.ins = ((x, ANY),)
        self.outs = ((jax.ShapeDtypeStruct(shape, x.dtype), ANY),)
        dma = pltpu.SemaphoreType.DMA
        self.scratch = (dma((n,)), dma((n,)), dma)

    def steps(self, ins, outs, scratch):
        return direct_steps(self.kind, self.axis, ins[0], outs[0], *scratch)


def direct_steps(kind, axis, x, out, send, recv, own_sem):
    n, me = lax.axis_size(axis), lax.axis_index(axis)
    links = Links(axis, send, recv)
    piece = lambda k: x if kind == "gather" else x.at[k]
    for k in range(1, n):
        peer = lax.rem(me + k, n)
        links.push(k, piece(peer), out.at[me], peer)
    own = pltpu.make_async_copy(piece(me), out.at[me], own_sem)
    own.start()
    yield
    for k in range(1, n):
        links.arrived(k, out.at[lax.rem(me - k + n, n)])
    own.wait()
    links.finish()


def run_tasks(tasks, number, name):
    operands, in_specs, out_shapes, out_specs, scratch, spans = [], [], [], [], [], []
    for task in tasks:
        spans.append((len(operands), len(out_shapes), len(scratch)))
        operands += [x for x, _ in task.ins]
        in_specs += [spec for _, spec in task.ins]
        out_shapes += [shape for shape, _ in task.outs]
        out_specs += [spec for _, spec in task.outs]
        scratch += list(task.scratch)

    def kernel(*refs):
        ins = refs[: len(operands)]
        outs = refs[len(operands) : len(operands) + len(out_shapes)]
        temps = refs[len(operands) + len(out_shapes) :]
        barrier = pltpu.get_barrier_semaphore()
        count = 0
        for axis in ("dp", "expert"):
            here = [everyone for task in tasks for name, everyone in task.reaches if name == axis]
            if here:
                peers = peers_of(axis, any(here))
                for peer in peers:
                    pl.semaphore_signal(
                        barrier, inc=1, device_id={axis: peer}, device_id_type=MESH
                    )
                count += len(peers)
        for task in tasks:
            count += task.greet(barrier)
        pl.semaphore_wait(barrier, count)
        running = []
        for task, (i, o, s) in zip(tasks, spans):
            steps = task.steps(
                ins[i : i + len(task.ins)],
                outs[o : o + len(task.outs)],
                temps[s : s + len(task.scratch)],
            )
            running.append((task.turns, steps))
        while running:
            left = []
            for turns, steps in running:
                if all(next(steps, "end") != "end" for _ in range(turns)):
                    left.append((turns, steps))
            running = left

    results = pl.pallas_call(
        kernel,
        out_shape=out_shapes,
        in_specs=in_specs,
        out_specs=out_specs,
        scratch_shapes=scratch,
        compiler_params=pltpu.CompilerParams(
            collective_id=number, has_side_effects=True, vmem_limit_bytes=VMEM_LIMIT
        ),
        name=name,
    )(*operands)
    return [results[o : o + len(task.outs)] for task, (_, o, _) in zip(tasks, spans)]


class Weights(Task):
    def __init__(self, x):
        self.reaches = (("dp", True), ("expert", False))
        self.swap, self.spread = Direct("all", "dp", x), Gather("expert", x)
        n = lax.axis_size("expert")
        full = jax.ShapeDtypeStruct((n,) + x.shape, x.dtype)
        self.ins = ((x, ANY),)
        self.outs = self.swap.outs + ((full, ANY),)
        self.scratch = self.swap.scratch + self.spread.scratch

    def steps(self, ins, outs, scratch):
        yield from direct_steps("all", "dp", ins[0], outs[0], *scratch[:3])
        yield
        yield from gather_steps("expert", outs[0], outs[1], *scratch[3:])


class ExpertGrads(Task):
    def __init__(self, x, pre_grad, gh, inc, experts, each, blocks):
        n, rows, _ = x.shape
        width, depth = gh.shape[2], inc.shape[1]
        self.experts, self.each = experts, each
        grads = jax.ShapeDtypeStruct(
            (blocks, depth // blocks + 2 * (each // blocks), 2 * width), BF
        )
        self.ins = tuple((v, ANY) for v in (x, pre_grad, gh, inc))
        self.outs = ((grads, ANY),)
        dma = pltpu.SemaphoreType.DMA
        vmem = lambda *dims: pltpu.VMEM(dims, BF)
        self.scratch = (
            vmem(n, rows, depth),
            vmem(*pre_grad.shape),
            vmem(*gh.shape),
            vmem(*inc.shape),
            dma((5,)),
            vmem(depth, n * rows),
            vmem(width, n * rows),
            vmem(*grads.shape),
        )

    def steps(self, ins, outs, scratch):
        x, pre_grad, gh, inc, sems, x_t, gh_t, grads = scratch
        n, rows, depth = x.shape
        width = gh.shape[2]
        experts, each = self.experts, self.each
        copy = lambda src, dst, k: pltpu.make_async_copy(src, dst, sems.at[k])
        load_x = copy(ins[0].at[:, :, pl.ds(0, depth)], x, 0)
        load_pre = copy(ins[1], pre_grad, 1)
        load_inc = copy(ins[3], inc, 3)
        load_gh = copy(ins[2], gh, 2)
        for load in (load_x, load_pre, load_gh, load_inc):
            load.start()
        yield
        tile = 256
        col = lambda i: pl.ds(pl.multiple_of(i * tile, tile), tile)
        load_x.wait()

        @pl.loop(0, depth // tile)
        def _(i):
            x_t[col(i), :] = x[:, :, col(i)].reshape(n * rows, tile).T

        load_pre.wait()
        blocks = grads.shape[0]
        up_rows = depth // blocks
        steps = 2 * width // tile
        for start, end in ((0, steps // 3), (steps // 3, steps)):

            @pl.loop(start, end)
            def _(i):
                value = mm(x_t[...], pre_grad[:, :, col(i)].reshape(n * rows, tile)).astype(BF)
                grads[:, :up_rows, col(i)] = value.reshape(blocks, up_rows, tile)

            yield
        load_gh.wait()

        @pl.loop(0, width // 128)
        def _(i):
            at_cols = pl.ds(pl.multiple_of(i * 128, 128), 128)
            gh_t[at_cols, :] = gh[:, :, at_cols].reshape(n * rows, 128).T

        load_inc.wait()
        piece_rows = each // blocks
        own = (width - experts * each) // blocks
        span = depth // 2
        spots = (((0, 0), (0, 2)), ((0, 1), (piece_rows, 0)))
        for half in range(2):

            @pl.loop(0, span // tile)
            def _(i):
                value = mm(gh_t[...], inc[:, col(half * span // tile + i)])
                for e in range(experts):
                    row, place = spots[half][e]
                    piece = value[e * each : (e + 1) * each].astype(BF)
                    grads[
                        :,
                        up_rows + row : up_rows + row + piece_rows,
                        col(place * span // tile + i),
                    ] = piece.reshape(blocks, piece_rows, tile)
                piece = value[experts * each :].reshape(blocks, own, tile)
                empty = jnp.zeros((blocks, piece_rows - own, tile), F32)
                piece = jnp.concatenate([piece, empty], axis=1).astype(BF)
                grads[:, up_rows + piece_rows :, col((1 + half) * span // tile + i)] = piece

        store = copy(grads, outs[0], 4)
        store.start()
        yield
        store.wait()


def chunks(rows, step=16):
    def over(work):
        @pl.loop(0, rows // step)
        def _(i):
            work(pl.ds(pl.multiple_of(i * step, step), step))

    return over


def sides(v):
    high = v.astype(BF).astype(F32)
    turn = (iota((128, 128), 0) + 16 == iota((128, 128), 1)).astype(F32)
    return (high + exact(v - high, turn, ((1,), (0,)))).astype(BF)


def joined(v):
    turn = (iota((128, 128), 0) - 16 == iota((128, 128), 1)).astype(F32)
    back = exact(v, turn, ((1,), (0,)))
    return jnp.where(iota((1, 128), 1) < 16, v + back, 0.0)


class MixerOut(Task):
    def __init__(self, payload, stream, gain, router, mask):
        self.reaches = (("dp", False),)
        self.reduce = Reduce("dp", payload)
        rows, wide = payload.shape[1:]
        self.ins = self.reduce.ins + tuple((v, IN_VMEM) for v in (stream, gain, router, mask))
        shape = jax.ShapeDtypeStruct
        self.outs = (
            (shape((rows, wide), BF), IN_VMEM),
            (shape((rows, D), F32), IN_VMEM),
            (shape((rows, D), F32), IN_VMEM),
            (shape((rows, 128), F32), IN_VMEM),
        )
        self.scratch = (pltpu.VMEM((rows, wide), F32),) + self.reduce.scratch

    def steps(self, ins, outs, scratch):
        x, stream, gain, router, mask = ins
        payload, after, mixed, factors = outs
        total = scratch[0]
        yield from reduce_steps("dp", x, total, *scratch[1:])

        @chunks(total.shape[0])
        def _(rows):
            squares = total[rows, D:]
            lane = iota((1, 128), 1)
            square = jnp.sum(jnp.where(lane < 2, squares, 0.0), axis=1, keepdims=True)
            r = lax.rsqrt(square / DI + EPSILON)
            mix = total[rows, :D] * r
            v = stream[rows, :].astype(F32) + mix
            inv = lax.rsqrt(jnp.mean(v * v, axis=1, keepdims=True) + EPSILON)
            low = (v * inv * gain[...]).astype(BF)
            logits = mm(low, router[...])
            chosen = mask[rows, :]
            top = jnp.max(jnp.where(chosen > 0.0, logits, -1e30), axis=1, keepdims=True)
            e = jnp.where(chosen > 0.0, jnp.exp(jnp.minimum(logits - top, 0.0)), 0.0)
            table = e / jnp.sum(e, axis=1, keepdims=True)
            payload[rows, :D] = low
            payload[rows, D:] = sides(table)
            after[rows, :] = v
            mixed[rows, :] = mix
            factors[rows, :] = jnp.where(lane == 0, r, jnp.where(lane == 1, inv, 0.0))


class StreamGrad(Task):
    def __init__(self, parts, stream, gain, after_grad):
        self.reaches = (("dp", False),)
        self.reduce = Reduce("dp", parts)
        self.ins = self.reduce.ins + tuple((v, IN_VMEM) for v in (stream, gain, after_grad))
        shape = jax.ShapeDtypeStruct
        self.outs = ((shape(stream.shape, F32), IN_VMEM), (shape((1, D), F32), IN_VMEM))
        self.scratch = (pltpu.VMEM(stream.shape, F32),) + self.reduce.scratch

    def steps(self, ins, outs, scratch):
        x, stream, gain, after_grad = ins
        out, gain_grad = outs
        total = scratch[0]
        yield from reduce_steps("dp", x, total, *scratch[1:])
        gain_grad[...] = jnp.zeros_like(gain_grad)

        @chunks(total.shape[0])
        def _(rows):
            v = stream[rows, :].astype(F32)
            inv = lax.rsqrt(jnp.mean(v * v, axis=1, keepdims=True) + EPSILON)
            g = total[rows, :]
            gg = g * gain[...]
            gain_grad[...] += jnp.sum(g * v * inv, axis=0, keepdims=True)
            mean = jnp.mean(gg * v, axis=1, keepdims=True)
            out[rows, :] = after_grad[rows, :] + inv * gg - v * (inv * inv * inv * mean)


class InputGrad(Task):
    def __init__(self, g, d_proj, out_grad):
        self.reaches = (("expert", False),)
        n = lax.axis_size("expert")
        wide = d_proj.shape[1]
        rows = (D + out_grad.size // wide) // n
        self.reduce = Reduce("expert", jax.ShapeDtypeStruct((n, rows, wide), BF), BF)
        self.ins = tuple((v, ANY) for v in (g, d_proj, out_grad.reshape(n, -1, wide)))
        self.outs = self.reduce.outs
        dma = pltpu.SemaphoreType.DMA
        self.scratch = (
            pltpu.VMEM(g.shape[:2] + (D,), BF),
            pltpu.VMEM(d_proj.shape, BF),
            pltpu.VMEM((n, rows, wide), BF),
            dma((3,)),
        ) + self.reduce.scratch

    def steps(self, ins, outs, scratch):
        g, d_proj, total, sems = scratch[:4]
        n, _, wide = total.shape
        each = D // n
        below = pl.ds(each, total.shape[1] - each)
        loads = (
            pltpu.make_async_copy(ins[0].at[:, :, pl.ds(0, D)], g, sems.at[0]),
            pltpu.make_async_copy(ins[1], d_proj, sems.at[1]),
            pltpu.make_async_copy(ins[2], total.at[:, below], sems.at[2]),
        )
        for load in loads:
            load.start()
        yield
        for load in loads:
            load.wait()
        flat = g.shape[0] * g.shape[1]

        @pl.loop(0, n // 2)
        def _(i):
            columns = pl.ds(pl.multiple_of(i * 2 * each, 2 * each), 2 * each)
            value = mm_tn(g[:, :, columns].reshape(flat, 2 * each), d_proj[...]).astype(BF)
            total[pl.ds(2 * i, 2), :each, :] = value.reshape(2, each, wide)

        yield from reduce_steps("expert", total, outs[0], *scratch[4:])


class InputRows(Task):
    def __init__(self, x, heads):
        nd, ne = lax.axis_size("dp"), lax.axis_size("expert")
        self.heads = heads
        self.slices = D // nd // 16
        self.reaches = (("expert", False),)
        wide = 2 * DI + 2 * S + 128
        row = jax.ShapeDtypeStruct((16, wide), BF)
        self.gather = Gather("expert", row)
        self.ins = ((x, ANY),)
        self.outs = ((jax.ShapeDtypeStruct((D // nd, IN_W), F32), IN_VMEM),)
        dma = pltpu.SemaphoreType.DMA
        self.scratch = (
            pltpu.VMEM((nd, 16, x.shape[1]), BF),
            pltpu.VMEM((16, wide), BF),
            pltpu.VMEM((ne, 16, wide), BF),
            dma((2 * ne,)),
            dma((nd,)),
        ) + self.gather.scratch

    def greet(self, barrier):
        nd = lax.axis_size("dp")
        j = lax.axis_index("dp")
        for source in range(nd):
            pl.semaphore_signal(
                barrier, inc=1, device_id={"dp": source, "expert": j // 2}, device_id_type=MESH
            )
        return 2 * lax.axis_size("expert")

    def steps(self, ins, outs, scratch):
        x = ins[0]
        got, row, full, send, recv = scratch[:5]
        nd, ne = lax.axis_size("dp"), lax.axis_size("expert")
        j, e = lax.axis_index("dp"), lax.axis_index("expert")
        heads, di = self.heads, self.heads * PS
        sent = []
        for k in range(2):
            for c in range(ne):
                src = x.at[pl.ds((k * self.slices + min(c, self.slices - 1)) * 16, 16)]
                mine = (j == 2 * e + k) & (e == c)
                away = pltpu.make_async_remote_copy(
                    src_ref=src,
                    dst_ref=got.at[j],
                    send_sem=send.at[k * ne + c],
                    recv_sem=recv.at[j],
                    device_id={"dp": 2 * e + k, "expert": c},
                    device_id_type=MESH,
                )
                here = pltpu.make_async_copy(src, got.at[j], recv.at[j])
                pl.when(mine)(here.start)
                pl.when(jnp.logical_not(mine))(away.start)
                sent.append((mine, away))
        yield
        for source in range(nd):
            pltpu.make_async_copy(got.at[source], got.at[source], recv.at[source]).wait()
        piece = lambda source, start, size: got[source, :, start : start + size].astype(F32)
        for source in range(0, nd, 2):
            for half in range(2):
                pair = [piece(source + k, half * di, di) for k in range(2)]
                start = half * DI + source * di
                row[:, start : start + 2 * di] = jnp.concatenate(pair, axis=1).astype(BF)
        total = piece(0, 2 * di, 2 * S)
        for source in range(1, nd):
            total = total + piece(source, 2 * di, 2 * S)
        row[:, 2 * DI : 2 * DI + 2 * S] = total.astype(BF)
        steps = [piece(source, 2 * di + 2 * S, 128)[:, :heads] for source in range(nd)]
        steps.append(jnp.zeros((16, 128 - nd * heads), F32))
        row[:, 2 * DI + 2 * S :] = jnp.concatenate(steps, axis=1).astype(BF)
        yield from gather_steps("expert", row, full, *scratch[5:])
        for c in range(self.slices):
            outs[0][c * 16 : (c + 1) * 16, :] = full[c, :, :IN_W].astype(F32)
        for mine, away in sent:
            pl.when(jnp.logical_not(mine))(away.wait_send)


class Small(Task):
    def __init__(self, x):
        self.reaches = (("expert", True), ("dp", True))
        nd, ne = lax.axis_size("dp"), lax.axis_size("expert")
        self.ins = ((x, ANY),)
        self.outs = ((jax.ShapeDtypeStruct((nd,) + x.shape, x.dtype), ANY),)
        dma = pltpu.SemaphoreType.DMA
        self.scratch = (
            pltpu.VMEM((ne,) + x.shape, x.dtype),
            pltpu.VMEM(x.shape, x.dtype),
            dma((ne,)),
            dma((ne,)),
            dma,
            dma((nd,)),
            dma((nd,)),
            dma,
        )

    def steps(self, ins, outs, scratch):
        parts, total = scratch[:2]
        yield from direct_steps("gather", "expert", ins[0], parts, *scratch[2:5])
        total[...] = jnp.sum(parts[...], axis=0)
        yield from direct_steps("gather", "dp", total, outs[0], *scratch[5:8])


class Experts(Task):
    def __init__(self, x, inc, w_up, w_down, s_up, s_down, after, mixed, factors, gain, router, own):
        self.reaches = (("expert", False),)
        self.gather = Gather("expert", x)
        n = lax.axis_size("expert")
        rows, wide = x.shape
        depth = inc.shape[1]
        experts, _, both = w_up.shape
        self.experts = experts
        all_rows = jax.ShapeDtypeStruct((n, rows, wide), BF)
        self.reduce = Reduce("expert", all_rows)
        hidden = experts * both // 2 + s_down.shape[0]
        pre = jax.ShapeDtypeStruct((n, rows, 2 * hidden), BF)
        gh = jax.ShapeDtypeStruct((n, rows, hidden), BF)
        self.ins = tuple((v, ANY) for v in (x, inc, w_up, w_down, s_up, s_down)) + tuple(
            (v, IN_VMEM) for v in (after, mixed, factors, gain, router, own)
        )
        part = jax.ShapeDtypeStruct((n, rows, depth), BF)
        shape = jax.ShapeDtypeStruct
        self.outs = (
            ((all_rows, IN_VMEM),)
            + tuple((v, ANY) for v in (pre, gh, part))
            + (
                (shape((rows, depth), F32), IN_VMEM),
                (shape((rows, wide), BF), IN_VMEM),
                (shape((1, depth), F32), IN_VMEM),
                (shape((16, depth), F32), IN_VMEM),
            )
        )
        dma = pltpu.SemaphoreType.DMA
        self.scratch = (
            (pltpu.VMEM((n, rows, depth), BF),)
            + tuple(pltpu.VMEM(v.shape, BF) for v in (w_up, w_down, s_up, s_down))
            + (pltpu.VMEM((2 * rows, wide), BF), pltpu.VMEM((2 * rows, depth), BF))
            + (pltpu.VMEM((2 * rows, 2 * hidden), BF), pltpu.VMEM((2 * rows, hidden), BF))
            + (pltpu.VMEM(pre.shape, BF), pltpu.VMEM(gh.shape, BF))
            + (pltpu.VMEM((2 * rows, 128), F32), dma((22,)), pltpu.VMEM(part.shape, BF))
            + (pltpu.VMEM((rows, wide), F32),)
            + self.gather.scratch
            + self.reduce.scratch
        )

    def steps(self, ins, outs, scratch):
        x, inc_in = ins[:2]
        after, mixed, factors, gain, router, own = ins[6:]
        x_all, pre_out, gh_out, part_out, after_grad, payload, gain_grad, router_grad = outs
        inc, w_up, w_down, s_up, s_down, xs, incs, pg, ghs, pre, gh, extra, sems = scratch[:13]
        part, dx, gather_scratch, reduce_scratch = scratch[13], scratch[14], scratch[15:18], scratch[18:]
        acc = reduce_scratch[0]
        me, at = places("expert")
        n, rows, depth = inc.shape
        experts, _, both = w_up.shape
        each = both // 2
        shared = s_down.shape[0]
        tile = min(256, each)
        loads = [
            pltpu.make_async_copy(src, dst, sems.at[k])
            for k, (src, dst) in enumerate(zip(ins[2:6], (w_up, w_down, s_up, s_down)))
        ]
        loads += [
            pltpu.make_async_copy(inc_in.at[pl.ds(k * rows, rows)], inc.at[k], sems.at[13 + k])
            for k in range(n)
        ]
        arriving = gather_steps("expert", x, x_all, *gather_scratch)
        next(arriving)
        for load in loads:
            load.start()
        next(arriving)
        for load in loads:
            load.wait()
        lane = lax.broadcasted_iota(jnp.int32, (1, 128), 1)
        stores = []

        def unit(a, b, u, scale):
            sig = jax.nn.sigmoid(a)
            act = a * sig
            hidden = act * b
            gu = u * scale
            da = gu * b * (sig + act * (1.0 - sig))
            return hidden * scale, da, gu * act, u * hidden

        def compute(hop, places_in_acc):
            slots = (at(hop, 0), at(hop, 1))
            for k, slot in enumerate(slots):
                part = pl.ds(k * rows, rows)
                xs[part, :] = x_all[slot]
                incs[part, :] = inc[slot]
            extra[...] = jnp.zeros_like(extra)

            @pl.loop(0, experts * (each // tile))
            def _(i):
                e, f = i // (each // tile), lax.rem(i, each // tile)
                place = me * experts + e
                table = xs[:, depth:].astype(F32)
                chosen = (lane == place) | (lane == place + n * experts)
                scale = jnp.sum(jnp.where(chosen, table, 0.0), axis=1, keepdims=True)
                left = pl.ds(pl.multiple_of(f * tile, tile), tile)
                right = pl.ds(pl.multiple_of(each + f * tile, tile), tile)
                a = mm(xs[:, :depth], w_up[e, :, left])
                b = mm(xs[:, :depth], w_up[e, :, right])
                u = mm_nt(incs[...], w_down[e, left, :])
                h, da, db, dots = unit(a, b, u, scale)
                ghs[:, pl.ds(pl.multiple_of(e * each + f * tile, tile), tile)] = h.astype(BF)
                pg[:, pl.ds(pl.multiple_of(e * both + f * tile, tile), tile)] = da.astype(BF)
                pg[:, pl.ds(pl.multiple_of(e * both + each + f * tile, tile), tile)] = db.astype(BF)
                extra[...] += jnp.where(lane == place, jnp.sum(dots, axis=1, keepdims=True), 0.0)

            a = mm(xs[:, :depth], s_up[:, :shared])
            b = mm(xs[:, :depth], s_up[:, shared:])
            u = mm_nt(incs[...], s_down[...])
            h, da, db, _ = unit(a, b, u, 1.0)
            ghs[:, experts * each :] = h.astype(BF)
            pg[:, experts * both : experts * both + shared] = da.astype(BF)
            pg[:, experts * both + shared :] = db.astype(BF)

            @pl.loop(0, depth // tile)
            def _(i):
                columns = pl.ds(pl.multiple_of(i * tile, tile), tile)
                total = mm_nt(pg[:, experts * both :], s_up[columns, :])
                for e in range(experts):
                    total += mm_nt(pg[:, e * both : (e + 1) * both], w_up[e, columns, :])
                for k, place in enumerate(places_in_acc):
                    acc[place, :, columns] = total[k * rows : (k + 1) * rows].astype(BF)

            grads = extra[...]
            both_parts = sides(grads)
            for k, (slot, place) in enumerate(zip(slots, places_in_acc)):
                part = pl.ds(k * rows, rows)
                acc[place, :, depth:] = both_parts[k * rows : (k + 1) * rows]
                pre[slot] = pg[part, :]
                gh[slot] = ghs[part, :]
                store = pltpu.make_async_copy(pre.at[slot], pre_out.at[slot], sems.at[4 + len(stores)])
                store.start()
                stores.append(store)

        compute(0, (7, 6))
        next(arriving)
        compute(1, (4, 2))
        compute(-1, (5, 3))
        for _ in arriving:
            pass
        compute(2, (1, 0))
        store = pltpu.make_async_copy(gh, gh_out, sems.at[12])
        store.start()
        stores.append(store)
        summing = reduce_steps("expert", None, dx, *reduce_scratch)
        next(summing)
        for half in range(2):
            next(summing)

            @pl.loop(half * depth // tile // 2, (half + 1) * depth // tile // 2)
            def _(i):
                columns = pl.ds(pl.multiple_of(i * tile, tile), tile)
                hid = lambda start, size: gh[:, :, start : start + size].reshape(n * rows, size)
                total = mm(hid(experts * each, shared), s_down[:, columns])
                for e in range(experts):
                    total += mm(hid(e * each, each), w_down[e, :, columns])
                part[:, :, columns] = total.astype(BF).reshape(n, rows, tile)

        store = pltpu.make_async_copy(part, part_out, sems.at[21])
        store.start()
        stores.append(store)
        yield from summing
        gain_grad[...] = jnp.zeros_like(gain_grad)
        router_grad[...] = jnp.zeros_like(router_grad)

        @chunks(rows)
        def _(at_rows):
            v, inv = after[at_rows, :], factors[at_rows, 1:2]
            low = x_all[me, at_rows, :depth]
            table = joined(x_all[me, at_rows, depth:].astype(F32))
            spread = joined(dx[at_rows, depth:])
            logit = table * (spread - jnp.sum(table * spread, axis=1, keepdims=True))
            logit_low = logit.astype(BF)
            router_grad[...] += mm_tn(logit_low, low)[:16]
            g = dx[at_rows, :depth] + mm_nt(logit_low, router[...])
            gg = g * gain[...]
            gain_grad[...] += jnp.sum(g * v * inv, axis=0, keepdims=True)
            mean = jnp.mean(gg * v, axis=1, keepdims=True)
            total = own[at_rows, :].astype(F32) + inv * gg - v * (inv * inv * inv * mean)
            after_grad[at_rows, :] = total
            total_low = total.astype(BF)
            payload[at_rows, :depth] = total_low
            s = jnp.sum(total_low.astype(F32) * mixed[at_rows, :], axis=1, keepdims=True)
            r = factors[at_rows, 0:1]
            r_high, s_high = r.astype(BF).astype(F32), s.astype(BF).astype(F32)
            extras = jnp.where(lane == 0, r_high, jnp.where(lane == 1, r - r_high, 0.0))
            extras = jnp.where(lane == 2, s_high, jnp.where(lane == 3, s - s_high, extras))
            payload[at_rows, depth:] = extras.astype(BF)

        for store in stores:
            store.wait()


EDGE = 8


def pieces(v, count):
    out = []
    for _ in range(count):
        out.append(v.astype(BF))
        v = v - out[-1].astype(F32)
    return out


def exact(v, ones, dims, count=2):
    ones = ones.astype(BF)
    parts = [
        lax.dot_general(p, ones, (dims, ((), ())), preferred_element_type=F32)
        for p in pieces(v, count)
    ]
    return sum(parts[1:], parts[0])


def exact_right(ones, v, dims, count=2):
    ones = ones.astype(BF)
    parts = [
        lax.dot_general(ones, p, (dims, ((), ())), preferred_element_type=F32)
        for p in pieces(v, count)
    ]
    return sum(parts[1:], parts[0])


def iota(shape, axis):
    return lax.broadcasted_iota(jnp.int32, shape, axis)


class Block:
    def __init__(self, m, start, proj, ext, lengths, taps, heads_vec, heads):
        loc = proj.shape[0]
        di = heads * PS
        width = di + 2 * S
        self.heads, self.di = heads, di
        first = lengths[m, 0]
        second = first + lengths[m, 1]

        def doc(p):
            return (p >= first).astype(jnp.int32) + (p >= second).astype(jnp.int32)

        self.doc = doc
        self.at = start + iota((loc, 1), 0)
        docs = doc(self.at)
        docs_row = doc(start + iota((1, loc), 1))
        last_doc, before_doc = doc(start + loc - 1), doc(start - 1)
        self.keep = (docs == before_doc).astype(F32)
        self.keep_last = (last_doc == before_doc).astype(F32)
        self.same_last = (docs == last_doc).astype(F32)
        self.gate = proj[:, :di]
        ext[m, EDGE : EDGE + loc, :] = proj[:, di : di + width].astype(BF).astype(F32)
        total = jnp.broadcast_to(taps[K : K + 1, :], (loc, width))
        self.shifted = []
        for k in range(K):
            back = K - 1 - k
            value = ext[m, EDGE - back : EDGE - back + loc, :]
            if back:
                value = value * (docs == doc(self.at - back)).astype(F32)
            self.shifted.append(value)
            total = total + taps[k : k + 1, :] * value
        self.sig = jax.nn.sigmoid(total)
        self.total = total
        filtered = total * self.sig
        self.x = filtered[:, :di]
        self.write = filtered[:, di : di + S].astype(BF)
        self.read = filtered[:, di + S :].astype(BF)
        self.raw = proj[:, di + width :] + heads_vec[0:1, :]
        self.steps = jnp.maximum(self.raw, 0.0) + jnp.log1p(jnp.exp(-jnp.abs(self.raw)))
        self.rate = heads_vec[1:2, :]
        rise = self.steps * self.rate
        rows, cols = iota((loc, loc), 0), iota((loc, loc), 1)
        self.lower = (cols <= rows).astype(F32)
        self.cum = exact_right(self.lower, rise, ((1,), (0,)), 3)
        cum_rows = exact(rise, (rows <= cols).astype(F32), ((0,), (0,)), 3)
        self.last = self.cum[loc - 1 : loc, :]
        self.grow = jnp.exp(self.cum) * self.keep
        self.fall = jnp.exp(self.last - self.cum) * self.same_last
        self.decay = jnp.exp(self.last) * self.keep_last
        allowed = (cols <= rows) & (docs == docs_row)
        scores = mm_nt(self.read, self.write)
        self.spread, self.mixing = [], []
        for h in range(heads):
            span = self.cum[:, h : h + 1] - cum_rows[h : h + 1, :]
            shape = jnp.exp(jnp.where(allowed, span, -1e30))
            self.spread.append(shape)
            self.mixing.append(shape * scores)
        self.lane = iota((1, di), 1)
        self.steps_wide = self.widen(self.steps)
        self.grow_wide = self.widen(self.grow)
        self.weight_wide = self.widen(self.fall * self.steps)
        self.scaled = self.x * self.steps_wide
        self.pushed = self.x * self.weight_wide

    def widen(self, v):
        out = jnp.broadcast_to(v[:, 0:1], (v.shape[0], self.di))
        for h in range(1, self.heads):
            out = jnp.where(self.lane >= h * PS, v[:, h : h + 1], out)
        return out

    def per_head(self, parts):
        out = parts[0]
        for h in range(1, self.heads):
            out = jnp.where(self.lane >= h * PS, parts[h], out)
        return out

    def decay_rows(self):
        rows = iota((self.di, 1), 0)
        out = jnp.broadcast_to(self.decay[:, 0:1], (self.di, 1))
        for h in range(1, self.heads):
            out = jnp.where(rows >= h * PS, self.decay[:, h : h + 1], out)
        return out


def load_weights(pieces_ref, w, sem):
    copies = [
        pltpu.make_async_copy(pieces_ref.at[k], w.at[:, k], sem.at[k]) for k in range(w.shape[1])
    ]
    for copy in copies:
        copy.start()
    for copy in copies:
        copy.wait()


def forward_kernel(
    heads,
    lengths,
    g,
    w_pieces,
    w_out,
    taps,
    heads_vec,
    lanes_vec,
    payload,
    proj,
    scan,
    states,
    ext,
    state,
    w,
    w_sem,
):
    b = pl.program_id(0)
    loc = g.shape[1] // MB
    di = heads * PS

    @pl.when(b == 0)
    def _():
        ext[...] = jnp.zeros_like(ext)
        state[...] = jnp.zeros_like(state)
        load_weights(w_pieces, w, w_sem)

    proj[0] = mm(g[0, :, :D], w[...].reshape(D, -1))
    column = iota((loc, payload.shape[2] - D), 1)
    for m in range(MB):
        rows = slice(m * loc, (m + 1) * loc)
        ext[m, 0:EDGE, :] = ext[m, loc : loc + EDGE, :]
        part = Block(m, b * loc, proj[0, rows, :], ext, lengths, taps, heads_vec, heads)
        before = state[m]
        states[0, m] = before
        scaled = part.scaled.astype(BF)
        inner = part.per_head([mm(part.mixing[h].astype(BF), scaled) for h in range(heads)])
        carried = mm_nt(part.read, before.astype(BF)) * part.grow_wide
        out = inner + carried + lanes_vec[1:2, :] * part.x
        scan[0, rows, :] = out
        state[m] = part.decay_rows() * before + mm_tn(part.pushed.astype(BF), part.write)
        y = out * (part.gate * jax.nn.sigmoid(part.gate))
        square = jnp.sum(y * y, axis=1, keepdims=True)
        high = square.astype(BF).astype(F32)
        payload[0, rows, :D] = mm((y * lanes_vec[0:1, :]).astype(BF), w_out[...]).astype(BF)
        sums = jnp.where(column == 0, high, jnp.where(column == 1, square - high, 0.0))
        payload[0, rows, D:] = sums.astype(BF)


def backward_kernel(
    heads,
    lengths,
    grad,
    w_pieces,
    w_out,
    taps,
    heads_vec,
    lanes_vec,
    proj,
    proj_before,
    scan,
    states,
    d_proj,
    normed_part,
    d_out,
    d_taps,
    d_heads,
    d_lanes,
    ext,
    d_ext,
    d_state,
    out_sum,
    w,
    w_sem,
):
    step = pl.program_id(0)
    b = pl.num_programs(0) - 1 - step
    loc = grad.shape[1] // MB
    di = heads * PS
    width = di + 2 * S

    @pl.when(step == 0)
    def _():
        for ref in (d_ext, d_state, out_sum, d_taps, d_heads, d_lanes):
            ref[...] = jnp.zeros_like(ref)
        load_weights(w_pieces, w, w_sem)

    gated_grad = mm_nt(grad[0, :, :D], w_out[...])
    extra = grad[0, :, D:].astype(F32)
    has_before = (b > 0).astype(F32)
    pick = (iota((di, S), 0) // PS == iota((di, S), 1)).astype(F32)
    for m in range(MB):
        rows = slice(m * loc, (m + 1) * loc)
        edge = proj_before[0, (m + 1) * loc - EDGE : (m + 1) * loc, di : di + width]
        ext[m, 0:EDGE, :] = edge.astype(BF).astype(F32) * has_before
        part = Block(m, b * loc, proj[0, rows, :], ext, lengths, taps, heads_vec, heads)
        gain, skip = lanes_vec[0:1, :], lanes_vec[1:2, :]
        r = extra[rows, 0:1] + extra[rows, 1:2]
        s = extra[rows, 2:3] + extra[rows, 3:4]
        out = scan[0, rows, :]
        sig = jax.nn.sigmoid(part.gate)
        act = part.gate * sig
        yr = out * act * r
        gg = gated_grad[rows]
        d_lanes[0:1, :] += jnp.sum(gg * yr, axis=0, keepdims=True)
        out_sum[...] += mm_tn((yr * gain).astype(BF), grad[0, rows, :D])
        dy = r * (gg * gain) - yr * (r * s / DI)
        d_gate = dy * out * (sig + act * (1.0 - sig))
        do = dy * act
        do_low = do.astype(BF)
        x = part.x
        d_lanes[1:2, :] += jnp.sum(do * x, axis=0, keepdims=True)
        dx = skip * do
        before = states[0, m]
        before_low = before.astype(BF)
        ds = d_state[m]
        ds_low = ds.astype(BF)

        d_scores = jnp.zeros((loc, loc), F32)
        d_scaled, d_cum = [], jnp.zeros((loc, S), F32)
        head_lane = iota((loc, S), 1)
        for h in range(heads):
            inside = (part.lane >= h * PS) & (part.lane < (h + 1) * PS)
            own = jnp.where(inside, part.scaled, 0.0).astype(BF)
            d_mix = mm_nt(do_low, own)
            d_scaled.append(mm_tn(part.mixing[h].astype(BF), do_low))
            d_scores = d_scores + d_mix * part.spread[h]
            d_span = d_mix * part.mixing[h]
            ones = (head_lane == h).astype(F32)
            d_cum = d_cum + exact(d_span, ones, ((1,), (0,))) - exact(d_span, ones, ((0,), (0,)))
        d_scaled = part.per_head(d_scaled)
        dx = dx + d_scaled * part.steps_wide
        d_scores_low = d_scores.astype(BF)
        d_read = mm(d_scores_low, part.write)
        d_write = mm_tn(d_scores_low, part.read)

        d_carry = do * part.grow_wide
        d_carry_low = d_carry.astype(BF)
        carried = mm_nt(part.read, before_low)
        d_read = d_read + mm(d_carry_low, before_low)

        d_pushed = mm_nt(part.write, ds_low)
        d_write = d_write + mm(part.pushed.astype(BF), ds_low)
        dx = dx + d_pushed * part.weight_wide
        sums = exact(
            jnp.concatenate([d_carry * carried, d_pushed * x, d_scaled * x], axis=0),
            pick,
            ((1,), (0,)),
        )
        d_weight = sums[loc : 2 * loc]
        d_fall = d_weight * part.fall * part.steps
        d_cum = d_cum + sums[:loc] - d_fall
        d_steps = sums[2 * loc :] + d_weight * part.fall
        state_dot = jnp.sum(ds * before, axis=1, keepdims=True)
        d_decay = exact(jnp.broadcast_to(state_dot, (di, S)), pick, ((0,), (0,)))[0:1, :]
        d_last = jnp.sum(d_fall, axis=0, keepdims=True) + d_decay * part.decay
        d_cum = d_cum + jnp.where(iota((loc, 1), 0) == loc - 1, d_last, 0.0)
        d_state[m] = part.decay_rows() * ds + mm_tn(d_carry_low, part.read)

        d_rise = exact_right(part.lower, d_cum, ((0,), (0,)))
        d_steps = d_steps + d_rise * part.rate
        d_raw = d_steps * jax.nn.sigmoid(part.raw)
        d_heads[0:1, :] += jnp.sum(d_raw, axis=0, keepdims=True)
        d_heads[1:2, :] += jnp.sum(d_rise * part.steps * part.rate, axis=0, keepdims=True)

        d_total = jnp.concatenate([dx, d_write, d_read], axis=1)
        d_total = d_total * (part.sig + part.total * part.sig * (1.0 - part.sig))
        for k in range(K):
            d_taps[k : k + 1, :] += jnp.sum(d_total * part.shifted[k], axis=0, keepdims=True)
        d_taps[K : K + 1, :] += jnp.sum(d_total, axis=0, keepdims=True)
        d_ext[m, loc : loc + EDGE, :] = d_ext[m, 0:EDGE, :]
        d_ext[m, 0:loc, :] = d_total
        d_seq = taps[K - 1 : K, :] * d_total
        docs = part.doc(part.at)
        for ahead in range(1, K):
            same = (docs == part.doc(part.at + ahead)).astype(F32)
            d_seq = d_seq + taps[K - 1 - ahead : K - ahead, :] * (
                same * d_ext[m, ahead : ahead + loc, :]
            )
        d_proj[0, rows, :di] = d_gate.astype(BF)
        d_proj[0, rows, di : di + width] = d_seq.astype(BF)
        d_proj[0, rows, di + width :] = jnp.where(head_lane < heads, d_raw, 0.0).astype(BF)
    for half in range(2):
        d_out[half] = out_sum[:, half * D // 2 : (half + 1) * D // 2].astype(BF)
    normed_part[0] = mm_nt(d_proj[0], w[...].reshape(D, -1)).astype(BF)


def weight_scratch(w):
    slices = D // w.shape[1] // w.shape[2]
    return [
        pltpu.VMEM((w.shape[1], slices) + w.shape[2:], BF),
        pltpu.SemaphoreType.DMA((slices,)),
    ]


def block_spec(shape, index):
    return pl.BlockSpec((1,) + shape[1:], lambda i: (index(i),) + (0,) * (len(shape) - 1))


def whole_spec(shape):
    return pl.BlockSpec(shape, lambda i: (0,) * len(shape))


def mixer_forward(lengths, g, w, w_out, taps, heads_vec, lanes_vec, heads):
    nb, rows, _ = g.shape
    di = heads * PS
    width = di + 2 * S
    shapes = [
        jax.ShapeDtypeStruct((nb, rows, D + 128), BF),
        jax.ShapeDtypeStruct((nb, rows, w.shape[-1]), F32),
        jax.ShapeDtypeStruct((nb, rows, di), F32),
        jax.ShapeDtypeStruct((nb, MB, di, S), F32),
    ]
    same = lambda i: i
    return pl.pallas_call(
        functools.partial(forward_kernel, heads),
        grid=(nb,),
        out_shape=shapes,
        in_specs=[pl.BlockSpec(memory_space=pltpu.SMEM), block_spec(g.shape, same)]
        + [pl.BlockSpec(memory_space=pl.ANY)]
        + [whole_spec(v.shape) for v in (w_out, taps, heads_vec, lanes_vec)],
        out_specs=[block_spec(v.shape, same) for v in shapes],
        scratch_shapes=[
            pltpu.VMEM((MB, rows // MB + EDGE, width), F32),
            pltpu.VMEM((MB, di, S), F32),
        ]
        + weight_scratch(w),
        compiler_params=pltpu.CompilerParams(vmem_limit_bytes=VMEM_LIMIT),
        name="mixer_forward",
    )(lengths, g, w, w_out, taps, heads_vec, lanes_vec)


def mixer_backward(lengths, grad, w, w_out, taps, heads_vec, lanes_vec, proj, scan, states, heads):
    nb, rows, _ = grad.shape
    di = heads * PS
    width = di + 2 * S
    back = lambda i: nb - 1 - i
    before = lambda i: jnp.maximum(nb - 2 - i, 0)
    per_block = [
        jax.ShapeDtypeStruct((nb, rows, w.shape[-1]), BF),
        jax.ShapeDtypeStruct((nb, rows, D), BF),
    ]
    sums = [
        jax.ShapeDtypeStruct((2, di, D // 2), BF),
        jax.ShapeDtypeStruct((8, width), F32),
        jax.ShapeDtypeStruct((8, S), F32),
        jax.ShapeDtypeStruct((8, di), F32),
    ]
    return pl.pallas_call(
        functools.partial(backward_kernel, heads),
        grid=(nb,),
        out_shape=per_block + sums,
        in_specs=[pl.BlockSpec(memory_space=pltpu.SMEM), block_spec(grad.shape, back)]
        + [pl.BlockSpec(memory_space=pl.ANY)]
        + [whole_spec(v.shape) for v in (w_out, taps, heads_vec, lanes_vec)]
        + [block_spec(proj.shape, back), block_spec(proj.shape, before)]
        + [block_spec(scan.shape, back), block_spec(states.shape, back)],
        out_specs=[block_spec(v.shape, back) for v in per_block]
        + [whole_spec(v.shape) for v in sums],
        scratch_shapes=[
            pltpu.VMEM((MB, rows // MB + EDGE, width), F32),
            pltpu.VMEM((MB, rows // MB + EDGE, width), F32),
            pltpu.VMEM((MB, di, S), F32),
            pltpu.VMEM((di, D), F32),
        ]
        + weight_scratch(w),
        compiler_params=pltpu.CompilerParams(vmem_limit_bytes=VMEM_LIMIT),
        name="mixer_backward",
    )(lengths, grad, w, w_out, taps, heads_vec, lanes_vec, proj, proj, scan, states)


def body(
    tokens,
    lengths,
    routes,
    cotangent,
    input_weight,
    filter_weight,
    filter_bias,
    step_bias,
    decay_log,
    skip_gain,
    norm_gain,
    gated_gain,
    output_weight,
    moe_gain,
    router_weight,
    shared_gate_up,
    shared_down,
    expert_gate_up,
    expert_down,
):
    nd, ne = lax.axis_size("dp"), lax.axis_size("expert")
    me_d, me_e = lax.axis_index("dp"), lax.axis_index("expert")
    loc = tokens.shape[2]
    heads = H // nd
    di = heads * PS
    rows_t = MB * loc
    experts = expert_gate_up.shape[0] * ne
    el = expert_gate_up.shape[0]
    dr = D // nd
    fs = FS // ne
    fsr = FS // nd
    fsl = fsr // ne

    pad = 128 - heads
    piece = 16
    place = jnp.minimum(me_e, dr // piece - 1) * piece
    mine = lax.dynamic_slice_in_dim(input_weight, place, piece, 0)
    blocks = jnp.concatenate(
        [
            jnp.moveaxis(mine[:, :DI].reshape(piece, nd, di), 1, 0),
            jnp.moveaxis(mine[:, DI : 2 * DI].reshape(piece, nd, di), 1, 0),
            jnp.broadcast_to(mine[None, :, 2 * DI : 2 * DI + 2 * S], (nd, piece, 2 * S)),
            jnp.moveaxis(mine[:, DI + CONV :].reshape(piece, nd, heads), 1, 0),
            jnp.zeros((nd, piece, pad), BF),
        ],
        axis=2,
    )
    wcols = blocks.shape[2]

    sg = shared_gate_up.reshape(dr, 2, nd, ne, fsl)
    sg = lax.dynamic_index_in_dim(sg, me_e, 3, False).reshape(dr, 2 * fs)
    sd = lax.dynamic_slice_in_dim(shared_down, me_e * fsl, fsl, 0)
    packed = jnp.concatenate([sg.reshape(-1), sd.reshape(-1), router_weight.reshape(-1)])
    packed_cols = packed.size // rows_t
    packed = jnp.pad(packed.reshape(rows_t, -1), ((0, 0), (0, 256 - packed_cols)))

    stream = tokens.reshape(rows_t, D).astype(F32)
    incoming = cotangent.reshape(rows_t, D)
    route_rows = routes.reshape(rows_t, TOP)
    normed = rms_scale(stream, norm_gain).astype(BF)
    (_, w_in), (normed_all,) = run_tasks(
        [Weights(blocks), Gather("dp", jnp.concatenate([normed, packed], axis=1))], 1, "begin"
    )
    early, _ = lax.optimization_barrier((incoming, normed_all))
    inc_all = lax.all_gather(early, "expert", axis=0, tiled=True)
    packed_all = normed_all[:, :, D:].reshape(nd, rows_t, 256)[:, :, : packed_cols]
    packed_all = packed_all.reshape(nd, -1)
    sg_full = packed_all[:, : sg.size].reshape(D, 2 * fs)
    sd_full = packed_all[:, sg.size : sg.size + sd.size].reshape(fs, D)
    router_full = packed_all[:, sg.size + sd.size :].reshape(D, experts)
    taps = jnp.concatenate(
        [lax.dynamic_slice_in_dim(filter_weight, me_d * di, di, 1), filter_weight[:, DI:]], axis=1
    )
    tap_bias = jnp.concatenate(
        [lax.dynamic_slice_in_dim(filter_bias, me_d * di, di, 0), filter_bias[DI:]], axis=0
    )
    my_heads = lambda v: lax.dynamic_slice_in_dim(v, me_d * heads, heads, 0)
    my_gain = lax.dynamic_slice_in_dim(gated_gain, me_d * di, di, 0)

    taps_vec = jnp.concatenate([taps, tap_bias[None], jnp.zeros((3, di + 2 * S), F32)], axis=0)
    heads_vec = jnp.stack([my_heads(step_bias), -jnp.exp(my_heads(decay_log))])
    heads_vec = jnp.pad(heads_vec, ((0, 6), (0, S - heads)))
    lanes_vec = jnp.pad(
        jnp.stack([my_gain, jnp.repeat(my_heads(skip_gain), PS)]), ((0, 6), (0, 0))
    )
    vectors = (taps_vec, heads_vec, lanes_vec)
    payload, proj, scan, states = mixer_forward(
        lengths[:, 0], normed_all, w_in, output_weight, *vectors, heads
    )
    mask = jnp.sum(
        (route_rows[:, :, None] == jnp.arange(128, dtype=jnp.int32)).astype(F32), axis=1
    )
    router_wide = jnp.pad(router_full, ((0, 0), (0, 128 - experts)))
    gain_row = moe_gain.reshape(1, D)
    ((moe_payload, after_mixer, mixed, factors),) = run_tasks(
        [MixerOut(payload, tokens.reshape(rows_t, D), gain_row, router_wide, mask)],
        2,
        "reduce_mixer",
    )
    ((moe_all, pre_grad, gh, out_part, after_grad, grad_payload, moe_gain_grad, router_part),) = (
        run_tasks(
            [
                Experts(
                    moe_payload,
                    inc_all,
                    expert_gate_up,
                    expert_down,
                    sg_full,
                    sd_full,
                    after_mixer,
                    mixed,
                    factors,
                    gain_row,
                    router_wide,
                    incoming,
                )
            ],
            3,
            "experts",
        )
    )
    width = gh.shape[2]
    (out_sum,), (grad_blocks,), (grad_all,) = run_tasks(
        [
            Reduce("expert", out_part),
            ExpertGrads(moe_all, pre_grad, gh, inc_all, el, FE, nd),
            Gather("dp", grad_payload),
        ],
        5,
        "gather_grad",
    )
    all_sum = lax.psum_scatter(grad_blocks, "dp", scatter_dimension=0, tiled=True)[0]
    up_sum = all_sum[:dr]
    each, span = FE // nd, D // 2
    down_sum = all_sum[dr : dr + each]
    last_sum = all_sum[dr + each :]
    d_proj, normed_part, output_part, d_taps, d_heads, d_lanes = mixer_backward(
        lengths[:, 0], grad_all, w_in, output_weight, *vectors, proj, scan, states, heads
    )
    def rows_of(parts, count):
        flat = jnp.concatenate([part.reshape(-1) for part in parts])
        return jnp.pad(flat, (0, count * 128 - flat.size)).reshape(count, 128)

    added = (d_taps[:K, di:], d_taps[K, di:], moe_gain_grad, router_part)
    own = (
        d_taps[:K, :di],
        d_taps[K, :di],
        d_heads[0, :heads],
        d_heads[1, :heads],
        jnp.sum(d_lanes[1].reshape(heads, PS), axis=1),
        d_lanes[0],
    )
    added_size = sum(part.size for part in added)
    added_rows = -(-added_size // (nd * 1024)) * 8
    own_rows = -(-sum(part.size for part in own) // 128)
    norm_rows = D // 128
    (tokens_grad, norm_gain_grad), (d_sum,), (added_in,) = run_tasks(
        [
            StreamGrad(normed_part, tokens.reshape(rows_t, D), norm_gain.reshape(1, D), after_grad),
            InputGrad(
                normed_all,
                d_proj.reshape(nd * rows_t, wcols),
                output_part,
            ),
            Direct("all", "dp", rows_of(added, nd * added_rows).reshape(nd, added_rows, 128)),
        ],
        6,
        "reduce_grads",
    )
    small = jnp.concatenate(
        [jnp.sum(added_in, axis=0), rows_of(own, own_rows), rows_of((norm_gain_grad,), norm_rows)],
        axis=0,
    )
    small = jnp.pad(small, ((0, -small.shape[0] % 8), (0, 0)))
    shared_part = jnp.concatenate(
        [up_sum[:, 2 * el * FE :], last_sum[:fsl, span:].reshape(dr, -1)], axis=1
    ).reshape(-1, wcols)
    main_rows = D // ne
    (small_all,), (rest_all,), (input_grad,) = run_tasks(
        [
            Small(small),
            Gather("expert", jnp.concatenate([d_sum[main_rows:], shared_part], axis=0)),
            InputRows(d_sum[:main_rows], heads),
        ],
        7,
        "finish",
    )
    cut_rows = d_sum.shape[0] - main_rows
    output_grad = rest_all[:, :cut_rows].reshape(2, di, D // 2)
    output_grad = jnp.moveaxis(output_grad, 0, 1).reshape(output_weight.shape)
    shared_all = rest_all[:, cut_rows:].reshape(ne, dr, -1)
    added_all = small_all[:, :added_rows].reshape(-1)
    own_all = small_all[:, added_rows : added_rows + own_rows].reshape(nd, -1)
    norm_gain_grad = jnp.sum(
        small_all[:, added_rows + own_rows : added_rows + own_rows + norm_rows], axis=0
    ).reshape(D)

    def split(flat, parts):
        out, start = [], 0
        for part in parts:
            out.append(flat[..., start : start + part.size].reshape(flat.shape[:-1] + part.shape))
            start += part.size
        return out

    added_taps, added_bias, moe_gain_grad, router_all = split(added_all, added)
    own_taps, own_bias, own_steps, own_decay, own_skip, own_gain = split(own_all, own)
    small = (
        jnp.concatenate([jnp.moveaxis(own_taps, 0, 1).reshape(K, DI), added_taps], axis=1),
        jnp.concatenate([own_bias.reshape(-1), added_bias]),
        own_steps.reshape(-1),
        own_decay.reshape(-1),
        own_skip.reshape(-1),
        norm_gain_grad,
        own_gain.reshape(-1),
        moe_gain_grad.reshape(D),
    )
    router_grad = lax.dynamic_slice_in_dim(router_all, me_d * dr, dr, 1).T
    expert_up_grad = jnp.moveaxis(up_sum[:, : 2 * el * FE].reshape(dr, el, 2 * FE), 1, 0)
    expert_up_grad = expert_up_grad.astype(F32)
    expert_down_grad = jnp.stack(
        [
            down_sum[:, : 2 * span],
            jnp.concatenate([down_sum[:, 2 * span :], last_sum[:, :span]], axis=1),
        ],
        axis=0,
    ).astype(F32)
    shared_up_grad = (
        jnp.moveaxis(shared_all[:, :, : 2 * fs].reshape(ne, dr, 2, nd, fsl), 0, 3)
        .reshape(dr, 2 * FS)
        .astype(F32)
    )
    shared_down_grad = shared_all[:, :, 2 * fs :].reshape(fsr, D).astype(F32)
    block_output = (after_mixer + out_sum).astype(BF)
    shape = (MB, 1, loc, D)
    return (
        block_output.reshape(shape),
        tokens_grad.reshape(shape),
        input_grad,
        small[0],
        small[1],
        small[2],
        small[3],
        small[4],
        small[5],
        small[6],
        output_grad.astype(F32),
        small[7],
        router_grad,
        shared_up_grad,
        shared_down_grad,
        expert_up_grad,
        expert_down_grad,
    )


def solution(mesh):
    in_specs = (
        P(None, "expert", "dp", None),
        P(None, "expert", None),
        P(None, "expert", "dp", None),
        P(None, "expert", "dp", None),
        P("dp", None),
        P(),
        P(),
        P(),
        P(),
        P(),
        P(),
        P(),
        P("dp", None),
        P(),
        P("dp", None),
        P("dp", None),
        P("dp", None),
        P("expert", None, None),
        P("expert", None, None),
    )
    out_specs = (
        P(None, "expert", "dp", None),
        P(None, "expert", "dp", None),
        P("dp", None),
        P(),
        P(),
        P(),
        P(),
        P(),
        P(),
        P(),
        P("dp", None),
        P(),
        P("dp", None),
        P("dp", None),
        P("dp", None),
        P("expert", "dp", None),
        P("expert", "dp", None),
    )
    return jax.shard_map(body, mesh=mesh, in_specs=in_specs, out_specs=out_specs, check_vma=False)
```

```python
import functools

import jax
import jax.numpy as jnp
from jax import lax
from jax.experimental import pallas as pl
from jax.experimental.pallas import tpu as pltpu
from jax.sharding import PartitionSpec as P

D = 1536
H = 48
PS = 64
S = 128
K = 4
FE = 512
FS = 1024
TOP = 6
MB = 2
DI = 3072
CONV = 3328
IN_W = 6448
EPSILON = 1e-05
BF = jnp.bfloat16
F32 = jnp.float32
MESH = pl.DeviceIdType.MESH
VMEM_LIMIT = 60 * 1024 * 1024


def mm(a, b):
    return jnp.dot(a, b, preferred_element_type=F32)


def mm_nt(a, b):
    return lax.dot_general(a, b, (((1,), (1,)), ((), ())), preferred_element_type=F32)


def mm_tn(a, b):
    return lax.dot_general(a, b, (((0,), (0,)), ((), ())), preferred_element_type=F32)


def rms_scale(values, gain):
    return values * lax.rsqrt(jnp.mean(values * values, axis=-1, keepdims=True) + EPSILON) * gain


ANY = pl.BlockSpec(memory_space=pl.ANY)
IN_VMEM = pl.BlockSpec(memory_space=pltpu.VMEM)


def places(axis):
    me = lax.axis_index(axis)
    if axis == "dp":
        core, ring, pair = lax.rem(me, 2), lax.rem(me // 2, 4), me // 8

        def at(hop, other, sibling=0):
            z = lax.rem(pair + other, 2)
            return (z * 4 + lax.rem(ring + hop + 4, 4)) * 2 + lax.rem(core + sibling, 2)
    else:
        pair, ring = lax.rem(me, 2), me // 2

        def at(hop, other, sibling=0):
            return lax.rem(ring + hop + 4, 4) * 2 + lax.rem(pair + other, 2)

    return me, at


class Task:
    ins, outs, scratch, reaches, turns = (), (), (), (), 1

    def greet(self, barrier):
        return 0


def peers_of(axis, everyone):
    me, at = places(axis)
    if everyone:
        n = lax.axis_size(axis)
        return [lax.rem(me + k, n) for k in range(1, n)]
    near = [at(1, 0), at(-1, 0), at(0, 1)]
    return near + [at(0, 0, 1)] if axis == "dp" else near


class Links:
    def __init__(self, axis, send, recv):
        self.axis, self.send, self.recv, self.started = axis, send, recv, []

    def push(self, number, src, dst, peer):
        copy = pltpu.make_async_remote_copy(
            src_ref=src,
            dst_ref=dst,
            send_sem=self.send.at[number],
            recv_sem=self.recv.at[number],
            device_id={self.axis: peer},
            device_id_type=MESH,
        )
        copy.start()
        self.started.append(copy)

    def arrived(self, number, dst):
        pltpu.make_async_copy(dst, dst, self.recv.at[number]).wait()

    def finish(self):
        for copy in self.started:
            copy.wait_send()


def halves(shape):
    rows = shape[0]
    cut = rows // 2 if len(shape) == 3 else rows // 32 * 16
    return pl.ds(0, rows), pl.ds(0, cut), pl.ds(cut, rows - cut), cut


class Gather(Task):
    def __init__(self, axis, x):
        self.axis, self.reaches = axis, ((axis, False),)
        self.ins = ((x, ANY),)
        n = lax.axis_size(axis)
        self.outs = ((jax.ShapeDtypeStruct((n,) + x.shape, x.dtype), ANY),)
        dma = pltpu.SemaphoreType.DMA
        self.scratch = (dma((17,)), dma((17,)), dma)

    def steps(self, ins, outs, scratch):
        return gather_steps(self.axis, ins[0], outs[0], *scratch)


def gather_steps(axis, x, out, send, recv, own_sem):
    me, at = places(axis)
    cores = axis == "dp"
    up, down, pair, sib = at(1, 0), at(-1, 0), at(0, 1), at(0, 0, 1)
    whole, first, second, _ = halves(x.shape)
    links = Links(axis, send, recv)

    def push(number, slot, rows, peer, src=None):
        src = out.at[slot] if src is None else src
        links.push(number, src.at[rows], out.at[slot].at[rows], peer)

    def arrived(number, slot, rows):
        links.arrived(number, out.at[slot].at[rows])

    push(0, me, whole, up, x)
    push(1, me, whole, down, x)
    push(2, me, whole, pair, x)
    if cores:
        push(3, me, whole, sib, x)
    own = pltpu.make_async_copy(x, out.at[me], own_sem)
    own.start()
    yield
    own.wait()
    arrived(2, pair, whole)
    push(4, pair, whole, up)
    push(5, pair, whole, down)
    arrived(0, down, whole)
    push(7, down, first, up)
    arrived(1, up, whole)
    push(8, up, second, down)
    if cores:
        push(6, pair, whole, sib)
        push(9, down, whole, sib)
        push(10, up, whole, sib)
    yield
    arrived(4, at(-1, 1), whole)
    push(11, at(-1, 1), first, up)
    arrived(5, at(1, 1), whole)
    push(12, at(1, 1), second, down)
    arrived(7, at(2, 0), first)
    arrived(8, at(2, 0), second)
    if cores:
        push(13, at(-1, 1), whole, sib)
        push(14, at(1, 1), whole, sib)
        push(15, at(2, 0), whole, sib)
    yield
    arrived(11, at(2, 1), first)
    arrived(12, at(2, 1), second)
    if cores:
        push(16, at(2, 1), whole, sib)
        yield
        for number, hop, other in (
            (3, 0, 0),
            (6, 0, 1),
            (9, -1, 0),
            (10, 1, 0),
            (13, -1, 1),
            (14, 1, 1),
            (15, 2, 0),
            (16, 2, 1),
        ):
            arrived(number, at(hop, other, 1), whole)
    links.finish()


ORDER = ((2, 1), (2, 0), (1, 1), (-1, 1), (1, 0), (-1, 0), (0, 1), (0, 0))


class Reduce(Task):
    def __init__(self, axis, x, dtype=F32):
        self.axis, self.reaches = axis, ((axis, False),)
        n, rows, columns = x.shape
        self.ins = ((x, ANY),)
        self.outs = ((jax.ShapeDtypeStruct((rows, columns), dtype), IN_VMEM),)
        _, _, _, cut = halves((rows, columns))
        buf = lambda *dims: pltpu.VMEM(dims + (columns,), BF)
        dma = pltpu.SemaphoreType.DMA
        dp = axis == "dp"
        self.scratch = (
            buf(8, rows),
            buf(8 if dp else 1, rows if dp else 16),
            buf(2, cut),
            buf(2, rows - cut),
            buf(2, rows),
            buf(2, rows),
            buf(rows),
            dma((17,)),
            dma((17,)),
            dma((8,)),
        )

    def steps(self, ins, outs, scratch):
        return reduce_steps(self.axis, ins[0], outs[0], *scratch)


def reduce_steps(axis, x, out, acc, sib_buf, a_buf, b_buf, c_buf, d_buf, e_buf, send, recv, load):
    me, at = places(axis)
    cores = axis == "dp"
    rows = acc.shape[1]
    step = 16
    block = lambda k: x.at[k] if len(x.shape) == 3 else x.at[pl.ds(pl.multiple_of(k * rows, 16), rows)]
    up, down, pair, sib = at(1, 0), at(-1, 0), at(0, 1), at(0, 0, 1)
    whole, first, second, cut = halves(acc.shape[1:])
    links = Links(axis, send, recv)
    push, arrived = links.push, links.arrived

    def add(dst, offset, count, *srcs):
        @pl.loop(0, count // step)
        def _(i):
            at_rows = pl.ds(pl.multiple_of(offset + i * step, step), step)
            total = dst[at_rows, :].astype(F32)
            for src in srcs:
                total += src[pl.ds(pl.multiple_of(i * step, step), step), :].astype(F32)
            dst[at_rows, :] = total.astype(dst.dtype)

    loads = []
    for k, (hop, other) in enumerate(ORDER if x is not None else ()):
        if cores:
            push(k, block(at(hop, other, 1)), sib_buf.at[k], sib)
        copy = pltpu.make_async_copy(block(at(hop, other)), acc.at[k], load.at[k])
        copy.start()
        loads.append(copy)

    def ready(k):
        if loads:
            loads[k].wait()
        if cores:
            arrived(k, sib_buf.at[k])
            add(acc.at[k], 0, rows, sib_buf.at[k])

    yield
    for k in range(2):
        ready(k)
        push(8 + 2 * k, acc.at[k].at[first], a_buf.at[k], up)
        push(9 + 2 * k, acc.at[k].at[second], b_buf.at[k], down)
    yield
    for k in range(2):
        above, below = 2 + 2 * k, 3 + 2 * k
        ready(above)
        ready(below)
        arrived(8 + 2 * k, a_buf.at[k])
        add(acc.at[above], 0, cut, a_buf.at[k])
        push(12 + 2 * k, acc.at[above], c_buf.at[k], up)
        arrived(9 + 2 * k, b_buf.at[k])
        add(acc.at[below], cut, rows - cut, b_buf.at[k])
        push(13 + 2 * k, acc.at[below], d_buf.at[k], down)
    yield
    ready(6)
    ready(7)
    arrived(12, c_buf.at[0])
    arrived(13, d_buf.at[0])
    add(acc.at[6], 0, rows, c_buf.at[0], d_buf.at[0])
    push(16, acc.at[6], e_buf, pair)
    yield
    arrived(14, c_buf.at[1])
    arrived(15, d_buf.at[1])
    yield
    arrived(16, e_buf)

    @pl.loop(0, rows // step)
    def _(i):
        at_rows = pl.ds(pl.multiple_of(i * step, step), step)
        total = acc[7, at_rows, :].astype(F32) + c_buf[1, at_rows, :].astype(F32)
        total += d_buf[1, at_rows, :].astype(F32) + e_buf[at_rows, :].astype(F32)
        out[at_rows, :] = total.astype(out.dtype)

    links.finish()


class Direct(Task):
    def __init__(self, kind, axis, x):
        self.kind, self.axis, self.reaches = kind, axis, ((axis, True),)
        n = lax.axis_size(axis)
        shape = (n,) + x.shape if kind == "gather" else x.shape
        self.ins = ((x, ANY),)
        self.outs = ((jax.ShapeDtypeStruct(shape, x.dtype), ANY),)
        dma = pltpu.SemaphoreType.DMA
        self.scratch = (dma((n,)), dma((n,)), dma)

    def steps(self, ins, outs, scratch):
        return direct_steps(self.kind, self.axis, ins[0], outs[0], *scratch)


def direct_steps(kind, axis, x, out, send, recv, own_sem):
    n, me = lax.axis_size(axis), lax.axis_index(axis)
    links = Links(axis, send, recv)
    piece = lambda k: x if kind == "gather" else x.at[k]
    for k in range(1, n):
        peer = lax.rem(me + k, n)
        links.push(k, piece(peer), out.at[me], peer)
    own = pltpu.make_async_copy(piece(me), out.at[me], own_sem)
    own.start()
    yield
    for k in range(1, n):
        links.arrived(k, out.at[lax.rem(me - k + n, n)])
    own.wait()
    links.finish()


def run_tasks(tasks, number, name):
    operands, in_specs, out_shapes, out_specs, scratch, spans = [], [], [], [], [], []
    for task in tasks:
        spans.append((len(operands), len(out_shapes), len(scratch)))
        operands += [x for x, _ in task.ins]
        in_specs += [spec for _, spec in task.ins]
        out_shapes += [shape for shape, _ in task.outs]
        out_specs += [spec for _, spec in task.outs]
        scratch += list(task.scratch)

    def kernel(*refs):
        ins = refs[: len(operands)]
        outs = refs[len(operands) : len(operands) + len(out_shapes)]
        temps = refs[len(operands) + len(out_shapes) :]
        barrier = pltpu.get_barrier_semaphore()
        count = 0
        for axis in ("dp", "expert"):
            here = [everyone for task in tasks for name, everyone in task.reaches if name == axis]
            if here:
                peers = peers_of(axis, any(here))
                for peer in peers:
                    pl.semaphore_signal(
                        barrier, inc=1, device_id={axis: peer}, device_id_type=MESH
                    )
                count += len(peers)
        for task in tasks:
            count += task.greet(barrier)
        pl.semaphore_wait(barrier, count)
        running = []
        for task, (i, o, s) in zip(tasks, spans):
            steps = task.steps(
                ins[i : i + len(task.ins)],
                outs[o : o + len(task.outs)],
                temps[s : s + len(task.scratch)],
            )
            running.append((task.turns, steps))
        while running:
            left = []
            for turns, steps in running:
                if all(next(steps, "end") != "end" for _ in range(turns)):
                    left.append((turns, steps))
            running = left

    results = pl.pallas_call(
        kernel,
        out_shape=out_shapes,
        in_specs=in_specs,
        out_specs=out_specs,
        scratch_shapes=scratch,
        compiler_params=pltpu.CompilerParams(
            collective_id=number, has_side_effects=True, vmem_limit_bytes=VMEM_LIMIT
        ),
        name=name,
    )(*operands)
    return [results[o : o + len(task.outs)] for task, (_, o, _) in zip(tasks, spans)]


class Weights(Task):
    def __init__(self, x):
        self.reaches = (("dp", True), ("expert", False))
        self.swap, self.spread = Direct("all", "dp", x), Gather("expert", x)
        n = lax.axis_size("expert")
        full = jax.ShapeDtypeStruct((n,) + x.shape, x.dtype)
        self.ins = ((x, ANY),)
        self.outs = self.swap.outs + ((full, ANY),)
        self.scratch = self.swap.scratch + self.spread.scratch

    def steps(self, ins, outs, scratch):
        yield from direct_steps("all", "dp", ins[0], outs[0], *scratch[:3])
        yield
        yield from gather_steps("expert", outs[0], outs[1], *scratch[3:])


class ExpertGrads(Task):
    def __init__(self, x, pre_grad, gh, inc, experts, each, blocks):
        n, rows, _ = x.shape
        width, depth = gh.shape[2], inc.shape[1]
        self.experts, self.each = experts, each
        grads = jax.ShapeDtypeStruct(
            (blocks, depth // blocks + 2 * (each // blocks), 2 * width), BF
        )
        self.ins = tuple((v, ANY) for v in (x, pre_grad, gh, inc))
        self.outs = ((grads, ANY),)
        dma = pltpu.SemaphoreType.DMA
        vmem = lambda *dims: pltpu.VMEM(dims, BF)
        self.scratch = (
            vmem(n, rows, depth),
            vmem(*pre_grad.shape),
            vmem(*gh.shape),
            vmem(*inc.shape),
            dma((5,)),
            vmem(depth, n * rows),
            vmem(width, n * rows),
            vmem(*grads.shape),
        )

    def steps(self, ins, outs, scratch):
        x, pre_grad, gh, inc, sems, x_t, gh_t, grads = scratch
        n, rows, depth = x.shape
        width = gh.shape[2]
        experts, each = self.experts, self.each
        copy = lambda src, dst, k: pltpu.make_async_copy(src, dst, sems.at[k])
        load_x = copy(ins[0].at[:, :, pl.ds(0, depth)], x, 0)
        load_pre = copy(ins[1], pre_grad, 1)
        load_inc = copy(ins[3], inc, 3)
        load_gh = copy(ins[2], gh, 2)
        for load in (load_x, load_pre, load_gh, load_inc):
            load.start()
        yield
        tile = 256
        col = lambda i: pl.ds(pl.multiple_of(i * tile, tile), tile)
        load_x.wait()

        @pl.loop(0, depth // tile)
        def _(i):
            x_t[col(i), :] = x[:, :, col(i)].reshape(n * rows, tile).T

        load_pre.wait()
        blocks = grads.shape[0]
        up_rows = depth // blocks
        steps = 2 * width // tile
        for start, end in ((0, steps // 3), (steps // 3, steps)):

            @pl.loop(start, end)
            def _(i):
                value = mm(x_t[...], pre_grad[:, :, col(i)].reshape(n * rows, tile)).astype(BF)
                grads[:, :up_rows, col(i)] = value.reshape(blocks, up_rows, tile)

            yield
        load_gh.wait()

        @pl.loop(0, width // 128)
        def _(i):
            at_cols = pl.ds(pl.multiple_of(i * 128, 128), 128)
            gh_t[at_cols, :] = gh[:, :, at_cols].reshape(n * rows, 128).T

        load_inc.wait()
        piece_rows = each // blocks
        own = (width - experts * each) // blocks
        span = depth // 2
        spots = (((0, 0), (0, 2)), ((0, 1), (piece_rows, 0)))
        for half in range(2):

            @pl.loop(0, span // tile)
            def _(i):
                value = mm(gh_t[...], inc[:, col(half * span // tile + i)])
                for e in range(experts):
                    row, place = spots[half][e]
                    piece = value[e * each : (e + 1) * each].astype(BF)
                    grads[
                        :,
                        up_rows + row : up_rows + row + piece_rows,
                        col(place * span // tile + i),
                    ] = piece.reshape(blocks, piece_rows, tile)
                piece = value[experts * each :].reshape(blocks, own, tile)
                empty = jnp.zeros((blocks, piece_rows - own, tile), F32)
                piece = jnp.concatenate([piece, empty], axis=1).astype(BF)
                grads[:, up_rows + piece_rows :, col((1 + half) * span // tile + i)] = piece

        store = copy(grads, outs[0], 4)
        store.start()
        yield
        store.wait()


def chunks(rows, step=16):
    def over(work):
        @pl.loop(0, rows // step)
        def _(i):
            work(pl.ds(pl.multiple_of(i * step, step), step))

    return over


def sides(v):
    high = v.astype(BF).astype(F32)
    turn = (iota((128, 128), 0) + 16 == iota((128, 128), 1)).astype(F32)
    return (high + exact(v - high, turn, ((1,), (0,)))).astype(BF)


def joined(v):
    turn = (iota((128, 128), 0) - 16 == iota((128, 128), 1)).astype(F32)
    back = exact(v, turn, ((1,), (0,)))
    return jnp.where(iota((1, 128), 1) < 16, v + back, 0.0)


class StreamGrad(Task):
    def __init__(self, parts, stream, gain, after_grad):
        self.reaches = (("dp", False),)
        self.reduce = Reduce("dp", parts)
        self.ins = self.reduce.ins + tuple((v, IN_VMEM) for v in (stream, gain, after_grad))
        shape = jax.ShapeDtypeStruct
        self.outs = ((shape(stream.shape, F32), IN_VMEM), (shape((1, D), F32), IN_VMEM))
        self.scratch = (pltpu.VMEM(stream.shape, F32),) + self.reduce.scratch

    def steps(self, ins, outs, scratch):
        x, stream, gain, after_grad = ins
        out, gain_grad = outs
        total = scratch[0]
        yield from reduce_steps("dp", x, total, *scratch[1:])
        gain_grad[...] = jnp.zeros_like(gain_grad)

        @chunks(total.shape[0])
        def _(rows):
            v = stream[rows, :].astype(F32)
            inv = lax.rsqrt(jnp.mean(v * v, axis=1, keepdims=True) + EPSILON)
            g = total[rows, :]
            gg = g * gain[...]
            gain_grad[...] += jnp.sum(g * v * inv, axis=0, keepdims=True)
            mean = jnp.mean(gg * v, axis=1, keepdims=True)
            out[rows, :] = after_grad[rows, :] + inv * gg - v * (inv * inv * inv * mean)


class InputGrad(Task):
    def __init__(self, gathered, d_proj, out_grad):
        self.reaches = (("expert", False),)
        n = lax.axis_size("expert")
        wide = d_proj.shape[1]
        rows = (D + out_grad.size // wide) // n
        self.reduce = Reduce("expert", jax.ShapeDtypeStruct((n, rows, wide), BF), BF)
        self.ins = tuple((v, ANY) for v in (*gathered, d_proj, out_grad.reshape(n, -1, wide)))
        self.outs = self.reduce.outs
        dma = pltpu.SemaphoreType.DMA
        self.scratch = (
            pltpu.VMEM((gathered[0].shape[0], MB * gathered[0].shape[1], D), BF),
            pltpu.VMEM(d_proj.shape, BF),
            pltpu.VMEM((n, rows, wide), BF),
            dma((4,)),
        ) + self.reduce.scratch

    def steps(self, ins, outs, scratch):
        g, d_proj, total, sems = scratch[:4]
        n, _, wide = total.shape
        each = D // n
        below = pl.ds(each, total.shape[1] - each)
        loads = (
            pltpu.make_async_copy(ins[2], d_proj, sems.at[0]),
            pltpu.make_async_copy(ins[3], total.at[:, below], sems.at[1]),
        ) + tuple(
            pltpu.make_async_copy(
                ins[m].at[:, :, pl.ds(0, D)],
                g.at[:, pl.ds(m * ins[m].shape[1], ins[m].shape[1])],
                sems.at[2 + m],
            )
            for m in range(MB)
        )
        for load in loads:
            load.start()
        yield
        for load in loads:
            load.wait()
        flat = g.shape[0] * g.shape[1]

        @pl.loop(0, n // 2)
        def _(i):
            columns = pl.ds(pl.multiple_of(i * 2 * each, 2 * each), 2 * each)
            value = mm_tn(g[:, :, columns].reshape(flat, 2 * each), d_proj[...]).astype(BF)
            total[pl.ds(2 * i, 2), :each, :] = value.reshape(2, each, wide)

        yield from reduce_steps("expert", total, outs[0], *scratch[4:])


class InputRows(Task):
    def __init__(self, x, heads):
        nd, ne = lax.axis_size("dp"), lax.axis_size("expert")
        self.heads = heads
        self.slices = D // nd // 16
        self.reaches = (("expert", False),)
        wide = 2 * DI + 2 * S + 128
        row = jax.ShapeDtypeStruct((16, wide), BF)
        self.gather = Gather("expert", row)
        self.ins = ((x, ANY),)
        self.outs = ((jax.ShapeDtypeStruct((D // nd, IN_W), F32), IN_VMEM),)
        dma = pltpu.SemaphoreType.DMA
        self.scratch = (
            pltpu.VMEM((nd, 16, x.shape[1]), BF),
            pltpu.VMEM((16, wide), BF),
            pltpu.VMEM((ne, 16, wide), BF),
            dma((2 * ne,)),
            dma((nd,)),
        ) + self.gather.scratch

    def greet(self, barrier):
        nd = lax.axis_size("dp")
        j = lax.axis_index("dp")
        for source in range(nd):
            pl.semaphore_signal(
                barrier, inc=1, device_id={"dp": source, "expert": j // 2}, device_id_type=MESH
            )
        return 2 * lax.axis_size("expert")

    def steps(self, ins, outs, scratch):
        x = ins[0]
        got, row, full, send, recv = scratch[:5]
        nd, ne = lax.axis_size("dp"), lax.axis_size("expert")
        j, e = lax.axis_index("dp"), lax.axis_index("expert")
        heads, di = self.heads, self.heads * PS
        sent = []
        for k in range(2):
            for c in range(ne):
                src = x.at[pl.ds((k * self.slices + min(c, self.slices - 1)) * 16, 16)]
                mine = (j == 2 * e + k) & (e == c)
                away = pltpu.make_async_remote_copy(
                    src_ref=src,
                    dst_ref=got.at[j],
                    send_sem=send.at[k * ne + c],
                    recv_sem=recv.at[j],
                    device_id={"dp": 2 * e + k, "expert": c},
                    device_id_type=MESH,
                )
                here = pltpu.make_async_copy(src, got.at[j], recv.at[j])
                pl.when(mine)(here.start)
                pl.when(jnp.logical_not(mine))(away.start)
                sent.append((mine, away))
        yield
        for source in range(nd):
            pltpu.make_async_copy(got.at[source], got.at[source], recv.at[source]).wait()
        piece = lambda source, start, size: got[source, :, start : start + size].astype(F32)
        for source in range(0, nd, 2):
            for half in range(2):
                pair = [piece(source + k, half * di, di) for k in range(2)]
                start = half * DI + source * di
                row[:, start : start + 2 * di] = jnp.concatenate(pair, axis=1).astype(BF)
        total = piece(0, 2 * di, 2 * S)
        for source in range(1, nd):
            total = total + piece(source, 2 * di, 2 * S)
        row[:, 2 * DI : 2 * DI + 2 * S] = total.astype(BF)
        steps = [piece(source, 2 * di + 2 * S, 128)[:, :heads] for source in range(nd)]
        steps.append(jnp.zeros((16, 128 - nd * heads), F32))
        row[:, 2 * DI + 2 * S :] = jnp.concatenate(steps, axis=1).astype(BF)
        yield from gather_steps("expert", row, full, *scratch[5:])
        for c in range(self.slices):
            outs[0][c * 16 : (c + 1) * 16, :] = full[c, :, :IN_W].astype(F32)
        for mine, away in sent:
            pl.when(jnp.logical_not(mine))(away.wait_send)


class Small(Task):
    def __init__(self, x):
        self.reaches = (("expert", True), ("dp", True))
        nd, ne = lax.axis_size("dp"), lax.axis_size("expert")
        self.ins = ((x, ANY),)
        self.outs = ((jax.ShapeDtypeStruct((nd,) + x.shape, x.dtype), ANY),)
        dma = pltpu.SemaphoreType.DMA
        self.scratch = (
            pltpu.VMEM((ne,) + x.shape, x.dtype),
            pltpu.VMEM(x.shape, x.dtype),
            dma((ne,)),
            dma((ne,)),
            dma,
            dma((nd,)),
            dma((nd,)),
            dma,
        )

    def steps(self, ins, outs, scratch):
        parts, total = scratch[:2]
        yield from direct_steps("gather", "expert", ins[0], parts, *scratch[2:5])
        total[...] = jnp.sum(parts[...], axis=0)
        yield from direct_steps("gather", "dp", total, outs[0], *scratch[5:8])


class Experts(Task):
    def __init__(
        self, low, mask, inc, w_up, w_down, s_up, s_down, after, mixed, factors, gain, router, own
    ):
        x = jax.ShapeDtypeStruct((low.shape[0], low.shape[1] + 128), BF)
        self.reaches = (("expert", False),)
        self.gather = Gather("expert", x)
        n = lax.axis_size("expert")
        rows, wide = x.shape
        depth = inc.shape[1]
        experts, _, both = w_up.shape
        self.experts = experts
        all_rows = jax.ShapeDtypeStruct((n, rows, wide), BF)
        self.reduce = Reduce("expert", all_rows)
        hidden = experts * both // 2 + s_down.shape[0]
        pre = jax.ShapeDtypeStruct((n, rows, 2 * hidden), BF)
        gh = jax.ShapeDtypeStruct((n, rows, hidden), BF)
        self.ins = tuple((v, ANY) for v in (inc, w_up, w_down, s_up, s_down)) + tuple(
            (v, IN_VMEM) for v in (low, mask, after, mixed, factors, gain, router, own)
        )
        part = jax.ShapeDtypeStruct((n, rows, depth), BF)
        shape = jax.ShapeDtypeStruct
        self.outs = (
            ((all_rows, IN_VMEM),)
            + tuple((v, ANY) for v in (pre, gh, part))
            + (
                (shape((rows, depth), F32), IN_VMEM),
                (shape((rows, wide), BF), IN_VMEM),
                (shape((1, depth), F32), IN_VMEM),
                (shape((16, depth), F32), IN_VMEM),
            )
        )
        dma = pltpu.SemaphoreType.DMA
        self.scratch = (
            (pltpu.VMEM((n, rows, depth), BF),)
            + tuple(pltpu.VMEM(v.shape, BF) for v in (w_up, w_down, s_up, s_down))
            + (pltpu.VMEM((2 * rows, wide), BF), pltpu.VMEM((2 * rows, depth), BF))
            + (pltpu.VMEM((2 * rows, 2 * hidden), BF), pltpu.VMEM((2 * rows, hidden), BF))
            + (pltpu.VMEM(pre.shape, BF), pltpu.VMEM(gh.shape, BF))
            + (pltpu.VMEM((2 * rows, 128), F32), dma((22,)), pltpu.VMEM(part.shape, BF))
            + (pltpu.VMEM((rows, wide), F32), pltpu.VMEM((rows, wide), BF))
            + self.gather.scratch
            + self.reduce.scratch
        )

    def steps(self, ins, outs, scratch):
        inc_in = ins[0]
        low_in, mask, after, mixed, factors, gain, router, own = ins[5:]
        x_all, pre_out, gh_out, part_out, after_grad, payload, gain_grad, router_grad = outs
        inc, w_up, w_down, s_up, s_down, xs, incs, pg, ghs, pre, gh, extra, sems = scratch[:13]
        part, dx, gather_scratch, reduce_scratch = scratch[13], scratch[14], scratch[16:19], scratch[19:]
        x = scratch[15]
        acc = reduce_scratch[0]
        me, at = places("expert")
        n, rows, depth = inc.shape
        experts, _, both = w_up.shape
        each = both // 2
        shared = s_down.shape[0]
        tile = min(256, each)
        loads = [
            pltpu.make_async_copy(src, dst, sems.at[k])
            for k, (src, dst) in enumerate(zip(ins[1:5], (w_up, w_down, s_up, s_down)))
        ]
        loads += [
            pltpu.make_async_copy(inc_in.at[pl.ds(k * rows, rows)], inc.at[k], sems.at[13 + k])
            for k in range(n)
        ]
        for load in loads:
            load.start()

        logits = mm(low_in[...], router[...])
        chosen = mask[...]
        top = jnp.max(jnp.where(chosen > 0.0, logits, -1e30), axis=1, keepdims=True)
        e = jnp.where(chosen > 0.0, jnp.exp(jnp.minimum(logits - top, 0.0)), 0.0)
        table = e / jnp.sum(e, axis=1, keepdims=True)
        x[:, :depth] = low_in[...]
        x[:, depth:] = sides(table)
        arriving = gather_steps("expert", x, x_all, *gather_scratch)
        next(arriving)
        next(arriving)
        for load in loads:
            load.wait()
        lane = lax.broadcasted_iota(jnp.int32, (1, 128), 1)
        stores = []

        def unit(a, b, u, scale):
            sig = jax.nn.sigmoid(a)
            act = a * sig
            hidden = act * b
            gu = u * scale
            da = gu * b * (sig + act * (1.0 - sig))
            return hidden * scale, da, gu * act, u * hidden

        def compute(hop, places_in_acc):
            slots = (at(hop, 0), at(hop, 1))
            for k, slot in enumerate(slots):
                part = pl.ds(k * rows, rows)
                xs[part, :] = x_all[slot]
                incs[part, :] = inc[slot]
            extra[...] = jnp.zeros_like(extra)

            @pl.loop(0, experts * (each // tile))
            def _(i):
                e, f = i // (each // tile), lax.rem(i, each // tile)
                place = me * experts + e
                table = xs[:, depth:].astype(F32)
                chosen = (lane == place) | (lane == place + n * experts)
                scale = jnp.sum(jnp.where(chosen, table, 0.0), axis=1, keepdims=True)
                left = pl.ds(pl.multiple_of(f * tile, tile), tile)
                right = pl.ds(pl.multiple_of(each + f * tile, tile), tile)
                a = mm(xs[:, :depth], w_up[e, :, left])
                b = mm(xs[:, :depth], w_up[e, :, right])
                u = mm_nt(incs[...], w_down[e, left, :])
                h, da, db, dots = unit(a, b, u, scale)
                ghs[:, pl.ds(pl.multiple_of(e * each + f * tile, tile), tile)] = h.astype(BF)
                pg[:, pl.ds(pl.multiple_of(e * both + f * tile, tile), tile)] = da.astype(BF)
                pg[:, pl.ds(pl.multiple_of(e * both + each + f * tile, tile), tile)] = db.astype(BF)
                extra[...] += jnp.where(lane == place, jnp.sum(dots, axis=1, keepdims=True), 0.0)

            a = mm(xs[:, :depth], s_up[:, :shared])
            b = mm(xs[:, :depth], s_up[:, shared:])
            u = mm_nt(incs[...], s_down[...])
            h, da, db, _ = unit(a, b, u, 1.0)
            ghs[:, experts * each :] = h.astype(BF)
            pg[:, experts * both : experts * both + shared] = da.astype(BF)
            pg[:, experts * both + shared :] = db.astype(BF)

            @pl.loop(0, depth // tile)
            def _(i):
                columns = pl.ds(pl.multiple_of(i * tile, tile), tile)
                total = mm_nt(pg[:, experts * both :], s_up[columns, :])
                for e in range(experts):
                    total += mm_nt(pg[:, e * both : (e + 1) * both], w_up[e, columns, :])
                for k, place in enumerate(places_in_acc):
                    acc[place, :, columns] = total[k * rows : (k + 1) * rows].astype(BF)

            grads = extra[...]
            both_parts = sides(grads)
            for k, (slot, place) in enumerate(zip(slots, places_in_acc)):
                part = pl.ds(k * rows, rows)
                acc[place, :, depth:] = both_parts[k * rows : (k + 1) * rows]
                pre[slot] = pg[part, :]
                gh[slot] = ghs[part, :]
                store = pltpu.make_async_copy(pre.at[slot], pre_out.at[slot], sems.at[4 + len(stores)])
                store.start()
                stores.append(store)

        compute(0, (7, 6))
        next(arriving)
        compute(1, (4, 2))
        compute(-1, (5, 3))
        for _ in arriving:
            pass
        compute(2, (1, 0))
        store = pltpu.make_async_copy(gh, gh_out, sems.at[12])
        store.start()
        stores.append(store)
        summing = reduce_steps("expert", None, dx, *reduce_scratch)
        next(summing)
        for half in range(2):
            next(summing)

            @pl.loop(half * depth // tile // 2, (half + 1) * depth // tile // 2)
            def _(i):
                columns = pl.ds(pl.multiple_of(i * tile, tile), tile)
                hid = lambda start, size: gh[:, :, start : start + size].reshape(n * rows, size)
                total = mm(hid(experts * each, shared), s_down[:, columns])
                for e in range(experts):
                    total += mm(hid(e * each, each), w_down[e, :, columns])
                part[:, :, columns] = total.astype(BF).reshape(n, rows, tile)

        store = pltpu.make_async_copy(part, part_out, sems.at[21])
        store.start()
        stores.append(store)
        yield from summing
        gain_grad[...] = jnp.zeros_like(gain_grad)
        spread = joined(dx[:, depth:])
        logit = table * (spread - jnp.sum(table * spread, axis=1, keepdims=True))
        logit_low = logit.astype(BF)
        router_grad[...] = mm_tn(logit_low, low_in[...])[:16]
        dx[:, :depth] += mm_nt(logit_low, router[...])

        @chunks(rows)
        def _(at_rows):
            v, inv = after[at_rows, :], factors[at_rows, 1:2]
            g = dx[at_rows, :depth]
            gg = g * gain[...]
            gain_grad[...] += jnp.sum(g * v * inv, axis=0, keepdims=True)
            mean = jnp.mean(gg * v, axis=1, keepdims=True)
            total = own[at_rows, :].astype(F32) + inv * gg - v * (inv * inv * inv * mean)
            after_grad[at_rows, :] = total
            total_low = total.astype(BF)
            payload[at_rows, :depth] = total_low
            s = jnp.sum(total_low.astype(F32) * mixed[at_rows, :], axis=1, keepdims=True)
            r = factors[at_rows, 0:1]
            r_high, s_high = r.astype(BF).astype(F32), s.astype(BF).astype(F32)
            extras = jnp.where(lane == 0, r_high, jnp.where(lane == 1, r - r_high, 0.0))
            extras = jnp.where(lane == 2, s_high, jnp.where(lane == 3, s - s_high, extras))
            payload[at_rows, depth:] = extras.astype(BF)

        for store in stores:
            store.wait()


EDGE = 8


def pieces(v, count):
    out = []
    for _ in range(count):
        out.append(v.astype(BF))
        v = v - out[-1].astype(F32)
    return out


def exact(v, ones, dims, count=2):
    ones = ones.astype(BF)
    parts = [
        lax.dot_general(p, ones, (dims, ((), ())), preferred_element_type=F32)
        for p in pieces(v, count)
    ]
    return sum(parts[1:], parts[0])


def exact_right(ones, v, dims, count=2):
    ones = ones.astype(BF)
    parts = [
        lax.dot_general(ones, p, (dims, ((), ())), preferred_element_type=F32)
        for p in pieces(v, count)
    ]
    return sum(parts[1:], parts[0])


def iota(shape, axis):
    return lax.broadcasted_iota(jnp.int32, shape, axis)


class Block:
    def __init__(self, m, slot, start, proj, ext, lengths, taps, heads_vec, heads):
        loc = proj.shape[0]
        di = heads * PS
        width = di + 2 * S
        self.heads, self.di = heads, di
        first = lengths[m, 0]
        second = first + lengths[m, 1]

        def doc(p):
            return (p >= first).astype(jnp.int32) + (p >= second).astype(jnp.int32)

        self.doc = doc
        self.at = start + iota((loc, 1), 0)
        docs = doc(self.at)
        docs_row = doc(start + iota((1, loc), 1))
        last_doc, before_doc = doc(start + loc - 1), doc(start - 1)
        self.keep = (docs == before_doc).astype(F32)
        self.keep_last = (last_doc == before_doc).astype(F32)
        self.same_last = (docs == last_doc).astype(F32)
        self.gate = proj[:, :di]
        ext[slot, EDGE : EDGE + loc, :] = proj[:, di : di + width].astype(BF).astype(F32)
        total = jnp.broadcast_to(taps[K : K + 1, :], (loc, width))
        self.shifted = []
        for k in range(K):
            back = K - 1 - k
            value = ext[slot, EDGE - back : EDGE - back + loc, :]
            if back:
                value = value * (docs == doc(self.at - back)).astype(F32)
            self.shifted.append(value)
            total = total + taps[k : k + 1, :] * value
        self.sig = jax.nn.sigmoid(total)
        self.total = total
        filtered = total * self.sig
        self.x = filtered[:, :di]
        self.write = filtered[:, di : di + S].astype(BF)
        self.read = filtered[:, di + S :].astype(BF)
        self.raw = proj[:, di + width :] + heads_vec[0:1, :]
        self.steps = jnp.maximum(self.raw, 0.0) + jnp.log1p(jnp.exp(-jnp.abs(self.raw)))
        self.rate = heads_vec[1:2, :]
        rise = self.steps * self.rate
        rows, cols = iota((loc, loc), 0), iota((loc, loc), 1)
        self.lower = (cols <= rows).astype(F32)
        self.cum = exact_right(self.lower, rise, ((1,), (0,)), 3)
        cum_rows = exact(rise, (rows <= cols).astype(F32), ((0,), (0,)), 3)
        self.last = self.cum[loc - 1 : loc, :]
        self.grow = jnp.exp(self.cum) * self.keep
        self.fall = jnp.exp(self.last - self.cum) * self.same_last
        self.decay = jnp.exp(self.last) * self.keep_last
        allowed = (cols <= rows) & (docs == docs_row)
        scores = mm_nt(self.read, self.write)
        self.spread, self.mixing = [], []
        for h in range(heads):
            span = self.cum[:, h : h + 1] - cum_rows[h : h + 1, :]
            shape = jnp.exp(jnp.where(allowed, span, -1e30))
            self.spread.append(shape)
            self.mixing.append(shape * scores)
        self.lane = iota((1, di), 1)
        self.steps_wide = self.widen(self.steps)
        self.grow_wide = self.widen(self.grow)
        self.weight_wide = self.widen(self.fall * self.steps)
        self.scaled = self.x * self.steps_wide
        self.pushed = self.x * self.weight_wide

    def widen(self, v):
        out = jnp.broadcast_to(v[:, 0:1], (v.shape[0], self.di))
        for h in range(1, self.heads):
            out = jnp.where(self.lane >= h * PS, v[:, h : h + 1], out)
        return out

    def per_head(self, parts):
        out = parts[0]
        for h in range(1, self.heads):
            out = jnp.where(self.lane >= h * PS, parts[h], out)
        return out

    def decay_rows(self):
        rows = iota((self.di, 1), 0)
        out = jnp.broadcast_to(self.decay[:, 0:1], (self.di, 1))
        for h in range(1, self.heads):
            out = jnp.where(rows >= h * PS, self.decay[:, h : h + 1], out)
        return out


def load_weights(pieces_ref, w, sem):
    copies = [
        pltpu.make_async_copy(pieces_ref.at[k], w.at[:, k], sem.at[k]) for k in range(w.shape[1])
    ]
    for copy in copies:
        copy.start()
    for copy in copies:
        copy.wait()


class Forward(Task):
    def __init__(self, blocks, x, incoming, lengths, w_out, vectors, stream, gain, heads):
        self.heads = heads
        self.reaches = (("dp", True), ("expert", False))
        nd = lax.axis_size("dp")
        loc = stream.shape[0] // MB
        di = heads * PS
        wide = blocks.shape[2]
        shape = jax.ShapeDtypeStruct
        self.weights = Weights(blocks)
        self.gathers = [Gather("dp", v) for v in x] + [Gather("expert", incoming)]
        part = shape((nd, loc, D + 128), BF)
        self.reduces = [Reduce("dp", part) for _ in range(MB)]
        self.saved = (
            shape((MB, nd, loc, wide), F32),
            shape((MB, nd, loc, di), F32),
            shape((MB, nd, di, S), F32),
        )
        self.ins = (
            ((blocks, ANY),)
            + tuple((v, ANY) for v in (*x, incoming))
            + ((lengths, pl.BlockSpec(memory_space=pltpu.SMEM)),)
            + tuple((v, IN_VMEM) for v in (w_out,) + tuple(vectors) + (stream, gain))
        )
        full = self.weights.outs[1][0]
        rows = stream.shape[0]
        self.outs = (
            ((full, ANY),)
            + tuple((gather.outs[0][0], ANY) for gather in self.gathers)
            + tuple((v, ANY) for v in self.saved)
            + (
                (shape((rows, D), BF), IN_VMEM),
                (shape((rows, D), F32), IN_VMEM),
                (shape((rows, D), F32), IN_VMEM),
                (shape((rows, 128), F32), IN_VMEM),
            )
        )
        vmem = lambda v: pltpu.VMEM(v.shape, v.dtype)
        dma = pltpu.SemaphoreType.DMA
        slices = D // nd // full.shape[2]
        self.scratch = (
            (vmem(self.weights.outs[0][0]), vmem(full))
            + tuple(vmem(gather.outs[0][0]) for gather in self.gathers[:MB])
            + tuple(vmem(v) for v in self.saved)
            + tuple(vmem(part) for _ in range(MB))
            + tuple(pltpu.VMEM((loc, D + 128), F32) for _ in range(MB))
            + (pltpu.VMEM((nd, slices, full.shape[2], wide), BF), dma((slices,)), dma((9,)))
            + (pltpu.VMEM((2, loc + EDGE, di + 2 * S), F32), pltpu.VMEM((di, S), F32))
            + (pltpu.VMEM((4, loc, di), BF),)
            + self.weights.scratch
            + self.gathers[0].scratch
            + self.gathers[1].scratch
            + self.gathers[2].scratch
            + self.reduces[0].scratch
            + self.reduces[1].scratch
        )

    def steps(self, ins, outs, scratch):
        x, incoming, lengths = ins[1:3], ins[3], ins[4]
        w_out, taps, heads_vec, lanes_vec, stream, gain = ins[5:]
        w_full, g_out, inc_out, saved_out = outs[0], outs[1:3], outs[3], outs[4:7]
        low_out, after, mixed, factors = outs[7:]
        swapped, pieces_all = scratch[:2]
        g, (proj, scan, states), parts, totals = scratch[2:4], scratch[4:7], scratch[7:9], scratch[9:11]
        w, w_sem, sems, ext, state, gated = scratch[11:17]
        rest = scratch[17:]
        rest, weight_sems = rest[6:], rest[:6]
        gather_sems, rest = (rest[:3], rest[3:6], rest[6:9]), rest[9:]
        count = len(self.reduces[0].scratch)
        reduce_scratch = (rest[:count], rest[count:])
        heads = self.heads
        nd, loc, _ = g[0].shape
        di = heads * PS
        stores = []

        def store(src, dst):
            copy = pltpu.make_async_copy(src, dst, sems.at[len(stores)])
            copy.start()
            stores.append(copy)

        def work(m, start, end):
            many = end - start
            rows = g[m][start:end, :, :D].reshape(many * loc, D)
            value = mm(rows, w[...].reshape(D, -1))
            proj[m, start:end] = value.reshape(many, loc, value.shape[1])

            @pl.loop(start // 2, end // 2)
            def _(pair):
                for k in range(2):
                    b = pair * 2 + k
                    ext[k, 0:EDGE, :] = ext[1 - k, loc : loc + EDGE, :]
                    part = Block(
                        m, k, b * loc, proj[m, b], ext, lengths, taps, heads_vec, heads
                    )
                    before = state[...]
                    states[m, b] = before
                    scaled = part.scaled.astype(BF)
                    inner = part.per_head(
                        [mm(part.mixing[h].astype(BF), scaled) for h in range(heads)]
                    )
                    carried = mm_nt(part.read, before.astype(BF)) * part.grow_wide
                    out = inner + carried + lanes_vec[1:2, :] * part.x
                    scan[m, b] = out
                    state[...] = part.decay_rows() * before + mm_tn(
                        part.pushed.astype(BF), part.write
                    )
                    y = out * (part.gate * jax.nn.sigmoid(part.gate))
                    square = jnp.sum(y * y, axis=1, keepdims=True)
                    high = square.astype(BF).astype(F32)
                    gated[b - start] = (y * lanes_vec[0:1, :]).astype(BF)
                    column = iota((loc, 128), 1)
                    sums = jnp.where(column == 0, high, jnp.where(column == 1, square - high, 0.0))
                    parts[m][b, :, D:] = sums.astype(BF)

            value = mm(gated[...].reshape(many * loc, di), w_out[...])
            parts[m][start:end, :, :D] = value.astype(BF).reshape(many, loc, D)

        def reset():
            ext[...] = jnp.zeros_like(ext)
            state[...] = jnp.zeros_like(state)

        def norm(m):
            @chunks(loc, 16)
            def _(rows):
                at_rows = pl.ds(pl.multiple_of(m * loc + rows.start, 16), rows.size)
                lane = iota((1, 128), 1)
                total = totals[m]
                squares = total[rows, D:]
                square = jnp.sum(jnp.where(lane < 2, squares, 0.0), axis=1, keepdims=True)
                r = lax.rsqrt(square / DI + EPSILON)
                mix = total[rows, :D] * r
                v = stream[at_rows, :].astype(F32) + mix
                inv = lax.rsqrt(jnp.mean(v * v, axis=1, keepdims=True) + EPSILON)
                low_out[at_rows, :] = (v * inv * gain[...]).astype(BF)
                after[at_rows, :] = v
                mixed[at_rows, :] = mix
                factors[at_rows, :] = jnp.where(lane == 0, r, jnp.where(lane == 1, inv, 0.0))

        weights = self.weights.steps(ins[:1], (swapped, pieces_all), weight_sems)
        first = gather_steps("dp", x[0], g[0], *gather_sems[0])
        second = gather_steps("dp", x[1], g[1], *gather_sems[1])
        third = gather_steps("expert", incoming, inc_out, *gather_sems[2])
        next(weights)
        next(first)
        next(weights)
        next(weights, None)
        next(first)
        next(weights, None)
        next(first)
        next(second)
        next(weights, None)
        next(first)
        for _ in weights:
            pass
        for _ in first:
            pass
        load_weights(pieces_all, w, w_sem)
        store(pieces_all, w_full)
        store(g[0], g_out[0])
        reset()
        for k in range(4):
            next(third, None)
            work(0, 4 * k, 4 * k + 4)
            next(second, None)
        for steps in (second, third):
            for _ in steps:
                pass
        store(g[1], g_out[1])
        sums = [
            reduce_steps("dp", parts[m], totals[m], *reduce_scratch[m]) for m in range(MB)
        ]
        next(sums[0])
        for src, dst in zip((proj, scan, states), saved_out):
            store(src.at[0], dst.at[0])
        reset()
        for k in range(4):
            next(sums[0])
            work(1, 4 * k, 4 * k + 4)
        next(sums[1])
        for src, dst in zip((proj, scan, states), saved_out):
            store(src.at[1], dst.at[1])
        for _ in sums[0]:
            pass
        next(sums[1])
        norm(0)
        for _ in sums[1]:
            pass
        norm(1)
        for copy in stores:
            copy.wait()
        yield


def backward_kernel(
    heads,
    lengths,
    grad,
    w_pieces,
    w_out,
    taps,
    heads_vec,
    lanes_vec,
    proj,
    proj_before,
    scan,
    states,
    d_proj,
    normed_part,
    d_out,
    d_taps,
    d_heads,
    d_lanes,
    ext,
    d_ext,
    d_state,
    out_sum,
    w,
    w_sem,
):
    step = pl.program_id(0)
    b = pl.num_programs(0) - 1 - step
    loc = grad.shape[1] // MB
    di = heads * PS
    width = di + 2 * S

    @pl.when(step == 0)
    def _():
        for ref in (d_ext, d_state, out_sum, d_taps, d_heads, d_lanes):
            ref[...] = jnp.zeros_like(ref)
        load_weights(w_pieces, w, w_sem)

    gated_grad = mm_nt(grad[0, :, :D], w_out[...])
    extra = grad[0, :, D:].astype(F32)
    has_before = (b > 0).astype(F32)
    pick = (iota((di, S), 0) // PS == iota((di, S), 1)).astype(F32)
    for m in range(MB):
        rows = slice(m * loc, (m + 1) * loc)
        edge = proj_before[m, 0, loc - EDGE : loc, di : di + width]
        ext[m, 0:EDGE, :] = edge.astype(BF).astype(F32) * has_before
        part = Block(m, m, b * loc, proj[m, 0], ext, lengths, taps, heads_vec, heads)
        gain, skip = lanes_vec[0:1, :], lanes_vec[1:2, :]
        r = extra[rows, 0:1] + extra[rows, 1:2]
        s = extra[rows, 2:3] + extra[rows, 3:4]
        out = scan[m, 0]
        sig = jax.nn.sigmoid(part.gate)
        act = part.gate * sig
        yr = out * act * r
        gg = gated_grad[rows]
        d_lanes[0:1, :] += jnp.sum(gg * yr, axis=0, keepdims=True)
        out_sum[...] += mm_tn((yr * gain).astype(BF), grad[0, rows, :D])
        dy = r * (gg * gain) - yr * (r * s / DI)
        d_gate = dy * out * (sig + act * (1.0 - sig))
        do = dy * act
        do_low = do.astype(BF)
        x = part.x
        d_lanes[1:2, :] += jnp.sum(do * x, axis=0, keepdims=True)
        dx = skip * do
        before = states[m, 0]
        before_low = before.astype(BF)
        ds = d_state[m]
        ds_low = ds.astype(BF)

        d_scores = jnp.zeros((loc, loc), F32)
        d_scaled, d_cum = [], jnp.zeros((loc, S), F32)
        head_lane = iota((loc, S), 1)
        for h in range(heads):
            inside = (part.lane >= h * PS) & (part.lane < (h + 1) * PS)
            own = jnp.where(inside, part.scaled, 0.0).astype(BF)
            d_mix = mm_nt(do_low, own)
            d_scaled.append(mm_tn(part.mixing[h].astype(BF), do_low))
            d_scores = d_scores + d_mix * part.spread[h]
            d_span = d_mix * part.mixing[h]
            ones = (head_lane == h).astype(F32)
            d_cum = d_cum + exact(d_span, ones, ((1,), (0,))) - exact(d_span, ones, ((0,), (0,)))
        d_scaled = part.per_head(d_scaled)
        dx = dx + d_scaled * part.steps_wide
        d_scores_low = d_scores.astype(BF)
        d_read = mm(d_scores_low, part.write)
        d_write = mm_tn(d_scores_low, part.read)

        d_carry = do * part.grow_wide
        d_carry_low = d_carry.astype(BF)
        carried = mm_nt(part.read, before_low)
        d_read = d_read + mm(d_carry_low, before_low)

        d_pushed = mm_nt(part.write, ds_low)
        d_write = d_write + mm(part.pushed.astype(BF), ds_low)
        dx = dx + d_pushed * part.weight_wide
        sums = exact(
            jnp.concatenate([d_carry * carried, d_pushed * x, d_scaled * x], axis=0),
            pick,
            ((1,), (0,)),
        )
        d_weight = sums[loc : 2 * loc]
        d_fall = d_weight * part.fall * part.steps
        d_cum = d_cum + sums[:loc] - d_fall
        d_steps = sums[2 * loc :] + d_weight * part.fall
        state_dot = jnp.sum(ds * before, axis=1, keepdims=True)
        d_decay = exact(jnp.broadcast_to(state_dot, (di, S)), pick, ((0,), (0,)))[0:1, :]
        d_last = jnp.sum(d_fall, axis=0, keepdims=True) + d_decay * part.decay
        d_cum = d_cum + jnp.where(iota((loc, 1), 0) == loc - 1, d_last, 0.0)
        d_state[m] = part.decay_rows() * ds + mm_tn(d_carry_low, part.read)

        d_rise = exact_right(part.lower, d_cum, ((0,), (0,)))
        d_steps = d_steps + d_rise * part.rate
        d_raw = d_steps * jax.nn.sigmoid(part.raw)
        d_heads[0:1, :] += jnp.sum(d_raw, axis=0, keepdims=True)
        d_heads[1:2, :] += jnp.sum(d_rise * part.steps * part.rate, axis=0, keepdims=True)

        d_total = jnp.concatenate([dx, d_write, d_read], axis=1)
        d_total = d_total * (part.sig + part.total * part.sig * (1.0 - part.sig))
        for k in range(K):
            d_taps[k : k + 1, :] += jnp.sum(d_total * part.shifted[k], axis=0, keepdims=True)
        d_taps[K : K + 1, :] += jnp.sum(d_total, axis=0, keepdims=True)
        d_ext[m, loc : loc + EDGE, :] = d_ext[m, 0:EDGE, :]
        d_ext[m, 0:loc, :] = d_total
        d_seq = taps[K - 1 : K, :] * d_total
        docs = part.doc(part.at)
        for ahead in range(1, K):
            same = (docs == part.doc(part.at + ahead)).astype(F32)
            d_seq = d_seq + taps[K - 1 - ahead : K - ahead, :] * (
                same * d_ext[m, ahead : ahead + loc, :]
            )
        d_proj[0, rows, :di] = d_gate.astype(BF)
        d_proj[0, rows, di : di + width] = d_seq.astype(BF)
        d_proj[0, rows, di + width :] = jnp.where(head_lane < heads, d_raw, 0.0).astype(BF)
    for half in range(2):
        d_out[half] = out_sum[:, half * D // 2 : (half + 1) * D // 2].astype(BF)
    normed_part[0] = mm_nt(d_proj[0], w[...].reshape(D, -1)).astype(BF)


def weight_scratch(w):
    slices = D // w.shape[1] // w.shape[2]
    return [
        pltpu.VMEM((w.shape[1], slices) + w.shape[2:], BF),
        pltpu.SemaphoreType.DMA((slices,)),
    ]


def block_spec(shape, index):
    return pl.BlockSpec((1,) + shape[1:], lambda i: (index(i),) + (0,) * (len(shape) - 1))


def pair_spec(shape, index):
    return pl.BlockSpec((MB, 1) + shape[2:], lambda i: (0, index(i)) + (0,) * (len(shape) - 2))


def whole_spec(shape):
    return pl.BlockSpec(shape, lambda i: (0,) * len(shape))


def mixer_backward(lengths, grad, w, w_out, taps, heads_vec, lanes_vec, proj, scan, states, heads):
    nb, rows, _ = grad.shape
    di = heads * PS
    width = di + 2 * S
    back = lambda i: nb - 1 - i
    before = lambda i: jnp.maximum(nb - 2 - i, 0)
    per_block = [
        jax.ShapeDtypeStruct((nb, rows, w.shape[-1]), BF),
        jax.ShapeDtypeStruct((nb, rows, D), BF),
    ]
    sums = [
        jax.ShapeDtypeStruct((2, di, D // 2), BF),
        jax.ShapeDtypeStruct((8, width), F32),
        jax.ShapeDtypeStruct((8, S), F32),
        jax.ShapeDtypeStruct((8, di), F32),
    ]
    return pl.pallas_call(
        functools.partial(backward_kernel, heads),
        grid=(nb,),
        out_shape=per_block + sums,
        in_specs=[pl.BlockSpec(memory_space=pltpu.SMEM), block_spec(grad.shape, back)]
        + [pl.BlockSpec(memory_space=pl.ANY)]
        + [whole_spec(v.shape) for v in (w_out, taps, heads_vec, lanes_vec)]
        + [pair_spec(proj.shape, back), pair_spec(proj.shape, before)]
        + [pair_spec(scan.shape, back), pair_spec(states.shape, back)],
        out_specs=[block_spec(v.shape, back) for v in per_block]
        + [whole_spec(v.shape) for v in sums],
        scratch_shapes=[
            pltpu.VMEM((MB, rows // MB + EDGE, width), F32),
            pltpu.VMEM((MB, rows // MB + EDGE, width), F32),
            pltpu.VMEM((MB, di, S), F32),
            pltpu.VMEM((di, D), F32),
        ]
        + weight_scratch(w),
        compiler_params=pltpu.CompilerParams(vmem_limit_bytes=VMEM_LIMIT),
        name="mixer_backward",
    )(lengths, grad, w, w_out, taps, heads_vec, lanes_vec, proj, proj, scan, states)


def body(
    tokens,
    lengths,
    routes,
    cotangent,
    input_weight,
    filter_weight,
    filter_bias,
    step_bias,
    decay_log,
    skip_gain,
    norm_gain,
    gated_gain,
    output_weight,
    moe_gain,
    router_weight,
    shared_gate_up,
    shared_down,
    expert_gate_up,
    expert_down,
):
    nd, ne = lax.axis_size("dp"), lax.axis_size("expert")
    me_d, me_e = lax.axis_index("dp"), lax.axis_index("expert")
    loc = tokens.shape[2]
    heads = H // nd
    di = heads * PS
    rows_t = MB * loc
    experts = expert_gate_up.shape[0] * ne
    el = expert_gate_up.shape[0]
    dr = D // nd
    fs = FS // ne
    fsr = FS // nd
    fsl = fsr // ne

    pad = 128 - heads
    piece = 16
    place = jnp.minimum(me_e, dr // piece - 1) * piece
    mine = lax.dynamic_slice_in_dim(input_weight, place, piece, 0)
    blocks = jnp.concatenate(
        [
            jnp.moveaxis(mine[:, :DI].reshape(piece, nd, di), 1, 0),
            jnp.moveaxis(mine[:, DI : 2 * DI].reshape(piece, nd, di), 1, 0),
            jnp.broadcast_to(mine[None, :, 2 * DI : 2 * DI + 2 * S], (nd, piece, 2 * S)),
            jnp.moveaxis(mine[:, DI + CONV :].reshape(piece, nd, heads), 1, 0),
            jnp.zeros((nd, piece, pad), BF),
        ],
        axis=2,
    )
    wcols = blocks.shape[2]

    sg = shared_gate_up.reshape(dr, 2, nd, ne, fsl)
    sg = lax.dynamic_index_in_dim(sg, me_e, 3, False).reshape(dr, 2 * fs)
    sd = lax.dynamic_slice_in_dim(shared_down, me_e * fsl, fsl, 0)
    packed = jnp.concatenate([sg.reshape(-1), sd.reshape(-1), router_weight.reshape(-1)])
    packed_cols = packed.size // loc
    packed = jnp.pad(packed.reshape(loc, -1), ((0, 0), (0, -packed_cols % 128)))

    stream = tokens.reshape(rows_t, D).astype(F32)
    incoming = cotangent.reshape(rows_t, D)
    route_rows = routes.reshape(rows_t, TOP)
    normed = rms_scale(stream, norm_gain).astype(BF)
    taps = jnp.concatenate(
        [lax.dynamic_slice_in_dim(filter_weight, me_d * di, di, 1), filter_weight[:, DI:]], axis=1
    )
    tap_bias = jnp.concatenate(
        [lax.dynamic_slice_in_dim(filter_bias, me_d * di, di, 0), filter_bias[DI:]], axis=0
    )
    my_heads = lambda v: lax.dynamic_slice_in_dim(v, me_d * heads, heads, 0)
    my_gain = lax.dynamic_slice_in_dim(gated_gain, me_d * di, di, 0)

    taps_vec = jnp.concatenate([taps, tap_bias[None], jnp.zeros((3, di + 2 * S), F32)], axis=0)
    heads_vec = jnp.stack([my_heads(step_bias), -jnp.exp(my_heads(decay_log))])
    heads_vec = jnp.pad(heads_vec, ((0, 6), (0, S - heads)))
    lanes_vec = jnp.pad(
        jnp.stack([my_gain, jnp.repeat(my_heads(skip_gain), PS)]), ((0, 6), (0, 0))
    )
    vectors = (taps_vec, heads_vec, lanes_vec)
    gain_row = moe_gain.reshape(1, D)
    own_tokens = tokens.reshape(rows_t, D)
    forward = Forward(
        blocks,
        (normed[:loc], jnp.concatenate([normed[loc:], packed], axis=1)),
        incoming,
        lengths[:, 0],
        output_weight,
        vectors,
        own_tokens,
        gain_row,
        heads,
    )
    (results,) = run_tasks([forward], 1, "forward")
    w_in, *gathered, inc_all, proj, scan, states, moe_in, after_mixer, mixed, factors = results
    inc_all = inc_all.reshape(ne * rows_t, D)
    packed_all = gathered[1][:, :, D : D + packed_cols]
    packed_all = packed_all.reshape(nd, -1)
    sg_full = packed_all[:, : sg.size].reshape(D, 2 * fs)
    sd_full = packed_all[:, sg.size : sg.size + sd.size].reshape(fs, D)
    router_full = packed_all[:, sg.size + sd.size :].reshape(D, experts)
    mask = jnp.sum(
        (route_rows[:, :, None] == jnp.arange(128, dtype=jnp.int32)).astype(F32), axis=1
    )
    router_wide = jnp.pad(router_full, ((0, 0), (0, 128 - experts)))
    ((moe_all, pre_grad, gh, out_part, after_grad, grad_payload, moe_gain_grad, router_part),) = (
        run_tasks(
            [
                Experts(
                    moe_in,
                    mask,
                    inc_all,
                    expert_gate_up,
                    expert_down,
                    sg_full,
                    sd_full,
                    after_mixer,
                    mixed,
                    factors,
                    gain_row,
                    router_wide,
                    incoming,
                )
            ],
            3,
            "experts",
        )
    )
    width = gh.shape[2]
    (out_sum,), (grad_blocks,), (grad_all,) = run_tasks(
        [
            Reduce("expert", out_part),
            ExpertGrads(moe_all, pre_grad, gh, inc_all, el, FE, nd),
            Gather("dp", grad_payload),
        ],
        5,
        "gather_grad",
    )
    all_sum = lax.psum_scatter(grad_blocks, "dp", scatter_dimension=0, tiled=True)[0]
    up_sum = all_sum[:dr]
    each, span = FE // nd, D // 2
    down_sum = all_sum[dr : dr + each]
    last_sum = all_sum[dr + each :]
    d_proj, normed_part, output_part, d_taps, d_heads, d_lanes = mixer_backward(
        lengths[:, 0], grad_all, w_in, output_weight, *vectors, proj, scan, states, heads
    )
    def rows_of(parts, count):
        flat = jnp.concatenate([part.reshape(-1) for part in parts])
        return jnp.pad(flat, (0, count * 128 - flat.size)).reshape(count, 128)

    added = (d_taps[:K, di:], d_taps[K, di:], moe_gain_grad, router_part)
    own = (
        d_taps[:K, :di],
        d_taps[K, :di],
        d_heads[0, :heads],
        d_heads[1, :heads],
        jnp.sum(d_lanes[1].reshape(heads, PS), axis=1),
        d_lanes[0],
    )
    added_size = sum(part.size for part in added)
    added_rows = -(-added_size // (nd * 1024)) * 8
    own_rows = -(-sum(part.size for part in own) // 128)
    norm_rows = D // 128
    (tokens_grad, norm_gain_grad), (d_sum,), (added_in,) = run_tasks(
        [
            StreamGrad(normed_part, own_tokens, norm_gain.reshape(1, D), after_grad),
            InputGrad(
                gathered,
                d_proj.reshape(nd * rows_t, wcols),
                output_part,
            ),
            Direct("all", "dp", rows_of(added, nd * added_rows).reshape(nd, added_rows, 128)),
        ],
        6,
        "reduce_grads",
    )
    small = jnp.concatenate(
        [jnp.sum(added_in, axis=0), rows_of(own, own_rows), rows_of((norm_gain_grad,), norm_rows)],
        axis=0,
    )
    small = jnp.pad(small, ((0, -small.shape[0] % 8), (0, 0)))
    shared_part = jnp.concatenate(
        [up_sum[:, 2 * el * FE :], last_sum[:fsl, span:].reshape(dr, -1)], axis=1
    ).reshape(-1, wcols)
    main_rows = D // ne
    (small_all,), (rest_all,), (input_grad,) = run_tasks(
        [
            Small(small),
            Gather("expert", jnp.concatenate([d_sum[main_rows:], shared_part], axis=0)),
            InputRows(d_sum[:main_rows], heads),
        ],
        7,
        "finish",
    )
    cut_rows = d_sum.shape[0] - main_rows
    output_grad = rest_all[:, :cut_rows].reshape(2, di, D // 2)
    output_grad = jnp.moveaxis(output_grad, 0, 1).reshape(output_weight.shape)
    shared_all = rest_all[:, cut_rows:].reshape(ne, dr, -1)
    added_all = small_all[:, :added_rows].reshape(-1)
    own_all = small_all[:, added_rows : added_rows + own_rows].reshape(nd, -1)
    norm_gain_grad = jnp.sum(
        small_all[:, added_rows + own_rows : added_rows + own_rows + norm_rows], axis=0
    ).reshape(D)

    def split(flat, parts):
        out, start = [], 0
        for part in parts:
            out.append(flat[..., start : start + part.size].reshape(flat.shape[:-1] + part.shape))
            start += part.size
        return out

    added_taps, added_bias, moe_gain_grad, router_all = split(added_all, added)
    own_taps, own_bias, own_steps, own_decay, own_skip, own_gain = split(own_all, own)
    small = (
        jnp.concatenate([jnp.moveaxis(own_taps, 0, 1).reshape(K, DI), added_taps], axis=1),
        jnp.concatenate([own_bias.reshape(-1), added_bias]),
        own_steps.reshape(-1),
        own_decay.reshape(-1),
        own_skip.reshape(-1),
        norm_gain_grad,
        own_gain.reshape(-1),
        moe_gain_grad.reshape(D),
    )
    router_grad = lax.dynamic_slice_in_dim(router_all, me_d * dr, dr, 1).T
    expert_up_grad = jnp.moveaxis(up_sum[:, : 2 * el * FE].reshape(dr, el, 2 * FE), 1, 0)
    expert_up_grad = expert_up_grad.astype(F32)
    expert_down_grad = jnp.stack(
        [
            down_sum[:, : 2 * span],
            jnp.concatenate([down_sum[:, 2 * span :], last_sum[:, :span]], axis=1),
        ],
        axis=0,
    ).astype(F32)
    shared_up_grad = (
        jnp.moveaxis(shared_all[:, :, : 2 * fs].reshape(ne, dr, 2, nd, fsl), 0, 3)
        .reshape(dr, 2 * FS)
        .astype(F32)
    )
    shared_down_grad = shared_all[:, :, 2 * fs :].reshape(fsr, D).astype(F32)
    block_output = (after_mixer + out_sum).astype(BF)
    shape = (MB, 1, loc, D)
    return (
        block_output.reshape(shape),
        tokens_grad.reshape(shape),
        input_grad,
        small[0],
        small[1],
        small[2],
        small[3],
        small[4],
        small[5],
        small[6],
        output_grad.astype(F32),
        small[7],
        router_grad,
        shared_up_grad,
        shared_down_grad,
        expert_up_grad,
        expert_down_grad,
    )


def solution(mesh):
    in_specs = (
        P(None, "expert", "dp", None),
        P(None, "expert", None),
        P(None, "expert", "dp", None),
        P(None, "expert", "dp", None),
        P("dp", None),
        P(),
        P(),
        P(),
        P(),
        P(),
        P(),
        P(),
        P("dp", None),
        P(),
        P("dp", None),
        P("dp", None),
        P("dp", None),
        P("expert", None, None),
        P("expert", None, None),
    )
    out_specs = (
        P(None, "expert", "dp", None),
        P(None, "expert", "dp", None),
        P("dp", None),
        P(),
        P(),
        P(),
        P(),
        P(),
        P(),
        P(),
        P("dp", None),
        P(),
        P("dp", None),
        P("dp", None),
        P("dp", None),
        P("expert", "dp", None),
        P("expert", "dp", None),
    )
    return jax.shard_map(body, mesh=mesh, in_specs=in_specs, out_specs=out_specs, check_vma=False)
```

```python
import functools

import jax
import jax.numpy as jnp
from jax import lax
from jax.experimental import pallas as pl
from jax.experimental.pallas import tpu as pltpu
from jax.sharding import PartitionSpec as P

D = 1536
H = 48
PS = 64
S = 128
K = 4
FE = 512
FS = 1024
TOP = 6
MB = 2
DI = 3072
CONV = 3328
IN_W = 6448
EPSILON = 1e-05
BF = jnp.bfloat16
F32 = jnp.float32
MESH = pl.DeviceIdType.MESH
VMEM_LIMIT = 60 * 1024 * 1024


def mm(a, b):
    return jnp.dot(a, b, preferred_element_type=F32)


def mm_nt(a, b):
    return lax.dot_general(a, b, (((1,), (1,)), ((), ())), preferred_element_type=F32)


def mm_tn(a, b):
    return lax.dot_general(a, b, (((0,), (0,)), ((), ())), preferred_element_type=F32)


def rms_scale(values, gain):
    return values * lax.rsqrt(jnp.mean(values * values, axis=-1, keepdims=True) + EPSILON) * gain


ANY = pl.BlockSpec(memory_space=pl.ANY)
IN_VMEM = pl.BlockSpec(memory_space=pltpu.VMEM)


def places(axis):
    me = lax.axis_index(axis)
    if axis == "dp":
        core, ring, pair = lax.rem(me, 2), lax.rem(me // 2, 4), me // 8

        def at(hop, other, sibling=0):
            z = lax.rem(pair + other, 2)
            return (z * 4 + lax.rem(ring + hop + 4, 4)) * 2 + lax.rem(core + sibling, 2)
    else:
        pair, ring = lax.rem(me, 2), me // 2

        def at(hop, other, sibling=0):
            return lax.rem(ring + hop + 4, 4) * 2 + lax.rem(pair + other, 2)

    return me, at


class Task:
    ins, outs, scratch, reaches, turns = (), (), (), (), 1

    def greet(self, barrier):
        return 0


def peers_of(axis, everyone):
    me, at = places(axis)
    if everyone:
        n = lax.axis_size(axis)
        return [lax.rem(me + k, n) for k in range(1, n)]
    near = [at(1, 0), at(-1, 0), at(0, 1)]
    return near + [at(0, 0, 1)] if axis == "dp" else near


class Links:
    def __init__(self, axis, send, recv):
        self.axis, self.send, self.recv, self.started = axis, send, recv, []

    def push(self, number, src, dst, peer):
        copy = pltpu.make_async_remote_copy(
            src_ref=src,
            dst_ref=dst,
            send_sem=self.send.at[number],
            recv_sem=self.recv.at[number],
            device_id={self.axis: peer},
            device_id_type=MESH,
        )
        copy.start()
        self.started.append(copy)

    def arrived(self, number, dst):
        pltpu.make_async_copy(dst, dst, self.recv.at[number]).wait()

    def finish(self):
        for copy in self.started:
            copy.wait_send()


def halves(shape):
    rows = shape[0]
    cut = rows // 2 if len(shape) == 3 else rows // 32 * 16
    return pl.ds(0, rows), pl.ds(0, cut), pl.ds(cut, rows - cut), cut


class Gather(Task):
    def __init__(self, axis, x):
        self.axis, self.reaches = axis, ((axis, False),)
        self.ins = ((x, ANY),)
        n = lax.axis_size(axis)
        self.outs = ((jax.ShapeDtypeStruct((n,) + x.shape, x.dtype), ANY),)
        dma = pltpu.SemaphoreType.DMA
        self.scratch = (dma((17,)), dma((17,)), dma)

    def steps(self, ins, outs, scratch):
        return gather_steps(self.axis, ins[0], outs[0], *scratch)


def gather_steps(axis, x, out, send, recv, own_sem):
    me, at = places(axis)
    cores = axis == "dp"
    up, down, pair, sib = at(1, 0), at(-1, 0), at(0, 1), at(0, 0, 1)
    whole, first, second, _ = halves(x.shape)
    links = Links(axis, send, recv)

    def push(number, slot, rows, peer, src=None):
        src = out.at[slot] if src is None else src
        links.push(number, src.at[rows], out.at[slot].at[rows], peer)

    def arrived(number, slot, rows):
        links.arrived(number, out.at[slot].at[rows])

    push(0, me, whole, up, x)
    push(1, me, whole, down, x)
    push(2, me, whole, pair, x)
    if cores:
        push(3, me, whole, sib, x)
    own = pltpu.make_async_copy(x, out.at[me], own_sem)
    own.start()
    yield
    own.wait()
    arrived(2, pair, whole)
    push(4, pair, whole, up)
    push(5, pair, whole, down)
    arrived(0, down, whole)
    push(7, down, first, up)
    arrived(1, up, whole)
    push(8, up, second, down)
    if cores:
        push(6, pair, whole, sib)
        push(9, down, whole, sib)
        push(10, up, whole, sib)
    yield
    arrived(4, at(-1, 1), whole)
    push(11, at(-1, 1), first, up)
    arrived(5, at(1, 1), whole)
    push(12, at(1, 1), second, down)
    arrived(7, at(2, 0), first)
    arrived(8, at(2, 0), second)
    if cores:
        push(13, at(-1, 1), whole, sib)
        push(14, at(1, 1), whole, sib)
        push(15, at(2, 0), whole, sib)
    yield
    arrived(11, at(2, 1), first)
    arrived(12, at(2, 1), second)
    if cores:
        push(16, at(2, 1), whole, sib)
        yield
        for number, hop, other in (
            (3, 0, 0),
            (6, 0, 1),
            (9, -1, 0),
            (10, 1, 0),
            (13, -1, 1),
            (14, 1, 1),
            (15, 2, 0),
            (16, 2, 1),
        ):
            arrived(number, at(hop, other, 1), whole)
    links.finish()


ORDER = ((2, 1), (2, 0), (1, 1), (-1, 1), (1, 0), (-1, 0), (0, 1), (0, 0))


class Reduce(Task):
    def __init__(self, axis, x, dtype=F32):
        self.axis, self.reaches = axis, ((axis, False),)
        n, rows, columns = x.shape
        self.ins = ((x, ANY),)
        self.outs = ((jax.ShapeDtypeStruct((rows, columns), dtype), IN_VMEM),)
        _, _, _, cut = halves((rows, columns))
        buf = lambda *dims: pltpu.VMEM(dims + (columns,), BF)
        dma = pltpu.SemaphoreType.DMA
        dp = axis == "dp"
        self.scratch = (
            buf(8, rows),
            buf(8 if dp else 1, rows if dp else 16),
            buf(2, cut),
            buf(2, rows - cut),
            buf(2, rows),
            buf(2, rows),
            buf(rows),
            dma((17,)),
            dma((17,)),
            dma((8,)),
        )

    def steps(self, ins, outs, scratch):
        return reduce_steps(self.axis, ins[0], outs[0], *scratch)


def reduce_steps(axis, x, out, acc, sib_buf, a_buf, b_buf, c_buf, d_buf, e_buf, send, recv, load):
    me, at = places(axis)
    cores = axis == "dp"
    rows = acc.shape[1]
    widest = lambda count: max(k for k in range(16, 129, 16) if count % k == 0)
    block = lambda k: x.at[k] if len(x.shape) == 3 else x.at[pl.ds(pl.multiple_of(k * rows, 16), rows)]
    up, down, pair, sib = at(1, 0), at(-1, 0), at(0, 1), at(0, 0, 1)
    whole, first, second, cut = halves(acc.shape[1:])
    links = Links(axis, send, recv)
    push, arrived = links.push, links.arrived

    def add(dst, offset, count, *srcs):
        step = widest(count)

        @pl.loop(0, count // step)
        def _(i):
            at_rows = pl.ds(pl.multiple_of(offset + i * step, 16), step)
            total = dst[at_rows, :].astype(F32)
            for src in srcs:
                total += src[pl.ds(pl.multiple_of(i * step, 16), step), :].astype(F32)
            dst[at_rows, :] = total.astype(dst.dtype)

    loads = []
    for k, (hop, other) in enumerate(ORDER if x is not None else ()):
        if cores:
            push(k, block(at(hop, other, 1)), sib_buf.at[k], sib)
        copy = pltpu.make_async_copy(block(at(hop, other)), acc.at[k], load.at[k])
        copy.start()
        loads.append(copy)

    def ready(k):
        if loads:
            loads[k].wait()
        if cores:
            arrived(k, sib_buf.at[k])
            add(acc.at[k], 0, rows, sib_buf.at[k])

    yield
    for k in range(2):
        ready(k)
        push(8 + 2 * k, acc.at[k].at[first], a_buf.at[k], up)
        push(9 + 2 * k, acc.at[k].at[second], b_buf.at[k], down)
    yield
    for k in range(2):
        above, below = 2 + 2 * k, 3 + 2 * k
        ready(above)
        ready(below)
        arrived(8 + 2 * k, a_buf.at[k])
        add(acc.at[above], 0, cut, a_buf.at[k])
        push(12 + 2 * k, acc.at[above], c_buf.at[k], up)
        arrived(9 + 2 * k, b_buf.at[k])
        add(acc.at[below], cut, rows - cut, b_buf.at[k])
        push(13 + 2 * k, acc.at[below], d_buf.at[k], down)
    yield
    ready(6)
    ready(7)
    arrived(12, c_buf.at[0])
    arrived(13, d_buf.at[0])
    add(acc.at[6], 0, rows, c_buf.at[0], d_buf.at[0])
    push(16, acc.at[6], e_buf, pair)
    yield
    arrived(14, c_buf.at[1])
    arrived(15, d_buf.at[1])
    yield
    arrived(16, e_buf)
    step = widest(rows)

    @pl.loop(0, rows // step)
    def _(i):
        at_rows = pl.ds(pl.multiple_of(i * step, 16), step)
        total = acc[7, at_rows, :].astype(F32) + c_buf[1, at_rows, :].astype(F32)
        total += d_buf[1, at_rows, :].astype(F32) + e_buf[at_rows, :].astype(F32)
        out[at_rows, :] = total.astype(out.dtype)

    links.finish()


class Direct(Task):
    def __init__(self, kind, axis, x):
        self.kind, self.axis, self.reaches = kind, axis, ((axis, True),)
        n = lax.axis_size(axis)
        shape = (n,) + x.shape if kind == "gather" else x.shape
        self.ins = ((x, ANY),)
        self.outs = ((jax.ShapeDtypeStruct(shape, x.dtype), ANY),)
        dma = pltpu.SemaphoreType.DMA
        self.scratch = (dma((n,)), dma((n,)), dma)

    def steps(self, ins, outs, scratch):
        return direct_steps(self.kind, self.axis, ins[0], outs[0], *scratch)


def direct_steps(kind, axis, x, out, send, recv, own_sem):
    n, me = lax.axis_size(axis), lax.axis_index(axis)
    links = Links(axis, send, recv)
    piece = lambda k: x if kind == "gather" else x.at[k]
    for k in range(1, n):
        peer = lax.rem(me + k, n)
        links.push(k, piece(peer), out.at[me], peer)
    own = pltpu.make_async_copy(piece(me), out.at[me], own_sem)
    own.start()
    yield
    for k in range(1, n):
        links.arrived(k, out.at[lax.rem(me - k + n, n)])
    own.wait()
    links.finish()


def run_tasks(tasks, number, name):
    operands, in_specs, out_shapes, out_specs, scratch, spans = [], [], [], [], [], []
    for task in tasks:
        spans.append((len(operands), len(out_shapes), len(scratch)))
        operands += [x for x, _ in task.ins]
        in_specs += [spec for _, spec in task.ins]
        out_shapes += [shape for shape, _ in task.outs]
        out_specs += [spec for _, spec in task.outs]
        scratch += list(task.scratch)

    def kernel(*refs):
        ins = refs[: len(operands)]
        outs = refs[len(operands) : len(operands) + len(out_shapes)]
        temps = refs[len(operands) + len(out_shapes) :]
        barrier = pltpu.get_barrier_semaphore()
        count = 0
        for axis in ("dp", "expert"):
            here = [everyone for task in tasks for name, everyone in task.reaches if name == axis]
            if here:
                peers = peers_of(axis, any(here))
                for peer in peers:
                    pl.semaphore_signal(
                        barrier, inc=1, device_id={axis: peer}, device_id_type=MESH
                    )
                count += len(peers)
        for task in tasks:
            count += task.greet(barrier)
        pl.semaphore_wait(barrier, count)
        running = []
        for task, (i, o, s) in zip(tasks, spans):
            steps = task.steps(
                ins[i : i + len(task.ins)],
                outs[o : o + len(task.outs)],
                temps[s : s + len(task.scratch)],
            )
            running.append((task.turns, steps))
        while running:
            left = []
            for turns, steps in running:
                if all(next(steps, "end") != "end" for _ in range(turns)):
                    left.append((turns, steps))
            running = left

    results = pl.pallas_call(
        kernel,
        out_shape=out_shapes,
        in_specs=in_specs,
        out_specs=out_specs,
        scratch_shapes=scratch,
        compiler_params=pltpu.CompilerParams(
            collective_id=number, has_side_effects=True, vmem_limit_bytes=VMEM_LIMIT
        ),
        name=name,
    )(*operands)
    return [results[o : o + len(task.outs)] for task, (_, o, _) in zip(tasks, spans)]


class Weights(Task):
    def __init__(self, x):
        self.reaches = (("dp", True), ("expert", False))
        self.swap, self.spread = Direct("all", "dp", x), Gather("expert", x)
        n = lax.axis_size("expert")
        full = jax.ShapeDtypeStruct((n,) + x.shape, x.dtype)
        self.ins = ((x, ANY),)
        self.outs = self.swap.outs + ((full, ANY),)
        self.scratch = self.swap.scratch + self.spread.scratch

    def steps(self, ins, outs, scratch):
        yield from direct_steps("all", "dp", ins[0], outs[0], *scratch[:3])
        yield
        yield from gather_steps("expert", outs[0], outs[1], *scratch[3:])


class ExpertGrads(Task):
    def __init__(self, x, pre_grad, gh, inc, experts, each, blocks):
        n, rows, _ = x.shape
        width, depth = gh.shape[2], inc.shape[1]
        self.experts, self.each = experts, each
        grads = jax.ShapeDtypeStruct(
            (blocks, depth // blocks + 2 * (each // blocks), 2 * width), BF
        )
        self.ins = tuple((v, ANY) for v in (x, pre_grad, gh, inc))
        self.outs = ((grads, ANY),)
        dma = pltpu.SemaphoreType.DMA
        vmem = lambda *dims: pltpu.VMEM(dims, BF)
        self.scratch = (
            vmem(n, rows, depth),
            vmem(*pre_grad.shape),
            vmem(*gh.shape),
            vmem(*inc.shape),
            dma((5,)),
            vmem(depth, n * rows),
            vmem(width, n * rows),
            vmem(*grads.shape),
        )

    def steps(self, ins, outs, scratch):
        x, pre_grad, gh, inc, sems, x_t, gh_t, grads = scratch
        n, rows, depth = x.shape
        width = gh.shape[2]
        experts, each = self.experts, self.each
        copy = lambda src, dst, k: pltpu.make_async_copy(src, dst, sems.at[k])
        load_x = copy(ins[0].at[:, :, pl.ds(0, depth)], x, 0)
        load_pre = copy(ins[1], pre_grad, 1)
        load_inc = copy(ins[3], inc, 3)
        load_gh = copy(ins[2], gh, 2)
        for load in (load_x, load_pre, load_gh, load_inc):
            load.start()
        yield
        tile = 256
        col = lambda i: pl.ds(pl.multiple_of(i * tile, tile), tile)
        load_x.wait()

        @pl.loop(0, depth // tile)
        def _(i):
            x_t[col(i), :] = x[:, :, col(i)].reshape(n * rows, tile).T

        load_pre.wait()
        blocks = grads.shape[0]
        up_rows = depth // blocks
        steps = 2 * width // tile
        for start, end in ((0, steps // 3), (steps // 3, steps)):

            @pl.loop(start, end)
            def _(i):
                value = mm(x_t[...], pre_grad[:, :, col(i)].reshape(n * rows, tile)).astype(BF)
                grads[:, :up_rows, col(i)] = value.reshape(blocks, up_rows, tile)

            yield
        load_gh.wait()

        @pl.loop(0, width // 128)
        def _(i):
            at_cols = pl.ds(pl.multiple_of(i * 128, 128), 128)
            gh_t[at_cols, :] = gh[:, :, at_cols].reshape(n * rows, 128).T

        load_inc.wait()
        piece_rows = each // blocks
        own = (width - experts * each) // blocks
        span = depth // 2
        spots = (((0, 0), (0, 2)), ((0, 1), (piece_rows, 0)))
        for half in range(2):

            @pl.loop(0, span // tile)
            def _(i):
                value = mm(gh_t[...], inc[:, col(half * span // tile + i)])
                for e in range(experts):
                    row, place = spots[half][e]
                    piece = value[e * each : (e + 1) * each].astype(BF)
                    grads[
                        :,
                        up_rows + row : up_rows + row + piece_rows,
                        col(place * span // tile + i),
                    ] = piece.reshape(blocks, piece_rows, tile)
                piece = value[experts * each :].reshape(blocks, own, tile)
                empty = jnp.zeros((blocks, piece_rows - own, tile), F32)
                piece = jnp.concatenate([piece, empty], axis=1).astype(BF)
                grads[:, up_rows + piece_rows :, col((1 + half) * span // tile + i)] = piece

        store = copy(grads, outs[0], 4)
        store.start()
        yield
        store.wait()


def chunks(rows, step=80):
    def over(work):
        @pl.loop(0, rows // step)
        def _(i):
            work(pl.ds(pl.multiple_of(i * step, 16), step))

    return over


def sides(v):
    high = v.astype(BF).astype(F32)
    turn = (iota((128, 128), 0) + 16 == iota((128, 128), 1)).astype(F32)
    return (high + exact(v - high, turn, ((1,), (0,)))).astype(BF)


def joined(v):
    turn = (iota((128, 128), 0) - 16 == iota((128, 128), 1)).astype(F32)
    back = exact(v, turn, ((1,), (0,)))
    return jnp.where(iota((1, 128), 1) < 16, v + back, 0.0)


class StreamGrad(Task):
    def __init__(self, parts, stream, gain, after_grad):
        self.reaches = (("dp", False),)
        self.reduce = Reduce("dp", parts)
        self.ins = self.reduce.ins + tuple((v, IN_VMEM) for v in (stream, gain, after_grad))
        shape = jax.ShapeDtypeStruct
        self.outs = ((shape(stream.shape, F32), IN_VMEM), (shape((1, D), F32), IN_VMEM))
        self.scratch = (pltpu.VMEM(stream.shape, F32),) + self.reduce.scratch

    def steps(self, ins, outs, scratch):
        x, stream, gain, after_grad = ins
        out, gain_grad = outs
        total = scratch[0]
        yield from reduce_steps("dp", x, total, *scratch[1:])
        gain_grad[...] = jnp.zeros_like(gain_grad)

        @chunks(total.shape[0])
        def _(rows):
            v = stream[rows, :].astype(F32)
            inv = lax.rsqrt(jnp.mean(v * v, axis=1, keepdims=True) + EPSILON)
            g = total[rows, :]
            gg = g * gain[...]
            gain_grad[...] += jnp.sum(g * v * inv, axis=0, keepdims=True)
            mean = jnp.mean(gg * v, axis=1, keepdims=True)
            out[rows, :] = after_grad[rows, :] + inv * gg - v * (inv * inv * inv * mean)


class InputGrad(Task):
    def __init__(self, gathered, d_proj, out_grad):
        self.reaches = (("expert", False),)
        n = lax.axis_size("expert")
        wide = d_proj.shape[1]
        rows = (D + out_grad.size // wide) // n
        self.reduce = Reduce("expert", jax.ShapeDtypeStruct((n, rows, wide), BF), BF)
        self.ins = tuple((v, ANY) for v in (*gathered, d_proj, out_grad.reshape(n, -1, wide)))
        self.outs = self.reduce.outs
        dma = pltpu.SemaphoreType.DMA
        self.scratch = (
            pltpu.VMEM((gathered[0].shape[0], MB * gathered[0].shape[1], D), BF),
            pltpu.VMEM(d_proj.shape, BF),
            pltpu.VMEM((n, rows, wide), BF),
            dma((4,)),
        ) + self.reduce.scratch

    def steps(self, ins, outs, scratch):
        g, d_proj, total, sems = scratch[:4]
        n, _, wide = total.shape
        each = D // n
        below = pl.ds(each, total.shape[1] - each)
        loads = (
            pltpu.make_async_copy(ins[2], d_proj, sems.at[0]),
            pltpu.make_async_copy(ins[3], total.at[:, below], sems.at[1]),
        ) + tuple(
            pltpu.make_async_copy(
                ins[m].at[:, :, pl.ds(0, D)],
                g.at[:, pl.ds(m * ins[m].shape[1], ins[m].shape[1])],
                sems.at[2 + m],
            )
            for m in range(MB)
        )
        for load in loads:
            load.start()
        yield
        for load in loads:
            load.wait()
        flat = g.shape[0] * g.shape[1]

        @pl.loop(0, n // 2)
        def _(i):
            columns = pl.ds(pl.multiple_of(i * 2 * each, 2 * each), 2 * each)
            value = mm_tn(g[:, :, columns].reshape(flat, 2 * each), d_proj[...]).astype(BF)
            total[pl.ds(2 * i, 2), :each, :] = value.reshape(2, each, wide)

        yield from reduce_steps("expert", total, outs[0], *scratch[4:])


class InputRows(Task):
    def __init__(self, x, heads):
        nd, ne = lax.axis_size("dp"), lax.axis_size("expert")
        self.heads = heads
        self.slices = D // nd // 16
        self.reaches = (("expert", False),)
        wide = 2 * DI + 2 * S + 128
        row = jax.ShapeDtypeStruct((16, wide), BF)
        self.gather = Gather("expert", row)
        self.ins = ((x, ANY),)
        self.outs = ((jax.ShapeDtypeStruct((D // nd, IN_W), F32), IN_VMEM),)
        dma = pltpu.SemaphoreType.DMA
        self.scratch = (
            pltpu.VMEM((nd, 16, x.shape[1]), BF),
            pltpu.VMEM((16, wide), BF),
            pltpu.VMEM((ne, 16, wide), BF),
            dma((2 * ne,)),
            dma((nd,)),
        ) + self.gather.scratch

    def greet(self, barrier):
        nd = lax.axis_size("dp")
        j = lax.axis_index("dp")
        for source in range(nd):
            pl.semaphore_signal(
                barrier, inc=1, device_id={"dp": source, "expert": j // 2}, device_id_type=MESH
            )
        return 2 * lax.axis_size("expert")

    def steps(self, ins, outs, scratch):
        x = ins[0]
        got, row, full, send, recv = scratch[:5]
        nd, ne = lax.axis_size("dp"), lax.axis_size("expert")
        j, e = lax.axis_index("dp"), lax.axis_index("expert")
        heads, di = self.heads, self.heads * PS
        sent = []
        for k in range(2):
            for c in range(ne):
                src = x.at[pl.ds((k * self.slices + min(c, self.slices - 1)) * 16, 16)]
                mine = (j == 2 * e + k) & (e == c)
                away = pltpu.make_async_remote_copy(
                    src_ref=src,
                    dst_ref=got.at[j],
                    send_sem=send.at[k * ne + c],
                    recv_sem=recv.at[j],
                    device_id={"dp": 2 * e + k, "expert": c},
                    device_id_type=MESH,
                )
                here = pltpu.make_async_copy(src, got.at[j], recv.at[j])
                pl.when(mine)(here.start)
                pl.when(jnp.logical_not(mine))(away.start)
                sent.append((mine, away))
        yield
        for source in range(nd):
            pltpu.make_async_copy(got.at[source], got.at[source], recv.at[source]).wait()
        piece = lambda source, start, size: got[source, :, start : start + size].astype(F32)
        for source in range(0, nd, 2):
            for half in range(2):
                pair = [piece(source + k, half * di, di) for k in range(2)]
                start = half * DI + source * di
                row[:, start : start + 2 * di] = jnp.concatenate(pair, axis=1).astype(BF)
        total = piece(0, 2 * di, 2 * S)
        for source in range(1, nd):
            total = total + piece(source, 2 * di, 2 * S)
        row[:, 2 * DI : 2 * DI + 2 * S] = total.astype(BF)
        steps = [piece(source, 2 * di + 2 * S, 128)[:, :heads] for source in range(nd)]
        steps.append(jnp.zeros((16, 128 - nd * heads), F32))
        row[:, 2 * DI + 2 * S :] = jnp.concatenate(steps, axis=1).astype(BF)
        yield from gather_steps("expert", row, full, *scratch[5:])
        for c in range(self.slices):
            outs[0][c * 16 : (c + 1) * 16, :] = full[c, :, :IN_W].astype(F32)
        for mine, away in sent:
            pl.when(jnp.logical_not(mine))(away.wait_send)


class Small(Task):
    def __init__(self, x):
        self.reaches = (("expert", True), ("dp", True))
        nd, ne = lax.axis_size("dp"), lax.axis_size("expert")
        self.ins = ((x, ANY),)
        self.outs = ((jax.ShapeDtypeStruct((nd,) + x.shape, x.dtype), ANY),)
        dma = pltpu.SemaphoreType.DMA
        self.scratch = (
            pltpu.VMEM((ne,) + x.shape, x.dtype),
            pltpu.VMEM(x.shape, x.dtype),
            dma((ne,)),
            dma((ne,)),
            dma,
            dma((nd,)),
            dma((nd,)),
            dma,
        )

    def steps(self, ins, outs, scratch):
        parts, total = scratch[:2]
        yield from direct_steps("gather", "expert", ins[0], parts, *scratch[2:5])
        total[...] = jnp.sum(parts[...], axis=0)
        yield from direct_steps("gather", "dp", total, outs[0], *scratch[5:8])


class Experts(Task):
    def __init__(
        self, low, mask, inc, w_up, w_down, s_up, s_down, after, mixed, factors, gain, router, own
    ):
        x = jax.ShapeDtypeStruct((low.shape[0], low.shape[1] + 128), BF)
        self.reaches = (("expert", False),)
        self.gather = Gather("expert", x)
        n = lax.axis_size("expert")
        rows, wide = x.shape
        depth = inc.shape[1]
        experts, _, both = w_up.shape
        self.experts = experts
        all_rows = jax.ShapeDtypeStruct((n, rows, wide), BF)
        self.reduce = Reduce("expert", all_rows)
        hidden = experts * both // 2 + s_down.shape[0]
        pre = jax.ShapeDtypeStruct((n, rows, 2 * hidden), BF)
        gh = jax.ShapeDtypeStruct((n, rows, hidden), BF)
        self.ins = tuple((v, ANY) for v in (inc, w_up, w_down, s_up, s_down)) + tuple(
            (v, IN_VMEM) for v in (low, mask, after, mixed, factors, gain, router, own)
        )
        part = jax.ShapeDtypeStruct((n, rows, depth), BF)
        shape = jax.ShapeDtypeStruct
        self.outs = (
            ((all_rows, IN_VMEM),)
            + tuple((v, ANY) for v in (pre, gh, part))
            + (
                (shape((rows, depth), F32), IN_VMEM),
                (shape((rows, wide), BF), IN_VMEM),
                (shape((1, depth), F32), IN_VMEM),
                (shape((16, depth), F32), IN_VMEM),
            )
        )
        dma = pltpu.SemaphoreType.DMA
        self.scratch = (
            (pltpu.VMEM((n, rows, depth), BF),)
            + tuple(pltpu.VMEM(v.shape, BF) for v in (w_up, w_down, s_up, s_down))
            + (pltpu.VMEM((2 * rows, wide), BF), pltpu.VMEM((2 * rows, depth), BF))
            + (pltpu.VMEM((2 * rows, 2 * hidden), BF), pltpu.VMEM((2 * rows, hidden), BF))
            + (pltpu.VMEM(pre.shape, BF), pltpu.VMEM(gh.shape, BF))
            + (pltpu.VMEM((2 * rows, 128), F32), dma((22,)), pltpu.VMEM(part.shape, BF))
            + (pltpu.VMEM((rows, wide), F32), pltpu.VMEM((rows, wide), BF))
            + self.gather.scratch
            + self.reduce.scratch
        )

    def steps(self, ins, outs, scratch):
        inc_in = ins[0]
        low_in, mask, after, mixed, factors, gain, router, own = ins[5:]
        x_all, pre_out, gh_out, part_out, after_grad, payload, gain_grad, router_grad = outs
        inc, w_up, w_down, s_up, s_down, xs, incs, pg, ghs, pre, gh, extra, sems = scratch[:13]
        part, dx, gather_scratch, reduce_scratch = scratch[13], scratch[14], scratch[16:19], scratch[19:]
        x = scratch[15]
        acc = reduce_scratch[0]
        me, at = places("expert")
        n, rows, depth = inc.shape
        experts, _, both = w_up.shape
        each = both // 2
        shared = s_down.shape[0]
        tile = min(256, each)
        loads = [
            pltpu.make_async_copy(src, dst, sems.at[k])
            for k, (src, dst) in enumerate(zip(ins[1:5], (w_up, w_down, s_up, s_down)))
        ]
        loads += [
            pltpu.make_async_copy(inc_in.at[pl.ds(k * rows, rows)], inc.at[k], sems.at[13 + k])
            for k in range(n)
        ]
        for load in loads:
            load.start()

        logits = mm(low_in[...], router[...])
        chosen = mask[...]
        top = jnp.max(jnp.where(chosen > 0.0, logits, -1e30), axis=1, keepdims=True)
        e = jnp.where(chosen > 0.0, jnp.exp(jnp.minimum(logits - top, 0.0)), 0.0)
        table = e / jnp.sum(e, axis=1, keepdims=True)
        x[:, :depth] = low_in[...]
        x[:, depth:] = sides(table)
        arriving = gather_steps("expert", x, x_all, *gather_scratch)
        next(arriving)
        next(arriving)
        for load in loads:
            load.wait()
        lane = lax.broadcasted_iota(jnp.int32, (1, 128), 1)
        stores = []

        def unit(a, b, u, scale):
            sig = jax.nn.sigmoid(a)
            act = a * sig
            hidden = act * b
            gu = u * scale
            da = gu * b * (sig + act * (1.0 - sig))
            return hidden * scale, da, gu * act, u * hidden

        def compute(hop, places_in_acc):
            slots = (at(hop, 0), at(hop, 1))
            for k, slot in enumerate(slots):
                part = pl.ds(k * rows, rows)
                xs[part, :] = x_all[slot]
                incs[part, :] = inc[slot]
            extra[...] = jnp.zeros_like(extra)

            @pl.loop(0, experts * (each // tile))
            def _(i):
                e, f = i // (each // tile), lax.rem(i, each // tile)
                place = me * experts + e
                table = xs[:, depth:].astype(F32)
                chosen = (lane == place) | (lane == place + n * experts)
                scale = jnp.sum(jnp.where(chosen, table, 0.0), axis=1, keepdims=True)
                left = pl.ds(pl.multiple_of(f * tile, tile), tile)
                right = pl.ds(pl.multiple_of(each + f * tile, tile), tile)
                a = mm(xs[:, :depth], w_up[e, :, left])
                b = mm(xs[:, :depth], w_up[e, :, right])
                u = mm_nt(incs[...], w_down[e, left, :])
                h, da, db, dots = unit(a, b, u, scale)
                ghs[:, pl.ds(pl.multiple_of(e * each + f * tile, tile), tile)] = h.astype(BF)
                pg[:, pl.ds(pl.multiple_of(e * both + f * tile, tile), tile)] = da.astype(BF)
                pg[:, pl.ds(pl.multiple_of(e * both + each + f * tile, tile), tile)] = db.astype(BF)
                extra[...] += jnp.where(lane == place, jnp.sum(dots, axis=1, keepdims=True), 0.0)

            a = mm(xs[:, :depth], s_up[:, :shared])
            b = mm(xs[:, :depth], s_up[:, shared:])
            u = mm_nt(incs[...], s_down[...])
            h, da, db, _ = unit(a, b, u, 1.0)
            ghs[:, experts * each :] = h.astype(BF)
            pg[:, experts * both : experts * both + shared] = da.astype(BF)
            pg[:, experts * both + shared :] = db.astype(BF)

            @pl.loop(0, depth // tile)
            def _(i):
                columns = pl.ds(pl.multiple_of(i * tile, tile), tile)
                total = mm_nt(pg[:, experts * both :], s_up[columns, :])
                for e in range(experts):
                    total += mm_nt(pg[:, e * both : (e + 1) * both], w_up[e, columns, :])
                for k, place in enumerate(places_in_acc):
                    acc[place, :, columns] = total[k * rows : (k + 1) * rows].astype(BF)

            grads = extra[...]
            both_parts = sides(grads)
            for k, (slot, place) in enumerate(zip(slots, places_in_acc)):
                part = pl.ds(k * rows, rows)
                acc[place, :, depth:] = both_parts[k * rows : (k + 1) * rows]
                pre[slot] = pg[part, :]
                gh[slot] = ghs[part, :]
                store = pltpu.make_async_copy(pre.at[slot], pre_out.at[slot], sems.at[4 + len(stores)])
                store.start()
                stores.append(store)

        compute(0, (7, 6))
        next(arriving)
        compute(1, (4, 2))
        compute(-1, (5, 3))
        for _ in arriving:
            pass
        compute(2, (1, 0))
        store = pltpu.make_async_copy(gh, gh_out, sems.at[12])
        store.start()
        stores.append(store)
        summing = reduce_steps("expert", None, dx, *reduce_scratch)
        next(summing)
        for half in range(2):
            next(summing)

            @pl.loop(half * depth // tile // 2, (half + 1) * depth // tile // 2)
            def _(i):
                columns = pl.ds(pl.multiple_of(i * tile, tile), tile)
                hid = lambda start, size: gh[:, :, start : start + size].reshape(n * rows, size)
                total = mm(hid(experts * each, shared), s_down[:, columns])
                for e in range(experts):
                    total += mm(hid(e * each, each), w_down[e, :, columns])
                part[:, :, columns] = total.astype(BF).reshape(n, rows, tile)

        store = pltpu.make_async_copy(part, part_out, sems.at[21])
        store.start()
        stores.append(store)
        yield from summing
        gain_grad[...] = jnp.zeros_like(gain_grad)
        spread = joined(dx[:, depth:])
        logit = table * (spread - jnp.sum(table * spread, axis=1, keepdims=True))
        logit_low = logit.astype(BF)
        router_grad[...] = mm_tn(logit_low, low_in[...])[:16]
        dx[:, :depth] += mm_nt(logit_low, router[...])

        @chunks(rows)
        def _(at_rows):
            v, inv = after[at_rows, :], factors[at_rows, 1:2]
            g = dx[at_rows, :depth]
            gg = g * gain[...]
            gain_grad[...] += jnp.sum(g * v * inv, axis=0, keepdims=True)
            mean = jnp.mean(gg * v, axis=1, keepdims=True)
            total = own[at_rows, :].astype(F32) + inv * gg - v * (inv * inv * inv * mean)
            after_grad[at_rows, :] = total
            total_low = total.astype(BF)
            payload[at_rows, :depth] = total_low
            s = jnp.sum(total_low.astype(F32) * mixed[at_rows, :], axis=1, keepdims=True)
            r = factors[at_rows, 0:1]
            r_high, s_high = r.astype(BF).astype(F32), s.astype(BF).astype(F32)
            extras = jnp.where(lane == 0, r_high, jnp.where(lane == 1, r - r_high, 0.0))
            extras = jnp.where(lane == 2, s_high, jnp.where(lane == 3, s - s_high, extras))
            payload[at_rows, depth:] = extras.astype(BF)

        for store in stores:
            store.wait()


EDGE = 8


def pieces(v, count):
    out = []
    for _ in range(count):
        out.append(v.astype(BF))
        v = v - out[-1].astype(F32)
    return out


def exact(v, ones, dims, count=2):
    ones = ones.astype(BF)
    parts = [
        lax.dot_general(p, ones, (dims, ((), ())), preferred_element_type=F32)
        for p in pieces(v, count)
    ]
    return sum(parts[1:], parts[0])


def exact_right(ones, v, dims, count=2):
    ones = ones.astype(BF)
    parts = [
        lax.dot_general(ones, p, (dims, ((), ())), preferred_element_type=F32)
        for p in pieces(v, count)
    ]
    return sum(parts[1:], parts[0])


def iota(shape, axis):
    return lax.broadcasted_iota(jnp.int32, shape, axis)


class Block:
    def __init__(self, m, slot, start, proj, ext, lengths, taps, heads_vec, heads):
        loc = proj.shape[0]
        di = heads * PS
        width = di + 2 * S
        self.heads, self.di = heads, di
        first = lengths[m, 0]
        second = first + lengths[m, 1]

        def doc(p):
            return (p >= first).astype(jnp.int32) + (p >= second).astype(jnp.int32)

        self.doc = doc
        self.at = start + iota((loc, 1), 0)
        docs = doc(self.at)
        docs_row = doc(start + iota((1, loc), 1))
        last_doc, before_doc = doc(start + loc - 1), doc(start - 1)
        self.keep = (docs == before_doc).astype(F32)
        self.keep_last = (last_doc == before_doc).astype(F32)
        self.same_last = (docs == last_doc).astype(F32)
        self.gate = proj[:, :di]
        ext[slot, EDGE : EDGE + loc, :] = proj[:, di : di + width].astype(BF).astype(F32)
        total = jnp.broadcast_to(taps[K : K + 1, :], (loc, width))
        self.shifted = []
        for k in range(K):
            back = K - 1 - k
            value = ext[slot, EDGE - back : EDGE - back + loc, :]
            if back:
                value = value * (docs == doc(self.at - back)).astype(F32)
            self.shifted.append(value)
            total = total + taps[k : k + 1, :] * value
        self.sig = jax.nn.sigmoid(total)
        self.total = total
        filtered = total * self.sig
        self.x = filtered[:, :di]
        self.write = filtered[:, di : di + S].astype(BF)
        self.read = filtered[:, di + S :].astype(BF)
        self.raw = proj[:, di + width :] + heads_vec[0:1, :]
        self.steps = jnp.maximum(self.raw, 0.0) + jnp.log1p(jnp.exp(-jnp.abs(self.raw)))
        self.rate = heads_vec[1:2, :]
        rise = self.steps * self.rate
        rows, cols = iota((loc, loc), 0), iota((loc, loc), 1)
        self.lower = (cols <= rows).astype(F32)
        self.cum = exact_right(self.lower, rise, ((1,), (0,)), 3)
        cum_rows = exact(rise, (rows <= cols).astype(F32), ((0,), (0,)), 3)
        self.last = self.cum[loc - 1 : loc, :]
        self.grow = jnp.exp(self.cum) * self.keep
        self.fall = jnp.exp(self.last - self.cum) * self.same_last
        self.decay = jnp.exp(self.last) * self.keep_last
        allowed = (cols <= rows) & (docs == docs_row)
        scores = mm_nt(self.read, self.write)
        self.spread, self.mixing = [], []
        for h in range(heads):
            span = self.cum[:, h : h + 1] - cum_rows[h : h + 1, :]
            shape = jnp.exp(jnp.where(allowed, span, -1e30))
            self.spread.append(shape)
            self.mixing.append(shape * scores)
        self.lane = iota((1, di), 1)
        self.steps_wide = self.widen(self.steps)
        self.grow_wide = self.widen(self.grow)
        self.weight_wide = self.widen(self.fall * self.steps)
        self.scaled = self.x * self.steps_wide
        self.pushed = self.x * self.weight_wide

    def widen(self, v):
        out = jnp.broadcast_to(v[:, 0:1], (v.shape[0], self.di))
        for h in range(1, self.heads):
            out = jnp.where(self.lane >= h * PS, v[:, h : h + 1], out)
        return out

    def per_head(self, parts):
        out = parts[0]
        for h in range(1, self.heads):
            out = jnp.where(self.lane >= h * PS, parts[h], out)
        return out

    def decay_rows(self):
        rows = iota((self.di, 1), 0)
        out = jnp.broadcast_to(self.decay[:, 0:1], (self.di, 1))
        for h in range(1, self.heads):
            out = jnp.where(rows >= h * PS, self.decay[:, h : h + 1], out)
        return out


def load_weights(pieces_ref, w, sem):
    copies = [
        pltpu.make_async_copy(pieces_ref.at[k], w.at[:, k], sem.at[k]) for k in range(w.shape[1])
    ]
    for copy in copies:
        copy.start()
    for copy in copies:
        copy.wait()


class Forward(Task):
    def __init__(self, blocks, x, incoming, lengths, w_out, vectors, stream, gain, heads):
        self.heads = heads
        self.reaches = (("dp", True), ("expert", False))
        nd = lax.axis_size("dp")
        loc = stream.shape[0] // MB
        di = heads * PS
        wide = blocks.shape[2]
        shape = jax.ShapeDtypeStruct
        self.weights = Weights(blocks)
        self.gathers = [Gather("dp", v) for v in x] + [Gather("expert", incoming)]
        part = shape((nd, loc, D + 128), BF)
        self.reduces = [Reduce("dp", part) for _ in range(MB)]
        self.saved = (
            shape((MB, nd, loc, wide), F32),
            shape((MB, nd, loc, di), F32),
            shape((MB, nd, di, S), F32),
        )
        self.ins = (
            ((blocks, ANY),)
            + tuple((v, ANY) for v in (*x, incoming))
            + ((lengths, pl.BlockSpec(memory_space=pltpu.SMEM)),)
            + tuple((v, IN_VMEM) for v in (w_out,) + tuple(vectors) + (stream, gain))
        )
        full = self.weights.outs[1][0]
        rows = stream.shape[0]
        self.outs = (
            ((full, ANY),)
            + tuple((gather.outs[0][0], ANY) for gather in self.gathers)
            + tuple((v, ANY) for v in self.saved)
            + (
                (shape((rows, D), BF), IN_VMEM),
                (shape((rows, D), F32), IN_VMEM),
                (shape((rows, D), F32), IN_VMEM),
                (shape((rows, 128), F32), IN_VMEM),
            )
        )
        vmem = lambda v: pltpu.VMEM(v.shape, v.dtype)
        dma = pltpu.SemaphoreType.DMA
        slices = D // nd // full.shape[2]
        self.scratch = (
            (vmem(self.weights.outs[0][0]), vmem(full))
            + tuple(vmem(gather.outs[0][0]) for gather in self.gathers[:MB])
            + tuple(vmem(v) for v in self.saved)
            + tuple(vmem(part) for _ in range(MB))
            + tuple(pltpu.VMEM((loc, D + 128), F32) for _ in range(MB))
            + (pltpu.VMEM((nd, slices, full.shape[2], wide), BF), dma((slices,)), dma((9,)))
            + (pltpu.VMEM((2, loc + EDGE, di + 2 * S), F32), pltpu.VMEM((di, S), F32))
            + (pltpu.VMEM((4, loc, di), BF),)
            + self.weights.scratch
            + self.gathers[0].scratch
            + self.gathers[1].scratch
            + self.gathers[2].scratch
            + self.reduces[0].scratch
            + self.reduces[1].scratch
        )

    def steps(self, ins, outs, scratch):
        x, incoming, lengths = ins[1:3], ins[3], ins[4]
        w_out, taps, heads_vec, lanes_vec, stream, gain = ins[5:]
        w_full, g_out, inc_out, saved_out = outs[0], outs[1:3], outs[3], outs[4:7]
        low_out, after, mixed, factors = outs[7:]
        swapped, pieces_all = scratch[:2]
        g, (proj, scan, states), parts, totals = scratch[2:4], scratch[4:7], scratch[7:9], scratch[9:11]
        w, w_sem, sems, ext, state, gated = scratch[11:17]
        rest = scratch[17:]
        rest, weight_sems = rest[6:], rest[:6]
        gather_sems, rest = (rest[:3], rest[3:6], rest[6:9]), rest[9:]
        count = len(self.reduces[0].scratch)
        reduce_scratch = (rest[:count], rest[count:])
        heads = self.heads
        nd, loc, _ = g[0].shape
        di = heads * PS
        stores = []

        def store(src, dst):
            copy = pltpu.make_async_copy(src, dst, sems.at[len(stores)])
            copy.start()
            stores.append(copy)

        def work(m, start, end):
            many = end - start
            rows = g[m][start:end, :, :D].reshape(many * loc, D)
            value = mm(rows, w[...].reshape(D, -1))
            proj[m, start:end] = value.reshape(many, loc, value.shape[1])

            @pl.loop(start // 2, end // 2)
            def _(pair):
                two = []
                for k in range(2):
                    b = pair * 2 + k
                    ext[k, 0:EDGE, :] = ext[1 - k, loc : loc + EDGE, :]
                    two.append(
                        Block(m, k, b * loc, proj[m, b], ext, lengths, taps, heads_vec, heads)
                    )
                before = [state[...]]
                for part in two:
                    before.append(
                        part.decay_rows() * before[-1] + mm_tn(part.pushed.astype(BF), part.write)
                    )
                state[...] = before[2]
                for k, part in enumerate(two):
                    b = pair * 2 + k
                    states[m, b] = before[k]
                    scaled = part.scaled.astype(BF)
                    inner = part.per_head(
                        [mm(part.mixing[h].astype(BF), scaled) for h in range(heads)]
                    )
                    carried = mm_nt(part.read, before[k].astype(BF)) * part.grow_wide
                    out = inner + carried + lanes_vec[1:2, :] * part.x
                    scan[m, b] = out
                    y = out * (part.gate * jax.nn.sigmoid(part.gate))
                    square = jnp.sum(y * y, axis=1, keepdims=True)
                    high = square.astype(BF).astype(F32)
                    gated[b - start] = (y * lanes_vec[0:1, :]).astype(BF)
                    column = iota((loc, 128), 1)
                    sums = jnp.where(column == 0, high, jnp.where(column == 1, square - high, 0.0))
                    parts[m][b, :, D:] = sums.astype(BF)

            value = mm(gated[...].reshape(many * loc, di), w_out[...])
            parts[m][start:end, :, :D] = value.astype(BF).reshape(many, loc, D)

        def reset():
            ext[...] = jnp.zeros_like(ext)
            state[...] = jnp.zeros_like(state)

        def norm(m):
            @chunks(loc)
            def _(rows):
                at_rows = pl.ds(pl.multiple_of(m * loc + rows.start, 16), rows.size)
                lane = iota((1, 128), 1)
                total = totals[m]
                squares = total[rows, D:]
                square = jnp.sum(jnp.where(lane < 2, squares, 0.0), axis=1, keepdims=True)
                r = lax.rsqrt(square / DI + EPSILON)
                mix = total[rows, :D] * r
                v = stream[at_rows, :].astype(F32) + mix
                inv = lax.rsqrt(jnp.mean(v * v, axis=1, keepdims=True) + EPSILON)
                low_out[at_rows, :] = (v * inv * gain[...]).astype(BF)
                after[at_rows, :] = v
                mixed[at_rows, :] = mix
                factors[at_rows, :] = jnp.where(lane == 0, r, jnp.where(lane == 1, inv, 0.0))

        weights = self.weights.steps(ins[:1], (swapped, pieces_all), weight_sems)
        first = gather_steps("dp", x[0], g[0], *gather_sems[0])
        second = gather_steps("dp", x[1], g[1], *gather_sems[1])
        third = gather_steps("expert", incoming, inc_out, *gather_sems[2])
        next(weights)
        next(first)
        next(weights)
        next(weights, None)
        next(first)
        next(weights, None)
        next(first)
        next(second)
        next(weights, None)
        next(first)
        for _ in weights:
            pass
        for _ in first:
            pass
        load_weights(pieces_all, w, w_sem)
        store(pieces_all, w_full)
        store(g[0], g_out[0])
        reset()
        for k in range(4):
            next(third, None)
            work(0, 4 * k, 4 * k + 4)
            next(second, None)
        for steps in (second, third):
            for _ in steps:
                pass
        store(g[1], g_out[1])
        sums = [
            reduce_steps("dp", parts[m], totals[m], *reduce_scratch[m]) for m in range(MB)
        ]
        next(sums[0])
        for src, dst in zip((proj, scan, states), saved_out):
            store(src.at[0], dst.at[0])
        reset()
        for k in range(4):
            next(sums[0])
            work(1, 4 * k, 4 * k + 4)
        next(sums[1])
        for src, dst in zip((proj, scan, states), saved_out):
            store(src.at[1], dst.at[1])
        for _ in sums[0]:
            pass
        next(sums[1])
        norm(0)
        for _ in sums[1]:
            pass
        norm(1)
        for copy in stores:
            copy.wait()
        yield


def backward_kernel(
    heads,
    lengths,
    grad,
    w_pieces,
    w_out,
    taps,
    heads_vec,
    lanes_vec,
    proj,
    proj_before,
    scan,
    states,
    d_proj,
    normed_part,
    d_out,
    d_taps,
    d_heads,
    d_lanes,
    ext,
    d_ext,
    d_state,
    out_sum,
    w,
    w_sem,
):
    step = pl.program_id(0)
    b = pl.num_programs(0) - 1 - step
    loc = grad.shape[1] // MB
    di = heads * PS
    width = di + 2 * S

    @pl.when(step == 0)
    def _():
        for ref in (d_ext, d_state, out_sum, d_taps, d_heads, d_lanes):
            ref[...] = jnp.zeros_like(ref)
        load_weights(w_pieces, w, w_sem)

    gated_grad = mm_nt(grad[0, :, :D], w_out[...])
    extra = grad[0, :, D:].astype(F32)
    has_before = (b > 0).astype(F32)
    pick = (iota((di, S), 0) // PS == iota((di, S), 1)).astype(F32)
    for m in range(MB):
        rows = slice(m * loc, (m + 1) * loc)
        edge = proj_before[m, 0, loc - EDGE : loc, di : di + width]
        ext[m, 0:EDGE, :] = edge.astype(BF).astype(F32) * has_before
        part = Block(m, m, b * loc, proj[m, 0], ext, lengths, taps, heads_vec, heads)
        gain, skip = lanes_vec[0:1, :], lanes_vec[1:2, :]
        r = extra[rows, 0:1] + extra[rows, 1:2]
        s = extra[rows, 2:3] + extra[rows, 3:4]
        out = scan[m, 0]
        sig = jax.nn.sigmoid(part.gate)
        act = part.gate * sig
        yr = out * act * r
        gg = gated_grad[rows]
        d_lanes[0:1, :] += jnp.sum(gg * yr, axis=0, keepdims=True)
        out_sum[...] += mm_tn((yr * gain).astype(BF), grad[0, rows, :D])
        dy = r * (gg * gain) - yr * (r * s / DI)
        d_gate = dy * out * (sig + act * (1.0 - sig))
        do = dy * act
        do_low = do.astype(BF)
        x = part.x
        d_lanes[1:2, :] += jnp.sum(do * x, axis=0, keepdims=True)
        dx = skip * do
        before = states[m, 0]
        before_low = before.astype(BF)
        ds = d_state[m]
        ds_low = ds.astype(BF)

        d_scores = jnp.zeros((loc, loc), F32)
        d_scaled, d_cum = [], jnp.zeros((loc, S), F32)
        head_lane = iota((loc, S), 1)
        for h in range(heads):
            inside = (part.lane >= h * PS) & (part.lane < (h + 1) * PS)
            own = jnp.where(inside, part.scaled, 0.0).astype(BF)
            d_mix = mm_nt(do_low, own)
            d_scaled.append(mm_tn(part.mixing[h].astype(BF), do_low))
            d_scores = d_scores + d_mix * part.spread[h]
            d_span = d_mix * part.mixing[h]
            ones = (head_lane == h).astype(F32)
            d_cum = d_cum + exact(d_span, ones, ((1,), (0,))) - exact(d_span, ones, ((0,), (0,)))
        d_scaled = part.per_head(d_scaled)
        dx = dx + d_scaled * part.steps_wide
        d_scores_low = d_scores.astype(BF)
        d_read = mm(d_scores_low, part.write)
        d_write = mm_tn(d_scores_low, part.read)

        d_carry = do * part.grow_wide
        d_carry_low = d_carry.astype(BF)
        carried = mm_nt(part.read, before_low)
        d_read = d_read + mm(d_carry_low, before_low)

        d_pushed = mm_nt(part.write, ds_low)
        d_write = d_write + mm(part.pushed.astype(BF), ds_low)
        dx = dx + d_pushed * part.weight_wide
        sums = exact(
            jnp.concatenate([d_carry * carried, d_pushed * x, d_scaled * x], axis=0),
            pick,
            ((1,), (0,)),
        )
        d_weight = sums[loc : 2 * loc]
        d_fall = d_weight * part.fall * part.steps
        d_cum = d_cum + sums[:loc] - d_fall
        d_steps = sums[2 * loc :] + d_weight * part.fall
        state_dot = jnp.sum(ds * before, axis=1, keepdims=True)
        d_decay = exact(jnp.broadcast_to(state_dot, (di, S)), pick, ((0,), (0,)))[0:1, :]
        d_last = jnp.sum(d_fall, axis=0, keepdims=True) + d_decay * part.decay
        d_cum = d_cum + jnp.where(iota((loc, 1), 0) == loc - 1, d_last, 0.0)
        d_state[m] = part.decay_rows() * ds + mm_tn(d_carry_low, part.read)

        d_rise = exact_right(part.lower, d_cum, ((0,), (0,)))
        d_steps = d_steps + d_rise * part.rate
        d_raw = d_steps * jax.nn.sigmoid(part.raw)
        d_heads[0:1, :] += jnp.sum(d_raw, axis=0, keepdims=True)
        d_heads[1:2, :] += jnp.sum(d_rise * part.steps * part.rate, axis=0, keepdims=True)

        d_total = jnp.concatenate([dx, d_write, d_read], axis=1)
        d_total = d_total * (part.sig + part.total * part.sig * (1.0 - part.sig))
        for k in range(K):
            d_taps[k : k + 1, :] += jnp.sum(d_total * part.shifted[k], axis=0, keepdims=True)
        d_taps[K : K + 1, :] += jnp.sum(d_total, axis=0, keepdims=True)
        d_ext[m, loc : loc + EDGE, :] = d_ext[m, 0:EDGE, :]
        d_ext[m, 0:loc, :] = d_total
        d_seq = taps[K - 1 : K, :] * d_total
        docs = part.doc(part.at)
        for ahead in range(1, K):
            same = (docs == part.doc(part.at + ahead)).astype(F32)
            d_seq = d_seq + taps[K - 1 - ahead : K - ahead, :] * (
                same * d_ext[m, ahead : ahead + loc, :]
            )
        d_proj[0, rows, :di] = d_gate.astype(BF)
        d_proj[0, rows, di : di + width] = d_seq.astype(BF)
        d_proj[0, rows, di + width :] = jnp.where(head_lane < heads, d_raw, 0.0).astype(BF)
    for half in range(2):
        d_out[half] = out_sum[:, half * D // 2 : (half + 1) * D // 2].astype(BF)
    normed_part[0] = mm_nt(d_proj[0], w[...].reshape(D, -1)).astype(BF)


def weight_scratch(w):
    slices = D // w.shape[1] // w.shape[2]
    return [
        pltpu.VMEM((w.shape[1], slices) + w.shape[2:], BF),
        pltpu.SemaphoreType.DMA((slices,)),
    ]


def block_spec(shape, index):
    return pl.BlockSpec((1,) + shape[1:], lambda i: (index(i),) + (0,) * (len(shape) - 1))


def pair_spec(shape, index):
    return pl.BlockSpec((MB, 1) + shape[2:], lambda i: (0, index(i)) + (0,) * (len(shape) - 2))


def whole_spec(shape):
    return pl.BlockSpec(shape, lambda i: (0,) * len(shape))


def mixer_backward(lengths, grad, w, w_out, taps, heads_vec, lanes_vec, proj, scan, states, heads):
    nb, rows, _ = grad.shape
    di = heads * PS
    width = di + 2 * S
    back = lambda i: nb - 1 - i
    before = lambda i: jnp.maximum(nb - 2 - i, 0)
    per_block = [
        jax.ShapeDtypeStruct((nb, rows, w.shape[-1]), BF),
        jax.ShapeDtypeStruct((nb, rows, D), BF),
    ]
    sums = [
        jax.ShapeDtypeStruct((2, di, D // 2), BF),
        jax.ShapeDtypeStruct((8, width), F32),
        jax.ShapeDtypeStruct((8, S), F32),
        jax.ShapeDtypeStruct((8, di), F32),
    ]
    return pl.pallas_call(
        functools.partial(backward_kernel, heads),
        grid=(nb,),
        out_shape=per_block + sums,
        in_specs=[pl.BlockSpec(memory_space=pltpu.SMEM), block_spec(grad.shape, back)]
        + [pl.BlockSpec(memory_space=pl.ANY)]
        + [whole_spec(v.shape) for v in (w_out, taps, heads_vec, lanes_vec)]
        + [pair_spec(proj.shape, back), pair_spec(proj.shape, before)]
        + [pair_spec(scan.shape, back), pair_spec(states.shape, back)],
        out_specs=[block_spec(v.shape, back) for v in per_block]
        + [whole_spec(v.shape) for v in sums],
        scratch_shapes=[
            pltpu.VMEM((MB, rows // MB + EDGE, width), F32),
            pltpu.VMEM((MB, rows // MB + EDGE, width), F32),
            pltpu.VMEM((MB, di, S), F32),
            pltpu.VMEM((di, D), F32),
        ]
        + weight_scratch(w),
        compiler_params=pltpu.CompilerParams(vmem_limit_bytes=VMEM_LIMIT),
        name="mixer_backward",
    )(lengths, grad, w, w_out, taps, heads_vec, lanes_vec, proj, proj, scan, states)


def body(
    tokens,
    lengths,
    routes,
    cotangent,
    input_weight,
    filter_weight,
    filter_bias,
    step_bias,
    decay_log,
    skip_gain,
    norm_gain,
    gated_gain,
    output_weight,
    moe_gain,
    router_weight,
    shared_gate_up,
    shared_down,
    expert_gate_up,
    expert_down,
):
    nd, ne = lax.axis_size("dp"), lax.axis_size("expert")
    me_d, me_e = lax.axis_index("dp"), lax.axis_index("expert")
    loc = tokens.shape[2]
    heads = H // nd
    di = heads * PS
    rows_t = MB * loc
    experts = expert_gate_up.shape[0] * ne
    el = expert_gate_up.shape[0]
    dr = D // nd
    fs = FS // ne
    fsr = FS // nd
    fsl = fsr // ne

    pad = 128 - heads
    piece = 16
    place = jnp.minimum(me_e, dr // piece - 1) * piece
    mine = lax.dynamic_slice_in_dim(input_weight, place, piece, 0)
    blocks = jnp.concatenate(
        [
            jnp.moveaxis(mine[:, :DI].reshape(piece, nd, di), 1, 0),
            jnp.moveaxis(mine[:, DI : 2 * DI].reshape(piece, nd, di), 1, 0),
            jnp.broadcast_to(mine[None, :, 2 * DI : 2 * DI + 2 * S], (nd, piece, 2 * S)),
            jnp.moveaxis(mine[:, DI + CONV :].reshape(piece, nd, heads), 1, 0),
            jnp.zeros((nd, piece, pad), BF),
        ],
        axis=2,
    )
    wcols = blocks.shape[2]

    sg = shared_gate_up.reshape(dr, 2, nd, ne, fsl)
    sg = lax.dynamic_index_in_dim(sg, me_e, 3, False).reshape(dr, 2 * fs)
    sd = lax.dynamic_slice_in_dim(shared_down, me_e * fsl, fsl, 0)
    packed = jnp.concatenate([sg.reshape(-1), sd.reshape(-1), router_weight.reshape(-1)])
    packed_cols = packed.size // loc
    packed = jnp.pad(packed.reshape(loc, -1), ((0, 0), (0, -packed_cols % 128)))

    stream = tokens.reshape(rows_t, D).astype(F32)
    incoming = cotangent.reshape(rows_t, D)
    route_rows = routes.reshape(rows_t, TOP)
    normed = rms_scale(stream, norm_gain).astype(BF)
    taps = jnp.concatenate(
        [lax.dynamic_slice_in_dim(filter_weight, me_d * di, di, 1), filter_weight[:, DI:]], axis=1
    )
    tap_bias = jnp.concatenate(
        [lax.dynamic_slice_in_dim(filter_bias, me_d * di, di, 0), filter_bias[DI:]], axis=0
    )
    my_heads = lambda v: lax.dynamic_slice_in_dim(v, me_d * heads, heads, 0)
    my_gain = lax.dynamic_slice_in_dim(gated_gain, me_d * di, di, 0)

    taps_vec = jnp.concatenate([taps, tap_bias[None], jnp.zeros((3, di + 2 * S), F32)], axis=0)
    heads_vec = jnp.stack([my_heads(step_bias), -jnp.exp(my_heads(decay_log))])
    heads_vec = jnp.pad(heads_vec, ((0, 6), (0, S - heads)))
    lanes_vec = jnp.pad(
        jnp.stack([my_gain, jnp.repeat(my_heads(skip_gain), PS)]), ((0, 6), (0, 0))
    )
    vectors = (taps_vec, heads_vec, lanes_vec)
    gain_row = moe_gain.reshape(1, D)
    own_tokens = tokens.reshape(rows_t, D)
    forward = Forward(
        blocks,
        (normed[:loc], jnp.concatenate([normed[loc:], packed], axis=1)),
        incoming,
        lengths[:, 0],
        output_weight,
        vectors,
        own_tokens,
        gain_row,
        heads,
    )
    (results,) = run_tasks([forward], 1, "forward")
    w_in, *gathered, inc_all, proj, scan, states, moe_in, after_mixer, mixed, factors = results
    inc_all = inc_all.reshape(ne * rows_t, D)
    packed_all = gathered[1][:, :, D : D + packed_cols]
    packed_all = packed_all.reshape(nd, -1)
    sg_full = packed_all[:, : sg.size].reshape(D, 2 * fs)
    sd_full = packed_all[:, sg.size : sg.size + sd.size].reshape(fs, D)
    router_full = packed_all[:, sg.size + sd.size :].reshape(D, experts)
    mask = jnp.sum(
        (route_rows[:, :, None] == jnp.arange(128, dtype=jnp.int32)).astype(F32), axis=1
    )
    router_wide = jnp.pad(router_full, ((0, 0), (0, 128 - experts)))
    ((moe_all, pre_grad, gh, out_part, after_grad, grad_payload, moe_gain_grad, router_part),) = (
        run_tasks(
            [
                Experts(
                    moe_in,
                    mask,
                    inc_all,
                    expert_gate_up,
                    expert_down,
                    sg_full,
                    sd_full,
                    after_mixer,
                    mixed,
                    factors,
                    gain_row,
                    router_wide,
                    incoming,
                )
            ],
            3,
            "experts",
        )
    )
    width = gh.shape[2]
    (out_sum,), (grad_blocks,), (grad_all,) = run_tasks(
        [
            Reduce("expert", out_part),
            ExpertGrads(moe_all, pre_grad, gh, inc_all, el, FE, nd),
            Gather("dp", grad_payload),
        ],
        5,
        "gather_grad",
    )
    all_sum = lax.psum_scatter(grad_blocks, "dp", scatter_dimension=0, tiled=True)[0]
    up_sum = all_sum[:dr]
    each, span = FE // nd, D // 2
    down_sum = all_sum[dr : dr + each]
    last_sum = all_sum[dr + each :]
    d_proj, normed_part, output_part, d_taps, d_heads, d_lanes = mixer_backward(
        lengths[:, 0], grad_all, w_in, output_weight, *vectors, proj, scan, states, heads
    )
    def rows_of(parts, count):
        flat = jnp.concatenate([part.reshape(-1) for part in parts])
        return jnp.pad(flat, (0, count * 128 - flat.size)).reshape(count, 128)

    added = (d_taps[:K, di:], d_taps[K, di:], moe_gain_grad, router_part)
    own = (
        d_taps[:K, :di],
        d_taps[K, :di],
        d_heads[0, :heads],
        d_heads[1, :heads],
        jnp.sum(d_lanes[1].reshape(heads, PS), axis=1),
        d_lanes[0],
    )
    added_size = sum(part.size for part in added)
    added_rows = -(-added_size // (nd * 1024)) * 8
    own_rows = -(-sum(part.size for part in own) // 128)
    norm_rows = D // 128
    (tokens_grad, norm_gain_grad), (d_sum,), (added_in,) = run_tasks(
        [
            StreamGrad(normed_part, own_tokens, norm_gain.reshape(1, D), after_grad),
            InputGrad(
                gathered,
                d_proj.reshape(nd * rows_t, wcols),
                output_part,
            ),
            Direct("all", "dp", rows_of(added, nd * added_rows).reshape(nd, added_rows, 128)),
        ],
        6,
        "reduce_grads",
    )
    small = jnp.concatenate(
        [jnp.sum(added_in, axis=0), rows_of(own, own_rows), rows_of((norm_gain_grad,), norm_rows)],
        axis=0,
    )
    small = jnp.pad(small, ((0, -small.shape[0] % 8), (0, 0)))
    shared_part = jnp.concatenate(
        [up_sum[:, 2 * el * FE :], last_sum[:fsl, span:].reshape(dr, -1)], axis=1
    ).reshape(-1, wcols)
    main_rows = D // ne
    (small_all,), (rest_all,), (input_grad,) = run_tasks(
        [
            Small(small),
            Gather("expert", jnp.concatenate([d_sum[main_rows:], shared_part], axis=0)),
            InputRows(d_sum[:main_rows], heads),
        ],
        7,
        "finish",
    )
    cut_rows = d_sum.shape[0] - main_rows
    output_grad = rest_all[:, :cut_rows].reshape(2, di, D // 2)
    output_grad = jnp.moveaxis(output_grad, 0, 1).reshape(output_weight.shape)
    shared_all = rest_all[:, cut_rows:].reshape(ne, dr, -1)
    added_all = small_all[:, :added_rows].reshape(-1)
    own_all = small_all[:, added_rows : added_rows + own_rows].reshape(nd, -1)
    norm_gain_grad = jnp.sum(
        small_all[:, added_rows + own_rows : added_rows + own_rows + norm_rows], axis=0
    ).reshape(D)

    def split(flat, parts):
        out, start = [], 0
        for part in parts:
            out.append(flat[..., start : start + part.size].reshape(flat.shape[:-1] + part.shape))
            start += part.size
        return out

    added_taps, added_bias, moe_gain_grad, router_all = split(added_all, added)
    own_taps, own_bias, own_steps, own_decay, own_skip, own_gain = split(own_all, own)
    small = (
        jnp.concatenate([jnp.moveaxis(own_taps, 0, 1).reshape(K, DI), added_taps], axis=1),
        jnp.concatenate([own_bias.reshape(-1), added_bias]),
        own_steps.reshape(-1),
        own_decay.reshape(-1),
        own_skip.reshape(-1),
        norm_gain_grad,
        own_gain.reshape(-1),
        moe_gain_grad.reshape(D),
    )
    router_grad = lax.dynamic_slice_in_dim(router_all, me_d * dr, dr, 1).T
    expert_up_grad = jnp.moveaxis(up_sum[:, : 2 * el * FE].reshape(dr, el, 2 * FE), 1, 0)
    expert_up_grad = expert_up_grad.astype(F32)
    expert_down_grad = jnp.stack(
        [
            down_sum[:, : 2 * span],
            jnp.concatenate([down_sum[:, 2 * span :], last_sum[:, :span]], axis=1),
        ],
        axis=0,
    ).astype(F32)
    shared_up_grad = (
        jnp.moveaxis(shared_all[:, :, : 2 * fs].reshape(ne, dr, 2, nd, fsl), 0, 3)
        .reshape(dr, 2 * FS)
        .astype(F32)
    )
    shared_down_grad = shared_all[:, :, 2 * fs :].reshape(fsr, D).astype(F32)
    block_output = (after_mixer + out_sum).astype(BF)
    shape = (MB, 1, loc, D)
    return (
        block_output.reshape(shape),
        tokens_grad.reshape(shape),
        input_grad,
        small[0],
        small[1],
        small[2],
        small[3],
        small[4],
        small[5],
        small[6],
        output_grad.astype(F32),
        small[7],
        router_grad,
        shared_up_grad,
        shared_down_grad,
        expert_up_grad,
        expert_down_grad,
    )


def solution(mesh):
    in_specs = (
        P(None, "expert", "dp", None),
        P(None, "expert", None),
        P(None, "expert", "dp", None),
        P(None, "expert", "dp", None),
        P("dp", None),
        P(),
        P(),
        P(),
        P(),
        P(),
        P(),
        P(),
        P("dp", None),
        P(),
        P("dp", None),
        P("dp", None),
        P("dp", None),
        P("expert", None, None),
        P("expert", None, None),
    )
    out_specs = (
        P(None, "expert", "dp", None),
        P(None, "expert", "dp", None),
        P("dp", None),
        P(),
        P(),
        P(),
        P(),
        P(),
        P(),
        P(),
        P("dp", None),
        P(),
        P("dp", None),
        P("dp", None),
        P("dp", None),
        P("expert", "dp", None),
        P("expert", "dp", None),
    )
    return jax.shard_map(body, mesh=mesh, in_specs=in_specs, out_specs=out_specs, check_vma=False)
```

```python
import functools

import jax
import jax.numpy as jnp
from jax import lax
from jax.experimental import pallas as pl
from jax.experimental.pallas import tpu as pltpu
from jax.sharding import PartitionSpec as P

D = 1536
H = 48
PS = 64
S = 128
K = 4
FE = 512
FS = 1024
TOP = 6
MB = 2
DI = 3072
CONV = 3328
IN_W = 6448
EPSILON = 1e-05
BF = jnp.bfloat16
F32 = jnp.float32
MESH = pl.DeviceIdType.MESH
VMEM_LIMIT = 60 * 1024 * 1024


def mm(a, b):
    return jnp.dot(a, b, preferred_element_type=F32)


def mm_nt(a, b):
    return lax.dot_general(a, b, (((1,), (1,)), ((), ())), preferred_element_type=F32)


def mm_tn(a, b):
    return lax.dot_general(a, b, (((0,), (0,)), ((), ())), preferred_element_type=F32)


def rms_scale(values, gain):
    return values * lax.rsqrt(jnp.mean(values * values, axis=-1, keepdims=True) + EPSILON) * gain


ANY = pl.BlockSpec(memory_space=pl.ANY)
IN_VMEM = pl.BlockSpec(memory_space=pltpu.VMEM)


def places(axis):
    me = lax.axis_index(axis)
    if axis == "dp":
        core, ring, pair = lax.rem(me, 2), lax.rem(me // 2, 4), me // 8

        def at(hop, other, sibling=0):
            z = lax.rem(pair + other, 2)
            return (z * 4 + lax.rem(ring + hop + 4, 4)) * 2 + lax.rem(core + sibling, 2)
    else:
        pair, ring = lax.rem(me, 2), me // 2

        def at(hop, other, sibling=0):
            return lax.rem(ring + hop + 4, 4) * 2 + lax.rem(pair + other, 2)

    return me, at


class Task:
    ins, outs, scratch, reaches, turns = (), (), (), (), 1

    def greet(self, barrier):
        return 0


def peers_of(axis, everyone):
    me, at = places(axis)
    if everyone:
        n = lax.axis_size(axis)
        return [lax.rem(me + k, n) for k in range(1, n)]
    near = [at(1, 0), at(-1, 0), at(0, 1)]
    return near + [at(0, 0, 1)] if axis == "dp" else near


class Links:
    def __init__(self, axis, send, recv):
        self.axis, self.send, self.recv, self.started = axis, send, recv, []

    def push(self, number, src, dst, peer):
        copy = pltpu.make_async_remote_copy(
            src_ref=src,
            dst_ref=dst,
            send_sem=self.send.at[number],
            recv_sem=self.recv.at[number],
            device_id={self.axis: peer},
            device_id_type=MESH,
        )
        copy.start()
        self.started.append(copy)

    def arrived(self, number, dst):
        pltpu.make_async_copy(dst, dst, self.recv.at[number]).wait()

    def finish(self):
        for copy in self.started:
            copy.wait_send()


def halves(shape):
    rows = shape[0]
    cut = rows // 2 if len(shape) == 3 else rows // 32 * 16
    return pl.ds(0, rows), pl.ds(0, cut), pl.ds(cut, rows - cut), cut


class Gather(Task):
    def __init__(self, axis, x):
        self.axis, self.reaches = axis, ((axis, False),)
        self.ins = ((x, ANY),)
        n = lax.axis_size(axis)
        self.outs = ((jax.ShapeDtypeStruct((n,) + x.shape, x.dtype), ANY),)
        dma = pltpu.SemaphoreType.DMA
        self.scratch = (dma((19,)), dma((19,)), dma)

    def steps(self, ins, outs, scratch):
        return gather_steps(self.axis, ins[0], outs[0], *scratch)


def gather_steps(axis, x, out, send, recv, own_sem):
    me, at = places(axis)
    cores = axis == "dp"
    up, down, pair, sib = at(1, 0), at(-1, 0), at(0, 1), at(0, 0, 1)
    whole, first, second, _ = halves(x.shape)
    links = Links(axis, send, recv)

    def push(number, slot, rows, peer, src=None):
        src = out.at[slot] if src is None else src
        links.push(number, src.at[rows], out.at[slot].at[rows], peer)

    def arrived(number, slot, rows):
        links.arrived(number, out.at[slot].at[rows])

    push(0, me, whole, up, x)
    push(1, me, whole, down, x)
    push(2, me, whole, pair, x)
    if cores:
        push(3, me, whole, sib, x)
    own = pltpu.make_async_copy(x, out.at[me], own_sem)
    own.start()
    yield
    own.wait()
    arrived(2, pair, whole)
    share = first if cores else whole
    push(4, pair, share, up)
    push(5, pair, share, down)
    arrived(0, down, whole)
    push(7, down, first, up)
    arrived(1, up, whole)
    push(8, up, second, down)
    if cores:
        push(17, down, second, pair)
        push(18, up, second, pair)
        push(6, pair, whole, sib)
        push(9, down, whole, sib)
        push(10, up, whole, sib)
    yield
    arrived(4, at(-1, 1), share)
    push(11, at(-1, 1), first, up)
    arrived(5, at(1, 1), share)
    if cores:
        arrived(17, at(-1, 1), second)
        arrived(18, at(1, 1), second)
    push(12, at(1, 1), second, down)
    arrived(7, at(2, 0), first)
    arrived(8, at(2, 0), second)
    if cores:
        push(13, at(-1, 1), whole, sib)
        push(14, at(1, 1), whole, sib)
        push(15, at(2, 0), whole, sib)
    yield
    arrived(11, at(2, 1), first)
    arrived(12, at(2, 1), second)
    if cores:
        push(16, at(2, 1), whole, sib)
        yield
        for number, hop, other in (
            (3, 0, 0),
            (6, 0, 1),
            (9, -1, 0),
            (10, 1, 0),
            (13, -1, 1),
            (14, 1, 1),
            (15, 2, 0),
            (16, 2, 1),
        ):
            arrived(number, at(hop, other, 1), whole)
    links.finish()


ORDER = ((2, 1), (2, 0), (1, 1), (-1, 1), (1, 0), (-1, 0), (0, 1), (0, 0))


class Reduce(Task):
    def __init__(self, axis, x, dtype=F32):
        self.axis, self.reaches = axis, ((axis, False),)
        n, rows, columns = x.shape
        self.ins = ((x, ANY),)
        self.outs = ((jax.ShapeDtypeStruct((rows, columns), dtype), IN_VMEM),)
        _, _, _, cut = halves((rows, columns))
        buf = lambda *dims: pltpu.VMEM(dims + (columns,), BF)
        dma = pltpu.SemaphoreType.DMA
        dp = axis == "dp"
        self.scratch = (
            buf(8, rows),
            buf(8 if dp else 1, rows if dp else 16),
            buf(2, cut),
            buf(2, rows - cut),
            buf(2, rows),
            buf(2, rows),
            buf(rows),
            buf(2 if dp else 1, rows - cut if dp else 16),
            dma((19,)),
            dma((19,)),
            dma((8,)),
        )

    def steps(self, ins, outs, scratch):
        return reduce_steps(self.axis, ins[0], outs[0], *scratch)


def reduce_steps(
    axis, x, out, acc, sib_buf, a_buf, b_buf, c_buf, d_buf, e_buf, p_buf, send, recv, load
):
    me, at = places(axis)
    cores = axis == "dp"
    rows = acc.shape[1]
    widest = lambda count: max(k for k in range(16, 129, 16) if count % k == 0)
    block = lambda k: x.at[k] if len(x.shape) == 3 else x.at[pl.ds(pl.multiple_of(k * rows, 16), rows)]
    up, down, pair, sib = at(1, 0), at(-1, 0), at(0, 1), at(0, 0, 1)
    whole, first, second, cut = halves(acc.shape[1:])
    links = Links(axis, send, recv)
    push, arrived = links.push, links.arrived

    def add(dst, offset, count, *srcs):
        step = widest(count)

        @pl.loop(0, count // step)
        def _(i):
            at_rows = pl.ds(pl.multiple_of(offset + i * step, 16), step)
            total = dst[at_rows, :].astype(F32)
            for src in srcs:
                total += src[pl.ds(pl.multiple_of(i * step, 16), step), :].astype(F32)
            dst[at_rows, :] = total.astype(dst.dtype)

    loads = []
    for k, (hop, other) in enumerate(ORDER if x is not None else ()):
        if cores:
            push(k, block(at(hop, other, 1)), sib_buf.at[k], sib)
        copy = pltpu.make_async_copy(block(at(hop, other)), acc.at[k], load.at[k])
        copy.start()
        loads.append(copy)

    def ready(k):
        if loads:
            loads[k].wait()
        if cores:
            arrived(k, sib_buf.at[k])
            add(acc.at[k], 0, rows, sib_buf.at[k])

    yield
    for k in range(2):
        ready(k)
        push(8 + 2 * k, acc.at[k].at[first], a_buf.at[k], up)
        push(9 + 2 * k, acc.at[k].at[second], b_buf.at[k], down)
    yield
    upper, lower = pl.ds(0, cut), pl.ds(0, rows - cut)
    if cores:
        ready(2)
        push(17, acc.at[2].at[second], p_buf.at[0].at[lower], pair)
        ready(3)
        push(18, acc.at[3].at[first], p_buf.at[1].at[upper], pair)
        arrived(8, a_buf.at[0])
        add(acc.at[2], 0, cut, a_buf.at[0])
        push(12, acc.at[2].at[first], c_buf.at[0].at[upper], up)
        arrived(9, b_buf.at[0])
        add(acc.at[3], cut, rows - cut, b_buf.at[0])
        push(13, acc.at[3].at[second], d_buf.at[0].at[lower], down)
        ready(4)
        ready(5)
        arrived(10, a_buf.at[1])
        add(acc.at[4], 0, cut, a_buf.at[1])
        arrived(17, p_buf.at[0].at[lower])
        add(acc.at[4], cut, rows - cut, p_buf.at[0])
        push(14, acc.at[4], c_buf.at[1], up)
        arrived(11, b_buf.at[1])
        add(acc.at[5], cut, rows - cut, b_buf.at[1])
        arrived(18, p_buf.at[1].at[upper])
        add(acc.at[5], 0, cut, p_buf.at[1])
        push(15, acc.at[5], d_buf.at[1], down)
        yield
        ready(6)
        ready(7)
        arrived(12, c_buf.at[0].at[upper])
        add(acc.at[6], 0, cut, c_buf.at[0])
        arrived(13, d_buf.at[0].at[lower])
        add(acc.at[6], cut, rows - cut, d_buf.at[0])
    else:
        for k in range(2):
            above, below = 2 + 2 * k, 3 + 2 * k
            ready(above)
            ready(below)
            arrived(8 + 2 * k, a_buf.at[k])
            add(acc.at[above], 0, cut, a_buf.at[k])
            push(12 + 2 * k, acc.at[above], c_buf.at[k], up)
            arrived(9 + 2 * k, b_buf.at[k])
            add(acc.at[below], cut, rows - cut, b_buf.at[k])
            push(13 + 2 * k, acc.at[below], d_buf.at[k], down)
        yield
        ready(6)
        ready(7)
        arrived(12, c_buf.at[0])
        arrived(13, d_buf.at[0])
        add(acc.at[6], 0, rows, c_buf.at[0], d_buf.at[0])
    push(16, acc.at[6], e_buf, pair)
    yield
    arrived(14, c_buf.at[1])
    arrived(15, d_buf.at[1])
    yield
    arrived(16, e_buf)
    step = widest(rows)

    @pl.loop(0, rows // step)
    def _(i):
        at_rows = pl.ds(pl.multiple_of(i * step, 16), step)
        total = acc[7, at_rows, :].astype(F32) + c_buf[1, at_rows, :].astype(F32)
        total += d_buf[1, at_rows, :].astype(F32) + e_buf[at_rows, :].astype(F32)
        out[at_rows, :] = total.astype(out.dtype)

    links.finish()


class Direct(Task):
    def __init__(self, kind, axis, x):
        self.kind, self.axis, self.reaches = kind, axis, ((axis, True),)
        n = lax.axis_size(axis)
        shape = (n,) + x.shape if kind == "gather" else x.shape
        self.ins = ((x, ANY),)
        self.outs = ((jax.ShapeDtypeStruct(shape, x.dtype), ANY),)
        dma = pltpu.SemaphoreType.DMA
        self.scratch = (dma((n,)), dma((n,)), dma)

    def steps(self, ins, outs, scratch):
        return direct_steps(self.kind, self.axis, ins[0], outs[0], *scratch)


def direct_steps(kind, axis, x, out, send, recv, own_sem):
    n, me = lax.axis_size(axis), lax.axis_index(axis)
    links = Links(axis, send, recv)
    piece = lambda k: x if kind == "gather" else x.at[k]
    for k in range(1, n):
        peer = lax.rem(me + k, n)
        links.push(k, piece(peer), out.at[me], peer)
    own = pltpu.make_async_copy(piece(me), out.at[me], own_sem)
    own.start()
    yield
    for k in range(1, n):
        links.arrived(k, out.at[lax.rem(me - k + n, n)])
    own.wait()
    links.finish()


def run_tasks(tasks, number, name):
    operands, in_specs, out_shapes, out_specs, scratch, spans = [], [], [], [], [], []
    for task in tasks:
        spans.append((len(operands), len(out_shapes), len(scratch)))
        operands += [x for x, _ in task.ins]
        in_specs += [spec for _, spec in task.ins]
        out_shapes += [shape for shape, _ in task.outs]
        out_specs += [spec for _, spec in task.outs]
        scratch += list(task.scratch)

    def kernel(*refs):
        ins = refs[: len(operands)]
        outs = refs[len(operands) : len(operands) + len(out_shapes)]
        temps = refs[len(operands) + len(out_shapes) :]
        barrier = pltpu.get_barrier_semaphore()
        count = 0
        for axis in ("dp", "expert"):
            here = [everyone for task in tasks for name, everyone in task.reaches if name == axis]
            if here:
                peers = peers_of(axis, any(here))
                for peer in peers:
                    pl.semaphore_signal(
                        barrier, inc=1, device_id={axis: peer}, device_id_type=MESH
                    )
                count += len(peers)
        for task in tasks:
            count += task.greet(barrier)
        pl.semaphore_wait(barrier, count)
        running = []
        for task, (i, o, s) in zip(tasks, spans):
            steps = task.steps(
                ins[i : i + len(task.ins)],
                outs[o : o + len(task.outs)],
                temps[s : s + len(task.scratch)],
            )
            running.append((task.turns, steps))
        while running:
            left = []
            for turns, steps in running:
                if all(next(steps, "end") != "end" for _ in range(turns)):
                    left.append((turns, steps))
            running = left

    results = pl.pallas_call(
        kernel,
        out_shape=out_shapes,
        in_specs=in_specs,
        out_specs=out_specs,
        scratch_shapes=scratch,
        compiler_params=pltpu.CompilerParams(
            collective_id=number, has_side_effects=True, vmem_limit_bytes=VMEM_LIMIT
        ),
        name=name,
    )(*operands)
    return [results[o : o + len(task.outs)] for task, (_, o, _) in zip(tasks, spans)]


class Weights(Task):
    def __init__(self, x):
        self.reaches = (("dp", True), ("expert", False))
        self.swap, self.spread = Direct("all", "dp", x), Gather("expert", x)
        n = lax.axis_size("expert")
        full = jax.ShapeDtypeStruct((n,) + x.shape, x.dtype)
        self.ins = ((x, ANY),)
        self.outs = self.swap.outs + ((full, ANY),)
        self.scratch = self.swap.scratch + self.spread.scratch

    def steps(self, ins, outs, scratch):
        yield from direct_steps("all", "dp", ins[0], outs[0], *scratch[:3])
        yield
        yield from gather_steps("expert", outs[0], outs[1], *scratch[3:])


class ExpertGrads(Task):
    def __init__(self, x, pre_grad, gh, inc, experts, each, blocks):
        n, rows, _ = x.shape
        width, depth = gh.shape[2], inc.shape[1]
        self.experts, self.each = experts, each
        grads = jax.ShapeDtypeStruct(
            (blocks, depth // blocks + 2 * (each // blocks), 2 * width), BF
        )
        self.ins = tuple((v, ANY) for v in (x, pre_grad, gh, inc))
        self.outs = ((grads, ANY),)
        dma = pltpu.SemaphoreType.DMA
        vmem = lambda *dims: pltpu.VMEM(dims, BF)
        self.scratch = (
            vmem(n, rows, depth),
            vmem(*pre_grad.shape),
            vmem(*gh.shape),
            vmem(*inc.shape),
            dma((5,)),
            vmem(depth, n * rows),
            vmem(width, n * rows),
            vmem(*grads.shape),
        )

    def steps(self, ins, outs, scratch):
        x, pre_grad, gh, inc, sems, x_t, gh_t, grads = scratch
        n, rows, depth = x.shape
        width = gh.shape[2]
        experts, each = self.experts, self.each
        copy = lambda src, dst, k: pltpu.make_async_copy(src, dst, sems.at[k])
        load_x = copy(ins[0].at[:, :, pl.ds(0, depth)], x, 0)
        load_pre = copy(ins[1], pre_grad, 1)
        load_inc = copy(ins[3], inc, 3)
        load_gh = copy(ins[2], gh, 2)
        for load in (load_x, load_pre, load_gh, load_inc):
            load.start()
        yield
        tile = 256
        col = lambda i: pl.ds(pl.multiple_of(i * tile, tile), tile)
        load_x.wait()

        @pl.loop(0, depth // tile)
        def _(i):
            x_t[col(i), :] = x[:, :, col(i)].reshape(n * rows, tile).T

        load_pre.wait()
        blocks = grads.shape[0]
        up_rows = depth // blocks
        steps = 2 * width // tile
        for start, end in ((0, steps // 3), (steps // 3, steps)):

            @pl.loop(start, end)
            def _(i):
                value = mm(x_t[...], pre_grad[:, :, col(i)].reshape(n * rows, tile)).astype(BF)
                grads[:, :up_rows, col(i)] = value.reshape(blocks, up_rows, tile)

            yield
        load_gh.wait()

        @pl.loop(0, width // 128)
        def _(i):
            at_cols = pl.ds(pl.multiple_of(i * 128, 128), 128)
            gh_t[at_cols, :] = gh[:, :, at_cols].reshape(n * rows, 128).T

        load_inc.wait()
        piece_rows = each // blocks
        own = (width - experts * each) // blocks
        span = depth // 2
        spots = (((0, 0), (0, 2)), ((0, 1), (piece_rows, 0)))
        for half in range(2):

            @pl.loop(0, span // tile)
            def _(i):
                value = mm(gh_t[...], inc[:, col(half * span // tile + i)])
                for e in range(experts):
                    row, place = spots[half][e]
                    piece = value[e * each : (e + 1) * each].astype(BF)
                    grads[
                        :,
                        up_rows + row : up_rows + row + piece_rows,
                        col(place * span // tile + i),
                    ] = piece.reshape(blocks, piece_rows, tile)
                piece = value[experts * each :].reshape(blocks, own, tile)
                empty = jnp.zeros((blocks, piece_rows - own, tile), F32)
                piece = jnp.concatenate([piece, empty], axis=1).astype(BF)
                grads[:, up_rows + piece_rows :, col((1 + half) * span // tile + i)] = piece

        store = copy(grads, outs[0], 4)
        store.start()
        yield
        store.wait()


def chunks(rows, step=80):
    def over(work):
        @pl.loop(0, rows // step)
        def _(i):
            work(pl.ds(pl.multiple_of(i * step, 16), step))

    return over


def sides(v):
    high = v.astype(BF).astype(F32)
    turn = (iota((128, 128), 0) + 16 == iota((128, 128), 1)).astype(F32)
    return (high + exact(v - high, turn, ((1,), (0,)))).astype(BF)


def joined(v):
    turn = (iota((128, 128), 0) - 16 == iota((128, 128), 1)).astype(F32)
    back = exact(v, turn, ((1,), (0,)))
    return jnp.where(iota((1, 128), 1) < 16, v + back, 0.0)


class StreamGrad(Task):
    def __init__(self, parts, stream, gain, after_grad):
        self.reaches = (("dp", False),)
        self.reduce = Reduce("dp", parts)
        self.ins = self.reduce.ins + tuple((v, IN_VMEM) for v in (stream, gain, after_grad))
        shape = jax.ShapeDtypeStruct
        self.outs = ((shape(stream.shape, F32), IN_VMEM), (shape((1, D), F32), IN_VMEM))
        self.scratch = (pltpu.VMEM(stream.shape, F32),) + self.reduce.scratch

    def steps(self, ins, outs, scratch):
        x, stream, gain, after_grad = ins
        out, gain_grad = outs
        total = scratch[0]
        yield from reduce_steps("dp", x, total, *scratch[1:])
        gain_grad[...] = jnp.zeros_like(gain_grad)

        @chunks(total.shape[0])
        def _(rows):
            v = stream[rows, :].astype(F32)
            inv = lax.rsqrt(jnp.mean(v * v, axis=1, keepdims=True) + EPSILON)
            g = total[rows, :]
            gg = g * gain[...]
            gain_grad[...] += jnp.sum(g * v * inv, axis=0, keepdims=True)
            mean = jnp.mean(gg * v, axis=1, keepdims=True)
            out[rows, :] = after_grad[rows, :] + inv * gg - v * (inv * inv * inv * mean)


class InputGrad(Task):
    def __init__(self, gathered, d_proj, out_grad):
        self.reaches = (("expert", False),)
        n = lax.axis_size("expert")
        wide = d_proj.shape[1]
        rows = (D + out_grad.size // wide) // n
        self.reduce = Reduce("expert", jax.ShapeDtypeStruct((n, rows, wide), BF), BF)
        self.ins = tuple((v, ANY) for v in (*gathered, d_proj, out_grad.reshape(n, -1, wide)))
        self.outs = self.reduce.outs
        dma = pltpu.SemaphoreType.DMA
        self.scratch = (
            pltpu.VMEM((gathered[0].shape[0], MB * gathered[0].shape[1], D), BF),
            pltpu.VMEM(d_proj.shape, BF),
            pltpu.VMEM((n, rows, wide), BF),
            dma((4,)),
        ) + self.reduce.scratch

    def steps(self, ins, outs, scratch):
        g, d_proj, total, sems = scratch[:4]
        n, _, wide = total.shape
        each = D // n
        below = pl.ds(each, total.shape[1] - each)
        loads = (
            pltpu.make_async_copy(ins[2], d_proj, sems.at[0]),
            pltpu.make_async_copy(ins[3], total.at[:, below], sems.at[1]),
        ) + tuple(
            pltpu.make_async_copy(
                ins[m].at[:, :, pl.ds(0, D)],
                g.at[:, pl.ds(m * ins[m].shape[1], ins[m].shape[1])],
                sems.at[2 + m],
            )
            for m in range(MB)
        )
        for load in loads:
            load.start()
        yield
        for load in loads:
            load.wait()
        flat = g.shape[0] * g.shape[1]

        @pl.loop(0, n // 2)
        def _(i):
            columns = pl.ds(pl.multiple_of(i * 2 * each, 2 * each), 2 * each)
            value = mm_tn(g[:, :, columns].reshape(flat, 2 * each), d_proj[...]).astype(BF)
            total[pl.ds(2 * i, 2), :each, :] = value.reshape(2, each, wide)

        yield from reduce_steps("expert", total, outs[0], *scratch[4:])


class InputRows(Task):
    def __init__(self, x, heads):
        nd, ne = lax.axis_size("dp"), lax.axis_size("expert")
        self.heads = heads
        self.slices = D // nd // 16
        self.reaches = (("expert", False),)
        wide = 2 * DI + 2 * S + 128
        row = jax.ShapeDtypeStruct((16, wide), BF)
        self.gather = Gather("expert", row)
        self.ins = ((x, ANY),)
        self.outs = self.gather.outs
        dma = pltpu.SemaphoreType.DMA
        self.scratch = (
            pltpu.VMEM((nd, 16, x.shape[1]), BF),
            pltpu.VMEM((16, wide), BF),
            dma((2 * ne,)),
            dma((nd,)),
        ) + self.gather.scratch

    def greet(self, barrier):
        nd = lax.axis_size("dp")
        j = lax.axis_index("dp")
        for source in range(nd):
            pl.semaphore_signal(
                barrier, inc=1, device_id={"dp": source, "expert": j // 2}, device_id_type=MESH
            )
        return 2 * lax.axis_size("expert")

    def steps(self, ins, outs, scratch):
        x = ins[0]
        got, row, send, recv = scratch[:4]
        nd, ne = lax.axis_size("dp"), lax.axis_size("expert")
        j, e = lax.axis_index("dp"), lax.axis_index("expert")
        heads, di = self.heads, self.heads * PS
        sent = []
        for k in range(2):
            for c in range(ne):
                src = x.at[pl.ds((k * self.slices + min(c, self.slices - 1)) * 16, 16)]
                mine = (j == 2 * e + k) & (e == c)
                away = pltpu.make_async_remote_copy(
                    src_ref=src,
                    dst_ref=got.at[j],
                    send_sem=send.at[k * ne + c],
                    recv_sem=recv.at[j],
                    device_id={"dp": 2 * e + k, "expert": c},
                    device_id_type=MESH,
                )
                here = pltpu.make_async_copy(src, got.at[j], recv.at[j])
                pl.when(mine)(here.start)
                pl.when(jnp.logical_not(mine))(away.start)
                sent.append((mine, away))
        yield
        for source in range(nd):
            pltpu.make_async_copy(got.at[source], got.at[source], recv.at[source]).wait()
        piece = lambda source, start, size: got[source, :, start : start + size].astype(F32)
        for source in range(0, nd, 2):
            for half in range(2):
                pair = [piece(source + k, half * di, di) for k in range(2)]
                start = half * DI + source * di
                row[:, start : start + 2 * di] = jnp.concatenate(pair, axis=1).astype(BF)
        total = piece(0, 2 * di, 2 * S)
        for source in range(1, nd):
            total = total + piece(source, 2 * di, 2 * S)
        row[:, 2 * DI : 2 * DI + 2 * S] = total.astype(BF)
        steps = [piece(source, 2 * di + 2 * S, 128)[:, :heads] for source in range(nd)]
        steps.append(jnp.zeros((16, 128 - nd * heads), F32))
        row[:, 2 * DI + 2 * S :] = jnp.concatenate(steps, axis=1).astype(BF)
        yield from gather_steps("expert", row, outs[0], *scratch[4:])
        for mine, away in sent:
            pl.when(jnp.logical_not(mine))(away.wait_send)


class Rest(Task):
    def __init__(self, d_sum, sums):
        self.reaches = (("expert", False),)
        self.top = d_sum.shape[0] - D // lax.axis_size("expert")
        wide = d_sum.shape[1]
        x = jax.ShapeDtypeStruct((self.top + 64, wide), BF)
        self.gather = Gather("expert", x)
        self.ins = ((d_sum, ANY), (sums, ANY))
        self.outs = self.gather.outs
        self.scratch = (
            pltpu.VMEM(x.shape, BF),
            pltpu.SemaphoreType.DMA((6,)),
        ) + self.gather.scratch

    def steps(self, ins, outs, scratch):
        d_sum, sums = ins
        x, sems = scratch[:2]
        top, wide = self.top, x.shape[1]
        third = wide // 3
        last = sums.shape[1] - third
        moves = [(d_sum.at[pl.ds(d_sum.shape[0] - top, top)], x.at[pl.ds(0, top)])]
        for q in range(3):
            moves.append(
                (
                    sums.at[pl.ds(32 * q, 32), pl.ds(last, third)],
                    x.at[pl.ds(top, 32), pl.ds(third * q, third)],
                )
            )
        for half in range(2):
            moves.append(
                (
                    sums.at[pl.ds(128, 16), pl.ds(wide * (1 + half), wide)],
                    x.at[pl.ds(top + 32 + 16 * half, 16)],
                )
            )
        copies = [pltpu.make_async_copy(a, b, sems.at[k]) for k, (a, b) in enumerate(moves)]
        for copy in copies:
            copy.start()
        for copy in copies:
            copy.wait()
        yield from gather_steps("expert", x, outs[0], *scratch[2:])


class Small(Task):
    def __init__(self, added, own, row):
        self.reaches = (("expert", True), ("dp", True))
        nd, ne = lax.axis_size("dp"), lax.axis_size("expert")
        self.ins = ((added, IN_VMEM), (own, IN_VMEM), (row, IN_VMEM))
        rows = added.shape[1] + own.shape[0] + row.shape[1] // 128
        shape = (rows + -rows % 8, 128)
        self.outs = ((jax.ShapeDtypeStruct((nd,) + shape, F32), ANY),)
        dma = pltpu.SemaphoreType.DMA
        self.scratch = (
            pltpu.VMEM(shape, F32),
            pltpu.VMEM((ne,) + shape, F32),
            pltpu.VMEM(shape, F32),
            dma((ne,)),
            dma((ne,)),
            dma,
            dma((nd,)),
            dma((nd,)),
            dma,
        )

    def steps(self, ins, outs, scratch):
        added, own, row = ins
        x, parts, total = scratch[:3]
        x[...] = jnp.zeros_like(x)
        first = added.shape[1]
        second = first + own.shape[0]
        x[:first, :] = jnp.sum(added[...], axis=0)
        x[first:second, :] = own[...]
        for k in range(row.shape[1] // 128):
            x[second + k : second + k + 1, :] = row[:, k * 128 : (k + 1) * 128]
        yield from direct_steps("gather", "expert", x, parts, *scratch[3:6])
        total[...] = jnp.sum(parts[...], axis=0)
        yield from direct_steps("gather", "dp", total, outs[0], *scratch[6:9])


def results_kernel(full, rest, sums, after, out_sum, *outs):
    input_grad, output_grad, shared_up, shared_down, up, down, block_output = outs
    for c in range(input_grad.shape[0] // 16):
        input_grad[c * 16 : (c + 1) * 16, :] = full[c, :, :IN_W].astype(F32)
    ne, rows, wide = rest.shape
    top = rows - 64
    for half in range(2):
        value = rest[half * ne // 2 : (half + 1) * ne // 2, :top, :].reshape(-1, wide)
        output_grad[:, half * wide : (half + 1) * wide] = value.astype(F32)

    each = shared_up.shape[1] // 2
    fs = each // ne
    unit = shared_down.shape[0] // ne
    column = iota((1, each), 1)
    source = lax.rem(column // unit, ne) * fs + column // (unit * ne) * unit + lax.rem(column, unit)
    order = (iota((each, each), 0) == source).astype(BF)
    for half in range(2):
        groups = []
        for q in range(3):
            start = q * 2 * fs + half * fs
            pieces = [rest[e, top : top + 32, start : start + fs] for e in range(ne)]
            groups.append(jnp.concatenate(pieces, axis=1))
        value = mm(jnp.concatenate(groups, axis=0), order)
        shared_up[:, half * each : (half + 1) * each] = value
        for e in range(ne):
            low = top + 32 + 16 * half
            value = rest[e, low : low + 16, :].astype(F32)[:unit]
            shared_down[e * unit : (e + 1) * unit, half * wide : (half + 1) * wide] = value
    experts, dr, both = up.shape
    for e in range(experts):
        up[e] = sums[:dr, e * both : (e + 1) * both].astype(F32)
    below = down.shape[1]
    down[0] = sums[dr : dr + below, : 2 * wide].astype(F32)
    down[1, :, :wide] = sums[dr : dr + below, 2 * wide :].astype(F32)
    down[1, :, wide:] = sums[dr + below :, :wide].astype(F32)
    block_output[...] = (after[...] + out_sum[...]).astype(BF)


def write_results(full, rest, sums, after, out_sum, shapes):
    return pl.pallas_call(
        results_kernel,
        out_shape=[jax.ShapeDtypeStruct(*shape) for shape in shapes],
        in_specs=[IN_VMEM] * 5,
        out_specs=[IN_VMEM] * len(shapes),
        compiler_params=pltpu.CompilerParams(vmem_limit_bytes=VMEM_LIMIT),
        name="results",
    )(full, rest, sums, after, out_sum)


class Experts(Task):
    def __init__(
        self, low, mask, inc, w_up, w_down, s_up, s_down, after, mixed, factors, gain, router, own
    ):
        x = jax.ShapeDtypeStruct((low.shape[0], low.shape[1] + 128), BF)
        self.reaches = (("expert", False),)
        self.gather = Gather("expert", x)
        n = lax.axis_size("expert")
        rows, wide = x.shape
        depth = inc.shape[1]
        experts, _, both = w_up.shape
        self.experts = experts
        all_rows = jax.ShapeDtypeStruct((n, rows, wide), BF)
        self.reduce = Reduce("expert", all_rows)
        hidden = experts * both // 2 + s_down.shape[0]
        pre = jax.ShapeDtypeStruct((n, rows, 2 * hidden), BF)
        gh = jax.ShapeDtypeStruct((n, rows, hidden), BF)
        self.ins = tuple((v, ANY) for v in (inc, w_up, w_down, s_up, s_down)) + tuple(
            (v, IN_VMEM) for v in (low, mask, after, mixed, factors, gain, router, own)
        )
        part = jax.ShapeDtypeStruct((n, rows, depth), BF)
        shape = jax.ShapeDtypeStruct
        self.outs = (
            ((all_rows, IN_VMEM),)
            + tuple((v, ANY) for v in (pre, gh, part))
            + (
                (shape((rows, depth), F32), IN_VMEM),
                (shape((rows, wide), BF), IN_VMEM),
                (shape((1, depth), F32), IN_VMEM),
                (shape((16, depth), F32), IN_VMEM),
            )
        )
        dma = pltpu.SemaphoreType.DMA
        self.scratch = (
            (pltpu.VMEM((n, rows, depth), BF),)
            + tuple(pltpu.VMEM(v.shape, BF) for v in (w_up, w_down, s_up, s_down))
            + (pltpu.VMEM((2 * rows, wide), BF), pltpu.VMEM((2 * rows, depth), BF))
            + (pltpu.VMEM((2 * rows, 2 * hidden), BF), pltpu.VMEM((2 * rows, hidden), BF))
            + (pltpu.VMEM(pre.shape, BF), pltpu.VMEM(gh.shape, BF))
            + (pltpu.VMEM((2 * rows, 128), F32), dma((22,)), pltpu.VMEM(part.shape, BF))
            + (pltpu.VMEM((rows, wide), F32), pltpu.VMEM((rows, wide), BF))
            + self.gather.scratch
            + self.reduce.scratch
        )

    def steps(self, ins, outs, scratch):
        inc_in = ins[0]
        low_in, mask, after, mixed, factors, gain, router, own = ins[5:]
        x_all, pre_out, gh_out, part_out, after_grad, payload, gain_grad, router_grad = outs
        inc, w_up, w_down, s_up, s_down, xs, incs, pg, ghs, pre, gh, extra, sems = scratch[:13]
        part, dx, gather_scratch, reduce_scratch = scratch[13], scratch[14], scratch[16:19], scratch[19:]
        x = scratch[15]
        acc = reduce_scratch[0]
        me, at = places("expert")
        n, rows, depth = inc.shape
        experts, _, both = w_up.shape
        each = both // 2
        shared = s_down.shape[0]
        tile = min(256, each)
        loads = [
            pltpu.make_async_copy(src, dst, sems.at[k])
            for k, (src, dst) in enumerate(zip(ins[1:5], (w_up, w_down, s_up, s_down)))
        ]
        loads += [
            pltpu.make_async_copy(inc_in.at[pl.ds(k * rows, rows)], inc.at[k], sems.at[13 + k])
            for k in range(n)
        ]
        for load in loads:
            load.start()

        logits = mm(low_in[...], router[...])
        chosen = mask[...]
        top = jnp.max(jnp.where(chosen > 0.0, logits, -1e30), axis=1, keepdims=True)
        e = jnp.where(chosen > 0.0, jnp.exp(jnp.minimum(logits - top, 0.0)), 0.0)
        table = e / jnp.sum(e, axis=1, keepdims=True)
        x[:, :depth] = low_in[...]
        x[:, depth:] = sides(table)
        arriving = gather_steps("expert", x, x_all, *gather_scratch)
        next(arriving)
        next(arriving)
        for load in loads:
            load.wait()
        lane = lax.broadcasted_iota(jnp.int32, (1, 128), 1)
        stores = []

        def unit(a, b, u, scale):
            sig = jax.nn.sigmoid(a)
            act = a * sig
            hidden = act * b
            gu = u * scale
            da = gu * b * (sig + act * (1.0 - sig))
            return hidden * scale, da, gu * act, u * hidden

        def compute(hop, places_in_acc):
            slots = (at(hop, 0), at(hop, 1))
            for k, slot in enumerate(slots):
                part = pl.ds(k * rows, rows)
                xs[part, :] = x_all[slot]
                incs[part, :] = inc[slot]
            extra[...] = jnp.zeros_like(extra)

            @pl.loop(0, experts * (each // tile))
            def _(i):
                e, f = i // (each // tile), lax.rem(i, each // tile)
                place = me * experts + e
                table = xs[:, depth:].astype(F32)
                chosen = (lane == place) | (lane == place + n * experts)
                scale = jnp.sum(jnp.where(chosen, table, 0.0), axis=1, keepdims=True)
                left = pl.ds(pl.multiple_of(f * tile, tile), tile)
                right = pl.ds(pl.multiple_of(each + f * tile, tile), tile)
                a = mm(xs[:, :depth], w_up[e, :, left])
                b = mm(xs[:, :depth], w_up[e, :, right])
                u = mm_nt(incs[...], w_down[e, left, :])
                h, da, db, dots = unit(a, b, u, scale)
                ghs[:, pl.ds(pl.multiple_of(e * each + f * tile, tile), tile)] = h.astype(BF)
                pg[:, pl.ds(pl.multiple_of(e * both + f * tile, tile), tile)] = da.astype(BF)
                pg[:, pl.ds(pl.multiple_of(e * both + each + f * tile, tile), tile)] = db.astype(BF)
                extra[...] += jnp.where(lane == place, jnp.sum(dots, axis=1, keepdims=True), 0.0)

            a = mm(xs[:, :depth], s_up[:, :shared])
            b = mm(xs[:, :depth], s_up[:, shared:])
            u = mm_nt(incs[...], s_down[...])
            h, da, db, _ = unit(a, b, u, 1.0)
            ghs[:, experts * each :] = h.astype(BF)
            pg[:, experts * both : experts * both + shared] = da.astype(BF)
            pg[:, experts * both + shared :] = db.astype(BF)

            @pl.loop(0, depth // tile)
            def _(i):
                columns = pl.ds(pl.multiple_of(i * tile, tile), tile)
                total = mm_nt(pg[:, experts * both :], s_up[columns, :])
                for e in range(experts):
                    total += mm_nt(pg[:, e * both : (e + 1) * both], w_up[e, columns, :])
                for k, place in enumerate(places_in_acc):
                    acc[place, :, columns] = total[k * rows : (k + 1) * rows].astype(BF)

            grads = extra[...]
            both_parts = sides(grads)
            for k, (slot, place) in enumerate(zip(slots, places_in_acc)):
                part = pl.ds(k * rows, rows)
                acc[place, :, depth:] = both_parts[k * rows : (k + 1) * rows]
                pre[slot] = pg[part, :]
                gh[slot] = ghs[part, :]
                store = pltpu.make_async_copy(pre.at[slot], pre_out.at[slot], sems.at[4 + len(stores)])
                store.start()
                stores.append(store)

        compute(0, (7, 6))
        next(arriving)
        compute(1, (4, 2))
        compute(-1, (5, 3))
        for _ in arriving:
            pass
        compute(2, (1, 0))
        store = pltpu.make_async_copy(gh, gh_out, sems.at[12])
        store.start()
        stores.append(store)
        summing = reduce_steps("expert", None, dx, *reduce_scratch)
        next(summing)
        for half in range(2):
            next(summing)

            @pl.loop(half * depth // tile // 2, (half + 1) * depth // tile // 2)
            def _(i):
                columns = pl.ds(pl.multiple_of(i * tile, tile), tile)
                hid = lambda start, size: gh[:, :, start : start + size].reshape(n * rows, size)
                total = mm(hid(experts * each, shared), s_down[:, columns])
                for e in range(experts):
                    total += mm(hid(e * each, each), w_down[e, :, columns])
                part[:, :, columns] = total.astype(BF).reshape(n, rows, tile)

        store = pltpu.make_async_copy(part, part_out, sems.at[21])
        store.start()
        stores.append(store)
        yield from summing
        gain_grad[...] = jnp.zeros_like(gain_grad)
        spread = joined(dx[:, depth:])
        logit = table * (spread - jnp.sum(table * spread, axis=1, keepdims=True))
        logit_low = logit.astype(BF)
        router_grad[...] = mm_tn(logit_low, low_in[...])[:16]
        dx[:, :depth] += mm_nt(logit_low, router[...])

        @chunks(rows)
        def _(at_rows):
            v, inv = after[at_rows, :], factors[at_rows, 1:2]
            g = dx[at_rows, :depth]
            gg = g * gain[...]
            gain_grad[...] += jnp.sum(g * v * inv, axis=0, keepdims=True)
            mean = jnp.mean(gg * v, axis=1, keepdims=True)
            total = own[at_rows, :].astype(F32) + inv * gg - v * (inv * inv * inv * mean)
            after_grad[at_rows, :] = total
            total_low = total.astype(BF)
            payload[at_rows, :depth] = total_low
            s = jnp.sum(total_low.astype(F32) * mixed[at_rows, :], axis=1, keepdims=True)
            r = factors[at_rows, 0:1]
            r_high, s_high = r.astype(BF).astype(F32), s.astype(BF).astype(F32)
            extras = jnp.where(lane == 0, r_high, jnp.where(lane == 1, r - r_high, 0.0))
            extras = jnp.where(lane == 2, s_high, jnp.where(lane == 3, s - s_high, extras))
            payload[at_rows, depth:] = extras.astype(BF)

        for store in stores:
            store.wait()


EDGE = 8


def pieces(v, count):
    out = []
    for _ in range(count):
        out.append(v.astype(BF))
        v = v - out[-1].astype(F32)
    return out


def exact(v, ones, dims, count=2):
    ones = ones.astype(BF)
    parts = [
        lax.dot_general(p, ones, (dims, ((), ())), preferred_element_type=F32)
        for p in pieces(v, count)
    ]
    return sum(parts[1:], parts[0])


def exact_right(ones, v, dims, count=2):
    ones = ones.astype(BF)
    parts = [
        lax.dot_general(ones, p, (dims, ((), ())), preferred_element_type=F32)
        for p in pieces(v, count)
    ]
    return sum(parts[1:], parts[0])


def iota(shape, axis):
    return lax.broadcasted_iota(jnp.int32, shape, axis)


class Block:
    def __init__(self, m, slot, start, proj, ext, lengths, taps, heads_vec, heads):
        loc = proj.shape[0]
        di = heads * PS
        width = di + 2 * S
        self.heads, self.di = heads, di
        first = lengths[m, 0]
        second = first + lengths[m, 1]

        def doc(p):
            return (p >= first).astype(jnp.int32) + (p >= second).astype(jnp.int32)

        self.doc = doc
        self.at = start + iota((loc, 1), 0)
        docs = doc(self.at)
        docs_row = doc(start + iota((1, loc), 1))
        last_doc, before_doc = doc(start + loc - 1), doc(start - 1)
        self.keep = (docs == before_doc).astype(F32)
        self.keep_last = (last_doc == before_doc).astype(F32)
        self.same_last = (docs == last_doc).astype(F32)
        self.gate = proj[:, :di]
        ext[slot, EDGE : EDGE + loc, :] = proj[:, di : di + width].astype(BF).astype(F32)
        total = jnp.broadcast_to(taps[K : K + 1, :], (loc, width))
        self.shifted = []
        for k in range(K):
            back = K - 1 - k
            value = ext[slot, EDGE - back : EDGE - back + loc, :]
            if back:
                value = value * (docs == doc(self.at - back)).astype(F32)
            self.shifted.append(value)
            total = total + taps[k : k + 1, :] * value
        self.sig = jax.nn.sigmoid(total)
        self.total = total
        filtered = total * self.sig
        self.x = filtered[:, :di]
        self.write = filtered[:, di : di + S].astype(BF)
        self.read = filtered[:, di + S :].astype(BF)
        self.raw = proj[:, di + width :] + heads_vec[0:1, :]
        self.steps = jnp.maximum(self.raw, 0.0) + jnp.log1p(jnp.exp(-jnp.abs(self.raw)))
        self.rate = heads_vec[1:2, :]
        rise = self.steps * self.rate
        rows, cols = iota((loc, loc), 0), iota((loc, loc), 1)
        self.lower = (cols <= rows).astype(F32)
        self.cum = exact_right(self.lower, rise, ((1,), (0,)), 3)
        cum_rows = exact(rise, (rows <= cols).astype(F32), ((0,), (0,)), 3)
        self.last = self.cum[loc - 1 : loc, :]
        self.grow = jnp.exp(self.cum) * self.keep
        self.fall = jnp.exp(self.last - self.cum) * self.same_last
        self.decay = jnp.exp(self.last) * self.keep_last
        allowed = (cols <= rows) & (docs == docs_row)
        scores = mm_nt(self.read, self.write)
        self.spread, self.mixing = [], []
        for h in range(heads):
            span = self.cum[:, h : h + 1] - cum_rows[h : h + 1, :]
            shape = jnp.exp(jnp.where(allowed, span, -1e30))
            self.spread.append(shape)
            self.mixing.append(shape * scores)
        self.lane = iota((1, di), 1)
        self.steps_wide = self.widen(self.steps)
        self.grow_wide = self.widen(self.grow)
        self.weight_wide = self.widen(self.fall * self.steps)
        self.scaled = self.x * self.steps_wide
        self.pushed = self.x * self.weight_wide

    def widen(self, v):
        out = jnp.broadcast_to(v[:, 0:1], (v.shape[0], self.di))
        for h in range(1, self.heads):
            out = jnp.where(self.lane >= h * PS, v[:, h : h + 1], out)
        return out

    def per_head(self, parts):
        out = parts[0]
        for h in range(1, self.heads):
            out = jnp.where(self.lane >= h * PS, parts[h], out)
        return out

    def decay_rows(self):
        rows = iota((self.di, 1), 0)
        out = jnp.broadcast_to(self.decay[:, 0:1], (self.di, 1))
        for h in range(1, self.heads):
            out = jnp.where(rows >= h * PS, self.decay[:, h : h + 1], out)
        return out


def load_weights(pieces_ref, w, sem):
    copies = [
        pltpu.make_async_copy(pieces_ref.at[k], w.at[:, k], sem.at[k]) for k in range(w.shape[1])
    ]
    for copy in copies:
        copy.start()
    for copy in copies:
        copy.wait()


class Forward(Task):
    def __init__(self, blocks, x, incoming, lengths, w_out, vectors, stream, gain, heads):
        self.heads = heads
        self.reaches = (("dp", True), ("expert", False))
        nd = lax.axis_size("dp")
        loc = stream.shape[0] // MB
        di = heads * PS
        wide = blocks.shape[2]
        shape = jax.ShapeDtypeStruct
        self.weights = Weights(blocks)
        self.gathers = [Gather("dp", v) for v in x] + [Gather("expert", incoming)]
        part = shape((nd, loc, D + 128), BF)
        self.reduces = [Reduce("dp", part) for _ in range(MB)]
        self.saved = (
            shape((MB, nd, loc, wide), F32),
            shape((MB, nd, loc, di), F32),
            shape((MB, nd, di, S), F32),
        )
        self.ins = (
            ((blocks, ANY),)
            + tuple((v, ANY) for v in (*x, incoming))
            + ((lengths, pl.BlockSpec(memory_space=pltpu.SMEM)),)
            + tuple((v, IN_VMEM) for v in (w_out,) + tuple(vectors) + (stream, gain))
        )
        full = self.weights.outs[1][0]
        rows = stream.shape[0]
        self.outs = (
            ((full, ANY),)
            + tuple((gather.outs[0][0], ANY) for gather in self.gathers)
            + tuple((v, ANY) for v in self.saved)
            + (
                (shape((rows, D), BF), IN_VMEM),
                (shape((rows, D), F32), IN_VMEM),
                (shape((rows, D), F32), IN_VMEM),
                (shape((rows, 128), F32), IN_VMEM),
            )
        )
        vmem = lambda v: pltpu.VMEM(v.shape, v.dtype)
        dma = pltpu.SemaphoreType.DMA
        slices = D // nd // full.shape[2]
        self.scratch = (
            (vmem(self.weights.outs[0][0]), vmem(full))
            + tuple(vmem(gather.outs[0][0]) for gather in self.gathers[:MB])
            + tuple(vmem(v) for v in self.saved)
            + tuple(vmem(part) for _ in range(MB))
            + tuple(pltpu.VMEM((loc, D + 128), F32) for _ in range(MB))
            + (pltpu.VMEM((nd, slices, full.shape[2], wide), BF), dma((slices,)), dma((9,)))
            + (pltpu.VMEM((2, loc + EDGE, di + 2 * S), F32), pltpu.VMEM((di, S), F32))
            + (pltpu.VMEM((4, loc, di), BF),)
            + self.weights.scratch
            + self.gathers[0].scratch
            + self.gathers[1].scratch
            + self.gathers[2].scratch
            + self.reduces[0].scratch
            + self.reduces[1].scratch
        )

    def steps(self, ins, outs, scratch):
        x, incoming, lengths = ins[1:3], ins[3], ins[4]
        w_out, taps, heads_vec, lanes_vec, stream, gain = ins[5:]
        w_full, g_out, inc_out, saved_out = outs[0], outs[1:3], outs[3], outs[4:7]
        low_out, after, mixed, factors = outs[7:]
        swapped, pieces_all = scratch[:2]
        g, (proj, scan, states), parts, totals = scratch[2:4], scratch[4:7], scratch[7:9], scratch[9:11]
        w, w_sem, sems, ext, state, gated = scratch[11:17]
        rest = scratch[17:]
        rest, weight_sems = rest[6:], rest[:6]
        gather_sems, rest = (rest[:3], rest[3:6], rest[6:9]), rest[9:]
        count = len(self.reduces[0].scratch)
        reduce_scratch = (rest[:count], rest[count:])
        heads = self.heads
        nd, loc, _ = g[0].shape
        di = heads * PS
        stores = []

        def store(src, dst):
            copy = pltpu.make_async_copy(src, dst, sems.at[len(stores)])
            copy.start()
            stores.append(copy)

        def work(m, start, end):
            many = end - start
            rows = g[m][start:end, :, :D].reshape(many * loc, D)
            value = mm(rows, w[...].reshape(D, -1))
            proj[m, start:end] = value.reshape(many, loc, value.shape[1])

            @pl.loop(start // 2, end // 2)
            def _(pair):
                two = []
                for k in range(2):
                    b = pair * 2 + k
                    ext[k, 0:EDGE, :] = ext[1 - k, loc : loc + EDGE, :]
                    two.append(
                        Block(m, k, b * loc, proj[m, b], ext, lengths, taps, heads_vec, heads)
                    )
                before = [state[...]]
                for part in two:
                    before.append(
                        part.decay_rows() * before[-1] + mm_tn(part.pushed.astype(BF), part.write)
                    )
                state[...] = before[2]
                for k, part in enumerate(two):
                    b = pair * 2 + k
                    states[m, b] = before[k]
                    scaled = part.scaled.astype(BF)
                    inner = part.per_head(
                        [mm(part.mixing[h].astype(BF), scaled) for h in range(heads)]
                    )
                    carried = mm_nt(part.read, before[k].astype(BF)) * part.grow_wide
                    out = inner + carried + lanes_vec[1:2, :] * part.x
                    scan[m, b] = out
                    y = out * (part.gate * jax.nn.sigmoid(part.gate))
                    square = jnp.sum(y * y, axis=1, keepdims=True)
                    high = square.astype(BF).astype(F32)
                    gated[b - start] = (y * lanes_vec[0:1, :]).astype(BF)
                    column = iota((loc, 128), 1)
                    sums = jnp.where(column == 0, high, jnp.where(column == 1, square - high, 0.0))
                    parts[m][b, :, D:] = sums.astype(BF)

            value = mm(gated[...].reshape(many * loc, di), w_out[...])
            parts[m][start:end, :, :D] = value.astype(BF).reshape(many, loc, D)

        def reset():
            ext[...] = jnp.zeros_like(ext)
            state[...] = jnp.zeros_like(state)

        def norm(m):
            @chunks(loc)
            def _(rows):
                at_rows = pl.ds(pl.multiple_of(m * loc + rows.start, 16), rows.size)
                lane = iota((1, 128), 1)
                total = totals[m]
                squares = total[rows, D:]
                square = jnp.sum(jnp.where(lane < 2, squares, 0.0), axis=1, keepdims=True)
                r = lax.rsqrt(square / DI + EPSILON)
                mix = total[rows, :D] * r
                v = stream[at_rows, :].astype(F32) + mix
                inv = lax.rsqrt(jnp.mean(v * v, axis=1, keepdims=True) + EPSILON)
                low_out[at_rows, :] = (v * inv * gain[...]).astype(BF)
                after[at_rows, :] = v
                mixed[at_rows, :] = mix
                factors[at_rows, :] = jnp.where(lane == 0, r, jnp.where(lane == 1, inv, 0.0))

        weights = self.weights.steps(ins[:1], (swapped, pieces_all), weight_sems)
        first = gather_steps("dp", x[0], g[0], *gather_sems[0])
        second = gather_steps("dp", x[1], g[1], *gather_sems[1])
        third = gather_steps("expert", incoming, inc_out, *gather_sems[2])
        next(weights)
        next(first)
        next(weights)
        next(weights, None)
        next(first)
        next(weights, None)
        next(first)
        next(second)
        next(weights, None)
        next(first)
        for _ in weights:
            pass
        for _ in first:
            pass
        load_weights(pieces_all, w, w_sem)
        store(pieces_all, w_full)
        store(g[0], g_out[0])
        reset()
        for k in range(4):
            next(third, None)
            work(0, 4 * k, 4 * k + 4)
            next(second, None)
        for steps in (second, third):
            for _ in steps:
                pass
        store(g[1], g_out[1])
        sums = [
            reduce_steps("dp", parts[m], totals[m], *reduce_scratch[m]) for m in range(MB)
        ]
        next(sums[0])
        for src, dst in zip((proj, scan, states), saved_out):
            store(src.at[0], dst.at[0])
        reset()
        for k in range(4):
            next(sums[0])
            work(1, 4 * k, 4 * k + 4)
        next(sums[1])
        for src, dst in zip((proj, scan, states), saved_out):
            store(src.at[1], dst.at[1])
        for _ in sums[0]:
            pass
        next(sums[1])
        norm(0)
        for _ in sums[1]:
            pass
        norm(1)
        for copy in stores:
            copy.wait()
        yield


def backward_kernel(
    heads,
    lengths,
    grad,
    w_pieces,
    w_out,
    taps,
    heads_vec,
    lanes_vec,
    proj,
    proj_before,
    scan,
    states,
    d_proj,
    normed_part,
    d_out,
    d_taps,
    d_heads,
    d_lanes,
    ext,
    d_ext,
    d_state,
    out_sum,
    w,
    w_sem,
):
    step = pl.program_id(0)
    b = pl.num_programs(0) - 1 - step
    loc = grad.shape[1] // MB
    di = heads * PS
    width = di + 2 * S

    @pl.when(step == 0)
    def _():
        for ref in (d_ext, d_state, out_sum, d_taps, d_heads, d_lanes):
            ref[...] = jnp.zeros_like(ref)
        load_weights(w_pieces, w, w_sem)

    gated_grad = mm_nt(grad[0, :, :D], w_out[...])
    extra = grad[0, :, D:].astype(F32)
    has_before = (b > 0).astype(F32)
    pick = (iota((di, S), 0) // PS == iota((di, S), 1)).astype(F32)
    for m in range(MB):
        rows = slice(m * loc, (m + 1) * loc)
        edge = proj_before[m, 0, loc - EDGE : loc, di : di + width]
        ext[m, 0:EDGE, :] = edge.astype(BF).astype(F32) * has_before
        part = Block(m, m, b * loc, proj[m, 0], ext, lengths, taps, heads_vec, heads)
        gain, skip = lanes_vec[0:1, :], lanes_vec[1:2, :]
        r = extra[rows, 0:1] + extra[rows, 1:2]
        s = extra[rows, 2:3] + extra[rows, 3:4]
        out = scan[m, 0]
        sig = jax.nn.sigmoid(part.gate)
        act = part.gate * sig
        yr = out * act * r
        gg = gated_grad[rows]
        d_lanes[0:1, :] += jnp.sum(gg * yr, axis=0, keepdims=True)
        out_sum[...] += mm_tn((yr * gain).astype(BF), grad[0, rows, :D])
        dy = r * (gg * gain) - yr * (r * s / DI)
        d_gate = dy * out * (sig + act * (1.0 - sig))
        do = dy * act
        do_low = do.astype(BF)
        x = part.x
        d_lanes[1:2, :] += jnp.sum(do * x, axis=0, keepdims=True)
        dx = skip * do
        before = states[m, 0]
        before_low = before.astype(BF)
        ds = d_state[m]
        ds_low = ds.astype(BF)

        d_scores = jnp.zeros((loc, loc), F32)
        d_scaled, d_cum = [], jnp.zeros((loc, S), F32)
        head_lane = iota((loc, S), 1)
        for h in range(heads):
            inside = (part.lane >= h * PS) & (part.lane < (h + 1) * PS)
            own = jnp.where(inside, part.scaled, 0.0).astype(BF)
            d_mix = mm_nt(do_low, own)
            d_scaled.append(mm_tn(part.mixing[h].astype(BF), do_low))
            d_scores = d_scores + d_mix * part.spread[h]
            d_span = d_mix * part.mixing[h]
            ones = (head_lane == h).astype(F32)
            d_cum = d_cum + exact(d_span, ones, ((1,), (0,))) - exact(d_span, ones, ((0,), (0,)))
        d_scaled = part.per_head(d_scaled)
        dx = dx + d_scaled * part.steps_wide
        d_scores_low = d_scores.astype(BF)
        d_read = mm(d_scores_low, part.write)
        d_write = mm_tn(d_scores_low, part.read)

        d_carry = do * part.grow_wide
        d_carry_low = d_carry.astype(BF)
        carried = mm_nt(part.read, before_low)
        d_read = d_read + mm(d_carry_low, before_low)

        d_pushed = mm_nt(part.write, ds_low)
        d_write = d_write + mm(part.pushed.astype(BF), ds_low)
        dx = dx + d_pushed * part.weight_wide
        sums = exact(
            jnp.concatenate([d_carry * carried, d_pushed * x, d_scaled * x], axis=0),
            pick,
            ((1,), (0,)),
        )
        d_weight = sums[loc : 2 * loc]
        d_fall = d_weight * part.fall * part.steps
        d_cum = d_cum + sums[:loc] - d_fall
        d_steps = sums[2 * loc :] + d_weight * part.fall
        state_dot = jnp.sum(ds * before, axis=1, keepdims=True)
        d_decay = exact(jnp.broadcast_to(state_dot, (di, S)), pick, ((0,), (0,)))[0:1, :]
        d_last = jnp.sum(d_fall, axis=0, keepdims=True) + d_decay * part.decay
        d_cum = d_cum + jnp.where(iota((loc, 1), 0) == loc - 1, d_last, 0.0)
        d_state[m] = part.decay_rows() * ds + mm_tn(d_carry_low, part.read)

        d_rise = exact_right(part.lower, d_cum, ((0,), (0,)))
        d_steps = d_steps + d_rise * part.rate
        d_raw = d_steps * jax.nn.sigmoid(part.raw)
        d_heads[0:1, :] += jnp.sum(d_raw, axis=0, keepdims=True)
        d_heads[1:2, :] += jnp.sum(d_rise * part.steps * part.rate, axis=0, keepdims=True)

        d_total = jnp.concatenate([dx, d_write, d_read], axis=1)
        d_total = d_total * (part.sig + part.total * part.sig * (1.0 - part.sig))
        for k in range(K):
            d_taps[k : k + 1, :] += jnp.sum(d_total * part.shifted[k], axis=0, keepdims=True)
        d_taps[K : K + 1, :] += jnp.sum(d_total, axis=0, keepdims=True)
        d_ext[m, loc : loc + EDGE, :] = d_ext[m, 0:EDGE, :]
        d_ext[m, 0:loc, :] = d_total
        d_seq = taps[K - 1 : K, :] * d_total
        docs = part.doc(part.at)
        for ahead in range(1, K):
            same = (docs == part.doc(part.at + ahead)).astype(F32)
            d_seq = d_seq + taps[K - 1 - ahead : K - ahead, :] * (
                same * d_ext[m, ahead : ahead + loc, :]
            )
        d_proj[0, rows, :di] = d_gate.astype(BF)
        d_proj[0, rows, di : di + width] = d_seq.astype(BF)
        d_proj[0, rows, di + width :] = jnp.where(head_lane < heads, d_raw, 0.0).astype(BF)
    for half in range(2):
        d_out[half] = out_sum[:, half * D // 2 : (half + 1) * D // 2].astype(BF)
    normed_part[0] = mm_nt(d_proj[0], w[...].reshape(D, -1)).astype(BF)


def weight_scratch(w):
    slices = D // w.shape[1] // w.shape[2]
    return [
        pltpu.VMEM((w.shape[1], slices) + w.shape[2:], BF),
        pltpu.SemaphoreType.DMA((slices,)),
    ]


def block_spec(shape, index):
    return pl.BlockSpec((1,) + shape[1:], lambda i: (index(i),) + (0,) * (len(shape) - 1))


def pair_spec(shape, index):
    return pl.BlockSpec((MB, 1) + shape[2:], lambda i: (0, index(i)) + (0,) * (len(shape) - 2))


def whole_spec(shape):
    return pl.BlockSpec(shape, lambda i: (0,) * len(shape))


def mixer_backward(lengths, grad, w, w_out, taps, heads_vec, lanes_vec, proj, scan, states, heads):
    nb, rows, _ = grad.shape
    di = heads * PS
    width = di + 2 * S
    back = lambda i: nb - 1 - i
    before = lambda i: jnp.maximum(nb - 2 - i, 0)
    per_block = [
        jax.ShapeDtypeStruct((nb, rows, w.shape[-1]), BF),
        jax.ShapeDtypeStruct((nb, rows, D), BF),
    ]
    sums = [
        jax.ShapeDtypeStruct((2, di, D // 2), BF),
        jax.ShapeDtypeStruct((8, width), F32),
        jax.ShapeDtypeStruct((8, S), F32),
        jax.ShapeDtypeStruct((8, di), F32),
    ]
    return pl.pallas_call(
        functools.partial(backward_kernel, heads),
        grid=(nb,),
        out_shape=per_block + sums,
        in_specs=[pl.BlockSpec(memory_space=pltpu.SMEM), block_spec(grad.shape, back)]
        + [pl.BlockSpec(memory_space=pl.ANY)]
        + [whole_spec(v.shape) for v in (w_out, taps, heads_vec, lanes_vec)]
        + [pair_spec(proj.shape, back), pair_spec(proj.shape, before)]
        + [pair_spec(scan.shape, back), pair_spec(states.shape, back)],
        out_specs=[block_spec(v.shape, back) for v in per_block]
        + [whole_spec(v.shape) for v in sums],
        scratch_shapes=[
            pltpu.VMEM((MB, rows // MB + EDGE, width), F32),
            pltpu.VMEM((MB, rows // MB + EDGE, width), F32),
            pltpu.VMEM((MB, di, S), F32),
            pltpu.VMEM((di, D), F32),
        ]
        + weight_scratch(w),
        compiler_params=pltpu.CompilerParams(vmem_limit_bytes=VMEM_LIMIT),
        name="mixer_backward",
    )(lengths, grad, w, w_out, taps, heads_vec, lanes_vec, proj, proj, scan, states)


def body(
    tokens,
    lengths,
    routes,
    cotangent,
    input_weight,
    filter_weight,
    filter_bias,
    step_bias,
    decay_log,
    skip_gain,
    norm_gain,
    gated_gain,
    output_weight,
    moe_gain,
    router_weight,
    shared_gate_up,
    shared_down,
    expert_gate_up,
    expert_down,
):
    nd, ne = lax.axis_size("dp"), lax.axis_size("expert")
    me_d, me_e = lax.axis_index("dp"), lax.axis_index("expert")
    loc = tokens.shape[2]
    heads = H // nd
    di = heads * PS
    rows_t = MB * loc
    experts = expert_gate_up.shape[0] * ne
    el = expert_gate_up.shape[0]
    dr = D // nd
    fs = FS // ne
    fsr = FS // nd
    fsl = fsr // ne

    pad = 128 - heads
    piece = 16
    place = jnp.minimum(me_e, dr // piece - 1) * piece
    mine = lax.dynamic_slice_in_dim(input_weight, place, piece, 0)
    blocks = jnp.concatenate(
        [
            jnp.moveaxis(mine[:, :DI].reshape(piece, nd, di), 1, 0),
            jnp.moveaxis(mine[:, DI : 2 * DI].reshape(piece, nd, di), 1, 0),
            jnp.broadcast_to(mine[None, :, 2 * DI : 2 * DI + 2 * S], (nd, piece, 2 * S)),
            jnp.moveaxis(mine[:, DI + CONV :].reshape(piece, nd, heads), 1, 0),
            jnp.zeros((nd, piece, pad), BF),
        ],
        axis=2,
    )
    wcols = blocks.shape[2]

    sg = shared_gate_up.reshape(dr, 2, nd, ne, fsl)
    sg = lax.dynamic_index_in_dim(sg, me_e, 3, False).reshape(dr, 2 * fs)
    sd = lax.dynamic_slice_in_dim(shared_down, me_e * fsl, fsl, 0)
    packed = jnp.concatenate([sg.reshape(-1), sd.reshape(-1), router_weight.reshape(-1)])
    packed_cols = packed.size // loc
    packed = jnp.pad(packed.reshape(loc, -1), ((0, 0), (0, -packed_cols % 128)))

    stream = tokens.reshape(rows_t, D).astype(F32)
    incoming = cotangent.reshape(rows_t, D)
    route_rows = routes.reshape(rows_t, TOP)
    normed = rms_scale(stream, norm_gain).astype(BF)
    taps = jnp.concatenate(
        [lax.dynamic_slice_in_dim(filter_weight, me_d * di, di, 1), filter_weight[:, DI:]], axis=1
    )
    tap_bias = jnp.concatenate(
        [lax.dynamic_slice_in_dim(filter_bias, me_d * di, di, 0), filter_bias[DI:]], axis=0
    )
    my_heads = lambda v: lax.dynamic_slice_in_dim(v, me_d * heads, heads, 0)
    my_gain = lax.dynamic_slice_in_dim(gated_gain, me_d * di, di, 0)

    taps_vec = jnp.concatenate([taps, tap_bias[None], jnp.zeros((3, di + 2 * S), F32)], axis=0)
    heads_vec = jnp.stack([my_heads(step_bias), -jnp.exp(my_heads(decay_log))])
    heads_vec = jnp.pad(heads_vec, ((0, 6), (0, S - heads)))
    lanes_vec = jnp.pad(
        jnp.stack([my_gain, jnp.repeat(my_heads(skip_gain), PS)]), ((0, 6), (0, 0))
    )
    vectors = (taps_vec, heads_vec, lanes_vec)
    gain_row = moe_gain.reshape(1, D)
    own_tokens = tokens.reshape(rows_t, D)
    forward = Forward(
        blocks,
        (normed[:loc], jnp.concatenate([normed[loc:], packed], axis=1)),
        incoming,
        lengths[:, 0],
        output_weight,
        vectors,
        own_tokens,
        gain_row,
        heads,
    )
    (results,) = run_tasks([forward], 1, "forward")
    w_in, *gathered, inc_all, proj, scan, states, moe_in, after_mixer, mixed, factors = results
    inc_all = inc_all.reshape(ne * rows_t, D)
    packed_all = gathered[1][:, :, D : D + packed_cols]
    packed_all = packed_all.reshape(nd, -1)
    sg_full = packed_all[:, : sg.size].reshape(D, 2 * fs)
    sd_full = packed_all[:, sg.size : sg.size + sd.size].reshape(fs, D)
    router_full = packed_all[:, sg.size + sd.size :].reshape(D, experts)
    mask = jnp.sum(
        (route_rows[:, :, None] == jnp.arange(128, dtype=jnp.int32)).astype(F32), axis=1
    )
    router_wide = jnp.pad(router_full, ((0, 0), (0, 128 - experts)))
    ((moe_all, pre_grad, gh, out_part, after_grad, grad_payload, moe_gain_grad, router_part),) = (
        run_tasks(
            [
                Experts(
                    moe_in,
                    mask,
                    inc_all,
                    expert_gate_up,
                    expert_down,
                    sg_full,
                    sd_full,
                    after_mixer,
                    mixed,
                    factors,
                    gain_row,
                    router_wide,
                    incoming,
                )
            ],
            3,
            "experts",
        )
    )
    width = gh.shape[2]
    (out_sum,), (grad_blocks,), (grad_all,) = run_tasks(
        [
            Reduce("expert", out_part),
            ExpertGrads(moe_all, pre_grad, gh, inc_all, el, FE, nd),
            Gather("dp", grad_payload),
        ],
        5,
        "gather_grad",
    )
    all_sum = lax.psum_scatter(grad_blocks, "dp", scatter_dimension=0, tiled=True)[0]
    d_proj, normed_part, output_part, d_taps, d_heads, d_lanes = mixer_backward(
        lengths[:, 0], grad_all, w_in, output_weight, *vectors, proj, scan, states, heads
    )
    def rows_of(parts, count):
        flat = jnp.concatenate([part.reshape(-1) for part in parts])
        return jnp.pad(flat, (0, count * 128 - flat.size)).reshape(count, 128)

    added = (d_taps[:K, di:], d_taps[K, di:], moe_gain_grad, router_part)
    own = (
        d_taps[:K, :di],
        d_taps[K, :di],
        d_heads[0, :heads],
        d_heads[1, :heads],
        jnp.sum(d_lanes[1].reshape(heads, PS), axis=1),
        d_lanes[0],
    )
    added_size = sum(part.size for part in added)
    added_rows = -(-added_size // (nd * 1024)) * 8
    own_rows = -(-sum(part.size for part in own) // 128)
    norm_rows = D // 128
    (tokens_grad, norm_gain_grad), (d_sum,), (added_in,) = run_tasks(
        [
            StreamGrad(normed_part, own_tokens, norm_gain.reshape(1, D), after_grad),
            InputGrad(
                gathered,
                d_proj.reshape(nd * rows_t, wcols),
                output_part,
            ),
            Direct("all", "dp", rows_of(added, nd * added_rows).reshape(nd, added_rows, 128)),
        ],
        6,
        "reduce_grads",
    )
    (small_all,), (rest_all,), (slices_all,) = run_tasks(
        [
            Small(added_in, rows_of(own, own_rows), norm_gain_grad),
            Rest(d_sum, all_sum),
            InputRows(d_sum, heads),
        ],
        7,
        "finish",
    )
    input_grad, output_grad, shared_up_grad, shared_down_grad, expert_up_grad, expert_down_grad, (
        block_output
    ) = write_results(
        slices_all,
        rest_all,
        all_sum,
        after_mixer,
        out_sum,
        (
            ((dr, IN_W), F32),
            (output_weight.shape, F32),
            ((dr, 2 * FS), F32),
            ((fsr, D), F32),
            ((el, dr, 2 * FE), F32),
            ((el, FE // nd, D), F32),
            ((rows_t, D), BF),
        ),
    )
    added_all = small_all[:, :added_rows].reshape(-1)
    own_all = small_all[:, added_rows : added_rows + own_rows].reshape(nd, -1)
    norm_gain_grad = jnp.sum(
        small_all[:, added_rows + own_rows : added_rows + own_rows + norm_rows], axis=0
    ).reshape(D)

    def split(flat, parts):
        out, start = [], 0
        for part in parts:
            out.append(flat[..., start : start + part.size].reshape(flat.shape[:-1] + part.shape))
            start += part.size
        return out

    added_taps, added_bias, moe_gain_grad, router_all = split(added_all, added)
    own_taps, own_bias, own_steps, own_decay, own_skip, own_gain = split(own_all, own)
    small = (
        jnp.concatenate([jnp.moveaxis(own_taps, 0, 1).reshape(K, DI), added_taps], axis=1),
        jnp.concatenate([own_bias.reshape(-1), added_bias]),
        own_steps.reshape(-1),
        own_decay.reshape(-1),
        own_skip.reshape(-1),
        norm_gain_grad,
        own_gain.reshape(-1),
        moe_gain_grad.reshape(D),
    )
    router_grad = lax.dynamic_slice_in_dim(router_all, me_d * dr, dr, 1).T
    shape = (MB, 1, loc, D)
    return (
        block_output.reshape(shape),
        tokens_grad.reshape(shape),
        input_grad,
        small[0],
        small[1],
        small[2],
        small[3],
        small[4],
        small[5],
        small[6],
        output_grad.astype(F32),
        small[7],
        router_grad,
        shared_up_grad,
        shared_down_grad,
        expert_up_grad,
        expert_down_grad,
    )


def solution(mesh):
    in_specs = (
        P(None, "expert", "dp", None),
        P(None, "expert", None),
        P(None, "expert", "dp", None),
        P(None, "expert", "dp", None),
        P("dp", None),
        P(),
        P(),
        P(),
        P(),
        P(),
        P(),
        P(),
        P("dp", None),
        P(),
        P("dp", None),
        P("dp", None),
        P("dp", None),
        P("expert", None, None),
        P("expert", None, None),
    )
    out_specs = (
        P(None, "expert", "dp", None),
        P(None, "expert", "dp", None),
        P("dp", None),
        P(),
        P(),
        P(),
        P(),
        P(),
        P(),
        P(),
        P("dp", None),
        P(),
        P("dp", None),
        P("dp", None),
        P("dp", None),
        P("expert", "dp", None),
        P("expert", "dp", None),
    )
    return jax.shard_map(body, mesh=mesh, in_specs=in_specs, out_specs=out_specs, check_vma=False)
```

```python
import functools

import jax
import jax.numpy as jnp
from jax import lax
from jax.experimental import pallas as pl
from jax.experimental.pallas import tpu as pltpu
from jax.sharding import PartitionSpec as P

D = 1536
H = 48
PS = 64
S = 128
K = 4
FE = 512
FS = 1024
TOP = 6
MB = 2
DI = 3072
CONV = 3328
IN_W = 6448
EPSILON = 1e-05
BF = jnp.bfloat16
F32 = jnp.float32
MESH = pl.DeviceIdType.MESH
VMEM_LIMIT = 60 * 1024 * 1024


def mm(a, b):
    return jnp.dot(a, b, preferred_element_type=F32)


def mm_nt(a, b):
    return lax.dot_general(a, b, (((1,), (1,)), ((), ())), preferred_element_type=F32)


def mm_tn(a, b):
    return lax.dot_general(a, b, (((0,), (0,)), ((), ())), preferred_element_type=F32)


def rms_scale(values, gain):
    return values * lax.rsqrt(jnp.mean(values * values, axis=-1, keepdims=True) + EPSILON) * gain


ANY = pl.BlockSpec(memory_space=pl.ANY)
IN_VMEM = pl.BlockSpec(memory_space=pltpu.VMEM)


def places(axis):
    me = lax.axis_index(axis)
    if axis == "dp":
        core, ring, pair = lax.rem(me, 2), lax.rem(me // 2, 4), me // 8

        def at(hop, other, sibling=0):
            z = lax.rem(pair + other, 2)
            return (z * 4 + lax.rem(ring + hop + 4, 4)) * 2 + lax.rem(core + sibling, 2)
    else:
        pair, ring = lax.rem(me, 2), me // 2

        def at(hop, other, sibling=0):
            return lax.rem(ring + hop + 4, 4) * 2 + lax.rem(pair + other, 2)

    return me, at


class Task:
    ins, outs, scratch, reaches, turns = (), (), (), (), 1

    def greet(self, barrier):
        return 0


def peers_of(axis, everyone):
    me, at = places(axis)
    if everyone:
        n = lax.axis_size(axis)
        return [lax.rem(me + k, n) for k in range(1, n)]
    near = [at(1, 0), at(-1, 0), at(0, 1)]
    return near + [at(0, 0, 1)] if axis == "dp" else near


class Links:
    def __init__(self, axis, send, recv):
        self.axis, self.send, self.recv, self.started = axis, send, recv, []

    def push(self, number, src, dst, peer):
        copy = pltpu.make_async_remote_copy(
            src_ref=src,
            dst_ref=dst,
            send_sem=self.send.at[number],
            recv_sem=self.recv.at[number],
            device_id={self.axis: peer},
            device_id_type=MESH,
        )
        copy.start()
        self.started.append(copy)

    def arrived(self, number, dst):
        pltpu.make_async_copy(dst, dst, self.recv.at[number]).wait()

    def finish(self):
        for copy in self.started:
            copy.wait_send()


def halves(shape):
    rows = shape[0]
    cut = rows // 2 if len(shape) == 3 else rows // 32 * 16
    return pl.ds(0, rows), pl.ds(0, cut), pl.ds(cut, rows - cut), cut


class Gather(Task):
    def __init__(self, axis, x):
        self.axis, self.reaches = axis, ((axis, False),)
        self.ins = ((x, ANY),)
        n = lax.axis_size(axis)
        self.outs = ((jax.ShapeDtypeStruct((n,) + x.shape, x.dtype), ANY),)
        dma = pltpu.SemaphoreType.DMA
        self.scratch = (dma((19,)), dma((19,)), dma)

    def steps(self, ins, outs, scratch):
        return gather_steps(self.axis, ins[0], outs[0], *scratch)


def gather_steps(axis, x, out, send, recv, own_sem):
    me, at = places(axis)
    cores = axis == "dp"
    up, down, pair, sib = at(1, 0), at(-1, 0), at(0, 1), at(0, 0, 1)
    whole, first, second, _ = halves(x.shape)
    links = Links(axis, send, recv)

    def push(number, slot, rows, peer, src=None):
        src = out.at[slot] if src is None else src
        links.push(number, src.at[rows], out.at[slot].at[rows], peer)

    def arrived(number, slot, rows):
        links.arrived(number, out.at[slot].at[rows])

    push(0, me, whole, up, x)
    push(1, me, whole, down, x)
    push(2, me, whole, pair, x)
    if cores:
        push(3, me, whole, sib, x)
    own = pltpu.make_async_copy(x, out.at[me], own_sem)
    own.start()
    yield
    own.wait()
    arrived(2, pair, whole)
    share = first if cores else whole
    push(4, pair, share, up)
    push(5, pair, share, down)
    arrived(0, down, whole)
    push(7, down, first, up)
    arrived(1, up, whole)
    push(8, up, second, down)
    if cores:
        push(17, down, second, pair)
        push(18, up, second, pair)
        push(6, pair, whole, sib)
        push(9, down, whole, sib)
        push(10, up, whole, sib)
    yield
    arrived(4, at(-1, 1), share)
    push(11, at(-1, 1), first, up)
    arrived(5, at(1, 1), share)
    if cores:
        arrived(17, at(-1, 1), second)
        arrived(18, at(1, 1), second)
    push(12, at(1, 1), second, down)
    arrived(7, at(2, 0), first)
    arrived(8, at(2, 0), second)
    if cores:
        push(13, at(-1, 1), whole, sib)
        push(14, at(1, 1), whole, sib)
        push(15, at(2, 0), whole, sib)
    yield
    arrived(11, at(2, 1), first)
    arrived(12, at(2, 1), second)
    if cores:
        push(16, at(2, 1), whole, sib)
        yield
        for number, hop, other in (
            (3, 0, 0),
            (6, 0, 1),
            (9, -1, 0),
            (10, 1, 0),
            (13, -1, 1),
            (14, 1, 1),
            (15, 2, 0),
            (16, 2, 1),
        ):
            arrived(number, at(hop, other, 1), whole)
    links.finish()


ORDER = ((2, 1), (2, 0), (1, 1), (-1, 1), (1, 0), (-1, 0), (0, 1), (0, 0))


class Reduce(Task):
    def __init__(self, axis, x, dtype=F32):
        self.axis, self.reaches = axis, ((axis, False),)
        n, rows, columns = x.shape
        self.ins = ((x, ANY),)
        self.outs = ((jax.ShapeDtypeStruct((rows, columns), dtype), IN_VMEM),)
        _, _, _, cut = halves((rows, columns))
        buf = lambda *dims: pltpu.VMEM(dims + (columns,), BF)
        dma = pltpu.SemaphoreType.DMA
        dp = axis == "dp"
        self.scratch = (
            buf(8, rows),
            buf(8 if dp else 1, rows if dp else 16),
            buf(2, cut),
            buf(2, rows - cut),
            buf(2, rows),
            buf(2, rows),
            buf(rows),
            buf(2 if dp else 1, rows - cut if dp else 16),
            dma((19,)),
            dma((19,)),
            dma((8,)),
        )

    def steps(self, ins, outs, scratch):
        return reduce_steps(self.axis, ins[0], outs[0], *scratch)


def reduce_steps(
    axis, x, out, acc, sib_buf, a_buf, b_buf, c_buf, d_buf, e_buf, p_buf, send, recv, load
):
    me, at = places(axis)
    cores = axis == "dp"
    rows = acc.shape[1]
    widest = lambda count: max(k for k in range(16, 129, 16) if count % k == 0)
    block = lambda k: x.at[k] if len(x.shape) == 3 else x.at[pl.ds(pl.multiple_of(k * rows, 16), rows)]
    up, down, pair, sib = at(1, 0), at(-1, 0), at(0, 1), at(0, 0, 1)
    whole, first, second, cut = halves(acc.shape[1:])
    links = Links(axis, send, recv)
    push, arrived = links.push, links.arrived

    def add(dst, offset, count, *srcs):
        step = widest(count)

        @pl.loop(0, count // step)
        def _(i):
            at_rows = pl.ds(pl.multiple_of(offset + i * step, 16), step)
            total = dst[at_rows, :].astype(F32)
            for src in srcs:
                total += src[pl.ds(pl.multiple_of(i * step, 16), step), :].astype(F32)
            dst[at_rows, :] = total.astype(dst.dtype)

    loads = []
    for k, (hop, other) in enumerate(ORDER if x is not None else ()):
        if cores:
            push(k, block(at(hop, other, 1)), sib_buf.at[k], sib)
        copy = pltpu.make_async_copy(block(at(hop, other)), acc.at[k], load.at[k])
        copy.start()
        loads.append(copy)

    def ready(k):
        if loads:
            loads[k].wait()
        if cores:
            arrived(k, sib_buf.at[k])
            add(acc.at[k], 0, rows, sib_buf.at[k])

    yield
    for k in range(2):
        ready(k)
        push(8 + 2 * k, acc.at[k].at[first], a_buf.at[k], up)
        push(9 + 2 * k, acc.at[k].at[second], b_buf.at[k], down)
    yield
    upper, lower = pl.ds(0, cut), pl.ds(0, rows - cut)
    if cores:
        ready(2)
        push(17, acc.at[2].at[second], p_buf.at[0].at[lower], pair)
        ready(3)
        push(18, acc.at[3].at[first], p_buf.at[1].at[upper], pair)
        arrived(8, a_buf.at[0])
        add(acc.at[2], 0, cut, a_buf.at[0])
        push(12, acc.at[2].at[first], c_buf.at[0].at[upper], up)
        arrived(9, b_buf.at[0])
        add(acc.at[3], cut, rows - cut, b_buf.at[0])
        push(13, acc.at[3].at[second], d_buf.at[0].at[lower], down)
        ready(4)
        ready(5)
        arrived(10, a_buf.at[1])
        add(acc.at[4], 0, cut, a_buf.at[1])
        arrived(17, p_buf.at[0].at[lower])
        add(acc.at[4], cut, rows - cut, p_buf.at[0])
        push(14, acc.at[4], c_buf.at[1], up)
        arrived(11, b_buf.at[1])
        add(acc.at[5], cut, rows - cut, b_buf.at[1])
        arrived(18, p_buf.at[1].at[upper])
        add(acc.at[5], 0, cut, p_buf.at[1])
        push(15, acc.at[5], d_buf.at[1], down)
        yield
        ready(6)
        ready(7)
        arrived(12, c_buf.at[0].at[upper])
        add(acc.at[6], 0, cut, c_buf.at[0])
        arrived(13, d_buf.at[0].at[lower])
        add(acc.at[6], cut, rows - cut, d_buf.at[0])
    else:
        for k in range(2):
            above, below = 2 + 2 * k, 3 + 2 * k
            ready(above)
            ready(below)
            arrived(8 + 2 * k, a_buf.at[k])
            add(acc.at[above], 0, cut, a_buf.at[k])
            push(12 + 2 * k, acc.at[above], c_buf.at[k], up)
            arrived(9 + 2 * k, b_buf.at[k])
            add(acc.at[below], cut, rows - cut, b_buf.at[k])
            push(13 + 2 * k, acc.at[below], d_buf.at[k], down)
        yield
        ready(6)
        ready(7)
        arrived(12, c_buf.at[0])
        arrived(13, d_buf.at[0])
        add(acc.at[6], 0, rows, c_buf.at[0], d_buf.at[0])
    push(16, acc.at[6], e_buf, pair)
    yield
    arrived(14, c_buf.at[1])
    arrived(15, d_buf.at[1])
    yield
    arrived(16, e_buf)
    step = widest(rows)

    @pl.loop(0, rows // step)
    def _(i):
        at_rows = pl.ds(pl.multiple_of(i * step, 16), step)
        total = acc[7, at_rows, :].astype(F32) + c_buf[1, at_rows, :].astype(F32)
        total += d_buf[1, at_rows, :].astype(F32) + e_buf[at_rows, :].astype(F32)
        out[at_rows, :] = total.astype(out.dtype)

    links.finish()


class Direct(Task):
    def __init__(self, kind, axis, x):
        self.kind, self.axis, self.reaches = kind, axis, ((axis, True),)
        n = lax.axis_size(axis)
        shape = (n,) + x.shape if kind == "gather" else x.shape
        self.ins = ((x, ANY),)
        self.outs = ((jax.ShapeDtypeStruct(shape, x.dtype), ANY),)
        dma = pltpu.SemaphoreType.DMA
        self.scratch = (dma((n,)), dma((n,)), dma)

    def steps(self, ins, outs, scratch):
        return direct_steps(self.kind, self.axis, ins[0], outs[0], *scratch)


def direct_steps(kind, axis, x, out, send, recv, own_sem):
    n, me = lax.axis_size(axis), lax.axis_index(axis)
    links = Links(axis, send, recv)
    piece = lambda k: x if kind == "gather" else x.at[k]
    for k in range(1, n):
        peer = lax.rem(me + k, n)
        links.push(k, piece(peer), out.at[me], peer)
    own = pltpu.make_async_copy(piece(me), out.at[me], own_sem)
    own.start()
    yield
    for k in range(1, n):
        links.arrived(k, out.at[lax.rem(me - k + n, n)])
    own.wait()
    links.finish()


def run_tasks(tasks, number, name):
    operands, in_specs, out_shapes, out_specs, scratch, spans = [], [], [], [], [], []
    for task in tasks:
        spans.append((len(operands), len(out_shapes), len(scratch)))
        operands += [x for x, _ in task.ins]
        in_specs += [spec for _, spec in task.ins]
        out_shapes += [shape for shape, _ in task.outs]
        out_specs += [spec for _, spec in task.outs]
        scratch += list(task.scratch)

    def kernel(*refs):
        ins = refs[: len(operands)]
        outs = refs[len(operands) : len(operands) + len(out_shapes)]
        temps = refs[len(operands) + len(out_shapes) :]
        barrier = pltpu.get_barrier_semaphore()
        count = 0
        for axis in ("dp", "expert"):
            here = [everyone for task in tasks for name, everyone in task.reaches if name == axis]
            if here:
                peers = peers_of(axis, any(here))
                for peer in peers:
                    pl.semaphore_signal(
                        barrier, inc=1, device_id={axis: peer}, device_id_type=MESH
                    )
                count += len(peers)
        for task in tasks:
            count += task.greet(barrier)
        pl.semaphore_wait(barrier, count)
        running = []
        for task, (i, o, s) in zip(tasks, spans):
            steps = task.steps(
                ins[i : i + len(task.ins)],
                outs[o : o + len(task.outs)],
                temps[s : s + len(task.scratch)],
            )
            running.append((task.turns, steps))
        while running:
            left = []
            for turns, steps in running:
                if all(next(steps, "end") != "end" for _ in range(turns)):
                    left.append((turns, steps))
            running = left

    results = pl.pallas_call(
        kernel,
        out_shape=out_shapes,
        in_specs=in_specs,
        out_specs=out_specs,
        scratch_shapes=scratch,
        compiler_params=pltpu.CompilerParams(
            collective_id=number, has_side_effects=True, vmem_limit_bytes=VMEM_LIMIT
        ),
        name=name,
    )(*operands)
    return [results[o : o + len(task.outs)] for task, (_, o, _) in zip(tasks, spans)]


class Weights(Task):
    def __init__(self, x):
        self.reaches = (("dp", True), ("expert", False))
        self.swap, self.spread = Direct("all", "dp", x), Gather("expert", x)
        n = lax.axis_size("expert")
        full = jax.ShapeDtypeStruct((n,) + x.shape, x.dtype)
        self.ins = ((x, ANY),)
        self.outs = self.swap.outs + ((full, ANY),)
        self.scratch = self.swap.scratch + self.spread.scratch

    def steps(self, ins, outs, scratch):
        yield from direct_steps("all", "dp", ins[0], outs[0], *scratch[:3])
        yield
        yield from gather_steps("expert", outs[0], outs[1], *scratch[3:])


class ExpertGrads(Task):
    def __init__(self, x, pre_grad, gh, inc, experts, each, blocks):
        n, rows, _ = x.shape
        width, depth = gh.shape[2], inc.shape[1]
        self.experts, self.each = experts, each
        grads = jax.ShapeDtypeStruct(
            (blocks, depth // blocks + 2 * (each // blocks), 2 * width), BF
        )
        self.ins = tuple((v, ANY) for v in (x, pre_grad, gh, inc))
        self.outs = ((grads, ANY),)
        dma = pltpu.SemaphoreType.DMA
        vmem = lambda *dims: pltpu.VMEM(dims, BF)
        self.scratch = (
            vmem(n, rows, depth),
            vmem(*pre_grad.shape),
            vmem(*gh.shape),
            vmem(*inc.shape),
            dma((5,)),
            vmem(depth, n * rows),
            vmem(width, n * rows),
            vmem(*grads.shape),
        )

    def steps(self, ins, outs, scratch):
        x, pre_grad, gh, inc, sems, x_t, gh_t, grads = scratch
        n, rows, depth = x.shape
        width = gh.shape[2]
        experts, each = self.experts, self.each
        copy = lambda src, dst, k: pltpu.make_async_copy(src, dst, sems.at[k])
        load_x = copy(ins[0].at[:, :, pl.ds(0, depth)], x, 0)
        load_pre = copy(ins[1], pre_grad, 1)
        load_inc = copy(ins[3], inc, 3)
        load_gh = copy(ins[2], gh, 2)
        for load in (load_x, load_pre, load_gh, load_inc):
            load.start()
        yield
        tile = 256
        col = lambda i: pl.ds(pl.multiple_of(i * tile, tile), tile)
        load_x.wait()

        @pl.loop(0, depth // tile)
        def _(i):
            x_t[col(i), :] = x[:, :, col(i)].reshape(n * rows, tile).T

        load_pre.wait()
        blocks = grads.shape[0]
        up_rows = depth // blocks
        steps = 2 * width // tile
        for start, end in ((0, steps // 3), (steps // 3, steps)):

            @pl.loop(start, end)
            def _(i):
                value = mm(x_t[...], pre_grad[:, :, col(i)].reshape(n * rows, tile)).astype(BF)
                grads[:, :up_rows, col(i)] = value.reshape(blocks, up_rows, tile)

            yield
        load_gh.wait()

        @pl.loop(0, width // 128)
        def _(i):
            at_cols = pl.ds(pl.multiple_of(i * 128, 128), 128)
            gh_t[at_cols, :] = gh[:, :, at_cols].reshape(n * rows, 128).T

        load_inc.wait()
        piece_rows = each // blocks
        own = (width - experts * each) // blocks
        span = depth // 2
        spots = (((0, 0), (0, 2)), ((0, 1), (piece_rows, 0)))
        for half in range(2):

            @pl.loop(0, span // tile)
            def _(i):
                value = mm(gh_t[...], inc[:, col(half * span // tile + i)])
                for e in range(experts):
                    row, place = spots[half][e]
                    piece = value[e * each : (e + 1) * each].astype(BF)
                    grads[
                        :,
                        up_rows + row : up_rows + row + piece_rows,
                        col(place * span // tile + i),
                    ] = piece.reshape(blocks, piece_rows, tile)
                piece = value[experts * each :].reshape(blocks, own, tile)
                empty = jnp.zeros((blocks, piece_rows - own, tile), F32)
                piece = jnp.concatenate([piece, empty], axis=1).astype(BF)
                grads[:, up_rows + piece_rows :, col((1 + half) * span // tile + i)] = piece

        store = copy(grads, outs[0], 4)
        store.start()
        yield
        store.wait()


def chunks(rows, step=80):
    def over(work):
        @pl.loop(0, rows // step)
        def _(i):
            work(pl.ds(pl.multiple_of(i * step, 16), step))

    return over


def sides(v):
    high = v.astype(BF).astype(F32)
    turn = (iota((128, 128), 0) + 16 == iota((128, 128), 1)).astype(F32)
    return (high + exact(v - high, turn, ((1,), (0,)))).astype(BF)


def joined(v):
    turn = (iota((128, 128), 0) - 16 == iota((128, 128), 1)).astype(F32)
    back = exact(v, turn, ((1,), (0,)))
    return jnp.where(iota((1, 128), 1) < 16, v + back, 0.0)


class StreamGrad(Task):
    def __init__(self, parts, stream, gain, after_grad):
        self.reaches = (("dp", False),)
        self.reduce = Reduce("dp", parts)
        self.ins = self.reduce.ins + tuple((v, IN_VMEM) for v in (stream, gain, after_grad))
        shape = jax.ShapeDtypeStruct
        self.outs = ((shape(stream.shape, F32), IN_VMEM), (shape((1, D), F32), IN_VMEM))
        self.scratch = (pltpu.VMEM(stream.shape, F32),) + self.reduce.scratch

    def steps(self, ins, outs, scratch):
        x, stream, gain, after_grad = ins
        out, gain_grad = outs
        total = scratch[0]
        yield from reduce_steps("dp", x, total, *scratch[1:])
        gain_grad[...] = jnp.zeros_like(gain_grad)

        @chunks(total.shape[0])
        def _(rows):
            v = stream[rows, :].astype(F32)
            inv = lax.rsqrt(jnp.mean(v * v, axis=1, keepdims=True) + EPSILON)
            g = total[rows, :]
            gg = g * gain[...]
            gain_grad[...] += jnp.sum(g * v * inv, axis=0, keepdims=True)
            mean = jnp.mean(gg * v, axis=1, keepdims=True)
            out[rows, :] = after_grad[rows, :] + inv * gg - v * (inv * inv * inv * mean)


class InputGrad(Task):
    def __init__(self, gathered, d_proj, out_grad):
        self.reaches = (("expert", False),)
        n = lax.axis_size("expert")
        wide = d_proj.shape[1]
        rows = (D + out_grad.size // wide) // n
        self.reduce = Reduce("expert", jax.ShapeDtypeStruct((n, rows, wide), BF), BF)
        self.ins = tuple((v, ANY) for v in (*gathered, d_proj, out_grad.reshape(n, -1, wide)))
        self.outs = self.reduce.outs
        dma = pltpu.SemaphoreType.DMA
        self.scratch = (
            pltpu.VMEM((gathered[0].shape[0], MB * gathered[0].shape[1], D), BF),
            pltpu.VMEM(d_proj.shape, BF),
            dma((3 + n,)),
        ) + self.reduce.scratch

    def steps(self, ins, outs, scratch):
        g, d_proj, sems = scratch[:3]
        reduce_scratch = scratch[3:]
        acc = reduce_scratch[0]
        me, at = places("expert")
        n, rows, wide = acc.shape
        each = D // n
        below = pl.ds(each, rows - each)
        loads = [pltpu.make_async_copy(ins[2], d_proj, sems.at[0])]
        for m in range(MB):
            part = pl.ds(m * ins[m].shape[1], ins[m].shape[1])
            loads.append(
                pltpu.make_async_copy(
                    ins[m].at[:, :, pl.ds(0, D)], g.at[:, part], sems.at[1 + m]
                )
            )
        for k, (hop, other) in enumerate(ORDER):
            loads.append(
                pltpu.make_async_copy(
                    ins[3].at[at(hop, other)], acc.at[k].at[below], sems.at[3 + k]
                )
            )
        for load in loads:
            load.start()
        yield
        for load in loads:
            load.wait()
        flat = g.shape[0] * g.shape[1]
        ring, pair = me // 2, lax.rem(me, 2)

        def compute(hop):
            place = lax.rem(ring + hop + 4, 4)
            columns = pl.ds(pl.multiple_of(place * 2 * each, 2 * each), 2 * each)
            value = mm_tn(g[:, :, columns].reshape(flat, 2 * each), d_proj[...]).astype(BF)
            same, across = ORDER.index((hop, 0)), ORDER.index((hop, 1))
            for side in range(2):
                slot = same + (across - same) * lax.rem(pair + side, 2)
                acc[slot, :each, :] = value[side * each : (side + 1) * each]

        summing = reduce_steps("expert", None, outs[0], *reduce_scratch)
        next(summing)
        compute(2)
        next(summing)
        yield
        compute(1)
        compute(-1)
        next(summing)
        yield
        compute(0)
        yield from summing


class InputRows(Task):
    def __init__(self, x, heads):
        nd, ne = lax.axis_size("dp"), lax.axis_size("expert")
        self.heads = heads
        self.slices = D // nd // 16
        self.reaches = (("expert", False),)
        wide = 2 * DI + 2 * S + 128
        row = jax.ShapeDtypeStruct((16, wide), BF)
        self.gather = Gather("expert", row)
        self.ins = ((x, ANY),)
        self.outs = self.gather.outs
        dma = pltpu.SemaphoreType.DMA
        self.scratch = (
            pltpu.VMEM((nd, 16, x.shape[1]), BF),
            pltpu.VMEM((16, wide), BF),
            dma((2 * ne,)),
            dma((nd,)),
        ) + self.gather.scratch

    def greet(self, barrier):
        nd = lax.axis_size("dp")
        j = lax.axis_index("dp")
        for source in range(nd):
            pl.semaphore_signal(
                barrier, inc=1, device_id={"dp": source, "expert": j // 2}, device_id_type=MESH
            )
        return 2 * lax.axis_size("expert")

    def steps(self, ins, outs, scratch):
        x = ins[0]
        got, row, send, recv = scratch[:4]
        nd, ne = lax.axis_size("dp"), lax.axis_size("expert")
        j, e = lax.axis_index("dp"), lax.axis_index("expert")
        heads, di = self.heads, self.heads * PS
        sent = []
        for k in range(2):
            for c in range(ne):
                src = x.at[pl.ds((k * self.slices + min(c, self.slices - 1)) * 16, 16)]
                mine = (j == 2 * e + k) & (e == c)
                away = pltpu.make_async_remote_copy(
                    src_ref=src,
                    dst_ref=got.at[j],
                    send_sem=send.at[k * ne + c],
                    recv_sem=recv.at[j],
                    device_id={"dp": 2 * e + k, "expert": c},
                    device_id_type=MESH,
                )
                here = pltpu.make_async_copy(src, got.at[j], recv.at[j])
                pl.when(mine)(here.start)
                pl.when(jnp.logical_not(mine))(away.start)
                sent.append((mine, away))
        yield
        for source in range(nd):
            pltpu.make_async_copy(got.at[source], got.at[source], recv.at[source]).wait()
        piece = lambda source, start, size: got[source, :, start : start + size].astype(F32)
        for source in range(0, nd, 2):
            for half in range(2):
                pair = [piece(source + k, half * di, di) for k in range(2)]
                start = half * DI + source * di
                row[:, start : start + 2 * di] = jnp.concatenate(pair, axis=1).astype(BF)
        total = piece(0, 2 * di, 2 * S)
        for source in range(1, nd):
            total = total + piece(source, 2 * di, 2 * S)
        row[:, 2 * DI : 2 * DI + 2 * S] = total.astype(BF)
        steps = [piece(source, 2 * di + 2 * S, 128)[:, :heads] for source in range(nd)]
        steps.append(jnp.zeros((16, 128 - nd * heads), F32))
        row[:, 2 * DI + 2 * S :] = jnp.concatenate(steps, axis=1).astype(BF)
        yield from gather_steps("expert", row, outs[0], *scratch[4:])
        for mine, away in sent:
            pl.when(jnp.logical_not(mine))(away.wait_send)


class Rest(Task):
    def __init__(self, d_sum, sums):
        self.reaches = (("expert", False),)
        self.top = d_sum.shape[0] - D // lax.axis_size("expert")
        wide = d_sum.shape[1]
        x = jax.ShapeDtypeStruct((self.top + 64, wide), BF)
        self.gather = Gather("expert", x)
        self.ins = ((d_sum, ANY), (sums, ANY))
        self.outs = self.gather.outs
        self.scratch = (
            pltpu.VMEM(x.shape, BF),
            pltpu.SemaphoreType.DMA((6,)),
        ) + self.gather.scratch

    def steps(self, ins, outs, scratch):
        d_sum, sums = ins
        x, sems = scratch[:2]
        top, wide = self.top, x.shape[1]
        third = wide // 3
        last = sums.shape[1] - third
        moves = [(d_sum.at[pl.ds(d_sum.shape[0] - top, top)], x.at[pl.ds(0, top)])]
        for q in range(3):
            moves.append(
                (
                    sums.at[pl.ds(32 * q, 32), pl.ds(last, third)],
                    x.at[pl.ds(top, 32), pl.ds(third * q, third)],
                )
            )
        for half in range(2):
            moves.append(
                (
                    sums.at[pl.ds(128, 16), pl.ds(wide * (1 + half), wide)],
                    x.at[pl.ds(top + 32 + 16 * half, 16)],
                )
            )
        copies = [pltpu.make_async_copy(a, b, sems.at[k]) for k, (a, b) in enumerate(moves)]
        for copy in copies:
            copy.start()
        for copy in copies:
            copy.wait()
        yield from gather_steps("expert", x, outs[0], *scratch[2:])


class Small(Task):
    def __init__(self, added, own, row):
        self.reaches = (("expert", True), ("dp", True))
        nd, ne = lax.axis_size("dp"), lax.axis_size("expert")
        self.ins = ((added, IN_VMEM), (own, IN_VMEM), (row, IN_VMEM))
        rows = added.shape[1] + own.shape[0] + row.shape[1] // 128
        shape = (rows + -rows % 8, 128)
        self.outs = ((jax.ShapeDtypeStruct((nd,) + shape, F32), ANY),)
        dma = pltpu.SemaphoreType.DMA
        self.scratch = (
            pltpu.VMEM(shape, F32),
            pltpu.VMEM((ne,) + shape, F32),
            pltpu.VMEM(shape, F32),
            dma((ne,)),
            dma((ne,)),
            dma,
            dma((nd,)),
            dma((nd,)),
            dma,
        )

    def steps(self, ins, outs, scratch):
        added, own, row = ins
        x, parts, total = scratch[:3]
        x[...] = jnp.zeros_like(x)
        first = added.shape[1]
        second = first + own.shape[0]
        x[:first, :] = jnp.sum(added[...], axis=0)
        x[first:second, :] = own[...]
        for k in range(row.shape[1] // 128):
            x[second + k : second + k + 1, :] = row[:, k * 128 : (k + 1) * 128]
        yield from direct_steps("gather", "expert", x, parts, *scratch[3:6])
        total[...] = jnp.sum(parts[...], axis=0)
        yield from direct_steps("gather", "dp", total, outs[0], *scratch[6:9])


def results_kernel(full, rest, sums, after, out_sum, *outs):
    input_grad, output_grad, shared_up, shared_down, up, down, block_output = outs
    for c in range(input_grad.shape[0] // 16):
        input_grad[c * 16 : (c + 1) * 16, :] = full[c, :, :IN_W].astype(F32)
    ne, rows, wide = rest.shape
    top = rows - 64
    for half in range(2):
        value = rest[half * ne // 2 : (half + 1) * ne // 2, :top, :].reshape(-1, wide)
        output_grad[:, half * wide : (half + 1) * wide] = value.astype(F32)

    each = shared_up.shape[1] // 2
    fs = each // ne
    unit = shared_down.shape[0] // ne
    column = iota((1, each), 1)
    source = lax.rem(column // unit, ne) * fs + column // (unit * ne) * unit + lax.rem(column, unit)
    order = (iota((each, each), 0) == source).astype(BF)
    for half in range(2):
        groups = []
        for q in range(3):
            start = q * 2 * fs + half * fs
            pieces = [rest[e, top : top + 32, start : start + fs] for e in range(ne)]
            groups.append(jnp.concatenate(pieces, axis=1))
        value = mm(jnp.concatenate(groups, axis=0), order)
        shared_up[:, half * each : (half + 1) * each] = value
        for e in range(ne):
            low = top + 32 + 16 * half
            value = rest[e, low : low + 16, :].astype(F32)[:unit]
            shared_down[e * unit : (e + 1) * unit, half * wide : (half + 1) * wide] = value
    experts, dr, both = up.shape
    for e in range(experts):
        up[e] = sums[:dr, e * both : (e + 1) * both].astype(F32)
    below = down.shape[1]
    down[0] = sums[dr : dr + below, : 2 * wide].astype(F32)
    down[1, :, :wide] = sums[dr : dr + below, 2 * wide :].astype(F32)
    down[1, :, wide:] = sums[dr + below :, :wide].astype(F32)
    block_output[...] = (after[...] + out_sum[...]).astype(BF)


def write_results(full, rest, sums, after, out_sum, shapes):
    return pl.pallas_call(
        results_kernel,
        out_shape=[jax.ShapeDtypeStruct(*shape) for shape in shapes],
        in_specs=[IN_VMEM] * 5,
        out_specs=[IN_VMEM] * len(shapes),
        compiler_params=pltpu.CompilerParams(vmem_limit_bytes=VMEM_LIMIT),
        name="results",
    )(full, rest, sums, after, out_sum)


class Experts(Task):
    def __init__(
        self, low, mask, inc, w_up, w_down, s_up, s_down, after, mixed, factors, gain, router, own
    ):
        x = jax.ShapeDtypeStruct((low.shape[0], low.shape[1] + 128), BF)
        self.reaches = (("expert", False),)
        self.gather = Gather("expert", x)
        n = lax.axis_size("expert")
        rows, wide = x.shape
        depth = inc.shape[1]
        experts, _, both = w_up.shape
        self.experts = experts
        all_rows = jax.ShapeDtypeStruct((n, rows, wide), BF)
        self.reduce = Reduce("expert", all_rows)
        hidden = experts * both // 2 + s_down.shape[0]
        pre = jax.ShapeDtypeStruct((n, rows, 2 * hidden), BF)
        gh = jax.ShapeDtypeStruct((n, rows, hidden), BF)
        self.ins = tuple((v, ANY) for v in (inc, w_up, w_down, s_up, s_down)) + tuple(
            (v, IN_VMEM) for v in (low, mask, after, mixed, factors, gain, router, own)
        )
        part = jax.ShapeDtypeStruct((n, rows, depth), BF)
        shape = jax.ShapeDtypeStruct
        self.outs = (
            ((all_rows, IN_VMEM),)
            + tuple((v, ANY) for v in (pre, gh, part))
            + (
                (shape((rows, depth), F32), IN_VMEM),
                (shape((rows, wide), BF), IN_VMEM),
                (shape((1, depth), F32), IN_VMEM),
                (shape((16, depth), F32), IN_VMEM),
            )
        )
        dma = pltpu.SemaphoreType.DMA
        self.scratch = (
            (pltpu.VMEM((n, rows, depth), BF),)
            + tuple(pltpu.VMEM(v.shape, BF) for v in (w_up, w_down, s_up, s_down))
            + (pltpu.VMEM((2 * rows, wide), BF), pltpu.VMEM((2 * rows, depth), BF))
            + (pltpu.VMEM((2 * rows, 2 * hidden), BF), pltpu.VMEM((2 * rows, hidden), BF))
            + (pltpu.VMEM(pre.shape, BF), pltpu.VMEM(gh.shape, BF))
            + (pltpu.VMEM((2 * rows, 128), F32), dma((22,)), pltpu.VMEM(part.shape, BF))
            + (pltpu.VMEM((rows, wide), F32), pltpu.VMEM((rows, wide), BF))
            + self.gather.scratch
            + self.reduce.scratch
        )

    def steps(self, ins, outs, scratch):
        inc_in = ins[0]
        low_in, mask, after, mixed, factors, gain, router, own = ins[5:]
        x_all, pre_out, gh_out, part_out, after_grad, payload, gain_grad, router_grad = outs
        inc, w_up, w_down, s_up, s_down, xs, incs, pg, ghs, pre, gh, extra, sems = scratch[:13]
        part, dx, gather_scratch, reduce_scratch = scratch[13], scratch[14], scratch[16:19], scratch[19:]
        x = scratch[15]
        acc = reduce_scratch[0]
        me, at = places("expert")
        n, rows, depth = inc.shape
        experts, _, both = w_up.shape
        each = both // 2
        shared = s_down.shape[0]
        tile = min(256, each)
        loads = [
            pltpu.make_async_copy(src, dst, sems.at[k])
            for k, (src, dst) in enumerate(zip(ins[1:5], (w_up, w_down, s_up, s_down)))
        ]
        loads += [
            pltpu.make_async_copy(inc_in.at[pl.ds(k * rows, rows)], inc.at[k], sems.at[13 + k])
            for k in range(n)
        ]
        for load in loads:
            load.start()

        logits = mm(low_in[...], router[...])
        chosen = mask[...]
        top = jnp.max(jnp.where(chosen > 0.0, logits, -1e30), axis=1, keepdims=True)
        e = jnp.where(chosen > 0.0, jnp.exp(jnp.minimum(logits - top, 0.0)), 0.0)
        table = e / jnp.sum(e, axis=1, keepdims=True)
        x[:, :depth] = low_in[...]
        x[:, depth:] = sides(table)
        arriving = gather_steps("expert", x, x_all, *gather_scratch)
        next(arriving)
        next(arriving)
        for load in loads:
            load.wait()
        lane = lax.broadcasted_iota(jnp.int32, (1, 128), 1)
        stores = []

        def unit(a, b, u, scale):
            sig = jax.nn.sigmoid(a)
            act = a * sig
            hidden = act * b
            gu = u * scale
            da = gu * b * (sig + act * (1.0 - sig))
            return hidden * scale, da, gu * act, u * hidden

        def compute(hop, places_in_acc):
            slots = (at(hop, 0), at(hop, 1))
            for k, slot in enumerate(slots):
                part = pl.ds(k * rows, rows)
                xs[part, :] = x_all[slot]
                incs[part, :] = inc[slot]
            extra[...] = jnp.zeros_like(extra)

            @pl.loop(0, experts * (each // tile))
            def _(i):
                e, f = i // (each // tile), lax.rem(i, each // tile)
                place = me * experts + e
                table = xs[:, depth:].astype(F32)
                chosen = (lane == place) | (lane == place + n * experts)
                scale = jnp.sum(jnp.where(chosen, table, 0.0), axis=1, keepdims=True)
                left = pl.ds(pl.multiple_of(f * tile, tile), tile)
                right = pl.ds(pl.multiple_of(each + f * tile, tile), tile)
                a = mm(xs[:, :depth], w_up[e, :, left])
                b = mm(xs[:, :depth], w_up[e, :, right])
                u = mm_nt(incs[...], w_down[e, left, :])
                h, da, db, dots = unit(a, b, u, scale)
                ghs[:, pl.ds(pl.multiple_of(e * each + f * tile, tile), tile)] = h.astype(BF)
                pg[:, pl.ds(pl.multiple_of(e * both + f * tile, tile), tile)] = da.astype(BF)
                pg[:, pl.ds(pl.multiple_of(e * both + each + f * tile, tile), tile)] = db.astype(BF)
                extra[...] += jnp.where(lane == place, jnp.sum(dots, axis=1, keepdims=True), 0.0)

            a = mm(xs[:, :depth], s_up[:, :shared])
            b = mm(xs[:, :depth], s_up[:, shared:])
            u = mm_nt(incs[...], s_down[...])
            h, da, db, _ = unit(a, b, u, 1.0)
            ghs[:, experts * each :] = h.astype(BF)
            pg[:, experts * both : experts * both + shared] = da.astype(BF)
            pg[:, experts * both + shared :] = db.astype(BF)

            @pl.loop(0, depth // tile)
            def _(i):
                columns = pl.ds(pl.multiple_of(i * tile, tile), tile)
                total = mm_nt(pg[:, experts * both :], s_up[columns, :])
                for e in range(experts):
                    total += mm_nt(pg[:, e * both : (e + 1) * both], w_up[e, columns, :])
                for k, place in enumerate(places_in_acc):
                    acc[place, :, columns] = total[k * rows : (k + 1) * rows].astype(BF)

            grads = extra[...]
            both_parts = sides(grads)
            for k, (slot, place) in enumerate(zip(slots, places_in_acc)):
                part = pl.ds(k * rows, rows)
                acc[place, :, depth:] = both_parts[k * rows : (k + 1) * rows]
                pre[slot] = pg[part, :]
                gh[slot] = ghs[part, :]
                store = pltpu.make_async_copy(pre.at[slot], pre_out.at[slot], sems.at[4 + len(stores)])
                store.start()
                stores.append(store)

        compute(0, (7, 6))
        next(arriving)
        compute(1, (4, 2))
        compute(-1, (5, 3))
        for _ in arriving:
            pass
        compute(2, (1, 0))
        store = pltpu.make_async_copy(gh, gh_out, sems.at[12])
        store.start()
        stores.append(store)
        summing = reduce_steps("expert", None, dx, *reduce_scratch)
        next(summing)
        for half in range(2):
            next(summing)

            @pl.loop(half * depth // tile // 2, (half + 1) * depth // tile // 2)
            def _(i):
                columns = pl.ds(pl.multiple_of(i * tile, tile), tile)
                hid = lambda start, size: gh[:, :, start : start + size].reshape(n * rows, size)
                total = mm(hid(experts * each, shared), s_down[:, columns])
                for e in range(experts):
                    total += mm(hid(e * each, each), w_down[e, :, columns])
                part[:, :, columns] = total.astype(BF).reshape(n, rows, tile)

        store = pltpu.make_async_copy(part, part_out, sems.at[21])
        store.start()
        stores.append(store)
        yield from summing
        gain_grad[...] = jnp.zeros_like(gain_grad)
        spread = joined(dx[:, depth:])
        logit = table * (spread - jnp.sum(table * spread, axis=1, keepdims=True))
        logit_low = logit.astype(BF)
        router_grad[...] = mm_tn(logit_low, low_in[...])[:16]
        dx[:, :depth] += mm_nt(logit_low, router[...])

        @chunks(rows)
        def _(at_rows):
            v, inv = after[at_rows, :], factors[at_rows, 1:2]
            g = dx[at_rows, :depth]
            gg = g * gain[...]
            gain_grad[...] += jnp.sum(g * v * inv, axis=0, keepdims=True)
            mean = jnp.mean(gg * v, axis=1, keepdims=True)
            total = own[at_rows, :].astype(F32) + inv * gg - v * (inv * inv * inv * mean)
            after_grad[at_rows, :] = total
            total_low = total.astype(BF)
            payload[at_rows, :depth] = total_low
            s = jnp.sum(total_low.astype(F32) * mixed[at_rows, :], axis=1, keepdims=True)
            r = factors[at_rows, 0:1]
            r_high, s_high = r.astype(BF).astype(F32), s.astype(BF).astype(F32)
            extras = jnp.where(lane == 0, r_high, jnp.where(lane == 1, r - r_high, 0.0))
            extras = jnp.where(lane == 2, s_high, jnp.where(lane == 3, s - s_high, extras))
            payload[at_rows, depth:] = extras.astype(BF)

        for store in stores:
            store.wait()


EDGE = 8


def pieces(v, count):
    out = []
    for _ in range(count):
        out.append(v.astype(BF))
        v = v - out[-1].astype(F32)
    return out


def exact(v, ones, dims, count=2):
    ones = ones.astype(BF)
    parts = [
        lax.dot_general(p, ones, (dims, ((), ())), preferred_element_type=F32)
        for p in pieces(v, count)
    ]
    return sum(parts[1:], parts[0])


def exact_right(ones, v, dims, count=2):
    ones = ones.astype(BF)
    parts = [
        lax.dot_general(ones, p, (dims, ((), ())), preferred_element_type=F32)
        for p in pieces(v, count)
    ]
    return sum(parts[1:], parts[0])


def iota(shape, axis):
    return lax.broadcasted_iota(jnp.int32, shape, axis)


class Block:
    def __init__(self, m, slot, start, proj, ext, lengths, taps, heads_vec, heads):
        loc = proj.shape[0]
        di = heads * PS
        width = di + 2 * S
        self.heads, self.di = heads, di
        first = lengths[m, 0]
        second = first + lengths[m, 1]

        def doc(p):
            return (p >= first).astype(jnp.int32) + (p >= second).astype(jnp.int32)

        self.doc = doc
        self.at = start + iota((loc, 1), 0)
        docs = doc(self.at)
        docs_row = doc(start + iota((1, loc), 1))
        last_doc, before_doc = doc(start + loc - 1), doc(start - 1)
        self.keep = (docs == before_doc).astype(F32)
        self.keep_last = (last_doc == before_doc).astype(F32)
        self.same_last = (docs == last_doc).astype(F32)
        self.gate = proj[:, :di]
        ext[slot, EDGE : EDGE + loc, :] = proj[:, di : di + width].astype(BF).astype(F32)
        total = jnp.broadcast_to(taps[K : K + 1, :], (loc, width))
        self.shifted = []
        for k in range(K):
            back = K - 1 - k
            value = ext[slot, EDGE - back : EDGE - back + loc, :]
            if back:
                value = value * (docs == doc(self.at - back)).astype(F32)
            self.shifted.append(value)
            total = total + taps[k : k + 1, :] * value
        self.sig = jax.nn.sigmoid(total)
        self.total = total
        filtered = total * self.sig
        self.x = filtered[:, :di]
        self.write = filtered[:, di : di + S].astype(BF)
        self.read = filtered[:, di + S :].astype(BF)
        self.raw = proj[:, di + width :] + heads_vec[0:1, :]
        self.steps = jnp.maximum(self.raw, 0.0) + jnp.log1p(jnp.exp(-jnp.abs(self.raw)))
        self.rate = heads_vec[1:2, :]
        rise = self.steps * self.rate
        rows, cols = iota((loc, loc), 0), iota((loc, loc), 1)
        self.lower = (cols <= rows).astype(F32)
        self.cum = exact_right(self.lower, rise, ((1,), (0,)), 3)
        cum_rows = exact(rise, (rows <= cols).astype(F32), ((0,), (0,)), 3)
        self.last = self.cum[loc - 1 : loc, :]
        self.grow = jnp.exp(self.cum) * self.keep
        self.fall = jnp.exp(self.last - self.cum) * self.same_last
        self.decay = jnp.exp(self.last) * self.keep_last
        allowed = (cols <= rows) & (docs == docs_row)
        scores = mm_nt(self.read, self.write)
        self.spread, self.mixing = [], []
        for h in range(heads):
            span = self.cum[:, h : h + 1] - cum_rows[h : h + 1, :]
            shape = jnp.exp(jnp.where(allowed, span, -1e30))
            self.spread.append(shape)
            self.mixing.append(shape * scores)
        self.lane = iota((1, di), 1)
        self.steps_wide = self.widen(self.steps)
        self.grow_wide = self.widen(self.grow)
        self.weight_wide = self.widen(self.fall * self.steps)
        self.scaled = self.x * self.steps_wide
        self.pushed = self.x * self.weight_wide

    def widen(self, v):
        out = jnp.broadcast_to(v[:, 0:1], (v.shape[0], self.di))
        for h in range(1, self.heads):
            out = jnp.where(self.lane >= h * PS, v[:, h : h + 1], out)
        return out

    def per_head(self, parts):
        out = parts[0]
        for h in range(1, self.heads):
            out = jnp.where(self.lane >= h * PS, parts[h], out)
        return out

    def decay_rows(self):
        rows = iota((self.di, 1), 0)
        out = jnp.broadcast_to(self.decay[:, 0:1], (self.di, 1))
        for h in range(1, self.heads):
            out = jnp.where(rows >= h * PS, self.decay[:, h : h + 1], out)
        return out


def load_weights(pieces_ref, w, sem):
    copies = [
        pltpu.make_async_copy(pieces_ref.at[k], w.at[:, k], sem.at[k]) for k in range(w.shape[1])
    ]
    for copy in copies:
        copy.start()
    for copy in copies:
        copy.wait()


class Forward(Task):
    def __init__(self, blocks, x, incoming, lengths, w_out, vectors, stream, gain, heads):
        self.heads = heads
        self.reaches = (("dp", True), ("expert", False))
        nd = lax.axis_size("dp")
        loc = stream.shape[0] // MB
        di = heads * PS
        wide = blocks.shape[2]
        shape = jax.ShapeDtypeStruct
        self.weights = Weights(blocks)
        self.gathers = [Gather("dp", v) for v in x] + [Gather("expert", incoming)]
        part = shape((nd, loc, D + 128), BF)
        self.reduces = [Reduce("dp", part) for _ in range(MB)]
        self.saved = (
            shape((MB, nd, loc, wide), F32),
            shape((MB, nd, loc, di), F32),
            shape((MB, nd, di, S), F32),
        )
        self.ins = (
            ((blocks, ANY),)
            + tuple((v, ANY) for v in (*x, incoming))
            + ((lengths, pl.BlockSpec(memory_space=pltpu.SMEM)),)
            + tuple((v, IN_VMEM) for v in (w_out,) + tuple(vectors) + (stream, gain))
        )
        full = self.weights.outs[1][0]
        rows = stream.shape[0]
        self.outs = (
            ((full, ANY),)
            + tuple((gather.outs[0][0], ANY) for gather in self.gathers)
            + tuple((v, ANY) for v in self.saved)
            + (
                (shape((rows, D), BF), IN_VMEM),
                (shape((rows, D), F32), IN_VMEM),
                (shape((rows, D), F32), IN_VMEM),
                (shape((rows, 128), F32), IN_VMEM),
            )
        )
        vmem = lambda v: pltpu.VMEM(v.shape, v.dtype)
        dma = pltpu.SemaphoreType.DMA
        slices = D // nd // full.shape[2]
        self.scratch = (
            (vmem(self.weights.outs[0][0]), vmem(full))
            + tuple(vmem(gather.outs[0][0]) for gather in self.gathers[:MB])
            + tuple(vmem(v) for v in self.saved)
            + tuple(vmem(part) for _ in range(MB))
            + tuple(pltpu.VMEM((loc, D + 128), F32) for _ in range(MB))
            + (pltpu.VMEM((nd, slices, full.shape[2], wide), BF), dma((slices,)), dma((9,)))
            + (pltpu.VMEM((2, loc + EDGE, di + 2 * S), F32), pltpu.VMEM((di, S), F32))
            + (pltpu.VMEM((4, loc, di), BF),)
            + self.weights.scratch
            + self.gathers[0].scratch
            + self.gathers[1].scratch
            + self.gathers[2].scratch
            + self.reduces[0].scratch
            + self.reduces[1].scratch
        )

    def steps(self, ins, outs, scratch):
        x, incoming, lengths = ins[1:3], ins[3], ins[4]
        w_out, taps, heads_vec, lanes_vec, stream, gain = ins[5:]
        w_full, g_out, inc_out, saved_out = outs[0], outs[1:3], outs[3], outs[4:7]
        low_out, after, mixed, factors = outs[7:]
        swapped, pieces_all = scratch[:2]
        g, (proj, scan, states), parts, totals = scratch[2:4], scratch[4:7], scratch[7:9], scratch[9:11]
        w, w_sem, sems, ext, state, gated = scratch[11:17]
        rest = scratch[17:]
        rest, weight_sems = rest[6:], rest[:6]
        gather_sems, rest = (rest[:3], rest[3:6], rest[6:9]), rest[9:]
        count = len(self.reduces[0].scratch)
        reduce_scratch = (rest[:count], rest[count:])
        heads = self.heads
        nd, loc, _ = g[0].shape
        di = heads * PS
        stores = []

        def store(src, dst):
            copy = pltpu.make_async_copy(src, dst, sems.at[len(stores)])
            copy.start()
            stores.append(copy)

        def work(m, start, end):
            many = end - start
            rows = g[m][start:end, :, :D].reshape(many * loc, D)
            value = mm(rows, w[...].reshape(D, -1))
            proj[m, start:end] = value.reshape(many, loc, value.shape[1])

            @pl.loop(start // 2, end // 2)
            def _(pair):
                two = []
                for k in range(2):
                    b = pair * 2 + k
                    ext[k, 0:EDGE, :] = ext[1 - k, loc : loc + EDGE, :]
                    two.append(
                        Block(m, k, b * loc, proj[m, b], ext, lengths, taps, heads_vec, heads)
                    )
                before = [state[...]]
                for part in two:
                    before.append(
                        part.decay_rows() * before[-1] + mm_tn(part.pushed.astype(BF), part.write)
                    )
                state[...] = before[2]
                for k, part in enumerate(two):
                    b = pair * 2 + k
                    states[m, b] = before[k]
                    scaled = part.scaled.astype(BF)
                    inner = part.per_head(
                        [mm(part.mixing[h].astype(BF), scaled) for h in range(heads)]
                    )
                    carried = mm_nt(part.read, before[k].astype(BF)) * part.grow_wide
                    out = inner + carried + lanes_vec[1:2, :] * part.x
                    scan[m, b] = out
                    y = out * (part.gate * jax.nn.sigmoid(part.gate))
                    square = jnp.sum(y * y, axis=1, keepdims=True)
                    high = square.astype(BF).astype(F32)
                    gated[b - start] = (y * lanes_vec[0:1, :]).astype(BF)
                    column = iota((loc, 128), 1)
                    sums = jnp.where(column == 0, high, jnp.where(column == 1, square - high, 0.0))
                    parts[m][b, :, D:] = sums.astype(BF)

            value = mm(gated[...].reshape(many * loc, di), w_out[...])
            parts[m][start:end, :, :D] = value.astype(BF).reshape(many, loc, D)

        def reset():
            ext[...] = jnp.zeros_like(ext)
            state[...] = jnp.zeros_like(state)

        def norm(m):
            @chunks(loc)
            def _(rows):
                at_rows = pl.ds(pl.multiple_of(m * loc + rows.start, 16), rows.size)
                lane = iota((1, 128), 1)
                total = totals[m]
                squares = total[rows, D:]
                square = jnp.sum(jnp.where(lane < 2, squares, 0.0), axis=1, keepdims=True)
                r = lax.rsqrt(square / DI + EPSILON)
                mix = total[rows, :D] * r
                v = stream[at_rows, :].astype(F32) + mix
                inv = lax.rsqrt(jnp.mean(v * v, axis=1, keepdims=True) + EPSILON)
                low_out[at_rows, :] = (v * inv * gain[...]).astype(BF)
                after[at_rows, :] = v
                mixed[at_rows, :] = mix
                factors[at_rows, :] = jnp.where(lane == 0, r, jnp.where(lane == 1, inv, 0.0))

        weights = self.weights.steps(ins[:1], (swapped, pieces_all), weight_sems)
        first = gather_steps("dp", x[0], g[0], *gather_sems[0])
        second = gather_steps("dp", x[1], g[1], *gather_sems[1])
        third = gather_steps("expert", incoming, inc_out, *gather_sems[2])
        for _ in range(3):
            next(weights)
        next(first)
        next(first)
        next(weights, None)
        next(first)
        next(second)
        next(weights, None)
        next(first)
        for _ in weights:
            pass
        for _ in first:
            pass
        load_weights(pieces_all, w, w_sem)
        store(pieces_all, w_full)
        store(g[0], g_out[0])
        reset()
        for k in range(4):
            next(third, None)
            work(0, 4 * k, 4 * k + 4)
            next(second, None)
        for steps in (second, third):
            for _ in steps:
                pass
        store(g[1], g_out[1])
        sums = [
            reduce_steps("dp", parts[m], totals[m], *reduce_scratch[m]) for m in range(MB)
        ]
        next(sums[0])
        for src, dst in zip((proj, scan, states), saved_out):
            store(src.at[0], dst.at[0])
        reset()
        for k in range(4):
            next(sums[0])
            work(1, 4 * k, 4 * k + 4)
        next(sums[1])
        for src, dst in zip((proj, scan, states), saved_out):
            store(src.at[1], dst.at[1])
        for _ in sums[0]:
            pass
        next(sums[1])
        norm(0)
        for _ in sums[1]:
            pass
        norm(1)
        for copy in stores:
            copy.wait()
        yield


def backward_kernel(
    heads,
    lengths,
    grad,
    w_pieces,
    w_out,
    taps,
    heads_vec,
    lanes_vec,
    proj,
    proj_before,
    scan,
    states,
    d_proj,
    normed_part,
    d_out,
    d_taps,
    d_heads,
    d_lanes,
    ext,
    d_ext,
    d_state,
    out_sum,
    w,
    w_sem,
):
    step = pl.program_id(0)
    b = pl.num_programs(0) - 1 - step
    loc = grad.shape[1] // MB
    di = heads * PS
    width = di + 2 * S

    @pl.when(step == 0)
    def _():
        for ref in (d_ext, d_state, out_sum, d_taps, d_heads, d_lanes):
            ref[...] = jnp.zeros_like(ref)
        load_weights(w_pieces, w, w_sem)

    gated_grad = mm_nt(grad[0, :, :D], w_out[...])
    extra = grad[0, :, D:].astype(F32)
    has_before = (b > 0).astype(F32)
    pick = (iota((di, S), 0) // PS == iota((di, S), 1)).astype(F32)
    for m in range(MB):
        rows = slice(m * loc, (m + 1) * loc)
        edge = proj_before[m, 0, loc - EDGE : loc, di : di + width]
        ext[m, 0:EDGE, :] = edge.astype(BF).astype(F32) * has_before
        part = Block(m, m, b * loc, proj[m, 0], ext, lengths, taps, heads_vec, heads)
        gain, skip = lanes_vec[0:1, :], lanes_vec[1:2, :]
        r = extra[rows, 0:1] + extra[rows, 1:2]
        s = extra[rows, 2:3] + extra[rows, 3:4]
        out = scan[m, 0]
        sig = jax.nn.sigmoid(part.gate)
        act = part.gate * sig
        yr = out * act * r
        gg = gated_grad[rows]
        d_lanes[0:1, :] += jnp.sum(gg * yr, axis=0, keepdims=True)
        out_sum[...] += mm_tn((yr * gain).astype(BF), grad[0, rows, :D])
        dy = r * (gg * gain) - yr * (r * s / DI)
        d_gate = dy * out * (sig + act * (1.0 - sig))
        do = dy * act
        do_low = do.astype(BF)
        x = part.x
        d_lanes[1:2, :] += jnp.sum(do * x, axis=0, keepdims=True)
        dx = skip * do
        before = states[m, 0]
        before_low = before.astype(BF)
        ds = d_state[m]
        ds_low = ds.astype(BF)

        d_scores = jnp.zeros((loc, loc), F32)
        d_scaled, d_cum = [], jnp.zeros((loc, S), F32)
        head_lane = iota((loc, S), 1)
        for h in range(heads):
            inside = (part.lane >= h * PS) & (part.lane < (h + 1) * PS)
            own = jnp.where(inside, part.scaled, 0.0).astype(BF)
            d_mix = mm_nt(do_low, own)
            d_scaled.append(mm_tn(part.mixing[h].astype(BF), do_low))
            d_scores = d_scores + d_mix * part.spread[h]
            d_span = d_mix * part.mixing[h]
            ones = (head_lane == h).astype(F32)
            d_cum = d_cum + exact(d_span, ones, ((1,), (0,))) - exact(d_span, ones, ((0,), (0,)))
        d_scaled = part.per_head(d_scaled)
        dx = dx + d_scaled * part.steps_wide
        d_scores_low = d_scores.astype(BF)
        d_read = mm(d_scores_low, part.write)
        d_write = mm_tn(d_scores_low, part.read)

        d_carry = do * part.grow_wide
        d_carry_low = d_carry.astype(BF)
        carried = mm_nt(part.read, before_low)
        d_read = d_read + mm(d_carry_low, before_low)

        d_pushed = mm_nt(part.write, ds_low)
        d_write = d_write + mm(part.pushed.astype(BF), ds_low)
        dx = dx + d_pushed * part.weight_wide
        sums = exact(
            jnp.concatenate([d_carry * carried, d_pushed * x, d_scaled * x], axis=0),
            pick,
            ((1,), (0,)),
        )
        d_weight = sums[loc : 2 * loc]
        d_fall = d_weight * part.fall * part.steps
        d_cum = d_cum + sums[:loc] - d_fall
        d_steps = sums[2 * loc :] + d_weight * part.fall
        state_dot = jnp.sum(ds * before, axis=1, keepdims=True)
        d_decay = exact(jnp.broadcast_to(state_dot, (di, S)), pick, ((0,), (0,)))[0:1, :]
        d_last = jnp.sum(d_fall, axis=0, keepdims=True) + d_decay * part.decay
        d_cum = d_cum + jnp.where(iota((loc, 1), 0) == loc - 1, d_last, 0.0)
        d_state[m] = part.decay_rows() * ds + mm_tn(d_carry_low, part.read)

        d_rise = exact_right(part.lower, d_cum, ((0,), (0,)))
        d_steps = d_steps + d_rise * part.rate
        d_raw = d_steps * jax.nn.sigmoid(part.raw)
        d_heads[0:1, :] += jnp.sum(d_raw, axis=0, keepdims=True)
        d_heads[1:2, :] += jnp.sum(d_rise * part.steps * part.rate, axis=0, keepdims=True)

        d_total = jnp.concatenate([dx, d_write, d_read], axis=1)
        d_total = d_total * (part.sig + part.total * part.sig * (1.0 - part.sig))
        for k in range(K):
            d_taps[k : k + 1, :] += jnp.sum(d_total * part.shifted[k], axis=0, keepdims=True)
        d_taps[K : K + 1, :] += jnp.sum(d_total, axis=0, keepdims=True)
        d_ext[m, loc : loc + EDGE, :] = d_ext[m, 0:EDGE, :]
        d_ext[m, 0:loc, :] = d_total
        d_seq = taps[K - 1 : K, :] * d_total
        docs = part.doc(part.at)
        for ahead in range(1, K):
            same = (docs == part.doc(part.at + ahead)).astype(F32)
            d_seq = d_seq + taps[K - 1 - ahead : K - ahead, :] * (
                same * d_ext[m, ahead : ahead + loc, :]
            )
        d_proj[0, rows, :di] = d_gate.astype(BF)
        d_proj[0, rows, di : di + width] = d_seq.astype(BF)
        d_proj[0, rows, di + width :] = jnp.where(head_lane < heads, d_raw, 0.0).astype(BF)
    for half in range(2):
        d_out[half] = out_sum[:, half * D // 2 : (half + 1) * D // 2].astype(BF)
    normed_part[0] = mm_nt(d_proj[0], w[...].reshape(D, -1)).astype(BF)


def weight_scratch(w):
    slices = D // w.shape[1] // w.shape[2]
    return [
        pltpu.VMEM((w.shape[1], slices) + w.shape[2:], BF),
        pltpu.SemaphoreType.DMA((slices,)),
    ]


def block_spec(shape, index):
    return pl.BlockSpec((1,) + shape[1:], lambda i: (index(i),) + (0,) * (len(shape) - 1))


def pair_spec(shape, index):
    return pl.BlockSpec((MB, 1) + shape[2:], lambda i: (0, index(i)) + (0,) * (len(shape) - 2))


def whole_spec(shape):
    return pl.BlockSpec(shape, lambda i: (0,) * len(shape))


def mixer_backward(lengths, grad, w, w_out, taps, heads_vec, lanes_vec, proj, scan, states, heads):
    nb, rows, _ = grad.shape
    di = heads * PS
    width = di + 2 * S
    back = lambda i: nb - 1 - i
    before = lambda i: jnp.maximum(nb - 2 - i, 0)
    per_block = [
        jax.ShapeDtypeStruct((nb, rows, w.shape[-1]), BF),
        jax.ShapeDtypeStruct((nb, rows, D), BF),
    ]
    sums = [
        jax.ShapeDtypeStruct((2, di, D // 2), BF),
        jax.ShapeDtypeStruct((8, width), F32),
        jax.ShapeDtypeStruct((8, S), F32),
        jax.ShapeDtypeStruct((8, di), F32),
    ]
    return pl.pallas_call(
        functools.partial(backward_kernel, heads),
        grid=(nb,),
        out_shape=per_block + sums,
        in_specs=[pl.BlockSpec(memory_space=pltpu.SMEM), block_spec(grad.shape, back)]
        + [pl.BlockSpec(memory_space=pl.ANY)]
        + [whole_spec(v.shape) for v in (w_out, taps, heads_vec, lanes_vec)]
        + [pair_spec(proj.shape, back), pair_spec(proj.shape, before)]
        + [pair_spec(scan.shape, back), pair_spec(states.shape, back)],
        out_specs=[block_spec(v.shape, back) for v in per_block]
        + [whole_spec(v.shape) for v in sums],
        scratch_shapes=[
            pltpu.VMEM((MB, rows // MB + EDGE, width), F32),
            pltpu.VMEM((MB, rows // MB + EDGE, width), F32),
            pltpu.VMEM((MB, di, S), F32),
            pltpu.VMEM((di, D), F32),
        ]
        + weight_scratch(w),
        compiler_params=pltpu.CompilerParams(vmem_limit_bytes=VMEM_LIMIT),
        name="mixer_backward",
    )(lengths, grad, w, w_out, taps, heads_vec, lanes_vec, proj, proj, scan, states)


def body(
    tokens,
    lengths,
    routes,
    cotangent,
    input_weight,
    filter_weight,
    filter_bias,
    step_bias,
    decay_log,
    skip_gain,
    norm_gain,
    gated_gain,
    output_weight,
    moe_gain,
    router_weight,
    shared_gate_up,
    shared_down,
    expert_gate_up,
    expert_down,
):
    nd, ne = lax.axis_size("dp"), lax.axis_size("expert")
    me_d, me_e = lax.axis_index("dp"), lax.axis_index("expert")
    loc = tokens.shape[2]
    heads = H // nd
    di = heads * PS
    rows_t = MB * loc
    experts = expert_gate_up.shape[0] * ne
    el = expert_gate_up.shape[0]
    dr = D // nd
    fs = FS // ne
    fsr = FS // nd
    fsl = fsr // ne

    pad = 128 - heads
    piece = 16
    place = jnp.minimum(me_e, dr // piece - 1) * piece
    mine = lax.dynamic_slice_in_dim(input_weight, place, piece, 0)
    blocks = jnp.concatenate(
        [
            jnp.moveaxis(mine[:, :DI].reshape(piece, nd, di), 1, 0),
            jnp.moveaxis(mine[:, DI : 2 * DI].reshape(piece, nd, di), 1, 0),
            jnp.broadcast_to(mine[None, :, 2 * DI : 2 * DI + 2 * S], (nd, piece, 2 * S)),
            jnp.moveaxis(mine[:, DI + CONV :].reshape(piece, nd, heads), 1, 0),
            jnp.zeros((nd, piece, pad), BF),
        ],
        axis=2,
    )
    wcols = blocks.shape[2]

    sg = shared_gate_up.reshape(dr, 2, nd, ne, fsl)
    sg = lax.dynamic_index_in_dim(sg, me_e, 3, False).reshape(dr, 2 * fs)
    sd = lax.dynamic_slice_in_dim(shared_down, me_e * fsl, fsl, 0)
    packed = jnp.concatenate([sg.reshape(-1), sd.reshape(-1), router_weight.reshape(-1)])
    packed_cols = packed.size // loc
    packed = jnp.pad(packed.reshape(loc, -1), ((0, 0), (0, -packed_cols % 128)))

    stream = tokens.reshape(rows_t, D).astype(F32)
    incoming = cotangent.reshape(rows_t, D)
    route_rows = routes.reshape(rows_t, TOP)
    normed = rms_scale(stream, norm_gain).astype(BF)
    taps = jnp.concatenate(
        [lax.dynamic_slice_in_dim(filter_weight, me_d * di, di, 1), filter_weight[:, DI:]], axis=1
    )
    tap_bias = jnp.concatenate(
        [lax.dynamic_slice_in_dim(filter_bias, me_d * di, di, 0), filter_bias[DI:]], axis=0
    )
    my_heads = lambda v: lax.dynamic_slice_in_dim(v, me_d * heads, heads, 0)
    my_gain = lax.dynamic_slice_in_dim(gated_gain, me_d * di, di, 0)

    taps_vec = jnp.concatenate([taps, tap_bias[None], jnp.zeros((3, di + 2 * S), F32)], axis=0)
    heads_vec = jnp.stack([my_heads(step_bias), -jnp.exp(my_heads(decay_log))])
    heads_vec = jnp.pad(heads_vec, ((0, 6), (0, S - heads)))
    lanes_vec = jnp.pad(
        jnp.stack([my_gain, jnp.repeat(my_heads(skip_gain), PS)]), ((0, 6), (0, 0))
    )
    vectors = (taps_vec, heads_vec, lanes_vec)
    gain_row = moe_gain.reshape(1, D)
    own_tokens = tokens.reshape(rows_t, D)
    forward = Forward(
        blocks,
        (normed[:loc], jnp.concatenate([normed[loc:], packed], axis=1)),
        incoming,
        lengths[:, 0],
        output_weight,
        vectors,
        own_tokens,
        gain_row,
        heads,
    )
    (results,) = run_tasks([forward], 1, "forward")
    w_in, *gathered, inc_all, proj, scan, states, moe_in, after_mixer, mixed, factors = results
    inc_all = inc_all.reshape(ne * rows_t, D)
    packed_all = gathered[1][:, :, D : D + packed_cols]
    packed_all = packed_all.reshape(nd, -1)
    sg_full = packed_all[:, : sg.size].reshape(D, 2 * fs)
    sd_full = packed_all[:, sg.size : sg.size + sd.size].reshape(fs, D)
    router_full = packed_all[:, sg.size + sd.size :].reshape(D, experts)
    mask = jnp.sum(
        (route_rows[:, :, None] == jnp.arange(128, dtype=jnp.int32)).astype(F32), axis=1
    )
    router_wide = jnp.pad(router_full, ((0, 0), (0, 128 - experts)))
    ((moe_all, pre_grad, gh, out_part, after_grad, grad_payload, moe_gain_grad, router_part),) = (
        run_tasks(
            [
                Experts(
                    moe_in,
                    mask,
                    inc_all,
                    expert_gate_up,
                    expert_down,
                    sg_full,
                    sd_full,
                    after_mixer,
                    mixed,
                    factors,
                    gain_row,
                    router_wide,
                    incoming,
                )
            ],
            3,
            "experts",
        )
    )
    width = gh.shape[2]
    (out_sum,), (grad_blocks,), (grad_all,) = run_tasks(
        [
            Reduce("expert", out_part),
            ExpertGrads(moe_all, pre_grad, gh, inc_all, el, FE, nd),
            Gather("dp", grad_payload),
        ],
        5,
        "gather_grad",
    )
    all_sum = lax.psum_scatter(grad_blocks, "dp", scatter_dimension=0, tiled=True)[0]
    d_proj, normed_part, output_part, d_taps, d_heads, d_lanes = mixer_backward(
        lengths[:, 0], grad_all, w_in, output_weight, *vectors, proj, scan, states, heads
    )
    def rows_of(parts, count):
        flat = jnp.concatenate([part.reshape(-1) for part in parts])
        return jnp.pad(flat, (0, count * 128 - flat.size)).reshape(count, 128)

    added = (d_taps[:K, di:], d_taps[K, di:], moe_gain_grad, router_part)
    own = (
        d_taps[:K, :di],
        d_taps[K, :di],
        d_heads[0, :heads],
        d_heads[1, :heads],
        jnp.sum(d_lanes[1].reshape(heads, PS), axis=1),
        d_lanes[0],
    )
    added_size = sum(part.size for part in added)
    added_rows = -(-added_size // (nd * 1024)) * 8
    own_rows = -(-sum(part.size for part in own) // 128)
    norm_rows = D // 128
    (tokens_grad, norm_gain_grad), (d_sum,), (added_in,) = run_tasks(
        [
            StreamGrad(normed_part, own_tokens, norm_gain.reshape(1, D), after_grad),
            InputGrad(
                gathered,
                d_proj.reshape(nd * rows_t, wcols),
                output_part,
            ),
            Direct("all", "dp", rows_of(added, nd * added_rows).reshape(nd, added_rows, 128)),
        ],
        6,
        "reduce_grads",
    )
    (small_all,), (rest_all,), (slices_all,) = run_tasks(
        [
            Small(added_in, rows_of(own, own_rows), norm_gain_grad),
            Rest(d_sum, all_sum),
            InputRows(d_sum, heads),
        ],
        7,
        "finish",
    )
    input_grad, output_grad, shared_up_grad, shared_down_grad, expert_up_grad, expert_down_grad, (
        block_output
    ) = write_results(
        slices_all,
        rest_all,
        all_sum,
        after_mixer,
        out_sum,
        (
            ((dr, IN_W), F32),
            (output_weight.shape, F32),
            ((dr, 2 * FS), F32),
            ((fsr, D), F32),
            ((el, dr, 2 * FE), F32),
            ((el, FE // nd, D), F32),
            ((rows_t, D), BF),
        ),
    )
    added_all = small_all[:, :added_rows].reshape(-1)
    own_all = small_all[:, added_rows : added_rows + own_rows].reshape(nd, -1)
    norm_gain_grad = jnp.sum(
        small_all[:, added_rows + own_rows : added_rows + own_rows + norm_rows], axis=0
    ).reshape(D)

    def split(flat, parts):
        out, start = [], 0
        for part in parts:
            out.append(flat[..., start : start + part.size].reshape(flat.shape[:-1] + part.shape))
            start += part.size
        return out

    added_taps, added_bias, moe_gain_grad, router_all = split(added_all, added)
    own_taps, own_bias, own_steps, own_decay, own_skip, own_gain = split(own_all, own)
    small = (
        jnp.concatenate([jnp.moveaxis(own_taps, 0, 1).reshape(K, DI), added_taps], axis=1),
        jnp.concatenate([own_bias.reshape(-1), added_bias]),
        own_steps.reshape(-1),
        own_decay.reshape(-1),
        own_skip.reshape(-1),
        norm_gain_grad,
        own_gain.reshape(-1),
        moe_gain_grad.reshape(D),
    )
    router_grad = lax.dynamic_slice_in_dim(router_all, me_d * dr, dr, 1).T
    shape = (MB, 1, loc, D)
    return (
        block_output.reshape(shape),
        tokens_grad.reshape(shape),
        input_grad,
        small[0],
        small[1],
        small[2],
        small[3],
        small[4],
        small[5],
        small[6],
        output_grad.astype(F32),
        small[7],
        router_grad,
        shared_up_grad,
        shared_down_grad,
        expert_up_grad,
        expert_down_grad,
    )


def solution(mesh):
    in_specs = (
        P(None, "expert", "dp", None),
        P(None, "expert", None),
        P(None, "expert", "dp", None),
        P(None, "expert", "dp", None),
        P("dp", None),
        P(),
        P(),
        P(),
        P(),
        P(),
        P(),
        P(),
        P("dp", None),
        P(),
        P("dp", None),
        P("dp", None),
        P("dp", None),
        P("expert", None, None),
        P("expert", None, None),
    )
    out_specs = (
        P(None, "expert", "dp", None),
        P(None, "expert", "dp", None),
        P("dp", None),
        P(),
        P(),
        P(),
        P(),
        P(),
        P(),
        P(),
        P("dp", None),
        P(),
        P("dp", None),
        P("dp", None),
        P("dp", None),
        P("expert", "dp", None),
        P("expert", "dp", None),
    )
    return jax.shard_map(body, mesh=mesh, in_specs=in_specs, out_specs=out_specs, check_vma=False)
```
